32 devices in a mesh: dp: 4 (over x, core), tm: 4 (over z), space: 2 (over y).
Axes of the slice: x: 2, y: 2, z: 4, core: 2. Of those that a mesh axis runs over, the one named last changes fastest.
Arguments:
- query_heads: bfloat16 [4, 4, 256, 3072], P('dp', 'tm', None, 'space')
- key_heads: bfloat16 [4, 4, 256, 3072], P('dp', 'tm', None, 'space')
- value_heads: bfloat16 [4, 4, 256, 3072], P('dp', 'tm', None, 'space')
- cotangent: bfloat16 [4, 4, 256, 3072], P('dp', 'tm', 'space'), may hold values from -6 to 6
- task_ids: int32 [4], P('dp'), may hold values from 0 to 15
- lengths: int32 [4], P('dp'), may hold values from 1 to 4, as said below
- gains: float32 [2, 16, 3072], P(None, None, 'space'), may hold values from 0.5 to 2
Outputs:
- grad_queries: bfloat16 [4, 4, 256, 3072], P('dp', 'tm', None, 'space')
- grad_keys: bfloat16 [4, 4, 256, 3072], P('dp', 'tm', None, 'space')
- grad_gains: float32 [2, 16, 3072], P(None, None, 'space')
The draws below stay inside these ranges and needn't reach their ends.
Inputs may be any that keep to these rules, and one draw needn't show every extreme that they name: `lengths`: at least one clip has all 4 frames valid.
All inputs are finite; a program needn't handle non-finite values.
Results may differ from the reference program's by a relative error of at most 0.003.
The reference program's roundings to bfloat16 on the way count: a program that leaves them out, or rounds other values in their place, can miss the bound.
Values may be sent and summed in bfloat16 or wider, within the bound.
No kernel may reach another device: no remote copies, remote signals or barrier semaphores. Data moves between devices by JAX's collectives and lax.ppermute only.
A program may use at most 128 MiB of HBM per device.

```python
import math
import jax
import jax.numpy as jnp
from jax import lax

HEADS = 24
HEAD_DIM = 128
TASKS = 16
CLIPS = 4
FRAMES = 4
PATCHES = 256
FEAT = 3072


def clip_frames(key, spread):
    clip_part = jnp.clip(jax.random.normal(jax.random.fold_in(key, 1), (CLIPS, 1, PATCHES, HEADS * HEAD_DIM), jnp.float32), -6.0, 6.0)
    frame_part = jnp.clip(jax.random.normal(jax.random.fold_in(key, 2), (CLIPS, FRAMES, PATCHES, HEADS * HEAD_DIM), jnp.float32), -6.0, 6.0)
    mixed = (1.0 - spread * spread) ** 0.5 * clip_part + spread * frame_part
    return jnp.clip(mixed, -6.0, 6.0)


def draw_query_heads(key, part):
    key = jax.random.fold_in(key, 11)
    normal_field = clip_frames(key, 0.25)
    return normal_field.astype(jnp.bfloat16)


def draw_key_heads(key, part):
    key = jax.random.fold_in(key, 12)
    normal_field = clip_frames(key, 0.25)
    return normal_field.astype(jnp.bfloat16)


def draw_value_heads(key, part):
    key = jax.random.fold_in(key, 14)
    normal_field = clip_frames(key, 0.25)
    return normal_field.astype(jnp.bfloat16)


def draw_lengths(key, part):
    key = jax.random.fold_in(key, 13)
    drawn = jax.random.randint(key, (CLIPS,), max(1, FRAMES // 4), FRAMES + 1, dtype=jnp.int32)
    chosen = jax.random.randint(jax.random.fold_in(key, 1), (), 0, CLIPS, dtype=jnp.int32)
    return jnp.where(jnp.arange(CLIPS, dtype=jnp.int32) == chosen, FRAMES, drawn).astype(jnp.int32)


def with_ends(entries, key, least, largest):
    index_at = [jax.random.randint(jax.random.fold_in(key, axis), (), 0, length) for axis, length in enumerate(entries.shape)]
    longest = entries.shape.index(max(entries.shape))
    beside = index_at[:longest] + [(index_at[longest] + 1) % entries.shape[longest]] + index_at[longest + 1:]
    return entries.at[tuple(index_at)].set(least).at[tuple(beside)].set(largest)


def block_levels(stream_key, dims, shards, least, high):
    loudness = 1.0
    for position, shards_of in shards:
        heights = jax.random.uniform(jax.random.fold_in(jax.random.fold_in(stream_key, 6), position), (shards_of,), jnp.float32, least / len(shards), high / len(shards))
        loudness = loudness * jnp.repeat(jnp.exp(heights), dims[position] // shards_of).reshape((-1,) + (1,) * (len(dims) - 1 - position))
    return loudness


def centred(own_key, dims, scale, most, pieces=(), held_as=jnp.bfloat16):
    values = scale * jax.random.normal(own_key, dims, jnp.float32)
    if pieces:
        values = values * block_levels(own_key, dims, pieces, -0.22, 0.18)
    return jnp.clip(values, -most, most).astype(held_as)


def setup_inputs(seed: int = 0) -> dict:
    keys = jax.random.split(jax.random.key(seed), 8)
    query_heads = draw_query_heads(jax.random.fold_in(keys[7], 71), 0)
    key_heads = draw_key_heads(jax.random.fold_in(keys[7], 71), 0)
    value_heads = draw_value_heads(jax.random.fold_in(keys[7], 71), 0)
    cotangent = centred(keys[3], (CLIPS, FRAMES, PATCHES, FEAT), 1.0, 6.0, ((0, 4), (1, 4), (2, 2)))
    task_ids = with_ends(jax.random.randint(keys[4], (CLIPS,), 0, TASKS), jax.random.fold_in(keys[4], 1), 0, TASKS - 1).astype(jnp.int32)
    lengths = draw_lengths(jax.random.fold_in(keys[7], 71), 0)
    gains = jnp.clip(jnp.exp(math.log(2.0) - 1.3862944 * jax.random.uniform(keys[6], (2, TASKS, FEAT), jnp.float32) ** block_levels(keys[6], (2, TASKS, FEAT), ((2, 2),), -0.2, 0.2)), 0.5, 2.0)
    return dict(query_heads=query_heads, key_heads=key_heads, value_heads=value_heads, cotangent=cotangent, task_ids=task_ids, lengths=lengths, gains=gains)


def head_probs(queries, key_rows):
    score_scale = queries.shape[-1] ** (-0.5)
    scores = jnp.dot(queries, key_rows.T, preferred_element_type=jnp.float32) * score_scale
    return jax.nn.softmax(scores, axis=-1)

def head_backward(weights, queries, key_rows, value_rows, grad_out):
    score_scale = queries.shape[-1] ** (-0.5)
    grad_weights = jnp.dot(grad_out, value_rows.T, preferred_element_type=jnp.float32)
    grad_scores = weights * (grad_weights - lax.optimization_barrier(jnp.sum(grad_weights * weights, axis=-1, keepdims=True)))
    scaled_low = (grad_scores * score_scale).astype(jnp.bfloat16)
    grad_queries = jnp.dot(scaled_low, key_rows, preferred_element_type=jnp.float32).astype(jnp.bfloat16)
    grad_keys = jnp.dot(scaled_low.T, queries, preferred_element_type=jnp.float32).astype(jnp.bfloat16)
    return (grad_queries, grad_keys)

def temporal_grads(attended, upstream, gain_query, gain_keys, length):
    highest = lax.Precision.HIGHEST
    frames = attended.shape[0]
    score_scale = attended.shape[-1] ** (-0.5)
    floats = attended.astype(jnp.float32)
    inverse_rms = lax.rsqrt(lax.optimization_barrier(jnp.mean(floats * floats, axis=-1, keepdims=True)) + 1e-06)
    normed = floats * inverse_rms
    t_query = normed * gain_query
    t_keys = normed * gain_keys
    scores = jnp.einsum('txhd,uxhd->xhtu', t_query, t_keys, precision=highest) * score_scale
    frame_ids = jnp.arange(frames, dtype=jnp.int32)
    allowed = (frame_ids[None, :] <= frame_ids[:, None]) & (frame_ids[None, :] < length)
    scores = jnp.where(allowed, scores, -1e+30)
    weights = jax.nn.softmax(scores, axis=-1)
    weights_low = lax.optimization_barrier(weights.astype(jnp.bfloat16)).astype(jnp.float32)
    valid_rows = (frame_ids < length).astype(jnp.float32)
    masked = upstream.astype(jnp.float32) * valid_rows[:, None, None, None]
    grad_weights = jnp.einsum('txhd,uxhd->xhtu', masked, floats, precision=highest)
    from_values = jnp.einsum('xhtu,txhd->uxhd', weights_low, masked, precision=highest)
    grad_scores = weights * (grad_weights - lax.optimization_barrier(jnp.sum(grad_weights * weights, axis=-1, keepdims=True))) * score_scale
    grad_tquery = jnp.einsum('xhtu,uxhd->txhd', grad_scores, t_keys, precision=highest)
    grad_tkeys = jnp.einsum('xhtu,txhd->uxhd', grad_scores, t_query, precision=highest)
    grad_normed = grad_tquery * gain_query + grad_tkeys * gain_keys
    grad_gain_query = lax.optimization_barrier(jnp.sum(grad_tquery * normed, axis=(0, 1)))
    grad_gain_keys = lax.optimization_barrier(jnp.sum(grad_tkeys * normed, axis=(0, 1)))
    from_norm = inverse_rms * (grad_normed - normed * lax.optimization_barrier(jnp.mean(grad_normed * normed, axis=-1, keepdims=True)))
    grad_total = (masked + from_values + from_norm).astype(jnp.bfloat16)
    return (grad_total, grad_gain_query, grad_gain_keys)

def to_heads(field):
    merged = field.reshape(CLIPS * FRAMES, PATCHES, HEADS, HEAD_DIM)
    return jnp.transpose(merged, (0, 2, 1, 3)).reshape(CLIPS * FRAMES * HEADS, PATCHES, HEAD_DIM)

def from_heads(stacked):
    merged = stacked.reshape(CLIPS * FRAMES, HEADS, PATCHES, HEAD_DIM)
    return jnp.transpose(merged, (0, 2, 1, 3)).reshape(CLIPS, FRAMES, PATCHES, HEADS * HEAD_DIM)

def reference(query_heads, key_heads, value_heads, cotangent, task_ids, lengths, gains):
    head_queries = to_heads(query_heads)
    head_keys = to_heads(key_heads)
    head_values = to_heads(value_heads)

    def forward_element(element):
        weights = head_probs(element[0], element[1])
        return jnp.dot(weights.astype(jnp.bfloat16), element[2], preferred_element_type=jnp.float32).astype(jnp.bfloat16)
    attended = from_heads(lax.map(forward_element, (head_queries, head_keys, head_values)))

    def temporal_element(element):
        clip_attended, clip_upstream, task_index, length = element
        gain_query = lax.dynamic_index_in_dim(gains[0], task_index, 0, keepdims=False).reshape(HEADS, HEAD_DIM)
        gain_keys = lax.dynamic_index_in_dim(gains[1], task_index, 0, keepdims=False).reshape(HEADS, HEAD_DIM)
        grad_total, grad_gq, grad_gk = temporal_grads(clip_attended.reshape(FRAMES, PATCHES, HEADS, HEAD_DIM), clip_upstream.reshape(FRAMES, PATCHES, HEADS, HEAD_DIM), gain_query, gain_keys, length)
        return (grad_total.reshape(FRAMES, PATCHES, HEADS * HEAD_DIM), grad_gq.reshape(HEADS * HEAD_DIM), grad_gk.reshape(HEADS * HEAD_DIM))
    grad_attended, grad_gq, grad_gk = lax.map(temporal_element, (attended, cotangent, task_ids, lengths))
    selector = (task_ids[:, None] == jnp.arange(TASKS, dtype=jnp.int32)[None, :]).astype(jnp.float32)
    grad_gains = jnp.stack([jnp.dot(selector.T, grad_gq, precision=lax.Precision.HIGHEST), jnp.dot(selector.T, grad_gk, precision=lax.Precision.HIGHEST)])
    head_grads = to_heads(grad_attended)

    def backward_element(element):
        weights = head_probs(element[0], element[1])
        return head_backward(weights, element[0], element[1], element[2], element[3])
    grad_queries, grad_keys = lax.map(backward_element, (head_queries, head_keys, head_values, head_grads))
    return (from_heads(grad_queries), from_heads(grad_keys), grad_gains)
```

```python
import functools

import jax
import jax.numpy as jnp
from jax import lax
from jax.experimental import pallas as pl
from jax.experimental.pallas import tpu as pltpu
from jax.sharding import PartitionSpec as P

HEAD_DIM = 128
GROUP = 16
VMEM_BYTES = 48 * 1024 * 1024


def params():
    return pltpu.CompilerParams(vmem_limit_bytes=VMEM_BYTES)


def columns_dot(left, right):
    return lax.dot_general(
        left, right, (((1,), (1,)), ((), ())), preferred_element_type=jnp.float32
    )


def dot(left, right):
    return jnp.dot(left, right, preferred_element_type=jnp.float32)


def forward_kernel(query_ref, key_ref, value_ref, weights_ref, attended_ref):
    score_scale = HEAD_DIM ** (-0.5)
    for head in range(weights_ref.shape[0]):
        cols = pl.ds(head * HEAD_DIM, HEAD_DIM)
        scores = columns_dot(key_ref[:, cols], query_ref[:, cols])
        largest = jnp.max(scores, axis=0, keepdims=True)
        raised = jnp.exp((scores - largest) * score_scale)
        weights = raised * (1.0 / jnp.sum(raised, axis=0, keepdims=True))
        weights_ref[head] = weights
        attended = dot(value_ref[:, cols].T, weights.astype(jnp.bfloat16))
        attended_ref[head] = attended.astype(jnp.bfloat16)


def forward(queries, key_rows, values, per_step):
    patches, feat = queries.shape
    heads = feat // HEAD_DIM
    field = pl.BlockSpec((patches, per_step * HEAD_DIM), lambda i: (0, i))
    return pl.pallas_call(
        forward_kernel,
        grid=(heads // per_step,),
        in_specs=[field] * 3,
        out_specs=[
            pl.BlockSpec((per_step, patches, patches), lambda i: (i, 0, 0)),
            pl.BlockSpec((per_step, HEAD_DIM, patches), lambda i: (i, 0, 0)),
        ],
        out_shape=[
            jax.ShapeDtypeStruct((heads, patches, patches), jnp.float32),
            jax.ShapeDtypeStruct((heads, HEAD_DIM, patches), jnp.bfloat16),
        ],
        compiler_params=params(),
        cost_estimate=pl.CostEstimate(
            flops=4 * heads * patches * patches * HEAD_DIM,
            bytes_accessed=heads * patches * (patches * 4 + 8 * HEAD_DIM),
            transcendentals=heads * patches * patches,
        ),
        name="spatial_forward",
    )(queries, key_rows, values)


def backward_kernel(query_ref, key_ref, value_ref, weights_ref, grad_ref, gq_ref, gk_ref):
    score_scale = HEAD_DIM ** (-0.5)
    for head in range(weights_ref.shape[0]):
        cols = pl.ds(head * HEAD_DIM, HEAD_DIM)
        weights = weights_ref[head]
        spatial_grad = dot(value_ref[:, cols], grad_ref[head])
        row_sum = jnp.sum(spatial_grad * weights, axis=0, keepdims=True)
        scores = (weights * (spatial_grad - row_sum) * score_scale).astype(jnp.bfloat16)
        gk_ref[:, cols] = dot(scores, query_ref[:, cols]).astype(jnp.bfloat16)
        grad_query = dot(key_ref[:, cols].T, scores).astype(jnp.bfloat16)
        gq_ref[:, cols] = grad_query.T


def backward(queries, key_rows, values, weights, grads, per_step):
    patches, feat = queries.shape
    heads = feat // HEAD_DIM
    field = pl.BlockSpec((patches, per_step * HEAD_DIM), lambda i: (0, i))
    return pl.pallas_call(
        backward_kernel,
        grid=(heads // per_step,),
        in_specs=[
            field,
            field,
            field,
            pl.BlockSpec((per_step, patches, patches), lambda i: (i, 0, 0)),
            pl.BlockSpec((per_step, HEAD_DIM, patches), lambda i: (i, 0, 0)),
        ],
        out_specs=[field, field],
        out_shape=[jax.ShapeDtypeStruct((patches, feat), jnp.bfloat16)] * 2,
        compiler_params=params(),
        cost_estimate=pl.CostEstimate(
            flops=6 * heads * patches * patches * HEAD_DIM,
            bytes_accessed=heads * patches * (patches * 4 + 12 * HEAD_DIM),
            transcendentals=0,
        ),
        name="spatial_backward",
    )(queries, key_rows, values, weights, grads)


def turn_kernel(field_ref, turned_ref):
    for head in range(turned_ref.shape[2]):
        cols = pl.ds(head * HEAD_DIM, HEAD_DIM)
        turned_ref[0, 0, head] = field_ref[:, cols].T


def turn(field, frames, spaces):
    patches, feat = field.shape
    heads = feat // (frames * spaces * HEAD_DIM)
    return pl.pallas_call(
        turn_kernel,
        grid=(frames, spaces),
        in_specs=[pl.BlockSpec((patches, heads * HEAD_DIM), lambda f, s: (0, s * frames + f))],
        out_specs=pl.BlockSpec((1, 1, heads, HEAD_DIM, patches), lambda f, s: (f, s, 0, 0, 0)),
        out_shape=jax.ShapeDtypeStruct((frames, spaces, heads, HEAD_DIM, patches), jnp.bfloat16),
        compiler_params=params(),
        cost_estimate=pl.CostEstimate(
            flops=0, bytes_accessed=4 * patches * feat, transcendentals=0
        ),
        name="turn_cotangent",
    )(field)


def temporal_kernel(length_ref, attended_ref, upstream_ref, gain_ref, grad_ref, mixed_ref, mixed_sum):
    frames, _, feat, lanes = attended_ref.shape
    half = GROUP // 2
    score_scale = feat ** (-0.5)
    length = length_ref[0]
    pairs = [(t, u) for t in range(frames) for u in range(t + 1)]
    every = range(frames)
    valid = [jnp.where(t < length, 1.0, 0.0).astype(jnp.float32) for t in every]
    bias = [jnp.where(u < length, 0.0, -1e30).astype(jnp.float32) for u in every]

    def load(ref, t, group):
        index = (t, 0) if len(ref.shape) == 4 else (t, 0, 0)
        block = ref[index + (pl.ds(group * GROUP, GROUP), slice(None))].astype(jnp.float32)
        return block[:half], block[half:]

    def total(piece):
        return jnp.broadcast_to(jnp.sum(piece, axis=0, keepdims=True), (half, lanes))

    squares = [jnp.zeros((half, lanes), jnp.float32) for _ in every]
    for group in range(feat // GROUP):
        for t in every:
            low, high = load(attended_ref, t, group)
            squares[t] = squares[t] + (low * low + high * high)
    inverse = [lax.rsqrt(total(squares[t]) * (1.0 / feat) + 1e-06) for t in every]

    raw = {pair: jnp.zeros((half, lanes), jnp.float32) for pair in pairs}
    grad = {pair: jnp.zeros((half, lanes), jnp.float32) for pair in pairs}
    for group in range(feat // GROUP):
        fields = [load(attended_ref, t, group) for t in every]
        ups = [load(upstream_ref, t, group) for t in every]
        for side in range(2):
            rows = pl.ds(group * GROUP + side * half, half)
            gain = gain_ref[0, rows, :]
            normed = [fields[t][side] * inverse[t] for t in every]
            gained = [normed[t] * gain for t in every]
            for t, u in pairs:
                raw[t, u] = raw[t, u] + gained[t] * normed[u]
                grad[t, u] = grad[t, u] + ups[t][side] * fields[u][side]

    value_part, score_part = {}, {}
    for t in every:
        seen = range(t + 1)
        for u in seen:
            raw[t, u] = total(raw[t, u])
            grad[t, u] = total(grad[t, u]) * valid[t]
        scores = [raw[t, u] * score_scale + bias[u] for u in seen]
        largest = functools.reduce(jnp.maximum, scores)
        raised = [jnp.exp(score - largest) for score in scores]
        over = 1.0 / functools.reduce(jnp.add, raised)
        weights = [piece * over for piece in raised]
        mean_grad = functools.reduce(jnp.add, [weights[u] * grad[t, u] for u in seen])
        for u in seen:
            rounded = weights[u].astype(jnp.bfloat16).astype(jnp.float32)
            value_part[t, u] = (rounded + (1.0 if u == t else 0.0)) * valid[t]
            score_part[t, u] = weights[u] * (grad[t, u] - mean_grad) * score_scale

    both = {(t, u): score_part[t, u] * (2.0 if t == u else 1.0) for t, u in pairs}
    both.update({(u, t): both[t, u] for t, u in pairs})
    raw.update({(u, t): raw[t, u] for t, u in pairs})
    mean_part = [
        functools.reduce(jnp.add, [both[u, v] * raw[u, v] for v in every]) * (1.0 / feat)
        for u in every
    ]

    @pl.when(pl.program_id(1) == 0)
    def _():
        mixed_sum[...] = jnp.zeros_like(mixed_sum)

    for group in range(feat // GROUP):
        fields = [load(attended_ref, t, group) for t in every]
        ups = [load(upstream_ref, t, group) for t in every]
        outs = [[] for _ in every]
        for side in range(2):
            rows = pl.ds(group * GROUP + side * half, half)
            gain = gain_ref[0, rows, :]
            normed = [fields[t][side] * inverse[t] for t in every]
            mixed = jnp.zeros((half, lanes), jnp.float32)
            for u in every:
                crossed = functools.reduce(jnp.add, [both[u, v] * normed[v] for v in every])
                mixed = mixed + crossed * normed[u]
                from_norm = inverse[u] * (gain * crossed - normed[u] * mean_part[u])
                direct = functools.reduce(
                    jnp.add, [value_part[t, u] * ups[t][side] for t in range(u, frames)]
                )
                outs[u].append(direct + from_norm)
            mixed_sum[rows, :] += mixed
        for u in every:
            grad_ref[u, 0, pl.ds(group * GROUP, GROUP), :] = jnp.concatenate(
                outs[u], axis=0
            ).astype(jnp.bfloat16)

    @pl.when(pl.program_id(1) == pl.num_programs(1) - 1)
    def _():
        summed = jnp.sum(mixed_sum[...].T, axis=0, keepdims=True) * 0.5
        mixed_ref[0] = jnp.broadcast_to(summed, mixed_ref.shape[1:])


def temporal(attended, upstream, gain, length):
    frames, heads, feat, patches = attended.shape
    spaces = upstream.shape[1]
    lanes = patches // spaces
    return pl.pallas_call(
        temporal_kernel,
        grid=(heads, spaces),
        in_specs=[
            pl.BlockSpec(memory_space=pltpu.SMEM),
            pl.BlockSpec((frames, 1, feat, lanes), lambda h, s: (0, h, 0, s)),
            pl.BlockSpec((frames, 1, 1, feat, lanes), lambda h, s: (0, s, h, 0, 0)),
            pl.BlockSpec((1, feat, lanes), lambda h, s: (h, 0, 0)),
        ],
        out_specs=[
            pl.BlockSpec((frames, 1, feat, lanes), lambda h, s: (0, h, 0, s)),
            pl.BlockSpec((1, 8, feat), lambda h, s: (h, 0, 0)),
        ],
        out_shape=[
            jax.ShapeDtypeStruct(attended.shape, jnp.bfloat16),
            jax.ShapeDtypeStruct((heads, 8, feat), jnp.float32),
        ],
        scratch_shapes=[pltpu.VMEM((feat, lanes), jnp.float32)],
        compiler_params=params(),
        cost_estimate=pl.CostEstimate(
            flops=heads * patches * feat * 200,
            bytes_accessed=6 * frames * heads * patches * feat,
            transcendentals=heads * patches * 16,
        ),
        name="temporal",
    )(length, attended, upstream, gain)


def split_by_heads(query_heads, key_heads, value_heads, cotangent, task_ids, lengths, gains, frames, spaces):
    patches, feat = query_heads.shape[2:]
    heads = feat // HEAD_DIM
    own = heads // frames
    tasks = gains.shape[1]
    queries, key_rows, values = (
        field.reshape(patches, feat) for field in (query_heads, key_heads, value_heads)
    )
    turned = turn(cotangent.reshape(cotangent.shape[2:]), frames, spaces)
    upstream = lax.all_to_all(
        turned.reshape((frames * spaces,) + turned.shape[2:]),
        ("tm", "space"),
        split_axis=0,
        concat_axis=0,
        tiled=True,
    ).reshape(turned.shape)
    weights, attended = forward(queries, key_rows, values, own)
    all_attended = lax.all_to_all(
        attended.reshape(frames, own, HEAD_DIM, patches), "tm", split_axis=0, concat_axis=0, tiled=True
    )
    rows = lax.dynamic_index_in_dim(gains, task_ids[0], 1, keepdims=False)
    product = lax.dynamic_slice_in_dim(
        rows[0] * rows[1], lax.axis_index("tm") * (own * HEAD_DIM), own * HEAD_DIM, 0
    )
    gain = jnp.broadcast_to(
        product.reshape(own, HEAD_DIM, 1), (own, HEAD_DIM, patches // spaces)
    )
    grads, mixed = temporal(all_attended, upstream, gain, lengths)
    returned = lax.all_to_all(grads, "tm", split_axis=0, concat_axis=0, tiled=True)
    marked = jnp.concatenate(
        [mixed[:, 0], jnp.full((1, HEAD_DIM), task_ids[0].astype(jnp.float32))], axis=0
    )
    gathered = lax.all_gather(marked, ("dp", "tm")).reshape(-1, frames, own + 1, HEAD_DIM)
    clip_tasks = gathered[:, 0, own, 0]
    clip_mixed = gathered[:, :, :own].reshape(-1, 1, feat)
    chosen = clip_tasks[:, None] == jnp.arange(tasks, dtype=jnp.float32)
    task_mixed = jnp.sum(jnp.where(chosen[:, :, None], clip_mixed, 0.0), axis=0)
    grad_gains = jnp.stack([gains[1] * task_mixed, gains[0] * task_mixed])
    grad_queries, grad_keys = backward(
        queries, key_rows, values, weights, returned.reshape(heads, HEAD_DIM, patches), own
    )
    return (
        grad_queries.reshape(query_heads.shape),
        grad_keys.reshape(query_heads.shape),
        grad_gains,
    )


def temporal_grads(attended, upstream, gain_query, gain_keys, length):
    highest = lax.Precision.HIGHEST
    frames = attended.shape[0]
    score_scale = attended.shape[-1] ** (-0.5)
    floats = attended.astype(jnp.float32)
    inverse_rms = lax.rsqrt(jnp.mean(floats * floats, axis=-1, keepdims=True) + 1e-06)
    normed = floats * inverse_rms
    t_query = normed * gain_query
    t_keys = normed * gain_keys
    scores = jnp.einsum("txhd,uxhd->xhtu", t_query, t_keys, precision=highest) * score_scale
    frame_ids = jnp.arange(frames, dtype=jnp.int32)
    allowed = (frame_ids[None, :] <= frame_ids[:, None]) & (frame_ids[None, :] < length)
    scores = jnp.where(allowed, scores, -1e30)
    weights = jax.nn.softmax(scores, axis=-1)
    weights_low = lax.optimization_barrier(weights.astype(jnp.bfloat16)).astype(jnp.float32)
    valid_rows = (frame_ids < length).astype(jnp.float32)
    masked = upstream.astype(jnp.float32) * valid_rows[:, None, None, None]
    grad_weights = jnp.einsum("txhd,uxhd->xhtu", masked, floats, precision=highest)
    from_values = jnp.einsum("xhtu,txhd->uxhd", weights_low, masked, precision=highest)
    grad_scores = (
        weights
        * (grad_weights - jnp.sum(grad_weights * weights, axis=-1, keepdims=True))
        * score_scale
    )
    grad_tquery = jnp.einsum("xhtu,uxhd->txhd", grad_scores, t_keys, precision=highest)
    grad_tkeys = jnp.einsum("xhtu,txhd->uxhd", grad_scores, t_query, precision=highest)
    grad_normed = grad_tquery * gain_query + grad_tkeys * gain_keys
    grad_gain_query = jnp.sum(grad_tquery * normed, axis=(0, 1))
    grad_gain_keys = jnp.sum(grad_tkeys * normed, axis=(0, 1))
    from_norm = inverse_rms * (
        grad_normed - normed * jnp.mean(grad_normed * normed, axis=-1, keepdims=True)
    )
    grad_total = (masked + from_values + from_norm).astype(jnp.bfloat16)
    return (grad_total, grad_gain_query, grad_gain_keys)


def split_by_patches(query_heads, key_heads, value_heads, cotangent, task_ids, lengths, gains):
    patches, feat = query_heads.shape[2:]
    heads = feat // HEAD_DIM
    queries, key_rows, values = (
        field.reshape(patches, feat) for field in (query_heads, key_heads, value_heads)
    )
    weights, attended = forward(queries, key_rows, values, 1)
    attended_field = jnp.transpose(attended, (2, 0, 1)).reshape(1, 1, patches, feat)
    upstream = lax.all_to_all(
        lax.all_to_all(cotangent, "space", split_axis=3, concat_axis=2, tiled=True),
        "tm",
        split_axis=2,
        concat_axis=1,
        tiled=True,
    )
    frames_attended = lax.all_to_all(attended_field, "tm", split_axis=2, concat_axis=1, tiled=True)
    frames, local_patches = frames_attended.shape[1:3]
    selector = (task_ids[0] == jnp.arange(gains.shape[1], dtype=jnp.int32)).astype(jnp.float32)
    gain_query = jnp.sum(selector[:, None] * gains[0], axis=0).reshape(heads, HEAD_DIM)
    gain_keys = jnp.sum(selector[:, None] * gains[1], axis=0).reshape(heads, HEAD_DIM)
    grad_total, grad_gq, grad_gk = temporal_grads(
        frames_attended.reshape(frames, local_patches, heads, HEAD_DIM),
        upstream.reshape(frames, local_patches, heads, HEAD_DIM),
        gain_query,
        gain_keys,
        lengths[0],
    )
    gain_terms = jnp.stack(
        [
            selector[:, None] * grad_gq.reshape(1, feat),
            selector[:, None] * grad_gk.reshape(1, feat),
        ]
    )
    grad_gains = lax.psum(gain_terms, ("dp", "tm"))
    returned = lax.all_to_all(
        grad_total.reshape(1, frames, local_patches, feat),
        "tm",
        split_axis=1,
        concat_axis=2,
        tiled=True,
    )
    head_grads = jnp.transpose(returned.reshape(patches, heads, HEAD_DIM), (1, 2, 0))
    grad_queries, grad_keys = backward(queries, key_rows, values, weights, head_grads, 1)
    return (
        grad_queries.reshape(query_heads.shape),
        grad_keys.reshape(query_heads.shape),
        grad_gains,
    )


def solution(mesh):
    frames, spaces = mesh.shape["tm"], mesh.shape["space"]

    def local(query_heads, *others):
        heads = query_heads.shape[3] // HEAD_DIM
        if frames <= 4 and heads % frames == 0:
            return split_by_heads(query_heads, *others, frames, spaces)
        return split_by_patches(query_heads, *others)

    return jax.shard_map(
        local,
        mesh=mesh,
        in_specs=(
            P("dp", "tm", None, "space"),
            P("dp", "tm", None, "space"),
            P("dp", "tm", None, "space"),
            P("dp", "tm", "space", None),
            P("dp"),
            P("dp"),
            P(None, None, "space"),
        ),
        out_specs=(
            P("dp", "tm", None, "space"),
            P("dp", "tm", None, "space"),
            P(None, None, "space"),
        ),
        check_vma=False,
    )
```

```python
import functools

import jax
import jax.numpy as jnp
from jax import lax
from jax.experimental import pallas as pl
from jax.experimental.pallas import tpu as pltpu
from jax.sharding import PartitionSpec as P

HEAD_DIM = 128
GROUP = 16
VMEM_BYTES = 48 * 1024 * 1024


def params():
    return pltpu.CompilerParams(vmem_limit_bytes=VMEM_BYTES)


def columns_dot(left, right):
    return lax.dot_general(
        left, right, (((1,), (1,)), ((), ())), preferred_element_type=jnp.float32
    )


def dot(left, right):
    return jnp.dot(left, right, preferred_element_type=jnp.float32)


def partner(scalars, distance):
    return jnp.bitwise_xor(scalars[0], distance)


def forward_kernel(scalars, query_ref, key_ref, value_ref, weights_ref, *attended_refs):
    score_scale = HEAD_DIM ** (-0.5)
    pieces = []
    for head in range(weights_ref.shape[0]):
        cols = pl.ds(head * HEAD_DIM, HEAD_DIM)
        scores = columns_dot(key_ref[:, cols], query_ref[:, cols])
        largest = jnp.max(scores, axis=0, keepdims=True)
        raised = jnp.exp((scores - largest) * score_scale)
        weights = raised * (1.0 / jnp.sum(raised, axis=0, keepdims=True))
        weights_ref[head] = weights
        attended = dot(value_ref[:, cols].T, weights.astype(jnp.bfloat16))
        pieces.append(attended.astype(jnp.bfloat16))
    for step, attended_ref in enumerate(attended_refs):

        @pl.when(pl.program_id(0) == step)
        def _():
            for head, piece in enumerate(pieces):
                attended_ref[head] = piece


def forward(scalars, queries, key_rows, values, groups):
    patches, feat = queries.shape
    heads = feat // HEAD_DIM
    own = heads // groups
    field = pl.BlockSpec((patches, own * HEAD_DIM), lambda d, sc: (0, partner(sc, d)))
    whole = pl.BlockSpec((own, HEAD_DIM, patches), lambda d, sc: (0, 0, 0))
    weights, *attended = pl.pallas_call(
        forward_kernel,
        grid_spec=pltpu.PrefetchScalarGridSpec(
            num_scalar_prefetch=1,
            grid=(groups,),
            in_specs=[field] * 3,
            out_specs=[pl.BlockSpec((own, patches, patches), lambda d, sc: (d, 0, 0))]
            + [whole] * groups,
        ),
        out_shape=[jax.ShapeDtypeStruct((heads, patches, patches), jnp.float32)]
        + [jax.ShapeDtypeStruct((own, HEAD_DIM, patches), jnp.bfloat16)] * groups,
        compiler_params=params(),
        cost_estimate=pl.CostEstimate(
            flops=4 * heads * patches * patches * HEAD_DIM,
            bytes_accessed=heads * patches * (patches * 4 + 8 * HEAD_DIM),
            transcendentals=heads * patches * patches,
        ),
        name="spatial_forward",
    )(scalars, queries, key_rows, values)
    return weights, attended


def backward_kernel(scalars, query_ref, key_ref, value_ref, weights_ref, grad_ref, *refs):
    gq_ref, gk_ref = refs[-2:]
    score_scale = HEAD_DIM ** (-0.5)
    for head in range(weights_ref.shape[0]):
        cols = pl.ds(head * HEAD_DIM, HEAD_DIM)
        weights = weights_ref[head]
        spatial_grad = dot(value_ref[:, cols], grad_ref[head])
        row_sum = jnp.sum(spatial_grad * weights, axis=0, keepdims=True)
        scores = (weights * (spatial_grad - row_sum) * score_scale).astype(jnp.bfloat16)
        gk_ref[:, cols] = dot(scores, query_ref[:, cols]).astype(jnp.bfloat16)
        grad_query = dot(key_ref[:, cols].T, scores).astype(jnp.bfloat16)
        gq_ref[:, cols] = grad_query.T


def backward(scalars, queries, key_rows, values, weights, grads, distance, earlier):
    patches, feat = queries.shape
    own = grads.shape[0]
    field = pl.BlockSpec(
        (patches, HEAD_DIM), lambda i, sc: (0, partner(sc, distance) * own + i)
    )
    return pl.pallas_call(
        backward_kernel,
        grid_spec=pltpu.PrefetchScalarGridSpec(
            num_scalar_prefetch=1,
            grid=(own,),
            in_specs=[
                field,
                field,
                field,
                pl.BlockSpec((1, patches, patches), lambda i, sc: (distance * own + i, 0, 0)),
                pl.BlockSpec((1, HEAD_DIM, patches), lambda i, sc: (i, 0, 0)),
            ]
            + [pl.BlockSpec(memory_space=pl.ANY)] * len(earlier),
            out_specs=[field, field],
        ),
        out_shape=[jax.ShapeDtypeStruct((patches, feat), jnp.bfloat16)] * 2,
        input_output_aliases={6 + index: index for index in range(len(earlier))},
        compiler_params=params(),
        cost_estimate=pl.CostEstimate(
            flops=6 * own * patches * patches * HEAD_DIM,
            bytes_accessed=own * patches * (patches * 4 + 12 * HEAD_DIM),
            transcendentals=0,
        ),
        name="spatial_backward",
    )(scalars, queries, key_rows, values, weights, grads, *earlier)


def turn_kernel(spaces, scalars, *refs):
    turned_ref = refs[-1]
    for index, ref in enumerate(refs[:-1]):
        frame = partner(scalars, index // spaces)
        part = jnp.bitwise_xor(scalars[1], index % spaces)
        turned_ref[frame, part, 0] = ref[...].T


def turn(scalars, pieces, frames, spaces):
    patches, feat = pieces[0].shape
    heads = feat // HEAD_DIM
    return pl.pallas_call(
        functools.partial(turn_kernel, spaces),
        grid_spec=pltpu.PrefetchScalarGridSpec(
            num_scalar_prefetch=1,
            grid=(heads,),
            in_specs=[pl.BlockSpec((patches, HEAD_DIM), lambda i, sc: (0, i))] * len(pieces),
            out_specs=pl.BlockSpec(
                (frames, spaces, 1, HEAD_DIM, patches), lambda i, sc: (0, 0, i, 0, 0)
            ),
        ),
        out_shape=jax.ShapeDtypeStruct((frames, spaces, heads, HEAD_DIM, patches), jnp.bfloat16),
        compiler_params=params(),
        cost_estimate=pl.CostEstimate(
            flops=0, bytes_accessed=4 * len(pieces) * patches * feat, transcendentals=0
        ),
        name="turn_cotangent",
    )(scalars, *pieces)


def temporal_part(length, attended_ref, upstream_ref, gain_ref, grad_ref, mixed_sum, part):
    frames, feat, _ = attended_ref.shape
    lanes = upstream_ref.shape[-1]
    here = pl.ds(part * lanes, lanes)
    half = GROUP // 2
    score_scale = feat ** (-0.5)
    pairs = [(t, u) for t in range(frames) for u in range(t + 1)]
    every = range(frames)
    valid = [jnp.where(t < length, 1.0, 0.0).astype(jnp.float32) for t in every]
    bias = [jnp.where(u < length, 0.0, -1e30).astype(jnp.float32) for u in every]

    def split(block):
        block = block.astype(jnp.float32)
        return block[:half], block[half:]

    def load_fields(group):
        return [split(attended_ref[t, pl.ds(group * GROUP, GROUP), here]) for t in every]

    def load_ups(group):
        return [split(upstream_ref[t, part, 0, pl.ds(group * GROUP, GROUP), :]) for t in every]

    def total(piece):
        return jnp.broadcast_to(jnp.sum(piece, axis=0, keepdims=True), (half, lanes))

    squares = [jnp.zeros((half, lanes), jnp.float32) for _ in every]
    for group in range(feat // GROUP):
        for t, (low, high) in enumerate(load_fields(group)):
            squares[t] = squares[t] + (low * low + high * high)
    inverse = [lax.rsqrt(total(squares[t]) * (1.0 / feat) + 1e-06) for t in every]

    raw = {pair: jnp.zeros((half, lanes), jnp.float32) for pair in pairs}
    grad = {pair: jnp.zeros((half, lanes), jnp.float32) for pair in pairs}
    for group in range(feat // GROUP):
        fields, ups = load_fields(group), load_ups(group)
        for side in range(2):
            gain = gain_ref[0, pl.ds(group * GROUP + side * half, half), :]
            normed = [fields[t][side] * inverse[t] for t in every]
            gained = [normed[t] * gain for t in every]
            for t, u in pairs:
                raw[t, u] = raw[t, u] + gained[t] * normed[u]
                grad[t, u] = grad[t, u] + ups[t][side] * fields[u][side]

    value_part, score_part = {}, {}
    for t in every:
        seen = range(t + 1)
        for u in seen:
            raw[t, u] = total(raw[t, u])
            grad[t, u] = total(grad[t, u]) * valid[t]
        scores = [raw[t, u] * score_scale + bias[u] for u in seen]
        largest = functools.reduce(jnp.maximum, scores)
        raised = [jnp.exp(score - largest) for score in scores]
        over = 1.0 / functools.reduce(jnp.add, raised)
        weights = [piece * over for piece in raised]
        mean_grad = functools.reduce(jnp.add, [weights[u] * grad[t, u] for u in seen])
        for u in seen:
            rounded = weights[u].astype(jnp.bfloat16).astype(jnp.float32)
            value_part[t, u] = (rounded + (1.0 if u == t else 0.0)) * valid[t]
            score_part[t, u] = weights[u] * (grad[t, u] - mean_grad) * score_scale

    both = {(t, u): score_part[t, u] * (2.0 if t == u else 1.0) for t, u in pairs}
    both.update({(u, t): both[t, u] for t, u in pairs})
    raw.update({(u, t): raw[t, u] for t, u in pairs})
    mean_part = [
        functools.reduce(jnp.add, [both[u, v] * raw[u, v] for v in every]) * (1.0 / feat)
        for u in every
    ]

    for group in range(feat // GROUP):
        fields, ups = load_fields(group), load_ups(group)
        outs = [[] for _ in every]
        for side in range(2):
            rows = pl.ds(group * GROUP + side * half, half)
            gain = gain_ref[0, rows, :]
            normed = [fields[t][side] * inverse[t] for t in every]
            mixed = jnp.zeros((half, lanes), jnp.float32)
            for u in every:
                crossed = functools.reduce(jnp.add, [both[u, v] * normed[v] for v in every])
                mixed = mixed + crossed * normed[u]
                from_norm = inverse[u] * (gain * crossed - normed[u] * mean_part[u])
                direct = functools.reduce(
                    jnp.add, [value_part[t, u] * ups[t][side] for t in range(u, frames)]
                )
                outs[u].append(direct + from_norm)
            mixed_sum[rows, :] = mixed if part == 0 else mixed_sum[rows, :] + mixed
        for u in every:
            grad_ref[u, pl.ds(group * GROUP, GROUP), here] = jnp.concatenate(
                outs[u], axis=0
            ).astype(jnp.bfloat16)


def temporal_kernel(frames, scalars, *refs):
    attended_refs, (upstream_ref, gain_ref) = refs[:frames], refs[frames : frames + 2]
    grad_refs, mixed_ref = refs[frames + 2 : 2 * frames + 2], refs[2 * frames + 2]
    attended, grads, mixed_sum = refs[2 * frames + 3 :]
    head = pl.program_id(0)
    for distance, ref in enumerate(attended_refs):
        attended[partner(scalars, distance)] = ref[0]
    for part in range(upstream_ref.shape[1]):
        temporal_part(scalars[2], attended, upstream_ref, gain_ref, grads, mixed_sum, part)
    for distance, ref in enumerate(grad_refs):
        ref[0] = grads[partner(scalars, distance)]

    @pl.when(head == 0)
    def _():
        mixed_ref[...] = jnp.full(mixed_ref.shape, scalars[3].astype(jnp.float32))

    mixed_ref[pl.ds(head, 1), :] = jnp.sum(mixed_sum[...].T, axis=0, keepdims=True) * 0.5


def temporal(scalars, attended, upstream, gain):
    frames, spaces, heads, feat, lanes = upstream.shape
    patches = spaces * lanes
    rows = -(-(heads + 1) // 8) * 8
    plane = pl.BlockSpec((1, feat, patches), lambda i, sc: (i, 0, 0))
    *grads, mixed = pl.pallas_call(
        functools.partial(temporal_kernel, frames),
        grid_spec=pltpu.PrefetchScalarGridSpec(
            num_scalar_prefetch=1,
            grid=(heads,),
            in_specs=[plane] * frames
            + [
                pl.BlockSpec((frames, spaces, 1, feat, lanes), lambda i, sc: (0, 0, i, 0, 0)),
                pl.BlockSpec((1, feat, lanes), lambda i, sc: (i, 0, 0)),
            ],
            out_specs=[plane] * frames + [pl.BlockSpec((rows, feat), lambda i, sc: (0, 0))],
            scratch_shapes=[
                pltpu.VMEM((frames, feat, patches), jnp.bfloat16),
                pltpu.VMEM((frames, feat, patches), jnp.bfloat16),
                pltpu.VMEM((feat, lanes), jnp.float32),
            ],
        ),
        out_shape=[jax.ShapeDtypeStruct((heads, feat, patches), jnp.bfloat16)] * frames
        + [jax.ShapeDtypeStruct((rows, feat), jnp.float32)],
        compiler_params=params(),
        cost_estimate=pl.CostEstimate(
            flops=heads * patches * feat * 200,
            bytes_accessed=6 * frames * heads * patches * feat,
            transcendentals=heads * patches * 16,
        ),
        name="temporal",
    )(scalars, *attended, upstream, gain)
    return grads, mixed


def gains_kernel(heads, frames, scalars, *refs):
    mixed_refs, gains_ref, grad_ref = refs[:-2], refs[-2], refs[-1]
    tasks = gains_ref.shape[1]
    rows = mixed_refs[0].shape[0] // frames
    task_ids = lax.broadcasted_iota(jnp.int32, (tasks, HEAD_DIM), 0).astype(jnp.float32)
    for distance in range(frames):
        for head in range(heads):
            mixed = jnp.zeros((tasks, HEAD_DIM), jnp.float32)
            for ref in mixed_refs:
                task = ref[pl.ds(distance * rows + heads, 1), :]
                row = ref[pl.ds(distance * rows + head, 1), :]
                mixed = mixed + jnp.where(task_ids == task, row, 0.0)
            start = (partner(scalars, distance) * heads + head) * HEAD_DIM
            cols = pl.ds(pl.multiple_of(start, HEAD_DIM), HEAD_DIM)
            grad_ref[0, :, cols] = gains_ref[1, :, cols] * mixed
            grad_ref[1, :, cols] = gains_ref[0, :, cols] * mixed


def gain_gradients(scalars, mixed, gains, heads, frames):
    return pl.pallas_call(
        functools.partial(gains_kernel, heads, frames),
        in_specs=[pl.BlockSpec(memory_space=pltpu.SMEM)]
        + [pl.BlockSpec(memory_space=pltpu.VMEM)] * (len(mixed) + 1),
        out_specs=pl.BlockSpec(memory_space=pltpu.VMEM),
        out_shape=jax.ShapeDtypeStruct(gains.shape, jnp.float32),
        compiler_params=params(),
        name="gain_gradients",
    )(scalars, *mixed, gains)


def swap(field, axis, size, distance):
    return lax.ppermute(field, axis, [(i, i ^ distance) for i in range(size)])


def split_by_heads(
    query_heads, key_heads, value_heads, cotangent, task_ids, lengths, gains, clips, frames, spaces
):
    patches, feat = query_heads.shape[2:]
    heads = feat // HEAD_DIM
    own = heads // frames
    width = own * HEAD_DIM
    queries, key_rows, values = (
        field.reshape(patches, feat) for field in (query_heads, key_heads, value_heads)
    )
    frame, space = lax.axis_index("tm"), lax.axis_index("space")
    scalars = jnp.stack([frame, space, lengths[0], task_ids[0]]).astype(jnp.int32)

    incoming = cotangent.reshape(cotangent.shape[2:])
    pieces = []
    for distance in range(frames * spaces):
        block = (space ^ (distance % spaces)) * frames + (frame ^ (distance // spaces))
        piece = lax.dynamic_slice_in_dim(incoming, block * width, width, 1)
        if distance:
            piece = swap(piece, ("tm", "space"), frames * spaces, distance)
        pieces.append(piece)
    weights, attended = forward(scalars, queries, key_rows, values, frames)
    attended = [attended[0]] + [
        swap(attended[distance], "tm", frames, distance) for distance in range(1, frames)
    ]
    upstream = turn(scalars, pieces, frames, spaces)
    rows = lax.dynamic_index_in_dim(gains, task_ids[0], 1, keepdims=False)
    product = lax.dynamic_slice_in_dim(rows[0] * rows[1], frame * width, width, 0)
    gain = jnp.broadcast_to(
        product.reshape(own, HEAD_DIM, 1), (own, HEAD_DIM, patches // spaces)
    )
    grads, mixed = temporal(scalars, attended, upstream, gain)
    grads = [grads[0]] + [
        swap(grads[distance], "tm", frames, distance) for distance in range(1, frames)
    ]
    mixed = jnp.concatenate(
        [mixed] + [swap(mixed, "tm", frames, distance) for distance in range(1, frames)], axis=0
    )
    mixed = [mixed] + [swap(mixed, "dp", clips, distance) for distance in range(1, clips)]
    grad_gains = gain_gradients(scalars, mixed, gains, own, frames)
    results = ()
    for distance in range(frames):
        results = backward(
            scalars, queries, key_rows, values, weights, grads[distance], distance, results
        )
    grad_queries, grad_keys = results
    return (
        grad_queries.reshape(query_heads.shape),
        grad_keys.reshape(query_heads.shape),
        grad_gains,
    )


def temporal_grads(attended, upstream, gain_query, gain_keys, length):
    highest = lax.Precision.HIGHEST
    frames = attended.shape[0]
    score_scale = attended.shape[-1] ** (-0.5)
    floats = attended.astype(jnp.float32)
    inverse_rms = lax.rsqrt(jnp.mean(floats * floats, axis=-1, keepdims=True) + 1e-06)
    normed = floats * inverse_rms
    t_query = normed * gain_query
    t_keys = normed * gain_keys
    scores = jnp.einsum("txhd,uxhd->xhtu", t_query, t_keys, precision=highest) * score_scale
    frame_ids = jnp.arange(frames, dtype=jnp.int32)
    allowed = (frame_ids[None, :] <= frame_ids[:, None]) & (frame_ids[None, :] < length)
    scores = jnp.where(allowed, scores, -1e30)
    weights = jax.nn.softmax(scores, axis=-1)
    weights_low = lax.optimization_barrier(weights.astype(jnp.bfloat16)).astype(jnp.float32)
    valid_rows = (frame_ids < length).astype(jnp.float32)
    masked = upstream.astype(jnp.float32) * valid_rows[:, None, None, None]
    grad_weights = jnp.einsum("txhd,uxhd->xhtu", masked, floats, precision=highest)
    from_values = jnp.einsum("xhtu,txhd->uxhd", weights_low, masked, precision=highest)
    grad_scores = (
        weights
        * (grad_weights - jnp.sum(grad_weights * weights, axis=-1, keepdims=True))
        * score_scale
    )
    grad_tquery = jnp.einsum("xhtu,uxhd->txhd", grad_scores, t_keys, precision=highest)
    grad_tkeys = jnp.einsum("xhtu,txhd->uxhd", grad_scores, t_query, precision=highest)
    grad_normed = grad_tquery * gain_query + grad_tkeys * gain_keys
    grad_gain_query = jnp.sum(grad_tquery * normed, axis=(0, 1))
    grad_gain_keys = jnp.sum(grad_tkeys * normed, axis=(0, 1))
    from_norm = inverse_rms * (
        grad_normed - normed * jnp.mean(grad_normed * normed, axis=-1, keepdims=True)
    )
    grad_total = (masked + from_values + from_norm).astype(jnp.bfloat16)
    return (grad_total, grad_gain_query, grad_gain_keys)


def split_by_patches(query_heads, key_heads, value_heads, cotangent, task_ids, lengths, gains):
    patches, feat = query_heads.shape[2:]
    heads = feat // HEAD_DIM
    queries, key_rows, values = (
        field.reshape(patches, feat) for field in (query_heads, key_heads, value_heads)
    )
    scalars = jnp.zeros((1,), jnp.int32)
    weights, attended = forward(scalars, queries, key_rows, values, heads)
    attended_field = jnp.transpose(jnp.concatenate(attended), (2, 0, 1)).reshape(1, 1, patches, feat)
    upstream = lax.all_to_all(
        lax.all_to_all(cotangent, "space", split_axis=3, concat_axis=2, tiled=True),
        "tm",
        split_axis=2,
        concat_axis=1,
        tiled=True,
    )
    frames_attended = lax.all_to_all(attended_field, "tm", split_axis=2, concat_axis=1, tiled=True)
    frames, local_patches = frames_attended.shape[1:3]
    selector = (task_ids[0] == jnp.arange(gains.shape[1], dtype=jnp.int32)).astype(jnp.float32)
    gain_query = jnp.sum(selector[:, None] * gains[0], axis=0).reshape(heads, HEAD_DIM)
    gain_keys = jnp.sum(selector[:, None] * gains[1], axis=0).reshape(heads, HEAD_DIM)
    grad_total, grad_gq, grad_gk = temporal_grads(
        frames_attended.reshape(frames, local_patches, heads, HEAD_DIM),
        upstream.reshape(frames, local_patches, heads, HEAD_DIM),
        gain_query,
        gain_keys,
        lengths[0],
    )
    gain_terms = jnp.stack(
        [
            selector[:, None] * grad_gq.reshape(1, feat),
            selector[:, None] * grad_gk.reshape(1, feat),
        ]
    )
    grad_gains = lax.psum(gain_terms, ("dp", "tm"))
    returned = lax.all_to_all(
        grad_total.reshape(1, frames, local_patches, feat),
        "tm",
        split_axis=1,
        concat_axis=2,
        tiled=True,
    )
    head_grads = jnp.transpose(returned.reshape(patches, heads, HEAD_DIM), (1, 2, 0))
    grad_queries, grad_keys = backward(
        scalars, queries, key_rows, values, weights, head_grads, 0, ()
    )
    return (
        grad_queries.reshape(query_heads.shape),
        grad_keys.reshape(query_heads.shape),
        grad_gains,
    )


def solution(mesh):
    clips, frames, spaces = (mesh.shape[axis] for axis in ("dp", "tm", "space"))

    def local(query_heads, *others):
        heads = query_heads.shape[3] // HEAD_DIM
        powers = all(size & (size - 1) == 0 for size in (clips, frames, spaces))
        if powers and frames <= 4 and heads % frames == 0:
            return split_by_heads(query_heads, *others, clips, frames, spaces)
        return split_by_patches(query_heads, *others)

    return jax.shard_map(
        local,
        mesh=mesh,
        in_specs=(
            P("dp", "tm", None, "space"),
            P("dp", "tm", None, "space"),
            P("dp", "tm", None, "space"),
            P("dp", "tm", "space", None),
            P("dp"),
            P("dp"),
            P(None, None, "space"),
        ),
        out_specs=(
            P("dp", "tm", None, "space"),
            P("dp", "tm", None, "space"),
            P(None, None, "space"),
        ),
        check_vma=False,
    )
```

```python
import functools

import jax
import jax.numpy as jnp
from jax import lax
from jax.experimental import pallas as pl
from jax.experimental.pallas import tpu as pltpu
from jax.sharding import PartitionSpec as P

HEAD_DIM = 128
GROUP = 16
MIB = 1024 * 1024


def params(patches):
    return pltpu.CompilerParams(vmem_limit_bytes=(16 if patches <= 512 else 60) * MIB)


def columns_dot(left, right):
    return lax.dot_general(
        left, right, (((1,), (1,)), ((), ())), preferred_element_type=jnp.float32
    )


def dot(left, right):
    return jnp.dot(left, right, preferred_element_type=jnp.float32)


def partner(scalars, distance):
    return jnp.bitwise_xor(scalars[0], distance)


def forward_kernel(scalars, query_ref, key_ref, value_ref, weights_ref, *refs):
    (queries, key_rows, values, arrived), attended_refs = refs[-4:], refs[:-4]
    score_scale = HEAD_DIM ** (-0.5)
    groups, _, width = queries.shape
    copies = []
    for group in range(groups):
        cols = pl.ds(pl.multiple_of(partner(scalars, group) * width, HEAD_DIM), width)
        for field, (source, target) in enumerate(
            ((query_ref, queries), (key_ref, key_rows), (value_ref, values))
        ):
            copy = pltpu.make_async_copy(
                source.at[:, cols], target.at[group], arrived.at[group, field]
            )
            copy.start()
            copies.append(copy)
    for group in range(groups):
        for copy in copies[3 * group : 3 * group + 3]:
            copy.wait()
        for head in range(width // HEAD_DIM):
            cols = pl.ds(head * HEAD_DIM, HEAD_DIM)
            scores = columns_dot(key_rows[group, :, cols], queries[group, :, cols])
            largest = jnp.max(scores, axis=0, keepdims=True)
            raised = jnp.exp((scores - largest) * score_scale)
            weights = raised * (1.0 / jnp.sum(raised, axis=0, keepdims=True))
            weights_ref[group * (width // HEAD_DIM) + head] = weights
            attended = dot(values[group, :, cols].T, weights.astype(jnp.bfloat16))
            attended_refs[group][head] = attended.astype(jnp.bfloat16)


def forward(scalars, queries, key_rows, values, groups):
    patches, feat = queries.shape
    heads = feat // HEAD_DIM
    own = heads // groups
    weights, *attended = pl.pallas_call(
        forward_kernel,
        in_specs=[pl.BlockSpec(memory_space=pltpu.SMEM)]
        + [pl.BlockSpec(memory_space=pltpu.HBM)] * 3,
        out_specs=[pl.BlockSpec(memory_space=pltpu.VMEM)] * (1 + groups),
        scratch_shapes=[pltpu.VMEM((groups, patches, feat // groups), jnp.bfloat16)] * 3
        + [pltpu.SemaphoreType.DMA((groups, 3))],
        out_shape=[jax.ShapeDtypeStruct((heads, patches, patches), jnp.float32)]
        + [jax.ShapeDtypeStruct((own, HEAD_DIM, patches), jnp.bfloat16)] * groups,
        compiler_params=params(patches),
        cost_estimate=pl.CostEstimate(
            flops=4 * heads * patches * patches * HEAD_DIM,
            bytes_accessed=heads * patches * (patches * 4 + 8 * HEAD_DIM),
            transcendentals=heads * patches * patches,
        ),
        name="spatial_forward",
    )(scalars, queries, key_rows, values)
    return weights, attended


def backward_kernel(scalars, query_ref, key_ref, value_ref, weights_ref, grad_ref, *refs):
    gq_ref, gk_ref = refs[-2:]
    score_scale = HEAD_DIM ** (-0.5)
    for head in range(weights_ref.shape[0]):
        cols = pl.ds(head * HEAD_DIM, HEAD_DIM)
        weights = weights_ref[head]
        spatial_grad = dot(value_ref[:, cols], grad_ref[head])
        row_sum = jnp.sum(spatial_grad * weights, axis=0, keepdims=True)
        scores = (weights * (spatial_grad - row_sum) * score_scale).astype(jnp.bfloat16)
        gk_ref[:, cols] = dot(scores, query_ref[:, cols]).astype(jnp.bfloat16)
        grad_query = dot(key_ref[:, cols].T, scores).astype(jnp.bfloat16)
        gq_ref[:, cols] = grad_query.T


def backward(scalars, queries, key_rows, values, weights, grads, distance, earlier):
    patches, feat = queries.shape
    own = grads.shape[0]
    field = pl.BlockSpec(
        (patches, own * HEAD_DIM), lambda i, sc: (0, partner(sc, distance))
    )
    return pl.pallas_call(
        backward_kernel,
        grid_spec=pltpu.PrefetchScalarGridSpec(
            num_scalar_prefetch=1,
            grid=(1,),
            in_specs=[
                field,
                field,
                field,
                pl.BlockSpec((own, patches, patches), lambda i, sc: (distance, 0, 0)),
                pl.BlockSpec((own, HEAD_DIM, patches), lambda i, sc: (0, 0, 0)),
            ]
            + [pl.BlockSpec(memory_space=pl.ANY)] * len(earlier),
            out_specs=[field, field],
        ),
        out_shape=[jax.ShapeDtypeStruct((patches, feat), jnp.bfloat16)] * 2,
        input_output_aliases={6 + index: index for index in range(len(earlier))},
        compiler_params=params(patches),
        cost_estimate=pl.CostEstimate(
            flops=6 * own * patches * patches * HEAD_DIM,
            bytes_accessed=own * patches * (patches * 4 + 12 * HEAD_DIM),
            transcendentals=0,
        ),
        name="spatial_backward",
    )(scalars, queries, key_rows, values, weights, grads, *earlier)


def pack_kernel(frames, spaces, field_ref, packed_ref, sent):
    width = packed_ref.shape[2]
    copies = []
    for frame in range(frames):
        for space in range(spaces):
            index = frame * spaces + space
            cols = pl.ds((space * frames + frame) * width, width)
            copy = pltpu.make_async_copy(field_ref.at[:, cols], packed_ref.at[index], sent.at[index])
            copy.start()
            copies.append(copy)
    for copy in copies:
        copy.wait()


def pack(field, frames, spaces):
    patches, feat = field.shape
    devices = frames * spaces
    return pl.pallas_call(
        functools.partial(pack_kernel, frames, spaces),
        in_specs=[pl.BlockSpec(memory_space=pl.ANY)],
        out_specs=pl.BlockSpec(memory_space=pl.ANY),
        out_shape=jax.ShapeDtypeStruct((devices, patches, feat // devices), field.dtype),
        scratch_shapes=[pltpu.SemaphoreType.DMA((devices,))],
        compiler_params=params(0),
        cost_estimate=pl.CostEstimate(
            flops=0, bytes_accessed=4 * patches * feat, transcendentals=0
        ),
        name="pack_cotangent",
    )(field)


def turn_kernel(field_ref, turned_ref):
    spaces, frames = turned_ref.shape[:2]
    for space in range(spaces):
        for frame in range(frames):
            turned_ref[space, frame, 0] = field_ref[frame * spaces + space].T


def turn(field, frames, spaces):
    devices, patches, feat = field.shape
    heads = feat // HEAD_DIM
    return pl.pallas_call(
        turn_kernel,
        grid=(heads,),
        in_specs=[pl.BlockSpec((devices, patches, HEAD_DIM), lambda i: (0, 0, i))],
        out_specs=pl.BlockSpec((spaces, frames, 1, HEAD_DIM, patches), lambda i: (0, 0, i, 0, 0)),
        out_shape=jax.ShapeDtypeStruct((spaces, frames, heads, HEAD_DIM, patches), field.dtype),
        compiler_params=params(patches),
        cost_estimate=pl.CostEstimate(
            flops=0, bytes_accessed=4 * devices * patches * feat, transcendentals=0
        ),
        name="turn_cotangent",
    )(field)


def temporal_part(length, attended_ref, upstream_ref, gain_ref, grad_ref, mixed_sum, part):
    frames, feat, _ = attended_ref.shape
    lanes = upstream_ref.shape[-1]
    here = pl.ds(part * lanes, lanes)
    half = GROUP // 2
    score_scale = feat ** (-0.5)
    pairs = [(t, u) for t in range(frames) for u in range(t + 1)]
    every = range(frames)
    valid = [jnp.where(t < length, 1.0, 0.0).astype(jnp.float32) for t in every]
    bias = [jnp.where(u < length, 0.0, -1e30).astype(jnp.float32) for u in every]

    def split(block):
        block = block.astype(jnp.float32)
        return block[:half], block[half:]

    def load_fields(group):
        return [split(attended_ref[t, pl.ds(group * GROUP, GROUP), here]) for t in every]

    def load_ups(group):
        return [split(upstream_ref[part, t, 0, pl.ds(group * GROUP, GROUP), :]) for t in every]

    def total(piece):
        return jnp.broadcast_to(jnp.sum(piece, axis=0, keepdims=True), (half, lanes))

    squares = [jnp.zeros((half, lanes), jnp.float32) for _ in every]
    for group in range(feat // GROUP):
        for t, (low, high) in enumerate(load_fields(group)):
            squares[t] = squares[t] + (low * low + high * high)
    inverse = [lax.rsqrt(total(squares[t]) * (1.0 / feat) + 1e-06) for t in every]

    raw = {pair: jnp.zeros((half, lanes), jnp.float32) for pair in pairs}
    grad = {pair: jnp.zeros((half, lanes), jnp.float32) for pair in pairs}
    for group in range(feat // GROUP):
        fields, ups = load_fields(group), load_ups(group)
        for side in range(2):
            gain = gain_ref[0, pl.ds(group * GROUP + side * half, half), :]
            normed = [fields[t][side] * inverse[t] for t in every]
            gained = [normed[t] * gain for t in every]
            for t, u in pairs:
                raw[t, u] = raw[t, u] + gained[t] * normed[u]
                grad[t, u] = grad[t, u] + ups[t][side] * fields[u][side]

    value_part, score_part = {}, {}
    for t in every:
        seen = range(t + 1)
        for u in seen:
            raw[t, u] = total(raw[t, u])
            grad[t, u] = total(grad[t, u]) * valid[t]
        scores = [raw[t, u] * score_scale + bias[u] for u in seen]
        largest = functools.reduce(jnp.maximum, scores)
        raised = [jnp.exp(score - largest) for score in scores]
        over = 1.0 / functools.reduce(jnp.add, raised)
        weights = [piece * over for piece in raised]
        mean_grad = functools.reduce(jnp.add, [weights[u] * grad[t, u] for u in seen])
        for u in seen:
            rounded = weights[u].astype(jnp.bfloat16).astype(jnp.float32)
            value_part[t, u] = (rounded + (1.0 if u == t else 0.0)) * valid[t]
            score_part[t, u] = weights[u] * (grad[t, u] - mean_grad) * score_scale

    both = {(t, u): score_part[t, u] * (2.0 if t == u else 1.0) for t, u in pairs}
    both.update({(u, t): both[t, u] for t, u in pairs})
    raw.update({(u, t): raw[t, u] for t, u in pairs})
    mean_part = [
        functools.reduce(jnp.add, [both[u, v] * raw[u, v] for v in every]) * (1.0 / feat)
        for u in every
    ]

    for group in range(feat // GROUP):
        fields, ups = load_fields(group), load_ups(group)
        outs = [[] for _ in every]
        for side in range(2):
            rows = pl.ds(group * GROUP + side * half, half)
            gain = gain_ref[0, rows, :]
            normed = [fields[t][side] * inverse[t] for t in every]
            mixed = jnp.zeros((half, lanes), jnp.float32)
            for u in every:
                crossed = functools.reduce(jnp.add, [both[u, v] * normed[v] for v in every])
                mixed = mixed + crossed * normed[u]
                from_norm = inverse[u] * (gain * crossed - normed[u] * mean_part[u])
                direct = functools.reduce(
                    jnp.add, [value_part[t, u] * ups[t][side] for t in range(u, frames)]
                )
                outs[u].append(direct + from_norm)
            mixed_sum[rows, :] = mixed if part == 0 else mixed_sum[rows, :] + mixed
        for u in every:
            grad_ref[u, pl.ds(group * GROUP, GROUP), here] = jnp.concatenate(
                outs[u], axis=0
            ).astype(jnp.bfloat16)


def temporal_kernel(frames, scalars, *refs):
    attended_refs, (upstream_ref, gain_ref) = refs[:frames], refs[frames : frames + 2]
    grad_refs, mixed_ref = refs[frames + 2 : 2 * frames + 2], refs[2 * frames + 2]
    attended, grads, mixed_sum = refs[2 * frames + 3 :]
    head = pl.program_id(0)
    for distance, ref in enumerate(attended_refs):
        attended[partner(scalars, distance)] = ref[0]
    for part in range(upstream_ref.shape[0]):
        temporal_part(scalars[1], attended, upstream_ref, gain_ref, grads, mixed_sum, part)
    for distance, ref in enumerate(grad_refs):
        ref[0] = grads[partner(scalars, distance)]

    @pl.when(head == 0)
    def _():
        mixed_ref[...] = jnp.full(mixed_ref.shape, scalars[2].astype(jnp.float32))

    mixed_ref[pl.ds(head, 1), :] = jnp.sum(mixed_sum[...].T, axis=0, keepdims=True) * 0.5


def temporal(scalars, attended, upstream, gain):
    spaces, frames, heads, feat, lanes = upstream.shape
    patches = spaces * lanes
    rows = -(-(heads + 1) // 8) * 8
    plane = pl.BlockSpec((1, feat, patches), lambda i, sc: (i, 0, 0))
    *grads, mixed = pl.pallas_call(
        functools.partial(temporal_kernel, frames),
        grid_spec=pltpu.PrefetchScalarGridSpec(
            num_scalar_prefetch=1,
            grid=(heads,),
            in_specs=[plane] * frames
            + [
                pl.BlockSpec((spaces, frames, 1, feat, lanes), lambda i, sc: (0, 0, i, 0, 0)),
                pl.BlockSpec((1, feat, lanes), lambda i, sc: (i, 0, 0)),
            ],
            out_specs=[plane] * frames + [pl.BlockSpec((rows, feat), lambda i, sc: (0, 0))],
            scratch_shapes=[
                pltpu.VMEM((frames, feat, patches), jnp.bfloat16),
                pltpu.VMEM((frames, feat, patches), jnp.bfloat16),
                pltpu.VMEM((feat, lanes), jnp.float32),
            ],
        ),
        out_shape=[jax.ShapeDtypeStruct((heads, feat, patches), jnp.bfloat16)] * frames
        + [jax.ShapeDtypeStruct((rows, feat), jnp.float32)],
        compiler_params=params(patches),
        cost_estimate=pl.CostEstimate(
            flops=heads * patches * feat * 200,
            bytes_accessed=6 * frames * heads * patches * feat,
            transcendentals=heads * patches * 16,
        ),
        name="temporal",
    )(scalars, *attended, upstream, gain)
    return grads, mixed


def gains_kernel(heads, frames, clips, scalars, *refs):
    mixed_refs, gains_ref, grad_ref = refs[:-2], refs[-2], refs[-1]
    tasks = gains_ref.shape[1]
    rows = sum(ref.shape[0] for ref in mixed_refs) // (frames * clips)
    each = mixed_refs[0].shape[0] // rows
    task_ids = lax.broadcasted_iota(jnp.int32, (tasks, HEAD_DIM), 0).astype(jnp.float32)
    for distance in range(frames):
        for head in range(heads):
            mixed = jnp.zeros((tasks, HEAD_DIM), jnp.float32)
            for clip in range(clips):
                block = distance * clips + clip
                ref, start = mixed_refs[block // each], block % each * rows
                task = ref[pl.ds(start + heads, 1), :]
                row = ref[pl.ds(start + head, 1), :]
                mixed = mixed + jnp.where(task_ids == task, row, 0.0)
            start = (partner(scalars, distance) * heads + head) * HEAD_DIM
            cols = pl.ds(pl.multiple_of(start, HEAD_DIM), HEAD_DIM)
            grad_ref[0, :, cols] = gains_ref[1, :, cols] * mixed
            grad_ref[1, :, cols] = gains_ref[0, :, cols] * mixed


def gain_gradients(scalars, mixed, gains, heads, frames, clips):
    return pl.pallas_call(
        functools.partial(gains_kernel, heads, frames, clips),
        in_specs=[pl.BlockSpec(memory_space=pltpu.SMEM)]
        + [pl.BlockSpec(memory_space=pltpu.VMEM)] * (len(mixed) + 1),
        out_specs=pl.BlockSpec(memory_space=pltpu.VMEM),
        out_shape=jax.ShapeDtypeStruct(gains.shape, jnp.float32),
        compiler_params=params(0),
        name="gain_gradients",
    )(scalars, *mixed, gains)


def swap(field, axis, size, distance):
    return lax.ppermute(field, axis, [(i, i ^ distance) for i in range(size)])


def split_by_heads(
    query_heads, key_heads, value_heads, cotangent, task_ids, lengths, gains, clips, frames, spaces
):
    patches, feat = query_heads.shape[2:]
    heads = feat // HEAD_DIM
    own = heads // frames
    width = own * HEAD_DIM
    queries, key_rows, values = (
        field.reshape(patches, feat) for field in (query_heads, key_heads, value_heads)
    )
    frame = lax.axis_index("tm")
    scalars = jnp.stack([frame, lengths[0], task_ids[0]]).astype(jnp.int32)

    packed = pack(cotangent.reshape(cotangent.shape[2:]), frames, spaces)
    incoming = lax.all_to_all(packed, ("tm", "space"), split_axis=0, concat_axis=0, tiled=True)
    queries, _ = lax.optimization_barrier((queries, packed))
    weights, attended = forward(scalars, queries, key_rows, values, frames)
    attended = [attended[0]] + [
        swap(attended[distance], "tm", frames, distance) for distance in range(1, frames)
    ]
    incoming, _ = lax.optimization_barrier((incoming, weights))
    upstream = turn(incoming, frames, spaces)
    rows = lax.dynamic_index_in_dim(gains, task_ids[0], 1, keepdims=False)
    product = lax.dynamic_slice_in_dim(rows[0] * rows[1], frame * width, width, 0)
    gain = jnp.broadcast_to(
        product.reshape(own, HEAD_DIM, 1), (own, HEAD_DIM, patches // spaces)
    )
    grads, mixed = temporal(scalars, attended, upstream, gain)
    grads = [grads[0]] + [
        swap(grads[distance], "tm", frames, distance) for distance in range(1, frames)
    ]
    rounds = [("dp", clips, 1 << bit) for bit in range(clips.bit_length() - 1)]
    rounds += [("tm", frames, 1 << bit) for bit in range(frames.bit_length() - 1)]
    mixed = [mixed]
    for axis, size, distance in rounds:
        joined = jnp.concatenate(mixed, axis=0)
        mixed = [joined, swap(joined, axis, size, distance)]
    grad_gains = gain_gradients(scalars, mixed, gains, own, frames, clips)
    results = ()
    for distance in range(frames):
        results = backward(
            scalars, queries, key_rows, values, weights, grads[distance], distance, results
        )
    grad_queries, grad_keys = results
    return (
        grad_queries.reshape(query_heads.shape),
        grad_keys.reshape(query_heads.shape),
        grad_gains,
    )


def temporal_grads(attended, upstream, gain_query, gain_keys, length):
    highest = lax.Precision.HIGHEST
    frames = attended.shape[0]
    score_scale = attended.shape[-1] ** (-0.5)
    floats = attended.astype(jnp.float32)
    inverse_rms = lax.rsqrt(jnp.mean(floats * floats, axis=-1, keepdims=True) + 1e-06)
    normed = floats * inverse_rms
    t_query = normed * gain_query
    t_keys = normed * gain_keys
    scores = jnp.einsum("txhd,uxhd->xhtu", t_query, t_keys, precision=highest) * score_scale
    frame_ids = jnp.arange(frames, dtype=jnp.int32)
    allowed = (frame_ids[None, :] <= frame_ids[:, None]) & (frame_ids[None, :] < length)
    scores = jnp.where(allowed, scores, -1e30)
    weights = jax.nn.softmax(scores, axis=-1)
    weights_low = lax.optimization_barrier(weights.astype(jnp.bfloat16)).astype(jnp.float32)
    valid_rows = (frame_ids < length).astype(jnp.float32)
    masked = upstream.astype(jnp.float32) * valid_rows[:, None, None, None]
    grad_weights = jnp.einsum("txhd,uxhd->xhtu", masked, floats, precision=highest)
    from_values = jnp.einsum("xhtu,txhd->uxhd", weights_low, masked, precision=highest)
    grad_scores = (
        weights
        * (grad_weights - jnp.sum(grad_weights * weights, axis=-1, keepdims=True))
        * score_scale
    )
    grad_tquery = jnp.einsum("xhtu,uxhd->txhd", grad_scores, t_keys, precision=highest)
    grad_tkeys = jnp.einsum("xhtu,txhd->uxhd", grad_scores, t_query, precision=highest)
    grad_normed = grad_tquery * gain_query + grad_tkeys * gain_keys
    grad_gain_query = jnp.sum(grad_tquery * normed, axis=(0, 1))
    grad_gain_keys = jnp.sum(grad_tkeys * normed, axis=(0, 1))
    from_norm = inverse_rms * (
        grad_normed - normed * jnp.mean(grad_normed * normed, axis=-1, keepdims=True)
    )
    grad_total = (masked + from_values + from_norm).astype(jnp.bfloat16)
    return (grad_total, grad_gain_query, grad_gain_keys)


def split_by_patches(query_heads, key_heads, value_heads, cotangent, task_ids, lengths, gains):
    patches, feat = query_heads.shape[2:]
    heads = feat // HEAD_DIM
    queries, key_rows, values = (
        field.reshape(patches, feat) for field in (query_heads, key_heads, value_heads)
    )
    scalars = jnp.zeros((1,), jnp.int32)
    weights, attended = forward(scalars, queries, key_rows, values, heads)
    attended_field = jnp.transpose(jnp.concatenate(attended), (2, 0, 1)).reshape(1, 1, patches, feat)
    upstream = lax.all_to_all(
        lax.all_to_all(cotangent, "space", split_axis=3, concat_axis=2, tiled=True),
        "tm",
        split_axis=2,
        concat_axis=1,
        tiled=True,
    )
    frames_attended = lax.all_to_all(attended_field, "tm", split_axis=2, concat_axis=1, tiled=True)
    frames, local_patches = frames_attended.shape[1:3]
    selector = (task_ids[0] == jnp.arange(gains.shape[1], dtype=jnp.int32)).astype(jnp.float32)
    gain_query = jnp.sum(selector[:, None] * gains[0], axis=0).reshape(heads, HEAD_DIM)
    gain_keys = jnp.sum(selector[:, None] * gains[1], axis=0).reshape(heads, HEAD_DIM)
    grad_total, grad_gq, grad_gk = temporal_grads(
        frames_attended.reshape(frames, local_patches, heads, HEAD_DIM),
        upstream.reshape(frames, local_patches, heads, HEAD_DIM),
        gain_query,
        gain_keys,
        lengths[0],
    )
    gain_terms = jnp.stack(
        [
            selector[:, None] * grad_gq.reshape(1, feat),
            selector[:, None] * grad_gk.reshape(1, feat),
        ]
    )
    grad_gains = lax.psum(gain_terms, ("dp", "tm"))
    returned = lax.all_to_all(
        grad_total.reshape(1, frames, local_patches, feat),
        "tm",
        split_axis=1,
        concat_axis=2,
        tiled=True,
    )
    head_grads = jnp.transpose(returned.reshape(patches, heads, HEAD_DIM), (1, 2, 0))
    grad_queries, grad_keys = backward(
        scalars, queries, key_rows, values, weights, head_grads, 0, ()
    )
    return (
        grad_queries.reshape(query_heads.shape),
        grad_keys.reshape(query_heads.shape),
        grad_gains,
    )


def solution(mesh):
    clips, frames, spaces = (mesh.shape[axis] for axis in ("dp", "tm", "space"))

    def local(query_heads, *others):
        heads = query_heads.shape[3] // HEAD_DIM
        powers = all(size & (size - 1) == 0 for size in (clips, frames))
        if powers and frames <= 4 and heads % frames == 0:
            return split_by_heads(query_heads, *others, clips, frames, spaces)
        return split_by_patches(query_heads, *others)

    return jax.shard_map(
        local,
        mesh=mesh,
        in_specs=(
            P("dp", "tm", None, "space"),
            P("dp", "tm", None, "space"),
            P("dp", "tm", None, "space"),
            P("dp", "tm", "space", None),
            P("dp"),
            P("dp"),
            P(None, None, "space"),
        ),
        out_specs=(
            P("dp", "tm", None, "space"),
            P("dp", "tm", None, "space"),
            P(None, None, "space"),
        ),
        check_vma=False,
    )
```

```python
import functools

import jax
import jax.numpy as jnp
from jax import lax
from jax.experimental import pallas as pl
from jax.experimental.pallas import tpu as pltpu
from jax.sharding import PartitionSpec as P

HEAD_DIM = 128
GROUP = 16
MIB = 1024 * 1024


def params(patches):
    return pltpu.CompilerParams(vmem_limit_bytes=(16 if patches <= 512 else 60) * MIB)


def cost(microseconds):
    return pl.CostEstimate(flops=int(microseconds * 1e8), bytes_accessed=0, transcendentals=0)


def columns_dot(left, right):
    return lax.dot_general(
        left, right, (((1,), (1,)), ((), ())), preferred_element_type=jnp.float32
    )


def dot(left, right):
    return jnp.dot(left, right, preferred_element_type=jnp.float32)


def partner(scalars, distance):
    return jnp.bitwise_xor(scalars[0], distance)


def forward_kernel(scalars, query_ref, key_ref, value_ref, *refs):
    (queries, turned_keys, values, weights_ref), refs = refs[:4], refs[4:]
    (key_rows, arrived), attended_refs = refs[-2:], refs[:-2]
    score_scale = HEAD_DIM ** (-0.5)
    groups, _, width = queries.shape
    own = width // HEAD_DIM
    copies = []
    for group in range(groups):
        cols = pl.ds(pl.multiple_of(partner(scalars, group) * width, HEAD_DIM), width)
        for field, (source, target) in enumerate(
            ((query_ref, queries), (key_ref, key_rows), (value_ref, values))
        ):
            copy = pltpu.make_async_copy(
                source.at[:, cols], target.at[group], arrived.at[group, field]
            )
            copy.start()
            copies.append(copy)
    for group in range(groups):
        for copy in copies[3 * group : 3 * group + 3]:
            copy.wait()
        for head in range(own):
            cols = pl.ds(head * HEAD_DIM, HEAD_DIM)
            keys_here = key_rows[group, :, cols]
            scores = columns_dot(keys_here, queries[group, :, cols])
            largest = jnp.max(scores, axis=0, keepdims=True)
            raised = jnp.exp((scores - largest) * score_scale)
            weights = raised * (1.0 / jnp.sum(raised, axis=0, keepdims=True))
            weights_ref[group * own + head] = weights
            attended = dot(values[group, :, cols].T, weights.astype(jnp.bfloat16))
            attended_refs[group][head] = attended.astype(jnp.bfloat16)
            turned_keys[group * own + head] = keys_here.T


def forward(scalars, queries, key_rows, values, groups):
    patches, feat = queries.shape
    heads = feat // HEAD_DIM
    own = heads // groups
    by_group = (groups, patches, feat // groups)
    *kept, weights, attended = [
        jax.ShapeDtypeStruct(by_group, jnp.bfloat16),
        jax.ShapeDtypeStruct((heads, HEAD_DIM, patches), jnp.bfloat16),
        jax.ShapeDtypeStruct(by_group, jnp.bfloat16),
        jax.ShapeDtypeStruct((heads, patches, patches), jnp.float32),
        jax.ShapeDtypeStruct((own, HEAD_DIM, patches), jnp.bfloat16),
    ]
    shapes = [*kept, weights] + [attended] * groups
    fields = [
        pltpu.with_memory_space_constraint(field, pltpu.HBM) for field in (queries, key_rows, values)
    ]
    results = pl.pallas_call(
        forward_kernel,
        in_specs=[pl.BlockSpec(memory_space=pltpu.SMEM)]
        + [pl.BlockSpec(memory_space=pltpu.HBM)] * 3,
        out_specs=[pl.BlockSpec(memory_space=pltpu.VMEM)] * len(shapes),
        scratch_shapes=[pltpu.VMEM(by_group, jnp.bfloat16), pltpu.SemaphoreType.DMA((groups, 3))],
        out_shape=shapes,
        compiler_params=params(patches),
        cost_estimate=cost(6),
        name="spatial_forward",
    )(scalars, *fields)
    return results[:4], results[4:]


def backward_kernel(distance, scalars, *refs):
    queries, turned_keys, values, weights_ref, grad_ref = refs[:5]
    gq_ref, gk_ref, gq, gk, sent = refs[-5:]
    score_scale = HEAD_DIM ** (-0.5)
    own = grad_ref.shape[0]
    copies = []
    for head in range(own):
        cols = pl.ds(head * HEAD_DIM, HEAD_DIM)
        weights = weights_ref[distance * own + head]
        spatial_grad = dot(values[distance, :, cols], grad_ref[head])
        row_sum = jnp.sum(spatial_grad * weights, axis=0, keepdims=True)
        scores = (weights * (spatial_grad - row_sum) * score_scale).astype(jnp.bfloat16)
        gk[head] = dot(scores, queries[distance, :, cols]).astype(jnp.bfloat16)
        gq[head] = dot(turned_keys[distance * own + head], scores).astype(jnp.bfloat16).T
        start = (partner(scalars, distance) * own + head) * HEAD_DIM
        there = pl.ds(pl.multiple_of(start, HEAD_DIM), HEAD_DIM)
        for side, (source, target) in enumerate(((gq, gq_ref), (gk, gk_ref))):
            copy = pltpu.make_async_copy(
                source.at[head], target.at[:, there], sent.at[head, side]
            )
            copy.start()
            copies.append(copy)
    for copy in copies:
        copy.wait()


def backward(scalars, kept, grads, distance, earlier):
    groups, patches, width = kept[0].shape
    own = grads.shape[0]
    return pl.pallas_call(
        functools.partial(backward_kernel, distance),
        in_specs=[pl.BlockSpec(memory_space=pltpu.SMEM)]
        + [pl.BlockSpec(memory_space=pltpu.VMEM)] * 5
        + [pl.BlockSpec(memory_space=pl.ANY)] * len(earlier),
        out_specs=[pl.BlockSpec(memory_space=pl.ANY)] * 2,
        scratch_shapes=[pltpu.VMEM((own, patches, HEAD_DIM), jnp.bfloat16)] * 2
        + [pltpu.SemaphoreType.DMA((own, 2))],
        out_shape=[jax.ShapeDtypeStruct((patches, groups * width), jnp.bfloat16)] * 2,
        input_output_aliases={6 + index: index for index in range(len(earlier))},
        compiler_params=params(patches),
        cost_estimate=cost(2),
        name="spatial_backward",
    )(scalars, *kept, grads, *earlier)


def pack_kernel(frames, spaces, field_ref, packed_ref, sent):
    width = packed_ref.shape[2]
    copies = []
    for frame in range(frames):
        for space in range(spaces):
            index = frame * spaces + space
            cols = pl.ds((space * frames + frame) * width, width)
            copy = pltpu.make_async_copy(field_ref.at[:, cols], packed_ref.at[index], sent.at[index])
            copy.start()
            copies.append(copy)
    for copy in copies:
        copy.wait()


def pack(field, frames, spaces):
    patches, feat = field.shape
    devices = frames * spaces
    return pl.pallas_call(
        functools.partial(pack_kernel, frames, spaces),
        in_specs=[pl.BlockSpec(memory_space=pl.ANY)],
        out_specs=pl.BlockSpec(memory_space=pl.ANY),
        out_shape=jax.ShapeDtypeStruct((devices, patches, feat // devices), field.dtype),
        scratch_shapes=[pltpu.SemaphoreType.DMA((devices,))],
        compiler_params=params(0),
        cost_estimate=cost(1),
        name="pack_cotangent",
    )(pltpu.with_memory_space_constraint(field, pltpu.HBM))


def turn_kernel(field_ref, turned_ref):
    spaces, frames = turned_ref.shape[:2]
    for space in range(spaces):
        for frame in range(frames):
            turned_ref[space, frame, 0] = field_ref[frame * spaces + space].T


def turn(field, frames, spaces):
    devices, patches, feat = field.shape
    heads = feat // HEAD_DIM
    return pl.pallas_call(
        turn_kernel,
        grid=(heads,),
        in_specs=[pl.BlockSpec((devices, patches, HEAD_DIM), lambda i: (0, 0, i))],
        out_specs=pl.BlockSpec((spaces, frames, 1, HEAD_DIM, patches), lambda i: (0, 0, i, 0, 0)),
        out_shape=jax.ShapeDtypeStruct((spaces, frames, heads, HEAD_DIM, patches), field.dtype),
        compiler_params=params(patches),
        cost_estimate=cost(2),
        name="turn_cotangent",
    )(field)


def temporal_part(length, attended_ref, upstream_ref, gain_ref, grad_ref, mixed_sum, part):
    frames, feat, _ = attended_ref.shape
    lanes = upstream_ref.shape[-1]
    here = pl.ds(part * lanes, lanes)
    half = GROUP // 2
    score_scale = feat ** (-0.5)
    pairs = [(t, u) for t in range(frames) for u in range(t + 1)]
    every = range(frames)
    valid = [jnp.where(t < length, 1.0, 0.0).astype(jnp.float32) for t in every]
    bias = [jnp.where(u < length, 0.0, -1e30).astype(jnp.float32) for u in every]

    def split(block):
        block = block.astype(jnp.float32)
        return block[:half], block[half:]

    def load_fields(group):
        return [split(attended_ref[t, pl.ds(group * GROUP, GROUP), here]) for t in every]

    def load_ups(group):
        return [split(upstream_ref[part, t, 0, pl.ds(group * GROUP, GROUP), :]) for t in every]

    def total(piece):
        return jnp.broadcast_to(jnp.sum(piece, axis=0, keepdims=True), (half, lanes))

    squares = [jnp.zeros((half, lanes), jnp.float32) for _ in every]
    for group in range(feat // GROUP):
        for t, (low, high) in enumerate(load_fields(group)):
            squares[t] = squares[t] + (low * low + high * high)
    inverse = [lax.rsqrt(total(squares[t]) * (1.0 / feat) + 1e-06) for t in every]

    raw = {pair: jnp.zeros((half, lanes), jnp.float32) for pair in pairs}
    grad = {pair: jnp.zeros((half, lanes), jnp.float32) for pair in pairs}
    for group in range(feat // GROUP):
        fields, ups = load_fields(group), load_ups(group)
        for side in range(2):
            gain = gain_ref[0, pl.ds(group * GROUP + side * half, half), :]
            normed = [fields[t][side] * inverse[t] for t in every]
            gained = [normed[t] * gain for t in every]
            for t, u in pairs:
                raw[t, u] = raw[t, u] + gained[t] * normed[u]
                grad[t, u] = grad[t, u] + ups[t][side] * fields[u][side]

    value_part, score_part = {}, {}
    for t in every:
        seen = range(t + 1)
        for u in seen:
            raw[t, u] = total(raw[t, u])
            grad[t, u] = total(grad[t, u]) * valid[t]
        scores = [raw[t, u] * score_scale + bias[u] for u in seen]
        largest = functools.reduce(jnp.maximum, scores)
        raised = [jnp.exp(score - largest) for score in scores]
        over = 1.0 / functools.reduce(jnp.add, raised)
        weights = [piece * over for piece in raised]
        mean_grad = functools.reduce(jnp.add, [weights[u] * grad[t, u] for u in seen])
        for u in seen:
            rounded = weights[u].astype(jnp.bfloat16).astype(jnp.float32)
            value_part[t, u] = (rounded + (1.0 if u == t else 0.0)) * valid[t]
            score_part[t, u] = weights[u] * (grad[t, u] - mean_grad) * score_scale

    both = {(t, u): score_part[t, u] * (2.0 if t == u else 1.0) for t, u in pairs}
    both.update({(u, t): both[t, u] for t, u in pairs})
    raw.update({(u, t): raw[t, u] for t, u in pairs})
    mean_part = [
        functools.reduce(jnp.add, [both[u, v] * raw[u, v] for v in every]) * (1.0 / feat)
        for u in every
    ]

    for group in range(feat // GROUP):
        fields, ups = load_fields(group), load_ups(group)
        outs = [[] for _ in every]
        for side in range(2):
            rows = pl.ds(group * GROUP + side * half, half)
            gain = gain_ref[0, rows, :]
            normed = [fields[t][side] * inverse[t] for t in every]
            mixed = jnp.zeros((half, lanes), jnp.float32)
            for u in every:
                crossed = functools.reduce(jnp.add, [both[u, v] * normed[v] for v in every])
                mixed = mixed + crossed * normed[u]
                from_norm = inverse[u] * (gain * crossed - normed[u] * mean_part[u])
                direct = functools.reduce(
                    jnp.add, [value_part[t, u] * ups[t][side] for t in range(u, frames)]
                )
                outs[u].append(direct + from_norm)
            mixed_sum[rows, :] = mixed if part == 0 else mixed_sum[rows, :] + mixed
        for u in every:
            grad_ref[u, pl.ds(group * GROUP, GROUP), here] = jnp.concatenate(
                outs[u], axis=0
            ).astype(jnp.bfloat16)


def temporal_kernel(frames, scalars, *refs):
    attended_refs, (upstream_ref, gain_ref) = refs[:frames], refs[frames : frames + 2]
    grad_refs, mixed_ref = refs[frames + 2 : 2 * frames + 2], refs[2 * frames + 2]
    attended, grads, mixed_sum = refs[2 * frames + 3 :]
    head = pl.program_id(0)
    for distance, ref in enumerate(attended_refs):
        attended[partner(scalars, distance)] = ref[0]
    for part in range(upstream_ref.shape[0]):
        temporal_part(scalars[1], attended, upstream_ref, gain_ref, grads, mixed_sum, part)
    for distance, ref in enumerate(grad_refs):
        ref[0] = grads[partner(scalars, distance)]

    @pl.when(head == 0)
    def _():
        mixed_ref[...] = jnp.full(mixed_ref.shape, scalars[2].astype(jnp.float32))

    mixed_ref[pl.ds(head, 1), :] = jnp.sum(mixed_sum[...].T, axis=0, keepdims=True) * 0.5


def temporal(scalars, attended, upstream, gain):
    spaces, frames, heads, feat, lanes = upstream.shape
    patches = spaces * lanes
    rows = -(-(heads + 1) // 8) * 8
    plane = pl.BlockSpec((1, feat, patches), lambda i, sc: (i, 0, 0))
    *grads, mixed = pl.pallas_call(
        functools.partial(temporal_kernel, frames),
        grid_spec=pltpu.PrefetchScalarGridSpec(
            num_scalar_prefetch=1,
            grid=(heads,),
            in_specs=[plane] * frames
            + [
                pl.BlockSpec((spaces, frames, 1, feat, lanes), lambda i, sc: (0, 0, i, 0, 0)),
                pl.BlockSpec((1, feat, lanes), lambda i, sc: (i, 0, 0)),
            ],
            out_specs=[plane] * frames + [pl.BlockSpec((rows, feat), lambda i, sc: (0, 0))],
            scratch_shapes=[
                pltpu.VMEM((frames, feat, patches), jnp.bfloat16),
                pltpu.VMEM((frames, feat, patches), jnp.bfloat16),
                pltpu.VMEM((feat, lanes), jnp.float32),
            ],
        ),
        out_shape=[jax.ShapeDtypeStruct((heads, feat, patches), jnp.bfloat16)] * frames
        + [jax.ShapeDtypeStruct((rows, feat), jnp.float32)],
        compiler_params=params(patches),
        cost_estimate=cost(4),
        name="temporal",
    )(scalars, *attended, upstream, gain)
    return grads, mixed


def gains_kernel(heads, frames, clips, scalars, *refs):
    mixed_refs, gains_ref, grad_ref = refs[:-2], refs[-2], refs[-1]
    tasks = gains_ref.shape[1]
    rows = sum(ref.shape[0] for ref in mixed_refs) // (frames * clips)
    each = mixed_refs[0].shape[0] // rows
    task_ids = lax.broadcasted_iota(jnp.int32, (tasks, HEAD_DIM), 0).astype(jnp.float32)
    for distance in range(frames):
        for head in range(heads):
            mixed = jnp.zeros((tasks, HEAD_DIM), jnp.float32)
            for clip in range(clips):
                block = distance * clips + clip
                ref, start = mixed_refs[block // each], block % each * rows
                task = ref[pl.ds(start + heads, 1), :]
                row = ref[pl.ds(start + head, 1), :]
                mixed = mixed + jnp.where(task_ids == task, row, 0.0)
            start = (partner(scalars, distance) * heads + head) * HEAD_DIM
            cols = pl.ds(pl.multiple_of(start, HEAD_DIM), HEAD_DIM)
            grad_ref[0, :, cols] = gains_ref[1, :, cols] * mixed
            grad_ref[1, :, cols] = gains_ref[0, :, cols] * mixed


def gain_gradients(scalars, mixed, gains, heads, frames, clips):
    return pl.pallas_call(
        functools.partial(gains_kernel, heads, frames, clips),
        in_specs=[pl.BlockSpec(memory_space=pltpu.SMEM)]
        + [pl.BlockSpec(memory_space=pltpu.VMEM)] * (len(mixed) + 1),
        out_specs=pl.BlockSpec(memory_space=pltpu.VMEM),
        out_shape=jax.ShapeDtypeStruct(gains.shape, jnp.float32),
        compiler_params=params(0),
        cost_estimate=cost(1),
        name="gain_gradients",
    )(scalars, *mixed, gains)


def swap(field, axis, size, distance):
    return lax.ppermute(field, axis, [(i, i ^ distance) for i in range(size)])


def split_by_heads(
    query_heads, key_heads, value_heads, cotangent, task_ids, lengths, gains, clips, frames, spaces
):
    patches, feat = query_heads.shape[2:]
    heads = feat // HEAD_DIM
    own = heads // frames
    width = own * HEAD_DIM
    queries, key_rows, values = (
        field.reshape(patches, feat) for field in (query_heads, key_heads, value_heads)
    )
    frame = lax.axis_index("tm")
    scalars = jnp.stack([frame, lengths[0], task_ids[0]]).astype(jnp.int32)

    packed = pack(cotangent.reshape(cotangent.shape[2:]), frames, spaces)
    incoming = lax.all_to_all(packed, ("tm", "space"), split_axis=0, concat_axis=0, tiled=True)
    queries, _ = lax.optimization_barrier((queries, packed))
    kept, attended = forward(scalars, queries, key_rows, values, frames)
    attended = [attended[0]] + [
        swap(attended[distance], "tm", frames, distance) for distance in range(1, frames)
    ]
    incoming, _ = lax.optimization_barrier((incoming, kept[3]))
    upstream = turn(incoming, frames, spaces)
    rows = lax.dynamic_index_in_dim(gains, task_ids[0], 1, keepdims=False)
    product = lax.dynamic_slice_in_dim(rows[0] * rows[1], frame * width, width, 0)
    gain = jnp.broadcast_to(
        product.reshape(own, HEAD_DIM, 1), (own, HEAD_DIM, patches // spaces)
    )
    grads, mixed = temporal(scalars, attended, upstream, gain)
    grads = [grads[0]] + [
        swap(grads[distance], "tm", frames, distance) for distance in range(1, frames)
    ]
    rounds = [("dp", clips, 1 << bit) for bit in range(clips.bit_length() - 1)]
    rounds += [("tm", frames, 1 << bit) for bit in range(frames.bit_length() - 1)]
    mixed, results, distance = [mixed], (), 0
    for number, (axis, size, step) in enumerate(rounds):
        joined = jnp.concatenate(mixed, axis=0)
        if results and number >= 2:
            joined, results = lax.optimization_barrier((joined, results))
        mixed = [joined, swap(joined, axis, size, step)]
        if number < 2 and distance < frames:
            here, mixed[1] = lax.optimization_barrier((grads[distance], mixed[1]))
            results = backward(scalars, kept, here, distance, results)
            distance += 1
    grad_gains = gain_gradients(scalars, mixed, gains, own, frames, clips)
    if results:
        grad_gains, results = lax.optimization_barrier((grad_gains, results))
    for distance in range(distance, frames):
        results = backward(scalars, kept, grads[distance], distance, results)
    grad_queries, grad_keys = results
    return (
        grad_queries.reshape(query_heads.shape),
        grad_keys.reshape(query_heads.shape),
        grad_gains,
    )


def temporal_grads(attended, upstream, gain_query, gain_keys, length):
    highest = lax.Precision.HIGHEST
    frames = attended.shape[0]
    score_scale = attended.shape[-1] ** (-0.5)
    floats = attended.astype(jnp.float32)
    inverse_rms = lax.rsqrt(jnp.mean(floats * floats, axis=-1, keepdims=True) + 1e-06)
    normed = floats * inverse_rms
    t_query = normed * gain_query
    t_keys = normed * gain_keys
    scores = jnp.einsum("txhd,uxhd->xhtu", t_query, t_keys, precision=highest) * score_scale
    frame_ids = jnp.arange(frames, dtype=jnp.int32)
    allowed = (frame_ids[None, :] <= frame_ids[:, None]) & (frame_ids[None, :] < length)
    scores = jnp.where(allowed, scores, -1e30)
    weights = jax.nn.softmax(scores, axis=-1)
    weights_low = lax.optimization_barrier(weights.astype(jnp.bfloat16)).astype(jnp.float32)
    valid_rows = (frame_ids < length).astype(jnp.float32)
    masked = upstream.astype(jnp.float32) * valid_rows[:, None, None, None]
    grad_weights = jnp.einsum("txhd,uxhd->xhtu", masked, floats, precision=highest)
    from_values = jnp.einsum("xhtu,txhd->uxhd", weights_low, masked, precision=highest)
    grad_scores = (
        weights
        * (grad_weights - jnp.sum(grad_weights * weights, axis=-1, keepdims=True))
        * score_scale
    )
    grad_tquery = jnp.einsum("xhtu,uxhd->txhd", grad_scores, t_keys, precision=highest)
    grad_tkeys = jnp.einsum("xhtu,txhd->uxhd", grad_scores, t_query, precision=highest)
    grad_normed = grad_tquery * gain_query + grad_tkeys * gain_keys
    grad_gain_query = jnp.sum(grad_tquery * normed, axis=(0, 1))
    grad_gain_keys = jnp.sum(grad_tkeys * normed, axis=(0, 1))
    from_norm = inverse_rms * (
        grad_normed - normed * jnp.mean(grad_normed * normed, axis=-1, keepdims=True)
    )
    grad_total = (masked + from_values + from_norm).astype(jnp.bfloat16)
    return (grad_total, grad_gain_query, grad_gain_keys)


def split_by_patches(query_heads, key_heads, value_heads, cotangent, task_ids, lengths, gains):
    patches, feat = query_heads.shape[2:]
    heads = feat // HEAD_DIM
    queries, key_rows, values = (
        field.reshape(patches, feat) for field in (query_heads, key_heads, value_heads)
    )
    scalars = jnp.zeros((1,), jnp.int32)
    kept, attended = forward(scalars, queries, key_rows, values, 1)
    attended_field = jnp.transpose(attended[0], (2, 0, 1)).reshape(1, 1, patches, feat)
    upstream = lax.all_to_all(
        lax.all_to_all(cotangent, "space", split_axis=3, concat_axis=2, tiled=True),
        "tm",
        split_axis=2,
        concat_axis=1,
        tiled=True,
    )
    frames_attended = lax.all_to_all(attended_field, "tm", split_axis=2, concat_axis=1, tiled=True)
    frames, local_patches = frames_attended.shape[1:3]
    selector = (task_ids[0] == jnp.arange(gains.shape[1], dtype=jnp.int32)).astype(jnp.float32)
    gain_query = jnp.sum(selector[:, None] * gains[0], axis=0).reshape(heads, HEAD_DIM)
    gain_keys = jnp.sum(selector[:, None] * gains[1], axis=0).reshape(heads, HEAD_DIM)
    grad_total, grad_gq, grad_gk = temporal_grads(
        frames_attended.reshape(frames, local_patches, heads, HEAD_DIM),
        upstream.reshape(frames, local_patches, heads, HEAD_DIM),
        gain_query,
        gain_keys,
        lengths[0],
    )
    gain_terms = jnp.stack(
        [
            selector[:, None] * grad_gq.reshape(1, feat),
            selector[:, None] * grad_gk.reshape(1, feat),
        ]
    )
    grad_gains = lax.psum(gain_terms, ("dp", "tm"))
    returned = lax.all_to_all(
        grad_total.reshape(1, frames, local_patches, feat),
        "tm",
        split_axis=1,
        concat_axis=2,
        tiled=True,
    )
    head_grads = jnp.transpose(returned.reshape(patches, heads, HEAD_DIM), (1, 2, 0))
    grad_queries, grad_keys = backward(scalars, kept, head_grads, 0, ())
    return (
        grad_queries.reshape(query_heads.shape),
        grad_keys.reshape(query_heads.shape),
        grad_gains,
    )


def solution(mesh):
    clips, frames, spaces = (mesh.shape[axis] for axis in ("dp", "tm", "space"))

    def local(query_heads, *others):
        heads = query_heads.shape[3] // HEAD_DIM
        powers = all(size & (size - 1) == 0 for size in (clips, frames))
        if powers and frames <= 4 and heads % frames == 0:
            return split_by_heads(query_heads, *others, clips, frames, spaces)
        return split_by_patches(query_heads, *others)

    return jax.shard_map(
        local,
        mesh=mesh,
        in_specs=(
            P("dp", "tm", None, "space"),
            P("dp", "tm", None, "space"),
            P("dp", "tm", None, "space"),
            P("dp", "tm", "space", None),
            P("dp"),
            P("dp"),
            P(None, None, "space"),
        ),
        out_specs=(
            P("dp", "tm", None, "space"),
            P("dp", "tm", None, "space"),
            P(None, None, "space"),
        ),
        check_vma=False,
    )
```

```python
import functools

import jax
import jax.numpy as jnp
from jax import lax
from jax.experimental import pallas as pl
from jax.experimental.pallas import tpu as pltpu
from jax.sharding import PartitionSpec as P

HEAD_DIM = 128
GROUP = 16
MIB = 1024 * 1024


def params(patches):
    return pltpu.CompilerParams(vmem_limit_bytes=(16 if patches <= 512 else 60) * MIB)


def cost(microseconds):
    return pl.CostEstimate(flops=int(microseconds * 1e8), bytes_accessed=0, transcendentals=0)


def columns_dot(left, right):
    return lax.dot_general(
        left, right, (((1,), (1,)), ((), ())), preferred_element_type=jnp.float32
    )


def dot(left, right):
    return jnp.dot(left, right, preferred_element_type=jnp.float32)


def partner(scalars, distance):
    return jnp.bitwise_xor(scalars[0], distance)


def forward_kernel(scalars, query_ref, key_ref, value_ref, weights_ref, *refs):
    (queries, key_rows, values, arrived), attended_refs = refs[-4:], refs[:-4]
    score_scale = HEAD_DIM ** (-0.5)
    groups, _, width = queries.shape
    own = width // HEAD_DIM
    copies = []
    for group in range(groups):
        cols = pl.ds(pl.multiple_of(partner(scalars, group) * width, HEAD_DIM), width)
        for field, (source, target) in enumerate(
            ((query_ref, queries), (key_ref, key_rows), (value_ref, values))
        ):
            copy = pltpu.make_async_copy(
                source.at[:, cols], target.at[group], arrived.at[group, field]
            )
            copy.start()
            copies.append(copy)
    for group in range(groups):
        for copy in copies[3 * group : 3 * group + 3]:
            copy.wait()
        for head in range(own):
            cols = pl.ds(head * HEAD_DIM, HEAD_DIM)
            scores = columns_dot(key_rows[group, :, cols], queries[group, :, cols])
            largest = jnp.max(scores, axis=0, keepdims=True)
            raised = jnp.exp((scores - largest) * score_scale)
            weights = raised * (1.0 / jnp.sum(raised, axis=0, keepdims=True))
            weights_ref[group * own + head] = weights
            attended = dot(values[group, :, cols].T, weights.astype(jnp.bfloat16))
            attended_refs[group][head] = attended.astype(jnp.bfloat16)


def forward(scalars, queries, key_rows, values, groups):
    patches, feat = queries.shape
    heads = feat // HEAD_DIM
    own = heads // groups
    fields = [
        pltpu.with_memory_space_constraint(field, pltpu.HBM) for field in (queries, key_rows, values)
    ]
    weights, *attended = pl.pallas_call(
        forward_kernel,
        in_specs=[pl.BlockSpec(memory_space=pltpu.SMEM)]
        + [pl.BlockSpec(memory_space=pltpu.HBM)] * 3,
        out_specs=[pl.BlockSpec(memory_space=pltpu.VMEM)] * (1 + groups),
        scratch_shapes=[pltpu.VMEM((groups, patches, feat // groups), jnp.bfloat16)] * 3
        + [pltpu.SemaphoreType.DMA((groups, 3))],
        out_shape=[jax.ShapeDtypeStruct((heads, patches, patches), jnp.float32)]
        + [jax.ShapeDtypeStruct((own, HEAD_DIM, patches), jnp.bfloat16)] * groups,
        compiler_params=params(patches),
        cost_estimate=cost(6),
        name="spatial_forward",
    )(scalars, *fields)
    return weights, attended


def backward_kernel(distance, scalars, query_ref, key_ref, value_ref, weights_ref, grad_ref, *refs):
    gq_ref, gk_ref, gq, gk, sent = refs[-5:]
    score_scale = HEAD_DIM ** (-0.5)
    own = grad_ref.shape[0]
    start = partner(scalars, distance) * (own * HEAD_DIM)
    columns = [
        pl.ds(pl.multiple_of(start + head * HEAD_DIM, HEAD_DIM), HEAD_DIM) for head in range(own)
    ]
    spatial_grads = [dot(value_ref[:, columns[head]], grad_ref[head]) for head in range(own)]
    all_scores = []
    for head, spatial_grad in enumerate(spatial_grads):
        weights = weights_ref[distance * own + head]
        row_sum = jnp.sum(spatial_grad * weights, axis=0, keepdims=True)
        scores = weights * (spatial_grad - row_sum) * score_scale
        all_scores.append(scores.astype(jnp.bfloat16))
    for head, scores in enumerate(all_scores):
        cols = pl.ds(head * HEAD_DIM, HEAD_DIM)
        gk[:, cols] = dot(scores, query_ref[:, columns[head]]).astype(jnp.bfloat16)
        gq[:, cols] = dot(key_ref[:, columns[head]].T, scores).astype(jnp.bfloat16).T
    there = pl.ds(pl.multiple_of(start, HEAD_DIM), own * HEAD_DIM)
    copies = [
        pltpu.make_async_copy(gq, gq_ref.at[:, there], sent.at[0]),
        pltpu.make_async_copy(gk, gk_ref.at[:, there], sent.at[1]),
    ]
    for copy in copies:
        copy.start()
    for copy in copies:
        copy.wait()


def backward(scalars, fields, weights, grads, distance, earlier):
    patches, feat = fields[0].shape
    own = grads.shape[0]
    return pl.pallas_call(
        functools.partial(backward_kernel, distance),
        in_specs=[pl.BlockSpec(memory_space=pltpu.SMEM)]
        + [pl.BlockSpec(memory_space=pltpu.VMEM)] * 5
        + [pl.BlockSpec(memory_space=pl.ANY)] * len(earlier),
        out_specs=[pl.BlockSpec(memory_space=pl.ANY)] * 2,
        scratch_shapes=[pltpu.VMEM((patches, own * HEAD_DIM), jnp.bfloat16)] * 2
        + [pltpu.SemaphoreType.DMA((2,))],
        out_shape=[jax.ShapeDtypeStruct((patches, feat), jnp.bfloat16)] * 2,
        input_output_aliases={6 + index: index for index in range(len(earlier))},
        compiler_params=params(patches),
        cost_estimate=cost(2),
        name="spatial_backward",
    )(scalars, *fields, weights, grads, *earlier)


def pack_kernel(frames, spaces, field_ref, packed_ref, sent):
    width = packed_ref.shape[2]
    copies = []
    for frame in range(frames):
        for space in range(spaces):
            index = frame * spaces + space
            cols = pl.ds((space * frames + frame) * width, width)
            copy = pltpu.make_async_copy(field_ref.at[:, cols], packed_ref.at[index], sent.at[index])
            copy.start()
            copies.append(copy)
    for copy in copies:
        copy.wait()


def pack(field, frames, spaces):
    patches, feat = field.shape
    devices = frames * spaces
    return pl.pallas_call(
        functools.partial(pack_kernel, frames, spaces),
        in_specs=[pl.BlockSpec(memory_space=pl.ANY)],
        out_specs=pl.BlockSpec(memory_space=pl.ANY),
        out_shape=jax.ShapeDtypeStruct((devices, patches, feat // devices), field.dtype),
        scratch_shapes=[pltpu.SemaphoreType.DMA((devices,))],
        compiler_params=params(0),
        cost_estimate=cost(1),
        name="pack_cotangent",
    )(field)


def turn_kernel(field_ref, turned_ref):
    spaces, frames = turned_ref.shape[:2]
    for space in range(spaces):
        for frame in range(frames):
            turned_ref[space, frame, 0] = field_ref[frame * spaces + space].T


def turn(field, frames, spaces):
    devices, patches, feat = field.shape
    heads = feat // HEAD_DIM
    return pl.pallas_call(
        turn_kernel,
        grid=(heads,),
        in_specs=[pl.BlockSpec((devices, patches, HEAD_DIM), lambda i: (0, 0, i))],
        out_specs=pl.BlockSpec((spaces, frames, 1, HEAD_DIM, patches), lambda i: (0, 0, i, 0, 0)),
        out_shape=jax.ShapeDtypeStruct((spaces, frames, heads, HEAD_DIM, patches), field.dtype),
        compiler_params=params(patches),
        cost_estimate=cost(2),
        name="turn_cotangent",
    )(field)


def temporal_part(length, attended_ref, upstream_ref, gain_ref, grad_ref, mixed_sum, part):
    frames, feat, _ = attended_ref.shape
    lanes = upstream_ref.shape[-1]
    here = pl.ds(part * lanes, lanes)
    half = GROUP // 2
    score_scale = feat ** (-0.5)
    pairs = [(t, u) for t in range(frames) for u in range(t + 1)]
    every = range(frames)
    valid = [jnp.where(t < length, 1.0, 0.0).astype(jnp.float32) for t in every]
    bias = [jnp.where(u < length, 0.0, -1e30).astype(jnp.float32) for u in every]

    def split(block):
        block = block.astype(jnp.float32)
        return block[:half], block[half:]

    def load_fields(group):
        return [split(attended_ref[t, pl.ds(group * GROUP, GROUP), here]) for t in every]

    def load_ups(group):
        return [split(upstream_ref[part, t, 0, pl.ds(group * GROUP, GROUP), :]) for t in every]

    def total(piece):
        return jnp.broadcast_to(jnp.sum(piece, axis=0, keepdims=True), (half, lanes))

    squares = [jnp.zeros((half, lanes), jnp.float32) for _ in every]
    for group in range(feat // GROUP):
        for t, (low, high) in enumerate(load_fields(group)):
            squares[t] = squares[t] + (low * low + high * high)
    inverse = [lax.rsqrt(total(squares[t]) * (1.0 / feat) + 1e-06) for t in every]

    raw = {pair: jnp.zeros((half, lanes), jnp.float32) for pair in pairs}
    grad = {pair: jnp.zeros((half, lanes), jnp.float32) for pair in pairs}
    for group in range(feat // GROUP):
        fields, ups = load_fields(group), load_ups(group)
        for side in range(2):
            gain = gain_ref[0, pl.ds(group * GROUP + side * half, half), :]
            normed = [fields[t][side] * inverse[t] for t in every]
            gained = [normed[t] * gain for t in every]
            for t, u in pairs:
                raw[t, u] = raw[t, u] + gained[t] * normed[u]
                grad[t, u] = grad[t, u] + ups[t][side] * fields[u][side]

    value_part, score_part = {}, {}
    for t in every:
        seen = range(t + 1)
        for u in seen:
            raw[t, u] = total(raw[t, u])
            grad[t, u] = total(grad[t, u]) * valid[t]
        scores = [raw[t, u] * score_scale + bias[u] for u in seen]
        largest = functools.reduce(jnp.maximum, scores)
        raised = [jnp.exp(score - largest) for score in scores]
        over = 1.0 / functools.reduce(jnp.add, raised)
        weights = [piece * over for piece in raised]
        mean_grad = functools.reduce(jnp.add, [weights[u] * grad[t, u] for u in seen])
        for u in seen:
            rounded = weights[u].astype(jnp.bfloat16).astype(jnp.float32)
            value_part[t, u] = (rounded + (1.0 if u == t else 0.0)) * valid[t]
            score_part[t, u] = weights[u] * (grad[t, u] - mean_grad) * score_scale

    both = {(t, u): score_part[t, u] * (2.0 if t == u else 1.0) for t, u in pairs}
    both.update({(u, t): both[t, u] for t, u in pairs})
    raw.update({(u, t): raw[t, u] for t, u in pairs})
    mean_part = [
        functools.reduce(jnp.add, [both[u, v] * raw[u, v] for v in every]) * (1.0 / feat)
        for u in every
    ]

    for group in range(feat // GROUP):
        fields, ups = load_fields(group), load_ups(group)
        outs = [[] for _ in every]
        for side in range(2):
            rows = pl.ds(group * GROUP + side * half, half)
            gain = gain_ref[0, rows, :]
            normed = [fields[t][side] * inverse[t] for t in every]
            mixed = jnp.zeros((half, lanes), jnp.float32)
            for u in every:
                crossed = functools.reduce(jnp.add, [both[u, v] * normed[v] for v in every])
                mixed = mixed + crossed * normed[u]
                from_norm = inverse[u] * (gain * crossed - normed[u] * mean_part[u])
                direct = functools.reduce(
                    jnp.add, [value_part[t, u] * ups[t][side] for t in range(u, frames)]
                )
                outs[u].append(direct + from_norm)
            mixed_sum[rows, :] = mixed if part == 0 else mixed_sum[rows, :] + mixed
        for u in every:
            grad_ref[u, pl.ds(group * GROUP, GROUP), here] = jnp.concatenate(
                outs[u], axis=0
            ).astype(jnp.bfloat16)


def temporal_kernel(frames, scalars, *refs):
    attended_refs, (upstream_ref, gain_ref) = refs[:frames], refs[frames : frames + 2]
    grad_refs, mixed_ref = refs[frames + 2 : 2 * frames + 2], refs[2 * frames + 2]
    attended, grads, mixed_sum = refs[2 * frames + 3 :]
    head = pl.program_id(0)
    for distance, ref in enumerate(attended_refs):
        attended[partner(scalars, distance)] = ref[0]
    for part in range(upstream_ref.shape[0]):
        temporal_part(scalars[1], attended, upstream_ref, gain_ref, grads, mixed_sum, part)
    for distance, ref in enumerate(grad_refs):
        ref[0] = grads[partner(scalars, distance)]

    @pl.when(head == 0)
    def _():
        mixed_ref[...] = jnp.full(mixed_ref.shape, scalars[2].astype(jnp.float32))

    mixed_ref[pl.ds(head, 1), :] = jnp.sum(mixed_sum[...].T, axis=0, keepdims=True) * 0.5


def temporal(scalars, attended, upstream, gain):
    spaces, frames, heads, feat, lanes = upstream.shape
    patches = spaces * lanes
    rows = -(-(heads + 1) // 8) * 8
    plane = pl.BlockSpec((1, feat, patches), lambda i, sc: (i, 0, 0))
    *grads, mixed = pl.pallas_call(
        functools.partial(temporal_kernel, frames),
        grid_spec=pltpu.PrefetchScalarGridSpec(
            num_scalar_prefetch=1,
            grid=(heads,),
            in_specs=[plane] * frames
            + [
                pl.BlockSpec((spaces, frames, 1, feat, lanes), lambda i, sc: (0, 0, i, 0, 0)),
                pl.BlockSpec((1, feat, lanes), lambda i, sc: (i, 0, 0)),
            ],
            out_specs=[plane] * frames + [pl.BlockSpec((rows, feat), lambda i, sc: (0, 0))],
            scratch_shapes=[
                pltpu.VMEM((frames, feat, patches), jnp.bfloat16),
                pltpu.VMEM((frames, feat, patches), jnp.bfloat16),
                pltpu.VMEM((feat, lanes), jnp.float32),
            ],
        ),
        out_shape=[jax.ShapeDtypeStruct((heads, feat, patches), jnp.bfloat16)] * frames
        + [jax.ShapeDtypeStruct((rows, feat), jnp.float32)],
        compiler_params=params(patches),
        cost_estimate=cost(4),
        name="temporal",
    )(scalars, *attended, upstream, gain)
    return grads, mixed


def gains_kernel(heads, frames, clips, scalars, *refs):
    mixed_refs, gains_ref, grad_ref = refs[:-2], refs[-2], refs[-1]
    tasks = gains_ref.shape[1]
    rows = sum(ref.shape[0] for ref in mixed_refs) // (frames * clips)
    each = mixed_refs[0].shape[0] // rows
    task_ids = lax.broadcasted_iota(jnp.int32, (tasks, HEAD_DIM), 0).astype(jnp.float32)
    for distance in range(frames):
        for head in range(heads):
            mixed = jnp.zeros((tasks, HEAD_DIM), jnp.float32)
            for clip in range(clips):
                block = distance * clips + clip
                ref, start = mixed_refs[block // each], block % each * rows
                task = ref[pl.ds(start + heads, 1), :]
                row = ref[pl.ds(start + head, 1), :]
                mixed = mixed + jnp.where(task_ids == task, row, 0.0)
            start = (partner(scalars, distance) * heads + head) * HEAD_DIM
            cols = pl.ds(pl.multiple_of(start, HEAD_DIM), HEAD_DIM)
            grad_ref[0, :, cols] = gains_ref[1, :, cols] * mixed
            grad_ref[1, :, cols] = gains_ref[0, :, cols] * mixed


def gain_gradients(scalars, mixed, gains, heads, frames, clips):
    return pl.pallas_call(
        functools.partial(gains_kernel, heads, frames, clips),
        in_specs=[pl.BlockSpec(memory_space=pltpu.SMEM)]
        + [pl.BlockSpec(memory_space=pltpu.VMEM)] * (len(mixed) + 1),
        out_specs=pl.BlockSpec(memory_space=pltpu.VMEM),
        out_shape=jax.ShapeDtypeStruct(gains.shape, jnp.float32),
        compiler_params=params(0),
        cost_estimate=cost(1),
        name="gain_gradients",
    )(scalars, *mixed, gains)


def swap(field, axis, size, distance):
    return lax.ppermute(field, axis, [(i, i ^ distance) for i in range(size)])


def split_by_heads(
    query_heads, key_heads, value_heads, cotangent, task_ids, lengths, gains, clips, frames, spaces
):
    patches, feat = query_heads.shape[2:]
    heads = feat // HEAD_DIM
    own = heads // frames
    width = own * HEAD_DIM
    queries, key_rows, values = (
        field.reshape(patches, feat) for field in (query_heads, key_heads, value_heads)
    )
    frame = lax.axis_index("tm")
    scalars = jnp.stack([frame, lengths[0], task_ids[0]]).astype(jnp.int32)

    packed = pack(cotangent.reshape(cotangent.shape[2:]), frames, spaces)
    incoming = lax.all_to_all(packed, ("tm", "space"), split_axis=0, concat_axis=0, tiled=True)
    queries, _ = lax.optimization_barrier((queries, packed))
    fields = (queries, key_rows, values)
    weights, attended = forward(scalars, *fields, frames)
    attended = [attended[0]] + [
        swap(attended[distance], "tm", frames, distance) for distance in range(1, frames)
    ]
    incoming, _ = lax.optimization_barrier((incoming, weights))
    upstream = turn(incoming, frames, spaces)
    rows = lax.dynamic_index_in_dim(gains, task_ids[0], 1, keepdims=False)
    product = lax.dynamic_slice_in_dim(rows[0] * rows[1], frame * width, width, 0)
    gain = jnp.broadcast_to(
        product.reshape(own, HEAD_DIM, 1), (own, HEAD_DIM, patches // spaces)
    )
    grads, mixed = temporal(scalars, attended, upstream, gain)
    grads = [grads[0]] + [
        swap(grads[distance], "tm", frames, distance) for distance in range(1, frames)
    ]
    rounds = [("dp", clips, 1 << bit) for bit in range(clips.bit_length() - 1)]
    rounds += [("tm", frames, 1 << bit) for bit in range(frames.bit_length() - 1)]
    mixed, results, distance = [mixed], (), 0
    for number, (axis, size, step) in enumerate(rounds):
        joined = jnp.concatenate(mixed, axis=0)
        if results and number >= 2:
            joined, results = lax.optimization_barrier((joined, results))
        mixed = [joined, swap(joined, axis, size, step)]
        here = grads[distance]
        if number == 0:
            here, mixed[1] = lax.optimization_barrier((here, mixed[1]))
        if number in (0, 2) and distance < frames - 1:
            results = backward(scalars, fields, weights, here, distance, results)
            distance += 1
    grad_gains = gain_gradients(scalars, mixed, gains, own, frames, clips)
    if results:
        grad_gains, results = lax.optimization_barrier((grad_gains, results))
    for distance in range(distance, frames):
        results = backward(scalars, fields, weights, grads[distance], distance, results)
    grad_queries, grad_keys = results
    return (
        grad_queries.reshape(query_heads.shape),
        grad_keys.reshape(query_heads.shape),
        grad_gains,
    )


def temporal_grads(attended, upstream, gain_query, gain_keys, length):
    highest = lax.Precision.HIGHEST
    frames = attended.shape[0]
    score_scale = attended.shape[-1] ** (-0.5)
    floats = attended.astype(jnp.float32)
    inverse_rms = lax.rsqrt(jnp.mean(floats * floats, axis=-1, keepdims=True) + 1e-06)
    normed = floats * inverse_rms
    t_query = normed * gain_query
    t_keys = normed * gain_keys
    scores = jnp.einsum("txhd,uxhd->xhtu", t_query, t_keys, precision=highest) * score_scale
    frame_ids = jnp.arange(frames, dtype=jnp.int32)
    allowed = (frame_ids[None, :] <= frame_ids[:, None]) & (frame_ids[None, :] < length)
    scores = jnp.where(allowed, scores, -1e30)
    weights = jax.nn.softmax(scores, axis=-1)
    weights_low = lax.optimization_barrier(weights.astype(jnp.bfloat16)).astype(jnp.float32)
    valid_rows = (frame_ids < length).astype(jnp.float32)
    masked = upstream.astype(jnp.float32) * valid_rows[:, None, None, None]
    grad_weights = jnp.einsum("txhd,uxhd->xhtu", masked, floats, precision=highest)
    from_values = jnp.einsum("xhtu,txhd->uxhd", weights_low, masked, precision=highest)
    grad_scores = (
        weights
        * (grad_weights - jnp.sum(grad_weights * weights, axis=-1, keepdims=True))
        * score_scale
    )
    grad_tquery = jnp.einsum("xhtu,uxhd->txhd", grad_scores, t_keys, precision=highest)
    grad_tkeys = jnp.einsum("xhtu,txhd->uxhd", grad_scores, t_query, precision=highest)
    grad_normed = grad_tquery * gain_query + grad_tkeys * gain_keys
    grad_gain_query = jnp.sum(grad_tquery * normed, axis=(0, 1))
    grad_gain_keys = jnp.sum(grad_tkeys * normed, axis=(0, 1))
    from_norm = inverse_rms * (
        grad_normed - normed * jnp.mean(grad_normed * normed, axis=-1, keepdims=True)
    )
    grad_total = (masked + from_values + from_norm).astype(jnp.bfloat16)
    return (grad_total, grad_gain_query, grad_gain_keys)


def split_by_patches(query_heads, key_heads, value_heads, cotangent, task_ids, lengths, gains):
    patches, feat = query_heads.shape[2:]
    heads = feat // HEAD_DIM
    queries, key_rows, values = (
        field.reshape(patches, feat) for field in (query_heads, key_heads, value_heads)
    )
    scalars = jnp.zeros((1,), jnp.int32)
    fields = (queries, key_rows, values)
    weights, attended = forward(scalars, *fields, 1)
    attended_field = jnp.transpose(attended[0], (2, 0, 1)).reshape(1, 1, patches, feat)
    upstream = lax.all_to_all(
        lax.all_to_all(cotangent, "space", split_axis=3, concat_axis=2, tiled=True),
        "tm",
        split_axis=2,
        concat_axis=1,
        tiled=True,
    )
    frames_attended = lax.all_to_all(attended_field, "tm", split_axis=2, concat_axis=1, tiled=True)
    frames, local_patches = frames_attended.shape[1:3]
    selector = (task_ids[0] == jnp.arange(gains.shape[1], dtype=jnp.int32)).astype(jnp.float32)
    gain_query = jnp.sum(selector[:, None] * gains[0], axis=0).reshape(heads, HEAD_DIM)
    gain_keys = jnp.sum(selector[:, None] * gains[1], axis=0).reshape(heads, HEAD_DIM)
    grad_total, grad_gq, grad_gk = temporal_grads(
        frames_attended.reshape(frames, local_patches, heads, HEAD_DIM),
        upstream.reshape(frames, local_patches, heads, HEAD_DIM),
        gain_query,
        gain_keys,
        lengths[0],
    )
    gain_terms = jnp.stack(
        [
            selector[:, None] * grad_gq.reshape(1, feat),
            selector[:, None] * grad_gk.reshape(1, feat),
        ]
    )
    grad_gains = lax.psum(gain_terms, ("dp", "tm"))
    returned = lax.all_to_all(
        grad_total.reshape(1, frames, local_patches, feat),
        "tm",
        split_axis=1,
        concat_axis=2,
        tiled=True,
    )
    head_grads = jnp.transpose(returned.reshape(patches, heads, HEAD_DIM), (1, 2, 0))
    grad_queries, grad_keys = backward(scalars, fields, weights, head_grads, 0, ())
    return (
        grad_queries.reshape(query_heads.shape),
        grad_keys.reshape(query_heads.shape),
        grad_gains,
    )


def solution(mesh):
    clips, frames, spaces = (mesh.shape[axis] for axis in ("dp", "tm", "space"))

    def local(query_heads, *others):
        heads = query_heads.shape[3] // HEAD_DIM
        powers = all(size & (size - 1) == 0 for size in (clips, frames))
        if powers and frames <= 4 and heads % frames == 0:
            return split_by_heads(query_heads, *others, clips, frames, spaces)
        return split_by_patches(query_heads, *others)

    return jax.shard_map(
        local,
        mesh=mesh,
        in_specs=(
            P("dp", "tm", None, "space"),
            P("dp", "tm", None, "space"),
            P("dp", "tm", None, "space"),
            P("dp", "tm", "space", None),
            P("dp"),
            P("dp"),
            P(None, None, "space"),
        ),
        out_specs=(
            P("dp", "tm", None, "space"),
            P("dp", "tm", None, "space"),
            P(None, None, "space"),
        ),
        check_vma=False,
    )
```

```python
import functools

import jax
import jax.numpy as jnp
from jax import lax
from jax.experimental import pallas as pl
from jax.experimental.pallas import tpu as pltpu
from jax.sharding import PartitionSpec as P

HEAD_DIM = 128
GROUP = 16
MIB = 1024 * 1024


def params(patches):
    return pltpu.CompilerParams(vmem_limit_bytes=(16 if patches <= 512 else 60) * MIB)


def cost(microseconds):
    return pl.CostEstimate(flops=int(microseconds * 1e8), bytes_accessed=0, transcendentals=0)


def columns_dot(left, right):
    return lax.dot_general(
        left, right, (((1,), (1,)), ((), ())), preferred_element_type=jnp.float32
    )


def dot(left, right):
    return jnp.dot(left, right, preferred_element_type=jnp.float32)


def partner(scalars, distance):
    return jnp.bitwise_xor(scalars[0], distance)


def forward_kernel(scalars, query_ref, key_ref, value_ref, weights_ref, *refs):
    (queries, key_rows, values, arrived), attended_refs = refs[-4:], refs[:-4]
    score_scale = HEAD_DIM ** (-0.5)
    groups, _, width = queries.shape
    own = width // HEAD_DIM
    copies = []
    for group in range(groups):
        cols = pl.ds(pl.multiple_of(partner(scalars, group) * width, HEAD_DIM), width)
        for field, (source, target) in enumerate(
            ((query_ref, queries), (key_ref, key_rows), (value_ref, values))
        ):
            copy = pltpu.make_async_copy(
                source.at[:, cols], target.at[group], arrived.at[group, field]
            )
            copy.start()
            copies.append(copy)
    for group in range(groups):
        for copy in copies[3 * group : 3 * group + 3]:
            copy.wait()
        for head in range(own):
            cols = pl.ds(head * HEAD_DIM, HEAD_DIM)
            scores = columns_dot(key_rows[group, :, cols], queries[group, :, cols])
            largest = jnp.max(scores, axis=0, keepdims=True)
            raised = jnp.exp((scores - largest) * score_scale)
            weights = raised * (1.0 / jnp.sum(raised, axis=0, keepdims=True))
            weights_ref[group * own + head] = weights
            attended = dot(values[group, :, cols].T, weights.astype(jnp.bfloat16))
            attended_refs[group][head] = attended.astype(jnp.bfloat16)


def forward(scalars, queries, key_rows, values, groups):
    patches, feat = queries.shape
    heads = feat // HEAD_DIM
    own = heads // groups
    fields = [
        pltpu.with_memory_space_constraint(field, pltpu.HBM) for field in (queries, key_rows, values)
    ]
    weights, *attended = pl.pallas_call(
        forward_kernel,
        in_specs=[pl.BlockSpec(memory_space=pltpu.SMEM)]
        + [pl.BlockSpec(memory_space=pltpu.HBM)] * 3,
        out_specs=[pl.BlockSpec(memory_space=pltpu.VMEM)] * (1 + groups),
        scratch_shapes=[pltpu.VMEM((groups, patches, feat // groups), jnp.bfloat16)] * 3
        + [pltpu.SemaphoreType.DMA((groups, 3))],
        out_shape=[jax.ShapeDtypeStruct((heads, patches, patches), jnp.float32)]
        + [jax.ShapeDtypeStruct((own, HEAD_DIM, patches), jnp.bfloat16)] * groups,
        compiler_params=params(patches),
        cost_estimate=cost(6),
        name="spatial_forward",
    )(scalars, *fields)
    return weights, attended


def backward_kernel(distance, scalars, query_ref, key_ref, value_ref, weights_ref, grad_ref, *refs):
    gq_ref, gk_ref, gq, gk, sent = refs[-5:]
    score_scale = HEAD_DIM ** (-0.5)
    own = grad_ref.shape[0]
    start = partner(scalars, distance) * (own * HEAD_DIM)
    columns = [
        pl.ds(pl.multiple_of(start + head * HEAD_DIM, HEAD_DIM), HEAD_DIM) for head in range(own)
    ]
    spatial_grads = [dot(value_ref[:, columns[head]], grad_ref[head]) for head in range(own)]
    all_scores = []
    for head, spatial_grad in enumerate(spatial_grads):
        weights = weights_ref[distance * own + head]
        row_sum = jnp.sum(spatial_grad * weights, axis=0, keepdims=True)
        scores = weights * (spatial_grad - row_sum) * score_scale
        all_scores.append(scores.astype(jnp.bfloat16))
    there = pl.ds(pl.multiple_of(start, HEAD_DIM), own * HEAD_DIM)
    copies = [
        pltpu.make_async_copy(gk, gk_ref.at[:, there], sent.at[0]),
        pltpu.make_async_copy(gq, gq_ref.at[:, there], sent.at[1]),
    ]
    for head, scores in enumerate(all_scores):
        cols = pl.ds(head * HEAD_DIM, HEAD_DIM)
        gk[:, cols] = dot(scores, query_ref[:, columns[head]]).astype(jnp.bfloat16)
    copies[0].start()
    for head, scores in enumerate(all_scores):
        cols = pl.ds(head * HEAD_DIM, HEAD_DIM)
        gq[:, cols] = dot(key_ref[:, columns[head]].T, scores).astype(jnp.bfloat16).T
    copies[1].start()
    for copy in copies:
        copy.wait()


def backward(scalars, fields, weights, grads, distance, earlier):
    patches, feat = fields[0].shape
    own = grads.shape[0]
    return pl.pallas_call(
        functools.partial(backward_kernel, distance),
        in_specs=[pl.BlockSpec(memory_space=pltpu.SMEM)]
        + [pl.BlockSpec(memory_space=pltpu.VMEM)] * 5
        + [pl.BlockSpec(memory_space=pl.ANY)] * len(earlier),
        out_specs=[pl.BlockSpec(memory_space=pl.ANY)] * 2,
        scratch_shapes=[pltpu.VMEM((patches, own * HEAD_DIM), jnp.bfloat16)] * 2
        + [pltpu.SemaphoreType.DMA((2,))],
        out_shape=[jax.ShapeDtypeStruct((patches, feat), jnp.bfloat16)] * 2,
        input_output_aliases={6 + index: index for index in range(len(earlier))},
        compiler_params=params(patches),
        cost_estimate=cost(2),
        name="spatial_backward",
    )(scalars, *fields, weights, grads, *earlier)


def pack_kernel(frames, spaces, field_ref, packed_ref, sent):
    width = packed_ref.shape[2]
    copies = []
    for frame in range(frames):
        for space in range(spaces):
            index = frame * spaces + space
            cols = pl.ds((space * frames + frame) * width, width)
            copy = pltpu.make_async_copy(field_ref.at[:, cols], packed_ref.at[index], sent.at[index])
            copy.start()
            copies.append(copy)
    for copy in copies:
        copy.wait()


def pack(field, frames, spaces):
    patches, feat = field.shape
    devices = frames * spaces
    return pl.pallas_call(
        functools.partial(pack_kernel, frames, spaces),
        in_specs=[pl.BlockSpec(memory_space=pl.ANY)],
        out_specs=pl.BlockSpec(memory_space=pl.ANY),
        out_shape=jax.ShapeDtypeStruct((devices, patches, feat // devices), field.dtype),
        scratch_shapes=[pltpu.SemaphoreType.DMA((devices,))],
        compiler_params=params(0),
        cost_estimate=cost(1),
        name="pack_cotangent",
    )(field)


def turn_kernel(field_ref, turned_ref):
    spaces, frames = turned_ref.shape[:2]
    for space in range(spaces):
        for frame in range(frames):
            turned_ref[space, frame, 0] = field_ref[frame * spaces + space].T


def turn(field, frames, spaces):
    devices, patches, feat = field.shape
    heads = feat // HEAD_DIM
    return pl.pallas_call(
        turn_kernel,
        grid=(heads,),
        in_specs=[pl.BlockSpec((devices, patches, HEAD_DIM), lambda i: (0, 0, i))],
        out_specs=pl.BlockSpec((spaces, frames, 1, HEAD_DIM, patches), lambda i: (0, 0, i, 0, 0)),
        out_shape=jax.ShapeDtypeStruct((spaces, frames, heads, HEAD_DIM, patches), field.dtype),
        compiler_params=params(patches),
        cost_estimate=cost(2),
        name="turn_cotangent",
    )(field)


def temporal_part(length, attended_ref, upstream_ref, gain_ref, grad_ref, mixed_sum, part):
    frames, feat, _ = attended_ref.shape
    lanes = upstream_ref.shape[-1]
    here = pl.ds(part * lanes, lanes)
    half = GROUP // 2
    score_scale = feat ** (-0.5)
    pairs = [(t, u) for t in range(frames) for u in range(t + 1)]
    every = range(frames)
    valid = [jnp.where(t < length, 1.0, 0.0).astype(jnp.float32) for t in every]
    bias = [jnp.where(u < length, 0.0, -1e30).astype(jnp.float32) for u in every]

    def split(block):
        block = block.astype(jnp.float32)
        return block[:half], block[half:]

    def load_fields(group):
        return [split(attended_ref[t, pl.ds(group * GROUP, GROUP), here]) for t in every]

    def load_ups(group):
        return [split(upstream_ref[part, t, 0, pl.ds(group * GROUP, GROUP), :]) for t in every]

    def total(piece):
        return jnp.broadcast_to(jnp.sum(piece, axis=0, keepdims=True), (half, lanes))

    squares = [jnp.zeros((half, lanes), jnp.float32) for _ in every]
    for group in range(feat // GROUP):
        for t, (low, high) in enumerate(load_fields(group)):
            squares[t] = squares[t] + (low * low + high * high)
    inverse = [lax.rsqrt(total(squares[t]) * (1.0 / feat) + 1e-06) for t in every]

    raw = {pair: jnp.zeros((half, lanes), jnp.float32) for pair in pairs}
    grad = {pair: jnp.zeros((half, lanes), jnp.float32) for pair in pairs}
    for group in range(feat // GROUP):
        fields, ups = load_fields(group), load_ups(group)
        for side in range(2):
            gain = gain_ref[0, pl.ds(group * GROUP + side * half, half), :]
            normed = [fields[t][side] * inverse[t] for t in every]
            gained = [normed[t] * gain for t in every]
            for t, u in pairs:
                raw[t, u] = raw[t, u] + gained[t] * normed[u]
                grad[t, u] = grad[t, u] + ups[t][side] * fields[u][side]

    value_part, score_part = {}, {}
    for t in every:
        seen = range(t + 1)
        for u in seen:
            raw[t, u] = total(raw[t, u])
            grad[t, u] = total(grad[t, u]) * valid[t]
        scores = [raw[t, u] * score_scale + bias[u] for u in seen]
        largest = functools.reduce(jnp.maximum, scores)
        raised = [jnp.exp(score - largest) for score in scores]
        over = 1.0 / functools.reduce(jnp.add, raised)
        weights = [piece * over for piece in raised]
        mean_grad = functools.reduce(jnp.add, [weights[u] * grad[t, u] for u in seen])
        for u in seen:
            rounded = weights[u].astype(jnp.bfloat16).astype(jnp.float32)
            value_part[t, u] = (rounded + (1.0 if u == t else 0.0)) * valid[t]
            score_part[t, u] = weights[u] * (grad[t, u] - mean_grad) * score_scale

    both = {(t, u): score_part[t, u] * (2.0 if t == u else 1.0) for t, u in pairs}
    both.update({(u, t): both[t, u] for t, u in pairs})
    raw.update({(u, t): raw[t, u] for t, u in pairs})
    mean_part = [
        functools.reduce(jnp.add, [both[u, v] * raw[u, v] for v in every]) * (1.0 / feat)
        for u in every
    ]

    for group in range(feat // GROUP):
        fields, ups = load_fields(group), load_ups(group)
        outs = [[] for _ in every]
        for side in range(2):
            rows = pl.ds(group * GROUP + side * half, half)
            gain = gain_ref[0, rows, :]
            normed = [fields[t][side] * inverse[t] for t in every]
            mixed = jnp.zeros((half, lanes), jnp.float32)
            for u in every:
                crossed = functools.reduce(jnp.add, [both[u, v] * normed[v] for v in every])
                mixed = mixed + crossed * normed[u]
                from_norm = inverse[u] * (gain * crossed - normed[u] * mean_part[u])
                direct = functools.reduce(
                    jnp.add, [value_part[t, u] * ups[t][side] for t in range(u, frames)]
                )
                outs[u].append(direct + from_norm)
            mixed_sum[rows, :] = mixed if part == 0 else mixed_sum[rows, :] + mixed
        for u in every:
            grad_ref[u, pl.ds(group * GROUP, GROUP), here] = jnp.concatenate(
                outs[u], axis=0
            ).astype(jnp.bfloat16)


def temporal_kernel(frames, scalars, *refs):
    attended_refs, (upstream_ref, gain_ref) = refs[:frames], refs[frames : frames + 2]
    grad_refs, mixed_ref = refs[frames + 2 : 2 * frames + 2], refs[2 * frames + 2]
    attended, grads, mixed_sum = refs[2 * frames + 3 :]
    head = pl.program_id(0)
    for distance, ref in enumerate(attended_refs):
        attended[partner(scalars, distance)] = ref[0]
    for part in range(upstream_ref.shape[0]):
        temporal_part(scalars[1], attended, upstream_ref, gain_ref, grads, mixed_sum, part)
    for distance, ref in enumerate(grad_refs):
        ref[0] = grads[partner(scalars, distance)]

    @pl.when(head == 0)
    def _():
        mixed_ref[...] = jnp.full(mixed_ref.shape, scalars[2].astype(jnp.float32))

    mixed_ref[pl.ds(head, 1), :] = jnp.sum(mixed_sum[...].T, axis=0, keepdims=True) * 0.5


def temporal(scalars, attended, upstream, gain):
    spaces, frames, heads, feat, lanes = upstream.shape
    patches = spaces * lanes
    rows = -(-(heads + 1) // 8) * 8
    plane = pl.BlockSpec((1, feat, patches), lambda i, sc: (i, 0, 0))
    *grads, mixed = pl.pallas_call(
        functools.partial(temporal_kernel, frames),
        grid_spec=pltpu.PrefetchScalarGridSpec(
            num_scalar_prefetch=1,
            grid=(heads,),
            in_specs=[plane] * frames
            + [
                pl.BlockSpec((spaces, frames, 1, feat, lanes), lambda i, sc: (0, 0, i, 0, 0)),
                pl.BlockSpec((1, feat, lanes), lambda i, sc: (i, 0, 0)),
            ],
            out_specs=[plane] * frames + [pl.BlockSpec((rows, feat), lambda i, sc: (0, 0))],
            scratch_shapes=[
                pltpu.VMEM((frames, feat, patches), jnp.bfloat16),
                pltpu.VMEM((frames, feat, patches), jnp.bfloat16),
                pltpu.VMEM((feat, lanes), jnp.float32),
            ],
        ),
        out_shape=[jax.ShapeDtypeStruct((heads, feat, patches), jnp.bfloat16)] * frames
        + [jax.ShapeDtypeStruct((rows, feat), jnp.float32)],
        compiler_params=params(patches),
        cost_estimate=cost(4),
        name="temporal",
    )(scalars, *attended, upstream, gain)
    return grads, mixed


def gains_kernel(heads, frames, clips, scalars, *refs):
    mixed_refs, gains_ref, grad_ref = refs[:-2], refs[-2], refs[-1]
    tasks = gains_ref.shape[1]
    rows = sum(ref.shape[0] for ref in mixed_refs) // (frames * clips)
    each = mixed_refs[0].shape[0] // rows
    task_ids = lax.broadcasted_iota(jnp.int32, (tasks, HEAD_DIM), 0).astype(jnp.float32)
    for distance in range(frames):
        for head in range(heads):
            mixed = jnp.zeros((tasks, HEAD_DIM), jnp.float32)
            for clip in range(clips):
                block = distance * clips + clip
                ref, start = mixed_refs[block // each], block % each * rows
                task = ref[pl.ds(start + heads, 1), :]
                row = ref[pl.ds(start + head, 1), :]
                mixed = mixed + jnp.where(task_ids == task, row, 0.0)
            start = (partner(scalars, distance) * heads + head) * HEAD_DIM
            cols = pl.ds(pl.multiple_of(start, HEAD_DIM), HEAD_DIM)
            grad_ref[0, :, cols] = gains_ref[1, :, cols] * mixed
            grad_ref[1, :, cols] = gains_ref[0, :, cols] * mixed


def gain_gradients(scalars, mixed, gains, heads, frames, clips):
    return pl.pallas_call(
        functools.partial(gains_kernel, heads, frames, clips),
        in_specs=[pl.BlockSpec(memory_space=pltpu.SMEM)]
        + [pl.BlockSpec(memory_space=pltpu.VMEM)] * (len(mixed) + 1),
        out_specs=pl.BlockSpec(memory_space=pltpu.VMEM),
        out_shape=jax.ShapeDtypeStruct(gains.shape, jnp.float32),
        compiler_params=params(0),
        cost_estimate=cost(1),
        name="gain_gradients",
    )(scalars, *mixed, gains)


def swap(field, axis, size, distance):
    return lax.ppermute(field, axis, [(i, i ^ distance) for i in range(size)])


def split_by_heads(
    query_heads, key_heads, value_heads, cotangent, task_ids, lengths, gains, clips, frames, spaces
):
    patches, feat = query_heads.shape[2:]
    heads = feat // HEAD_DIM
    own = heads // frames
    width = own * HEAD_DIM
    queries, key_rows, values = (
        field.reshape(patches, feat) for field in (query_heads, key_heads, value_heads)
    )
    frame = lax.axis_index("tm")
    scalars = jnp.stack([frame, lengths[0], task_ids[0]]).astype(jnp.int32)

    packed = pack(cotangent.reshape(cotangent.shape[2:]), frames, spaces)
    incoming = lax.all_to_all(packed, ("tm", "space"), split_axis=0, concat_axis=0, tiled=True)
    queries, _ = lax.optimization_barrier((queries, packed))
    fields = (queries, key_rows, values)
    weights, attended = forward(scalars, *fields, frames)
    attended = [attended[0]] + [
        swap(attended[distance], "tm", frames, distance) for distance in range(1, frames)
    ]
    incoming, _ = lax.optimization_barrier((incoming, weights))
    upstream = turn(incoming, frames, spaces)
    rows = lax.dynamic_index_in_dim(gains, task_ids[0], 1, keepdims=False)
    product = lax.dynamic_slice_in_dim(rows[0] * rows[1], frame * width, width, 0)
    gain = jnp.broadcast_to(
        product.reshape(own, HEAD_DIM, 1), (own, HEAD_DIM, patches // spaces)
    )
    grads, mixed = temporal(scalars, attended, upstream, gain)
    grads = [grads[0]] + [
        swap(grads[distance], "tm", frames, distance) for distance in range(1, frames)
    ]
    here = grads[0]
    for bit in range(clips.bit_length() - 1):
        other = swap(mixed, "dp", clips, 1 << bit)
        if bit == 0:
            here, other = lax.optimization_barrier((here, other))
        mixed = jnp.concatenate([mixed, other], axis=0)
    results = backward(scalars, fields, weights, here, 0, ())
    mixed, results = lax.optimization_barrier((mixed, results))
    mixed = [mixed] + [swap(mixed, "tm", frames, distance) for distance in range(1, frames)]
    distance = 1
    if frames > 2:
        results = backward(scalars, fields, weights, grads[1], 1, results)
        mixed, results = lax.optimization_barrier((mixed, results))
        distance = 2
    grad_gains = gain_gradients(scalars, mixed, gains, own, frames, clips)
    grad_gains, results = lax.optimization_barrier((grad_gains, results))
    for distance in range(distance, frames):
        results = backward(scalars, fields, weights, grads[distance], distance, results)
    grad_queries, grad_keys = results
    return (
        grad_queries.reshape(query_heads.shape),
        grad_keys.reshape(query_heads.shape),
        grad_gains,
    )


def temporal_grads(attended, upstream, gain_query, gain_keys, length):
    highest = lax.Precision.HIGHEST
    frames = attended.shape[0]
    score_scale = attended.shape[-1] ** (-0.5)
    floats = attended.astype(jnp.float32)
    inverse_rms = lax.rsqrt(jnp.mean(floats * floats, axis=-1, keepdims=True) + 1e-06)
    normed = floats * inverse_rms
    t_query = normed * gain_query
    t_keys = normed * gain_keys
    scores = jnp.einsum("txhd,uxhd->xhtu", t_query, t_keys, precision=highest) * score_scale
    frame_ids = jnp.arange(frames, dtype=jnp.int32)
    allowed = (frame_ids[None, :] <= frame_ids[:, None]) & (frame_ids[None, :] < length)
    scores = jnp.where(allowed, scores, -1e30)
    weights = jax.nn.softmax(scores, axis=-1)
    weights_low = lax.optimization_barrier(weights.astype(jnp.bfloat16)).astype(jnp.float32)
    valid_rows = (frame_ids < length).astype(jnp.float32)
    masked = upstream.astype(jnp.float32) * valid_rows[:, None, None, None]
    grad_weights = jnp.einsum("txhd,uxhd->xhtu", masked, floats, precision=highest)
    from_values = jnp.einsum("xhtu,txhd->uxhd", weights_low, masked, precision=highest)
    grad_scores = (
        weights
        * (grad_weights - jnp.sum(grad_weights * weights, axis=-1, keepdims=True))
        * score_scale
    )
    grad_tquery = jnp.einsum("xhtu,uxhd->txhd", grad_scores, t_keys, precision=highest)
    grad_tkeys = jnp.einsum("xhtu,txhd->uxhd", grad_scores, t_query, precision=highest)
    grad_normed = grad_tquery * gain_query + grad_tkeys * gain_keys
    grad_gain_query = jnp.sum(grad_tquery * normed, axis=(0, 1))
    grad_gain_keys = jnp.sum(grad_tkeys * normed, axis=(0, 1))
    from_norm = inverse_rms * (
        grad_normed - normed * jnp.mean(grad_normed * normed, axis=-1, keepdims=True)
    )
    grad_total = (masked + from_values + from_norm).astype(jnp.bfloat16)
    return (grad_total, grad_gain_query, grad_gain_keys)


def split_by_patches(query_heads, key_heads, value_heads, cotangent, task_ids, lengths, gains):
    patches, feat = query_heads.shape[2:]
    heads = feat // HEAD_DIM
    queries, key_rows, values = (
        field.reshape(patches, feat) for field in (query_heads, key_heads, value_heads)
    )
    scalars = jnp.zeros((1,), jnp.int32)
    fields = (queries, key_rows, values)
    weights, attended = forward(scalars, *fields, 1)
    attended_field = jnp.transpose(attended[0], (2, 0, 1)).reshape(1, 1, patches, feat)
    upstream = lax.all_to_all(
        lax.all_to_all(cotangent, "space", split_axis=3, concat_axis=2, tiled=True),
        "tm",
        split_axis=2,
        concat_axis=1,
        tiled=True,
    )
    frames_attended = lax.all_to_all(attended_field, "tm", split_axis=2, concat_axis=1, tiled=True)
    frames, local_patches = frames_attended.shape[1:3]
    selector = (task_ids[0] == jnp.arange(gains.shape[1], dtype=jnp.int32)).astype(jnp.float32)
    gain_query = jnp.sum(selector[:, None] * gains[0], axis=0).reshape(heads, HEAD_DIM)
    gain_keys = jnp.sum(selector[:, None] * gains[1], axis=0).reshape(heads, HEAD_DIM)
    grad_total, grad_gq, grad_gk = temporal_grads(
        frames_attended.reshape(frames, local_patches, heads, HEAD_DIM),
        upstream.reshape(frames, local_patches, heads, HEAD_DIM),
        gain_query,
        gain_keys,
        lengths[0],
    )
    gain_terms = jnp.stack(
        [
            selector[:, None] * grad_gq.reshape(1, feat),
            selector[:, None] * grad_gk.reshape(1, feat),
        ]
    )
    grad_gains = lax.psum(gain_terms, ("dp", "tm"))
    returned = lax.all_to_all(
        grad_total.reshape(1, frames, local_patches, feat),
        "tm",
        split_axis=1,
        concat_axis=2,
        tiled=True,
    )
    head_grads = jnp.transpose(returned.reshape(patches, heads, HEAD_DIM), (1, 2, 0))
    grad_queries, grad_keys = backward(scalars, fields, weights, head_grads, 0, ())
    return (
        grad_queries.reshape(query_heads.shape),
        grad_keys.reshape(query_heads.shape),
        grad_gains,
    )


def solution(mesh):
    clips, frames, spaces = (mesh.shape[axis] for axis in ("dp", "tm", "space"))

    def local(query_heads, *others):
        heads = query_heads.shape[3] // HEAD_DIM
        powers = all(size & (size - 1) == 0 for size in (clips, frames))
        if powers and frames <= 4 and heads % frames == 0:
            return split_by_heads(query_heads, *others, clips, frames, spaces)
        return split_by_patches(query_heads, *others)

    return jax.shard_map(
        local,
        mesh=mesh,
        in_specs=(
            P("dp", "tm", None, "space"),
            P("dp", "tm", None, "space"),
            P("dp", "tm", None, "space"),
            P("dp", "tm", "space", None),
            P("dp"),
            P("dp"),
            P(None, None, "space"),
        ),
        out_specs=(
            P("dp", "tm", None, "space"),
            P("dp", "tm", None, "space"),
            P(None, None, "space"),
        ),
        check_vma=False,
    )
```

```python
import functools

import jax
import jax.numpy as jnp
from jax import lax
from jax.experimental import pallas as pl
from jax.experimental.pallas import tpu as pltpu
from jax.sharding import PartitionSpec as P

HEAD_DIM = 128
GROUP = 16
MIB = 1024 * 1024


def params(patches):
    return pltpu.CompilerParams(vmem_limit_bytes=(16 if patches <= 512 else 60) * MIB)


def cost(microseconds):
    return pl.CostEstimate(flops=int(microseconds * 1e8), bytes_accessed=0, transcendentals=0)


def columns_dot(left, right):
    return lax.dot_general(
        left, right, (((1,), (1,)), ((), ())), preferred_element_type=jnp.float32
    )


def dot(left, right):
    return jnp.dot(left, right, preferred_element_type=jnp.float32)


def partner(scalars, distance):
    return jnp.bitwise_xor(scalars[0], distance)


def forward_kernel(first, scalars, query_ref, key_ref, value_ref, weights_ref, *refs):
    (queries, key_rows, values, arrived), attended_refs = refs[-4:], refs[:-4]
    score_scale = HEAD_DIM ** (-0.5)
    groups, _, width = queries.shape
    own = width // HEAD_DIM
    copies = []
    for group in range(groups):
        cols = pl.ds(pl.multiple_of(partner(scalars, group) * width, HEAD_DIM), width)
        for field, (source, target) in enumerate(
            ((query_ref, queries), (key_ref, key_rows), (value_ref, values))
        ):
            copy = pltpu.make_async_copy(
                source.at[:, cols], target.at[group], arrived.at[group, field]
            )
            copy.start()
            copies.append(copy)
    for group in range(groups):
        for copy in copies[3 * group : 3 * group + 3]:
            copy.wait()
        for head in range(own):
            cols = pl.ds(head * HEAD_DIM, HEAD_DIM)
            scores = columns_dot(key_rows[group, :, cols], queries[group, :, cols])
            largest = jnp.max(scores, axis=0, keepdims=True)
            raised = jnp.exp((scores - largest) * score_scale)
            weights = raised * (1.0 / jnp.sum(raised, axis=0, keepdims=True))
            weights_ref[group * own + head] = weights
            attended = dot(values[group, :, cols].T, weights.astype(jnp.bfloat16))
            chunk, place = (0, head) if head < first else (1, head - first)
            attended_refs[chunk * groups + group][place] = attended.astype(jnp.bfloat16)


def forward(scalars, queries, key_rows, values, groups, first):
    patches, feat = queries.shape
    heads = feat // HEAD_DIM
    chunks = [first, heads // groups - first] if first < heads // groups else [first]
    fields = [
        pltpu.with_memory_space_constraint(field, pltpu.HBM) for field in (queries, key_rows, values)
    ]
    weights, *attended = pl.pallas_call(
        functools.partial(forward_kernel, first),
        in_specs=[pl.BlockSpec(memory_space=pltpu.SMEM)]
        + [pl.BlockSpec(memory_space=pltpu.HBM)] * 3,
        out_specs=[pl.BlockSpec(memory_space=pltpu.VMEM)] * (1 + groups * len(chunks)),
        scratch_shapes=[pltpu.VMEM((groups, patches, feat // groups), jnp.bfloat16)] * 3
        + [pltpu.SemaphoreType.DMA((groups, 3))],
        out_shape=[jax.ShapeDtypeStruct((heads, patches, patches), jnp.float32)]
        + [
            jax.ShapeDtypeStruct((size, HEAD_DIM, patches), jnp.bfloat16)
            for size in chunks
            for _ in range(groups)
        ],
        compiler_params=params(patches),
        cost_estimate=cost(6),
        name="spatial_forward",
    )(scalars, *fields)
    return weights, [attended[start : start + groups] for start in range(0, len(attended), groups)]


def backward_kernel(
    runs_of, scalars, query_ref, key_ref, value_ref, weights_ref, grad_ref, *refs
):
    gq_ref, gk_ref, gq, gk, sent = refs[-5:]
    score_scale = HEAD_DIM ** (-0.5)
    runs = runs_of(scalars)
    each = grad_ref.shape[0] // len(runs)
    heads = [
        (pl.ds(pl.multiple_of((column + place) * HEAD_DIM, HEAD_DIM), HEAD_DIM), weight + place)
        for column, weight in runs
        for place in range(each)
    ]
    spatial_grads = [
        dot(value_ref[:, columns], grad_ref[head]) for head, (columns, _) in enumerate(heads)
    ]
    all_scores = []
    for spatial_grad, (_, weight) in zip(spatial_grads, heads):
        weights = weights_ref[weight]
        row_sum = jnp.sum(spatial_grad * weights, axis=0, keepdims=True)
        scores = weights * (spatial_grad - row_sum) * score_scale
        all_scores.append(scores.astype(jnp.bfloat16))
    copies = []

    def send(side, source, target):
        for run, (column, _) in enumerate(runs):
            here = pl.ds(run * each * HEAD_DIM, each * HEAD_DIM)
            there = pl.ds(pl.multiple_of(column * HEAD_DIM, HEAD_DIM), each * HEAD_DIM)
            copy = pltpu.make_async_copy(
                source.at[:, here], target.at[:, there], sent.at[side, run]
            )
            copy.start()
            copies.append(copy)

    for head, scores in enumerate(all_scores):
        cols = pl.ds(head * HEAD_DIM, HEAD_DIM)
        gk[:, cols] = dot(scores, query_ref[:, heads[head][0]]).astype(jnp.bfloat16)
    send(0, gk, gk_ref)
    for head, scores in enumerate(all_scores):
        cols = pl.ds(head * HEAD_DIM, HEAD_DIM)
        gq[:, cols] = dot(key_ref[:, heads[head][0]].T, scores).astype(jnp.bfloat16).T
    send(1, gq, gq_ref)
    for copy in copies:
        copy.wait()


def backward(scalars, fields, weights, grads, runs_of, earlier):
    patches, feat = fields[0].shape
    heads = grads.shape[0]
    runs = len(runs_of([0]))
    return pl.pallas_call(
        functools.partial(backward_kernel, runs_of),
        in_specs=[pl.BlockSpec(memory_space=pltpu.SMEM)]
        + [pl.BlockSpec(memory_space=pltpu.VMEM)] * 5
        + [pl.BlockSpec(memory_space=pl.ANY)] * len(earlier),
        out_specs=[pl.BlockSpec(memory_space=pl.ANY)] * 2,
        scratch_shapes=[pltpu.VMEM((patches, heads * HEAD_DIM), jnp.bfloat16)] * 2
        + [pltpu.SemaphoreType.DMA((2, runs))],
        out_shape=[jax.ShapeDtypeStruct((patches, feat), jnp.bfloat16)] * 2,
        input_output_aliases={6 + index: index for index in range(len(earlier))},
        compiler_params=params(patches),
        cost_estimate=cost(2),
        name="spatial_backward",
    )(scalars, *fields, weights, grads, *earlier)


def pack_kernel(frames, spaces, field_ref, packed_ref, sent):
    width = packed_ref.shape[2]
    copies = []
    for frame in range(frames):
        for space in range(spaces):
            index = frame * spaces + space
            cols = pl.ds((space * frames + frame) * width, width)
            copy = pltpu.make_async_copy(field_ref.at[:, cols], packed_ref.at[index], sent.at[index])
            copy.start()
            copies.append(copy)
    for copy in copies:
        copy.wait()


def pack(field, frames, spaces):
    patches, feat = field.shape
    devices = frames * spaces
    return pl.pallas_call(
        functools.partial(pack_kernel, frames, spaces),
        in_specs=[pl.BlockSpec(memory_space=pl.ANY)],
        out_specs=pl.BlockSpec(memory_space=pl.ANY),
        out_shape=jax.ShapeDtypeStruct((devices, patches, feat // devices), field.dtype),
        scratch_shapes=[pltpu.SemaphoreType.DMA((devices,))],
        compiler_params=params(0),
        cost_estimate=cost(1),
        name="pack_cotangent",
    )(field)


def turn_kernel(field_ref, turned_ref):
    spaces, frames = turned_ref.shape[:2]
    for space in range(spaces):
        for frame in range(frames):
            turned_ref[space, frame, 0] = field_ref[frame * spaces + space].T


def turn(field, frames, spaces):
    devices, patches, feat = field.shape
    heads = feat // HEAD_DIM
    return pl.pallas_call(
        turn_kernel,
        grid=(heads,),
        in_specs=[pl.BlockSpec((devices, patches, HEAD_DIM), lambda i: (0, 0, i))],
        out_specs=pl.BlockSpec((spaces, frames, 1, HEAD_DIM, patches), lambda i: (0, 0, i, 0, 0)),
        out_shape=jax.ShapeDtypeStruct((spaces, frames, heads, HEAD_DIM, patches), field.dtype),
        compiler_params=params(patches),
        cost_estimate=cost(2),
        name="turn_cotangent",
    )(field)


def temporal_part(length, attended_ref, upstream_ref, gain_ref, grad_ref, mixed_sum, part):
    frames, feat, _ = attended_ref.shape
    lanes = upstream_ref.shape[-1]
    here = pl.ds(part * lanes, lanes)
    half = GROUP // 2
    score_scale = feat ** (-0.5)
    pairs = [(t, u) for t in range(frames) for u in range(t + 1)]
    every = range(frames)
    valid = [jnp.where(t < length, 1.0, 0.0).astype(jnp.float32) for t in every]
    bias = [jnp.where(u < length, 0.0, -1e30).astype(jnp.float32) for u in every]

    def split(block):
        block = block.astype(jnp.float32)
        return block[:half], block[half:]

    def load_fields(group):
        return [split(attended_ref[t, pl.ds(group * GROUP, GROUP), here]) for t in every]

    def load_ups(group):
        return [split(upstream_ref[part, t, 0, pl.ds(group * GROUP, GROUP), :]) for t in every]

    def total(piece):
        return jnp.broadcast_to(jnp.sum(piece, axis=0, keepdims=True), (half, lanes))

    squares = [jnp.zeros((half, lanes), jnp.float32) for _ in every]
    for group in range(feat // GROUP):
        for t, (low, high) in enumerate(load_fields(group)):
            squares[t] = squares[t] + (low * low + high * high)
    inverse = [lax.rsqrt(total(squares[t]) * (1.0 / feat) + 1e-06) for t in every]

    raw = {pair: jnp.zeros((half, lanes), jnp.float32) for pair in pairs}
    grad = {pair: jnp.zeros((half, lanes), jnp.float32) for pair in pairs}
    for group in range(feat // GROUP):
        fields, ups = load_fields(group), load_ups(group)
        for side in range(2):
            gain = gain_ref[0, pl.ds(group * GROUP + side * half, half), :]
            normed = [fields[t][side] * inverse[t] for t in every]
            gained = [normed[t] * gain for t in every]
            for t, u in pairs:
                raw[t, u] = raw[t, u] + gained[t] * normed[u]
                grad[t, u] = grad[t, u] + ups[t][side] * fields[u][side]

    value_part, score_part = {}, {}
    for t in every:
        seen = range(t + 1)
        for u in seen:
            raw[t, u] = total(raw[t, u])
            grad[t, u] = total(grad[t, u]) * valid[t]
        scores = [raw[t, u] * score_scale + bias[u] for u in seen]
        largest = functools.reduce(jnp.maximum, scores)
        raised = [jnp.exp(score - largest) for score in scores]
        over = 1.0 / functools.reduce(jnp.add, raised)
        weights = [piece * over for piece in raised]
        mean_grad = functools.reduce(jnp.add, [weights[u] * grad[t, u] for u in seen])
        for u in seen:
            rounded = weights[u].astype(jnp.bfloat16).astype(jnp.float32)
            value_part[t, u] = (rounded + (1.0 if u == t else 0.0)) * valid[t]
            score_part[t, u] = weights[u] * (grad[t, u] - mean_grad) * score_scale

    both = {(t, u): score_part[t, u] * (2.0 if t == u else 1.0) for t, u in pairs}
    both.update({(u, t): both[t, u] for t, u in pairs})
    raw.update({(u, t): raw[t, u] for t, u in pairs})
    mean_part = [
        functools.reduce(jnp.add, [both[u, v] * raw[u, v] for v in every]) * (1.0 / feat)
        for u in every
    ]

    for group in range(feat // GROUP):
        fields, ups = load_fields(group), load_ups(group)
        outs = [[] for _ in every]
        for side in range(2):
            rows = pl.ds(group * GROUP + side * half, half)
            gain = gain_ref[0, rows, :]
            normed = [fields[t][side] * inverse[t] for t in every]
            mixed = jnp.zeros((half, lanes), jnp.float32)
            for u in every:
                crossed = functools.reduce(jnp.add, [both[u, v] * normed[v] for v in every])
                mixed = mixed + crossed * normed[u]
                from_norm = inverse[u] * (gain * crossed - normed[u] * mean_part[u])
                direct = functools.reduce(
                    jnp.add, [value_part[t, u] * ups[t][side] for t in range(u, frames)]
                )
                outs[u].append(direct + from_norm)
            mixed_sum[rows, :] = mixed if part == 0 else mixed_sum[rows, :] + mixed
        for u in every:
            grad_ref[u, pl.ds(group * GROUP, GROUP), here] = jnp.concatenate(
                outs[u], axis=0
            ).astype(jnp.bfloat16)


def temporal_kernel(frames, first, scalars, *refs):
    attended_refs, (upstream_ref, gain_ref, earlier_ref) = refs[:frames], refs[frames : frames + 3]
    *grad_refs, mixed_ref, attended, grads, mixed_sum = refs[frames + 3 :]
    head = pl.program_id(0)
    for distance, ref in enumerate(attended_refs):
        attended[partner(scalars, distance)] = ref[0]
    for part in range(upstream_ref.shape[0]):
        temporal_part(scalars[1], attended, upstream_ref, gain_ref, grads, mixed_sum, part)
    for distance, ref in enumerate(grad_refs):
        ref[0] = grads[partner(scalars, distance)]

    @pl.when(head == 0)
    def _():
        mixed_ref[...] = earlier_ref[...]

    summed = jnp.sum(mixed_sum[...].T, axis=0, keepdims=True) * 0.5
    mixed_ref[pl.ds(first + head, 1), :] = summed


def temporal(scalars, attended, upstream, gain, earlier, first):
    spaces, frames, _, feat, lanes = upstream.shape
    heads, _, patches = attended[0].shape
    plane = pl.BlockSpec((1, feat, patches), lambda i, sc: (i, 0, 0))
    rows = pl.BlockSpec(earlier.shape, lambda i, sc: (0, 0))
    *grads, mixed = pl.pallas_call(
        functools.partial(temporal_kernel, frames, first),
        grid_spec=pltpu.PrefetchScalarGridSpec(
            num_scalar_prefetch=1,
            grid=(heads,),
            in_specs=[plane] * frames
            + [
                pl.BlockSpec(
                    (spaces, frames, 1, feat, lanes), lambda i, sc: (0, 0, first + i, 0, 0)
                ),
                pl.BlockSpec((1, feat, lanes), lambda i, sc: (first + i, 0, 0)),
                rows,
            ],
            out_specs=[plane] * frames + [rows],
            scratch_shapes=[
                pltpu.VMEM((frames, feat, patches), jnp.bfloat16),
                pltpu.VMEM((frames, feat, patches), jnp.bfloat16),
                pltpu.VMEM((feat, lanes), jnp.float32),
            ],
        ),
        out_shape=[jax.ShapeDtypeStruct((heads, feat, patches), jnp.bfloat16)] * frames
        + [jax.ShapeDtypeStruct(earlier.shape, jnp.float32)],
        compiler_params=params(patches),
        cost_estimate=cost(2000),
        name="temporal",
    )(scalars, *attended, upstream, gain, earlier)
    return grads, mixed


def gains_kernel(heads, frames, clips, scalars, *refs):
    mixed_refs, gains_ref, grad_ref = refs[:-2], refs[-2], refs[-1]
    tasks = gains_ref.shape[1]
    rows = sum(ref.shape[0] for ref in mixed_refs) // (frames * clips)
    each = mixed_refs[0].shape[0] // rows
    task_ids = lax.broadcasted_iota(jnp.int32, (tasks, HEAD_DIM), 0).astype(jnp.float32)
    for distance in range(frames):
        for head in range(heads):
            mixed = jnp.zeros((tasks, HEAD_DIM), jnp.float32)
            for clip in range(clips):
                block = distance * clips + clip
                ref, start = mixed_refs[block // each], block % each * rows
                task = ref[pl.ds(start + heads, 1), :]
                row = ref[pl.ds(start + head, 1), :]
                mixed = mixed + jnp.where(task_ids == task, row, 0.0)
            start = (partner(scalars, distance) * heads + head) * HEAD_DIM
            cols = pl.ds(pl.multiple_of(start, HEAD_DIM), HEAD_DIM)
            grad_ref[0, :, cols] = gains_ref[1, :, cols] * mixed
            grad_ref[1, :, cols] = gains_ref[0, :, cols] * mixed


def gain_gradients(scalars, mixed, gains, heads, frames, clips):
    return pl.pallas_call(
        functools.partial(gains_kernel, heads, frames, clips),
        in_specs=[pl.BlockSpec(memory_space=pltpu.SMEM)]
        + [pl.BlockSpec(memory_space=pltpu.VMEM)] * (len(mixed) + 1),
        out_specs=pl.BlockSpec(memory_space=pltpu.VMEM),
        out_shape=jax.ShapeDtypeStruct(gains.shape, jnp.float32),
        compiler_params=params(0),
        cost_estimate=cost(1),
        name="gain_gradients",
    )(scalars, *mixed, gains)


def swap(field, axis, size, distance):
    return lax.ppermute(field, axis, [(i, i ^ distance) for i in range(size)])


def split_by_heads(
    query_heads, key_heads, value_heads, cotangent, task_ids, lengths, gains, clips, frames, spaces
):
    patches, feat = query_heads.shape[2:]
    heads = feat // HEAD_DIM
    own = heads // frames
    width = own * HEAD_DIM
    queries, key_rows, values = (
        field.reshape(patches, feat) for field in (query_heads, key_heads, value_heads)
    )
    frame = lax.axis_index("tm")
    scalars = jnp.stack([frame, lengths[0], task_ids[0]]).astype(jnp.int32)

    packed = pack(cotangent.reshape(cotangent.shape[2:]), frames, spaces)
    incoming = lax.all_to_all(packed, ("tm", "space"), split_axis=0, concat_axis=0, tiled=True)
    queries, _ = lax.optimization_barrier((queries, packed))
    fields = (queries, key_rows, values)
    first = max(1, own // 3)
    weights, attended = forward(scalars, *fields, frames, first)
    incoming, _ = lax.optimization_barrier((incoming, weights))

    def exchange(planes):
        return [planes[0]] + [
            swap(planes[distance], "tm", frames, distance) for distance in range(1, frames)
        ]

    early, later = attended
    early, later, incoming = lax.optimization_barrier((exchange(early), later, incoming))
    later = exchange(later)
    upstream = turn(incoming, frames, spaces)
    rows = lax.dynamic_index_in_dim(gains, task_ids[0], 1, keepdims=False)
    product = lax.dynamic_slice_in_dim(rows[0] * rows[1], frame * width, width, 0)
    gain = jnp.broadcast_to(
        product.reshape(own, HEAD_DIM, 1), (own, HEAD_DIM, patches // spaces)
    )
    marks = jnp.full((-(-(own + 1) // 8) * 8, HEAD_DIM), task_ids[0].astype(jnp.float32))
    early_grads, mixed = temporal(scalars, early, upstream, gain, marks, 0)
    early_grads = exchange(early_grads)
    grads, mixed = temporal(scalars, later, upstream, gain, mixed, first)
    grads = exchange(grads)

    def first_heads(results):
        return backward(
            scalars,
            fields,
            weights,
            jnp.concatenate(early_grads),
            lambda scalars: [
                (partner(scalars, group) * own, group * own) for group in range(frames)
            ],
            results,
        )

    def other_heads(distance, results):
        return backward(
            scalars,
            fields,
            weights,
            grads[distance],
            lambda scalars: [(partner(scalars, distance) * own + first, distance * own + first)],
            results,
        )

    for bit in range(clips.bit_length() - 1):
        other = swap(mixed, "dp", clips, 1 << bit)
        if bit == 0:
            grads[0], early_grads, other = lax.optimization_barrier(
                (grads[0], early_grads, other)
            )
        mixed = jnp.concatenate([mixed, other], axis=0)
    results = other_heads(0, ())
    mixed, results = lax.optimization_barrier((mixed, results))
    mixed = [mixed] + [swap(mixed, "tm", frames, distance) for distance in range(1, frames)]
    results = first_heads(results)
    distance = 1
    if frames > 2:
        results = other_heads(1, results)
        distance = 2
    mixed, results = lax.optimization_barrier((mixed, results))
    grad_gains = gain_gradients(scalars, mixed, gains, own, frames, clips)
    grad_gains, results = lax.optimization_barrier((grad_gains, results))
    for distance in range(distance, frames):
        results = other_heads(distance, results)
    grad_queries, grad_keys = results
    return (
        grad_queries.reshape(query_heads.shape),
        grad_keys.reshape(query_heads.shape),
        grad_gains,
    )


def temporal_grads(attended, upstream, gain_query, gain_keys, length):
    highest = lax.Precision.HIGHEST
    frames = attended.shape[0]
    score_scale = attended.shape[-1] ** (-0.5)
    floats = attended.astype(jnp.float32)
    inverse_rms = lax.rsqrt(jnp.mean(floats * floats, axis=-1, keepdims=True) + 1e-06)
    normed = floats * inverse_rms
    t_query = normed * gain_query
    t_keys = normed * gain_keys
    scores = jnp.einsum("txhd,uxhd->xhtu", t_query, t_keys, precision=highest) * score_scale
    frame_ids = jnp.arange(frames, dtype=jnp.int32)
    allowed = (frame_ids[None, :] <= frame_ids[:, None]) & (frame_ids[None, :] < length)
    scores = jnp.where(allowed, scores, -1e30)
    weights = jax.nn.softmax(scores, axis=-1)
    weights_low = lax.optimization_barrier(weights.astype(jnp.bfloat16)).astype(jnp.float32)
    valid_rows = (frame_ids < length).astype(jnp.float32)
    masked = upstream.astype(jnp.float32) * valid_rows[:, None, None, None]
    grad_weights = jnp.einsum("txhd,uxhd->xhtu", masked, floats, precision=highest)
    from_values = jnp.einsum("xhtu,txhd->uxhd", weights_low, masked, precision=highest)
    grad_scores = (
        weights
        * (grad_weights - jnp.sum(grad_weights * weights, axis=-1, keepdims=True))
        * score_scale
    )
    grad_tquery = jnp.einsum("xhtu,uxhd->txhd", grad_scores, t_keys, precision=highest)
    grad_tkeys = jnp.einsum("xhtu,txhd->uxhd", grad_scores, t_query, precision=highest)
    grad_normed = grad_tquery * gain_query + grad_tkeys * gain_keys
    grad_gain_query = jnp.sum(grad_tquery * normed, axis=(0, 1))
    grad_gain_keys = jnp.sum(grad_tkeys * normed, axis=(0, 1))
    from_norm = inverse_rms * (
        grad_normed - normed * jnp.mean(grad_normed * normed, axis=-1, keepdims=True)
    )
    grad_total = (masked + from_values + from_norm).astype(jnp.bfloat16)
    return (grad_total, grad_gain_query, grad_gain_keys)


def split_by_patches(query_heads, key_heads, value_heads, cotangent, task_ids, lengths, gains):
    patches, feat = query_heads.shape[2:]
    heads = feat // HEAD_DIM
    queries, key_rows, values = (
        field.reshape(patches, feat) for field in (query_heads, key_heads, value_heads)
    )
    scalars = jnp.zeros((1,), jnp.int32)
    fields = (queries, key_rows, values)
    weights, attended = forward(scalars, *fields, 1, heads)
    attended_field = jnp.transpose(attended[0][0], (2, 0, 1)).reshape(1, 1, patches, feat)
    upstream = lax.all_to_all(
        lax.all_to_all(cotangent, "space", split_axis=3, concat_axis=2, tiled=True),
        "tm",
        split_axis=2,
        concat_axis=1,
        tiled=True,
    )
    frames_attended = lax.all_to_all(attended_field, "tm", split_axis=2, concat_axis=1, tiled=True)
    frames, local_patches = frames_attended.shape[1:3]
    selector = (task_ids[0] == jnp.arange(gains.shape[1], dtype=jnp.int32)).astype(jnp.float32)
    gain_query = jnp.sum(selector[:, None] * gains[0], axis=0).reshape(heads, HEAD_DIM)
    gain_keys = jnp.sum(selector[:, None] * gains[1], axis=0).reshape(heads, HEAD_DIM)
    grad_total, grad_gq, grad_gk = temporal_grads(
        frames_attended.reshape(frames, local_patches, heads, HEAD_DIM),
        upstream.reshape(frames, local_patches, heads, HEAD_DIM),
        gain_query,
        gain_keys,
        lengths[0],
    )
    gain_terms = jnp.stack(
        [
            selector[:, None] * grad_gq.reshape(1, feat),
            selector[:, None] * grad_gk.reshape(1, feat),
        ]
    )
    grad_gains = lax.psum(gain_terms, ("dp", "tm"))
    returned = lax.all_to_all(
        grad_total.reshape(1, frames, local_patches, feat),
        "tm",
        split_axis=1,
        concat_axis=2,
        tiled=True,
    )
    head_grads = jnp.transpose(returned.reshape(patches, heads, HEAD_DIM), (1, 2, 0))
    grad_queries, grad_keys = backward(
        scalars, fields, weights, head_grads, lambda scalars: [(0, 0)], ()
    )
    return (
        grad_queries.reshape(query_heads.shape),
        grad_keys.reshape(query_heads.shape),
        grad_gains,
    )


def solution(mesh):
    clips, frames, spaces = (mesh.shape[axis] for axis in ("dp", "tm", "space"))

    def local(query_heads, *others):
        heads = query_heads.shape[3] // HEAD_DIM
        powers = all(size & (size - 1) == 0 for size in (clips, frames))
        if powers and frames <= 4 and heads % frames == 0 and heads > frames:
            return split_by_heads(query_heads, *others, clips, frames, spaces)
        return split_by_patches(query_heads, *others)

    return jax.shard_map(
        local,
        mesh=mesh,
        in_specs=(
            P("dp", "tm", None, "space"),
            P("dp", "tm", None, "space"),
            P("dp", "tm", None, "space"),
            P("dp", "tm", "space", None),
            P("dp"),
            P("dp"),
            P(None, None, "space"),
        ),
        out_specs=(
            P("dp", "tm", None, "space"),
            P("dp", "tm", None, "space"),
            P(None, None, "space"),
        ),
        check_vma=False,
    )
```

```python
import functools

import jax
import jax.numpy as jnp
from jax import lax
from jax.experimental import pallas as pl
from jax.experimental.pallas import tpu as pltpu
from jax.sharding import PartitionSpec as P

HEAD_DIM = 128
GROUP = 16
MIB = 1024 * 1024


def params(patches):
    return pltpu.CompilerParams(vmem_limit_bytes=(16 if patches <= 512 else 60) * MIB)


def cost(microseconds):
    return pl.CostEstimate(flops=int(microseconds * 1e8), bytes_accessed=0, transcendentals=0)


def columns_dot(left, right):
    return lax.dot_general(
        left, right, (((1,), (1,)), ((), ())), preferred_element_type=jnp.float32
    )


def dot(left, right):
    return jnp.dot(left, right, preferred_element_type=jnp.float32)


def partner(scalars, distance):
    return jnp.bitwise_xor(scalars[0], distance)


def forward_kernel(scalars, query_ref, key_ref, value_ref, weights_ref, *refs):
    (queries, key_rows, values, arrived), attended_refs = refs[-4:], refs[:-4]
    score_scale = HEAD_DIM ** (-0.5)
    groups, _, width = queries.shape
    own = width // HEAD_DIM
    copies = []
    for group in range(groups):
        cols = pl.ds(pl.multiple_of(partner(scalars, group) * width, HEAD_DIM), width)
        for field, (source, target) in enumerate(
            ((query_ref, queries), (key_ref, key_rows), (value_ref, values))
        ):
            copy = pltpu.make_async_copy(
                source.at[:, cols], target.at[group], arrived.at[group, field]
            )
            copy.start()
            copies.append(copy)
    for group in range(groups):
        for copy in copies[3 * group : 3 * group + 3]:
            copy.wait()
        for head in range(own):
            cols = pl.ds(head * HEAD_DIM, HEAD_DIM)
            scores = columns_dot(key_rows[group, :, cols], queries[group, :, cols])
            largest = jnp.max(scores, axis=0, keepdims=True)
            raised = jnp.exp((scores - largest) * score_scale)
            weights = raised * (1.0 / jnp.sum(raised, axis=0, keepdims=True))
            weights_ref[group * own + head] = weights
            attended = dot(values[group, :, cols].T, weights.astype(jnp.bfloat16))
            attended_refs[group][head] = attended.astype(jnp.bfloat16)


def forward(scalars, queries, key_rows, values, groups):
    patches, feat = queries.shape
    heads = feat // HEAD_DIM
    own = heads // groups
    fields = [
        pltpu.with_memory_space_constraint(field, pltpu.HBM) for field in (queries, key_rows, values)
    ]
    weights, *attended = pl.pallas_call(
        forward_kernel,
        in_specs=[pl.BlockSpec(memory_space=pltpu.SMEM)]
        + [pl.BlockSpec(memory_space=pltpu.HBM)] * 3,
        out_specs=[pl.BlockSpec(memory_space=pltpu.VMEM)] * (1 + groups),
        scratch_shapes=[pltpu.VMEM((groups, patches, feat // groups), jnp.bfloat16)] * 3
        + [pltpu.SemaphoreType.DMA((groups, 3))],
        out_shape=[jax.ShapeDtypeStruct((heads, patches, patches), jnp.float32)]
        + [jax.ShapeDtypeStruct((own, HEAD_DIM, patches), jnp.bfloat16)] * groups,
        compiler_params=params(patches),
        cost_estimate=cost(6),
        name="spatial_forward",
    )(scalars, *fields)
    return weights, attended


def backward_group(scalars, fields, weights_ref, grad_ref, distance, scratch, results, sent):
    query_ref, key_ref, value_ref = fields
    score_scale = HEAD_DIM ** (-0.5)
    own = grad_ref.shape[0]
    start = partner(scalars, distance) * (own * HEAD_DIM)
    columns = [
        pl.ds(pl.multiple_of(start + head * HEAD_DIM, HEAD_DIM), HEAD_DIM) for head in range(own)
    ]
    spatial_grads = [dot(value_ref[:, columns[head]], grad_ref[head]) for head in range(own)]
    all_scores = []
    for head, spatial_grad in enumerate(spatial_grads):
        weights = weights_ref[distance * own + head]
        row_sum = jnp.sum(spatial_grad * weights, axis=0, keepdims=True)
        scores = weights * (spatial_grad - row_sum) * score_scale
        all_scores.append(scores.astype(jnp.bfloat16))
    gq, gk = scratch
    for head, scores in enumerate(all_scores):
        cols = pl.ds(head * HEAD_DIM, HEAD_DIM)
        gk[:, cols] = dot(scores, query_ref[:, columns[head]]).astype(jnp.bfloat16)
        gq[:, cols] = dot(key_ref[:, columns[head]].T, scores).astype(jnp.bfloat16).T
    there = pl.ds(pl.multiple_of(start, HEAD_DIM), own * HEAD_DIM)
    copies = [
        pltpu.make_async_copy(source, target.at[:, there], sent.at[side])
        for side, (source, target) in enumerate(zip(scratch, results))
    ]
    for copy in copies:
        copy.start()
    return copies


def backward_kernel(distances, gains_of, scalars, *refs):
    fields, weights_ref, refs = refs[:3], refs[3], refs[4:]
    grad_refs, refs = refs[: len(distances)], refs[len(distances) :]
    *refs, gq, gk, sent = refs
    copies = []
    if gains_of:
        *mixed_refs, gains_ref, _, _, gq_ref, gk_ref, grad_gains_ref, grad_gains = refs
        gain_gradients(*gains_of, scalars, mixed_refs, gains_ref, grad_gains)
        copy = pltpu.make_async_copy(grad_gains, grad_gains_ref, sent.at[len(distances), 0])
        copy.start()
        copies.append(copy)
    else:
        gq_ref, gk_ref = refs
    for place, (distance, grad_ref) in enumerate(zip(distances, grad_refs)):
        copies += backward_group(
            scalars,
            fields,
            weights_ref,
            grad_ref,
            distance,
            (gq.at[place], gk.at[place]),
            (gq_ref, gk_ref),
            sent.at[place],
        )
    for copy in copies:
        copy.wait()


def backward(scalars, fields, weights, grads, distances, earlier=(), mixed=(), gains=None, gains_of=()):
    patches, feat = fields[0].shape
    own = grads[0].shape[0]
    operands = [*fields, weights, *grads] + ([*mixed, gains] if gains_of else [])
    block = pltpu.VMEM((len(distances), patches, own * HEAD_DIM), jnp.bfloat16)
    out_shape = [jax.ShapeDtypeStruct((patches, feat), jnp.bfloat16)] * 2
    scratch = [block, block, pltpu.SemaphoreType.DMA((len(distances) + 1, 2))]
    if gains_of:
        out_shape.append(jax.ShapeDtypeStruct(gains.shape, jnp.float32))
        scratch.insert(0, pltpu.VMEM(gains.shape, jnp.float32))
    return pl.pallas_call(
        functools.partial(backward_kernel, distances, gains_of),
        in_specs=[pl.BlockSpec(memory_space=pltpu.SMEM)]
        + [pl.BlockSpec(memory_space=pltpu.VMEM)] * len(operands)
        + [pl.BlockSpec(memory_space=pl.ANY)] * len(earlier),
        out_specs=[pl.BlockSpec(memory_space=pl.ANY)] * len(out_shape),
        scratch_shapes=scratch,
        out_shape=out_shape,
        input_output_aliases={len(operands) + 1 + index: index for index in range(len(earlier))},
        compiler_params=params(patches),
        cost_estimate=cost(2),
        name="spatial_backward",
    )(scalars, *operands, *earlier)


def pack_kernel(frames, spaces, field_ref, packed_ref, sent):
    width = packed_ref.shape[2]
    copies = []
    for frame in range(frames):
        for space in range(spaces):
            index = frame * spaces + space
            cols = pl.ds((space * frames + frame) * width, width)
            copy = pltpu.make_async_copy(field_ref.at[:, cols], packed_ref.at[index], sent.at[index])
            copy.start()
            copies.append(copy)
    for copy in copies:
        copy.wait()


def pack(field, frames, spaces):
    patches, feat = field.shape
    devices = frames * spaces
    return pl.pallas_call(
        functools.partial(pack_kernel, frames, spaces),
        in_specs=[pl.BlockSpec(memory_space=pltpu.HBM)],
        out_specs=pl.BlockSpec(memory_space=pltpu.VMEM),
        out_shape=jax.ShapeDtypeStruct((devices, patches, feat // devices), field.dtype),
        scratch_shapes=[pltpu.SemaphoreType.DMA((devices,))],
        compiler_params=params(patches),
        cost_estimate=cost(1),
        name="pack_cotangent",
    )(pltpu.with_memory_space_constraint(field, pltpu.HBM))


def turn_kernel(field_ref, turned_ref):
    spaces, frames, heads = turned_ref.shape[:3]
    for space in range(spaces):
        for frame in range(frames):
            for head in range(heads):
                cols = pl.ds(head * HEAD_DIM, HEAD_DIM)
                turned_ref[space, frame, head] = field_ref[frame * spaces + space, :, cols].T


def turn(field, frames, spaces):
    devices, patches, feat = field.shape
    heads = feat // HEAD_DIM
    return pl.pallas_call(
        turn_kernel,
        in_specs=[pl.BlockSpec(memory_space=pltpu.VMEM)],
        out_specs=pl.BlockSpec(memory_space=pltpu.VMEM),
        out_shape=jax.ShapeDtypeStruct((spaces, frames, heads, HEAD_DIM, patches), field.dtype),
        compiler_params=params(patches),
        cost_estimate=cost(2),
        name="turn_cotangent",
    )(field)


def temporal_part(length, attended_ref, load_upstream, load_gain, grad_ref):
    frames, feat, lanes = attended_ref.shape
    half = GROUP // 2
    score_scale = feat ** (-0.5)
    pairs = [(t, u) for t in range(frames) for u in range(t + 1)]
    every = range(frames)
    valid = [jnp.where(t < length, 1.0, 0.0).astype(jnp.float32) for t in every]
    bias = [jnp.where(u < length, 0.0, -1e30).astype(jnp.float32) for u in every]

    def split(block):
        block = block.astype(jnp.float32)
        return block[:half], block[half:]

    def load_fields(group):
        return [split(attended_ref[t, pl.ds(group * GROUP, GROUP), :]) for t in every]

    def load_ups(group):
        return [split(load_upstream(t, pl.ds(group * GROUP, GROUP))) for t in every]

    def total(piece):
        return jnp.broadcast_to(jnp.sum(piece, axis=0, keepdims=True), (half, lanes))

    squares = [jnp.zeros((half, lanes), jnp.float32) for _ in every]
    for group in range(feat // GROUP):
        for t, (low, high) in enumerate(load_fields(group)):
            squares[t] = squares[t] + (low * low + high * high)
    inverse = [lax.rsqrt(total(squares[t]) * (1.0 / feat) + 1e-06) for t in every]

    raw = {pair: jnp.zeros((half, lanes), jnp.float32) for pair in pairs}
    grad = {pair: jnp.zeros((half, lanes), jnp.float32) for pair in pairs}
    for group in range(feat // GROUP):
        fields, ups = load_fields(group), load_ups(group)
        for side in range(2):
            gain = load_gain(pl.ds(group * GROUP + side * half, half))
            normed = [fields[t][side] * inverse[t] for t in every]
            gained = [normed[t] * gain for t in every]
            for t, u in pairs:
                raw[t, u] = raw[t, u] + gained[t] * normed[u]
                grad[t, u] = grad[t, u] + ups[t][side] * fields[u][side]

    value_part, score_part = {}, {}
    for t in every:
        seen = range(t + 1)
        for u in seen:
            raw[t, u] = total(raw[t, u])
            grad[t, u] = total(grad[t, u]) * valid[t]
        scores = [raw[t, u] * score_scale + bias[u] for u in seen]
        largest = functools.reduce(jnp.maximum, scores)
        raised = [jnp.exp(score - largest) for score in scores]
        over = 1.0 / functools.reduce(jnp.add, raised)
        weights = [piece * over for piece in raised]
        mean_grad = functools.reduce(jnp.add, [weights[u] * grad[t, u] for u in seen])
        for u in seen:
            rounded = weights[u].astype(jnp.bfloat16).astype(jnp.float32)
            value_part[t, u] = (rounded + (1.0 if u == t else 0.0)) * valid[t]
            score_part[t, u] = weights[u] * (grad[t, u] - mean_grad) * score_scale

    both = {(t, u): score_part[t, u] * (2.0 if t == u else 1.0) for t, u in pairs}
    both.update({(u, t): both[t, u] for t, u in pairs})
    raw.update({(u, t): raw[t, u] for t, u in pairs})
    mean_part = [
        functools.reduce(jnp.add, [both[u, v] * raw[u, v] for v in every]) * (1.0 / feat)
        for u in every
    ]

    all_mixed = []
    for group in range(feat // GROUP):
        fields, ups = load_fields(group), load_ups(group)
        outs = [[] for _ in every]
        for side in range(2):
            rows = pl.ds(group * GROUP + side * half, half)
            gain = load_gain(rows)
            normed = [fields[t][side] * inverse[t] for t in every]
            mixed = jnp.zeros((half, lanes), jnp.float32)
            for u in every:
                crossed = functools.reduce(jnp.add, [both[u, v] * normed[v] for v in every])
                mixed = mixed + crossed * normed[u]
                from_norm = inverse[u] * (gain * crossed - normed[u] * mean_part[u])
                direct = functools.reduce(
                    jnp.add, [value_part[t, u] * ups[t][side] for t in range(u, frames)]
                )
                outs[u].append(direct + from_norm)
            all_mixed.append(mixed)
        for u in every:
            grad_ref[u, pl.ds(group * GROUP, GROUP), :] = jnp.concatenate(
                outs[u], axis=0
            ).astype(jnp.bfloat16)
    return jnp.sum(jnp.concatenate(all_mixed, axis=0).T, axis=0, keepdims=True) * 0.5


def temporal_kernel(frames, scalars, *refs):
    attended_refs, (upstream_ref, gain_ref) = refs[:frames], refs[frames : frames + 2]
    grad_refs, mixed_ref = refs[frames + 2 : 2 * frames + 2], refs[2 * frames + 2]
    attended, grads = refs[2 * frames + 3 :]
    parts, _, heads, _, lanes = upstream_ref.shape
    row_ids = lax.broadcasted_iota(jnp.int32, mixed_ref.shape, 0)
    mixed_ref[...] = jnp.where(row_ids < heads, 0.0, scalars[2].astype(jnp.float32))

    def step(index, carry):
        head, part = index // parts, index % parts
        here = pl.ds(pl.multiple_of(part * lanes, lanes), lanes)
        for distance, ref in enumerate(reversed(attended_refs)):
            attended[partner(scalars, distance)] = ref[head, :, here]
        mixed_ref[pl.ds(head, 1), :] += temporal_part(
            scalars[1],
            attended,
            lambda t, rows: upstream_ref[part, t, head, rows, :],
            lambda rows: gain_ref[head, rows, :],
            grads,
        )
        for distance, ref in enumerate(grad_refs):
            ref[head, :, here] = grads[partner(scalars, distance)]
        return carry

    lax.fori_loop(0, heads * parts, step, 0)


def temporal(scalars, attended, upstream, gain):
    spaces, frames, heads, feat, lanes = upstream.shape
    patches = spaces * lanes
    rows = -(-(heads + 1) // 8) * 8
    *grads, mixed = pl.pallas_call(
        functools.partial(temporal_kernel, frames),
        in_specs=[pl.BlockSpec(memory_space=pltpu.SMEM)]
        + [pl.BlockSpec(memory_space=pltpu.VMEM)] * (frames + 2),
        out_specs=[pl.BlockSpec(memory_space=pltpu.VMEM)] * (frames + 1),
        scratch_shapes=[pltpu.VMEM((frames, feat, lanes), jnp.bfloat16)] * 2,
        out_shape=[jax.ShapeDtypeStruct((heads, feat, patches), jnp.bfloat16)] * frames
        + [jax.ShapeDtypeStruct((rows, feat), jnp.float32)],
        compiler_params=params(patches),
        cost_estimate=cost(4),
        name="temporal",
    )(scalars, *reversed(attended), upstream, gain)
    return grads, mixed


def gain_gradients(heads, frames, clips, scalars, mixed_refs, gains_ref, grad_ref):
    tasks = gains_ref.shape[1]
    rows = sum(ref.shape[0] for ref in mixed_refs) // (frames * clips)
    each = mixed_refs[0].shape[0] // rows
    task_ids = lax.broadcasted_iota(jnp.int32, (tasks, HEAD_DIM), 0).astype(jnp.float32)
    for distance in range(frames):
        for head in range(heads):
            mixed = jnp.zeros((tasks, HEAD_DIM), jnp.float32)
            for clip in range(clips):
                block = distance * clips + clip
                ref, start = mixed_refs[block // each], block % each * rows
                task = ref[pl.ds(start + heads, 1), :]
                row = ref[pl.ds(start + head, 1), :]
                mixed = mixed + jnp.where(task_ids == task, row, 0.0)
            start = (partner(scalars, distance) * heads + head) * HEAD_DIM
            cols = pl.ds(pl.multiple_of(start, HEAD_DIM), HEAD_DIM)
            grad_ref[0, :, cols] = gains_ref[1, :, cols] * mixed
            grad_ref[1, :, cols] = gains_ref[0, :, cols] * mixed


def swap(field, axis, size, distance):
    return lax.ppermute(field, axis, [(i, i ^ distance) for i in range(size)])


def split_by_heads(
    query_heads, key_heads, value_heads, cotangent, task_ids, lengths, gains, clips, frames, spaces
):
    patches, feat = query_heads.shape[2:]
    heads = feat // HEAD_DIM
    own = heads // frames
    width = own * HEAD_DIM
    queries, key_rows, values = (
        field.reshape(patches, feat) for field in (query_heads, key_heads, value_heads)
    )
    frame = lax.axis_index("tm")
    scalars = jnp.stack([frame, lengths[0], task_ids[0]]).astype(jnp.int32)

    packed = pack(cotangent.reshape(cotangent.shape[2:]), frames, spaces)
    incoming = lax.all_to_all(packed, ("tm", "space"), split_axis=0, concat_axis=0, tiled=True)
    queries, _ = lax.optimization_barrier((queries, packed))
    fields = (queries, key_rows, values)
    weights, attended = forward(scalars, *fields, frames)
    for distance in reversed(range(1, frames)):
        attended[distance] = swap(attended[distance], "tm", frames, distance)
    incoming, _ = lax.optimization_barrier((incoming, weights))
    upstream = turn(incoming, frames, spaces)
    rows = lax.dynamic_index_in_dim(gains, task_ids[0], 1, keepdims=False)
    product = lax.dynamic_slice_in_dim(rows[0] * rows[1], frame * width, width, 0)
    gain = jnp.broadcast_to(
        product.reshape(own, HEAD_DIM, 1), (own, HEAD_DIM, patches // spaces)
    )
    grads, mixed = temporal(scalars, attended, upstream, gain)
    for distance in reversed(range(1, frames)):
        grads[distance] = swap(grads[distance], "tm", frames, distance)
    here = grads[0]
    for bit in range(clips.bit_length() - 1):
        other = swap(mixed, "dp", clips, 1 << bit)
        if bit == 0:
            here, other = lax.optimization_barrier((here, other))
        mixed = jnp.concatenate([mixed, other], axis=0)
    results = backward(scalars, fields, weights, [here], [0])
    mixed, results = lax.optimization_barrier((mixed, results))
    mixed = [mixed] + [swap(mixed, "tm", frames, distance) for distance in range(1, frames)]
    grad_queries, grad_keys, grad_gains = backward(
        scalars,
        fields,
        weights,
        grads[:0:-1],
        list(range(frames - 1, 0, -1)),
        results,
        mixed,
        gains,
        (own, frames, clips),
    )
    return (
        grad_queries.reshape(query_heads.shape),
        grad_keys.reshape(query_heads.shape),
        grad_gains,
    )


def temporal_grads(attended, upstream, gain_query, gain_keys, length):
    highest = lax.Precision.HIGHEST
    frames = attended.shape[0]
    score_scale = attended.shape[-1] ** (-0.5)
    floats = attended.astype(jnp.float32)
    inverse_rms = lax.rsqrt(jnp.mean(floats * floats, axis=-1, keepdims=True) + 1e-06)
    normed = floats * inverse_rms
    t_query = normed * gain_query
    t_keys = normed * gain_keys
    scores = jnp.einsum("txhd,uxhd->xhtu", t_query, t_keys, precision=highest) * score_scale
    frame_ids = jnp.arange(frames, dtype=jnp.int32)
    allowed = (frame_ids[None, :] <= frame_ids[:, None]) & (frame_ids[None, :] < length)
    scores = jnp.where(allowed, scores, -1e30)
    weights = jax.nn.softmax(scores, axis=-1)
    weights_low = lax.optimization_barrier(weights.astype(jnp.bfloat16)).astype(jnp.float32)
    valid_rows = (frame_ids < length).astype(jnp.float32)
    masked = upstream.astype(jnp.float32) * valid_rows[:, None, None, None]
    grad_weights = jnp.einsum("txhd,uxhd->xhtu", masked, floats, precision=highest)
    from_values = jnp.einsum("xhtu,txhd->uxhd", weights_low, masked, precision=highest)
    grad_scores = (
        weights
        * (grad_weights - jnp.sum(grad_weights * weights, axis=-1, keepdims=True))
        * score_scale
    )
    grad_tquery = jnp.einsum("xhtu,uxhd->txhd", grad_scores, t_keys, precision=highest)
    grad_tkeys = jnp.einsum("xhtu,txhd->uxhd", grad_scores, t_query, precision=highest)
    grad_normed = grad_tquery * gain_query + grad_tkeys * gain_keys
    grad_gain_query = jnp.sum(grad_tquery * normed, axis=(0, 1))
    grad_gain_keys = jnp.sum(grad_tkeys * normed, axis=(0, 1))
    from_norm = inverse_rms * (
        grad_normed - normed * jnp.mean(grad_normed * normed, axis=-1, keepdims=True)
    )
    grad_total = (masked + from_values + from_norm).astype(jnp.bfloat16)
    return (grad_total, grad_gain_query, grad_gain_keys)


def split_by_patches(query_heads, key_heads, value_heads, cotangent, task_ids, lengths, gains):
    patches, feat = query_heads.shape[2:]
    heads = feat // HEAD_DIM
    queries, key_rows, values = (
        field.reshape(patches, feat) for field in (query_heads, key_heads, value_heads)
    )
    scalars = jnp.zeros((1,), jnp.int32)
    fields = (queries, key_rows, values)
    weights, attended = forward(scalars, *fields, 1)
    attended_field = jnp.transpose(attended[0], (2, 0, 1)).reshape(1, 1, patches, feat)
    upstream = lax.all_to_all(
        lax.all_to_all(cotangent, "space", split_axis=3, concat_axis=2, tiled=True),
        "tm",
        split_axis=2,
        concat_axis=1,
        tiled=True,
    )
    frames_attended = lax.all_to_all(attended_field, "tm", split_axis=2, concat_axis=1, tiled=True)
    frames, local_patches = frames_attended.shape[1:3]
    selector = (task_ids[0] == jnp.arange(gains.shape[1], dtype=jnp.int32)).astype(jnp.float32)
    gain_query = jnp.sum(selector[:, None] * gains[0], axis=0).reshape(heads, HEAD_DIM)
    gain_keys = jnp.sum(selector[:, None] * gains[1], axis=0).reshape(heads, HEAD_DIM)
    grad_total, grad_gq, grad_gk = temporal_grads(
        frames_attended.reshape(frames, local_patches, heads, HEAD_DIM),
        upstream.reshape(frames, local_patches, heads, HEAD_DIM),
        gain_query,
        gain_keys,
        lengths[0],
    )
    gain_terms = jnp.stack(
        [
            selector[:, None] * grad_gq.reshape(1, feat),
            selector[:, None] * grad_gk.reshape(1, feat),
        ]
    )
    grad_gains = lax.psum(gain_terms, ("dp", "tm"))
    returned = lax.all_to_all(
        grad_total.reshape(1, frames, local_patches, feat),
        "tm",
        split_axis=1,
        concat_axis=2,
        tiled=True,
    )
    head_grads = jnp.transpose(returned.reshape(patches, heads, HEAD_DIM), (1, 2, 0))
    grad_queries, grad_keys = backward(scalars, fields, weights, [head_grads], [0])
    return (
        grad_queries.reshape(query_heads.shape),
        grad_keys.reshape(query_heads.shape),
        grad_gains,
    )


def solution(mesh):
    clips, frames, spaces = (mesh.shape[axis] for axis in ("dp", "tm", "space"))

    def local(query_heads, *others):
        heads = query_heads.shape[3] // HEAD_DIM
        powers = all(size & (size - 1) == 0 for size in (clips, frames))
        if powers and frames <= 4 and heads % frames == 0:
            return split_by_heads(query_heads, *others, clips, frames, spaces)
        return split_by_patches(query_heads, *others)

    return jax.shard_map(
        local,
        mesh=mesh,
        in_specs=(
            P("dp", "tm", None, "space"),
            P("dp", "tm", None, "space"),
            P("dp", "tm", None, "space"),
            P("dp", "tm", "space", None),
            P("dp"),
            P("dp"),
            P(None, None, "space"),
        ),
        out_specs=(
            P("dp", "tm", None, "space"),
            P("dp", "tm", None, "space"),
            P(None, None, "space"),
        ),
        check_vma=False,
    )
```

```python
import functools

import jax
import jax.numpy as jnp
from jax import lax
from jax.experimental import pallas as pl
from jax.experimental.pallas import tpu as pltpu
from jax.sharding import PartitionSpec as P

HEAD_DIM = 128
GROUP = 16
MIB = 1024 * 1024


def params(patches):
    return pltpu.CompilerParams(vmem_limit_bytes=(16 if patches <= 512 else 60) * MIB)


def cost(microseconds):
    return pl.CostEstimate(flops=int(microseconds * 1e8), bytes_accessed=0, transcendentals=0)


def columns_dot(left, right):
    return lax.dot_general(
        left, right, (((1,), (1,)), ((), ())), preferred_element_type=jnp.float32
    )


def dot(left, right):
    return jnp.dot(left, right, preferred_element_type=jnp.float32)


def partner(scalars, distance):
    return jnp.bitwise_xor(scalars[0], distance)


def forward_kernel(scalars, query_ref, key_ref, value_ref, weights_ref, *refs):
    (queries, key_rows, values, arrived), attended_refs = refs[-4:], refs[:-4]
    score_scale = HEAD_DIM ** (-0.5)
    groups, _, width = queries.shape
    own = width // HEAD_DIM
    copies = []
    for group in range(groups):
        cols = pl.ds(pl.multiple_of(partner(scalars, group) * width, HEAD_DIM), width)
        for field, (source, target) in enumerate(
            ((query_ref, queries), (key_ref, key_rows), (value_ref, values))
        ):
            copy = pltpu.make_async_copy(
                source.at[:, cols], target.at[group], arrived.at[group, field]
            )
            copy.start()
            copies.append(copy)
    for group in range(groups):
        for copy in copies[3 * group : 3 * group + 3]:
            copy.wait()
        for head in range(own):
            cols = pl.ds(head * HEAD_DIM, HEAD_DIM)
            scores = columns_dot(key_rows[group, :, cols], queries[group, :, cols])
            largest = jnp.max(scores, axis=0, keepdims=True)
            raised = jnp.exp((scores - largest) * score_scale)
            weights = raised * (1.0 / jnp.sum(raised, axis=0, keepdims=True))
            weights_ref[group * own + head] = weights
            attended = dot(values[group, :, cols].T, weights.astype(jnp.bfloat16))
            attended_refs[group][head] = attended.astype(jnp.bfloat16)


def forward(scalars, queries, key_rows, values, groups):
    patches, feat = queries.shape
    heads = feat // HEAD_DIM
    own = heads // groups
    fields = [
        pltpu.with_memory_space_constraint(field, pltpu.HBM) for field in (queries, key_rows, values)
    ]
    weights, *attended = pl.pallas_call(
        forward_kernel,
        in_specs=[pl.BlockSpec(memory_space=pltpu.SMEM)]
        + [pl.BlockSpec(memory_space=pltpu.HBM)] * 3,
        out_specs=[pl.BlockSpec(memory_space=pltpu.VMEM)] * (1 + groups),
        scratch_shapes=[pltpu.VMEM((groups, patches, feat // groups), jnp.bfloat16)] * 3
        + [pltpu.SemaphoreType.DMA((groups, 3))],
        out_shape=[jax.ShapeDtypeStruct((heads, patches, patches), jnp.float32)]
        + [jax.ShapeDtypeStruct((own, HEAD_DIM, patches), jnp.bfloat16)] * groups,
        compiler_params=params(patches),
        cost_estimate=cost(6),
        name="spatial_forward",
    )(scalars, *fields)
    return weights, attended


def backward_group(scalars, fields, weights_ref, grad_ref, distance, scratch, results, sent):
    query_ref, key_ref, value_ref = fields
    score_scale = HEAD_DIM ** (-0.5)
    own = grad_ref.shape[0]
    start = partner(scalars, distance) * (own * HEAD_DIM)
    columns = [
        pl.ds(pl.multiple_of(start + head * HEAD_DIM, HEAD_DIM), HEAD_DIM) for head in range(own)
    ]
    spatial_grads = [dot(value_ref[:, columns[head]], grad_ref[head]) for head in range(own)]
    all_scores = []
    for head, spatial_grad in enumerate(spatial_grads):
        weights = weights_ref[distance * own + head]
        row_sum = jnp.sum(spatial_grad * weights, axis=0, keepdims=True)
        scores = weights * (spatial_grad - row_sum) * score_scale
        all_scores.append(scores.astype(jnp.bfloat16))
    gq, gk = scratch
    for head, scores in enumerate(all_scores):
        cols = pl.ds(head * HEAD_DIM, HEAD_DIM)
        gk[:, cols] = dot(scores, query_ref[:, columns[head]]).astype(jnp.bfloat16)
        gq[:, cols] = dot(key_ref[:, columns[head]].T, scores).astype(jnp.bfloat16).T
    there = pl.ds(pl.multiple_of(start, HEAD_DIM), own * HEAD_DIM)
    copies = [
        pltpu.make_async_copy(source, target.at[:, there], sent.at[side])
        for side, (source, target) in enumerate(zip(scratch, results))
    ]
    for copy in copies:
        copy.start()
    return copies


def backward_kernel(distances, gains_of, scalars, *refs):
    fields, weights_ref, refs = refs[:3], refs[3], refs[4:]
    grad_refs, refs = refs[: len(distances)], refs[len(distances) :]
    *refs, gq, gk, sent = refs
    copies = []
    if gains_of:
        *mixed_refs, gains_ref, _, _, gq_ref, gk_ref, grad_gains_ref, grad_gains = refs
        gain_gradients(*gains_of, scalars, mixed_refs, gains_ref, grad_gains)
        copy = pltpu.make_async_copy(grad_gains, grad_gains_ref, sent.at[len(distances), 0])
        copy.start()
        copies.append(copy)
    else:
        gq_ref, gk_ref = refs
    for place, (distance, grad_ref) in enumerate(zip(distances, grad_refs)):
        copies += backward_group(
            scalars,
            fields,
            weights_ref,
            grad_ref,
            distance,
            (gq.at[place], gk.at[place]),
            (gq_ref, gk_ref),
            sent.at[place],
        )
    for copy in copies:
        copy.wait()


def backward(scalars, fields, weights, grads, distances, earlier=(), mixed=(), gains=None, gains_of=()):
    patches, feat = fields[0].shape
    own = grads[0].shape[0]
    operands = [*fields, weights, *grads] + ([*mixed, gains] if gains_of else [])
    block = pltpu.VMEM((len(distances), patches, own * HEAD_DIM), jnp.bfloat16)
    out_shape = [jax.ShapeDtypeStruct((patches, feat), jnp.bfloat16)] * 2
    scratch = [block, block, pltpu.SemaphoreType.DMA((len(distances) + 1, 2))]
    if gains_of:
        out_shape.append(jax.ShapeDtypeStruct(gains.shape, jnp.float32))
        scratch.insert(0, pltpu.VMEM(gains.shape, jnp.float32))
    return pl.pallas_call(
        functools.partial(backward_kernel, distances, gains_of),
        in_specs=[pl.BlockSpec(memory_space=pltpu.SMEM)]
        + [pl.BlockSpec(memory_space=pltpu.VMEM)] * len(operands)
        + [pl.BlockSpec(memory_space=pl.ANY)] * len(earlier),
        out_specs=[pl.BlockSpec(memory_space=pl.ANY)] * len(out_shape),
        scratch_shapes=scratch,
        out_shape=out_shape,
        input_output_aliases={len(operands) + 1 + index: index for index in range(len(earlier))},
        compiler_params=params(patches),
        cost_estimate=cost(2),
        name="spatial_backward",
    )(scalars, *operands, *earlier)


def pack_kernel(frames, spaces, field_ref, packed_ref, rows, arrived):
    chunks, size, _ = rows.shape
    width = packed_ref.shape[2]
    copies = [
        pltpu.make_async_copy(
            field_ref.at[pl.ds(chunk * size, size), :], rows.at[chunk], arrived.at[chunk]
        )
        for chunk in range(chunks)
    ]
    for copy in copies:
        copy.start()
    for chunk, copy in enumerate(copies):
        copy.wait()
        for frame in range(frames):
            for space in range(spaces):
                cols = pl.ds((space * frames + frame) * width, width)
                packed_ref[frame * spaces + space, pl.ds(chunk * size, size), :] = rows[
                    chunk, :, cols
                ]


def pack(field, frames, spaces):
    patches, feat = field.shape
    devices = frames * spaces
    chunks = patches // GROUP
    return pl.pallas_call(
        functools.partial(pack_kernel, frames, spaces),
        in_specs=[pl.BlockSpec(memory_space=pltpu.HBM)],
        out_specs=pl.BlockSpec(memory_space=pltpu.VMEM),
        out_shape=jax.ShapeDtypeStruct((devices, patches, feat // devices), field.dtype),
        scratch_shapes=[
            pltpu.VMEM((chunks, patches // chunks, feat), field.dtype),
            pltpu.SemaphoreType.DMA((chunks,)),
        ],
        compiler_params=params(patches),
        cost_estimate=cost(1),
        name="pack_cotangent",
    )(pltpu.with_memory_space_constraint(field, pltpu.HBM))


def turn_kernel(field_ref, turned_ref):
    spaces, frames, heads = turned_ref.shape[:3]
    for space in range(spaces):
        for frame in range(frames):
            for head in range(heads):
                cols = pl.ds(head * HEAD_DIM, HEAD_DIM)
                turned_ref[space, frame, head] = field_ref[frame * spaces + space, :, cols].T


def turn(field, frames, spaces):
    devices, patches, feat = field.shape
    heads = feat // HEAD_DIM
    return pl.pallas_call(
        turn_kernel,
        in_specs=[pl.BlockSpec(memory_space=pltpu.VMEM)],
        out_specs=pl.BlockSpec(memory_space=pltpu.VMEM),
        out_shape=jax.ShapeDtypeStruct((spaces, frames, heads, HEAD_DIM, patches), field.dtype),
        compiler_params=params(patches),
        cost_estimate=cost(2),
        name="turn_cotangent",
    )(field)


def temporal_part(length, attended_ref, load_upstream, load_gain, grad_ref):
    frames, feat, lanes = attended_ref.shape
    half = GROUP // 2
    score_scale = feat ** (-0.5)
    pairs = [(t, u) for t in range(frames) for u in range(t + 1)]
    every = range(frames)
    valid = [jnp.where(t < length, 1.0, 0.0).astype(jnp.float32) for t in every]
    bias = [jnp.where(u < length, 0.0, -1e30).astype(jnp.float32) for u in every]

    def split(block):
        block = block.astype(jnp.float32)
        return block[:half], block[half:]

    def load_fields(group):
        return [split(attended_ref[t, pl.ds(group * GROUP, GROUP), :]) for t in every]

    def load_ups(group):
        return [split(load_upstream(t, pl.ds(group * GROUP, GROUP))) for t in every]

    def total(piece):
        return jnp.broadcast_to(jnp.sum(piece, axis=0, keepdims=True), (half, lanes))

    squares = [jnp.zeros((half, lanes), jnp.float32) for _ in every]
    for group in range(feat // GROUP):
        for t, (low, high) in enumerate(load_fields(group)):
            squares[t] = squares[t] + (low * low + high * high)
    inverse = [lax.rsqrt(total(squares[t]) * (1.0 / feat) + 1e-06) for t in every]

    raw = {pair: jnp.zeros((half, lanes), jnp.float32) for pair in pairs}
    grad = {pair: jnp.zeros((half, lanes), jnp.float32) for pair in pairs}
    for group in range(feat // GROUP):
        fields, ups = load_fields(group), load_ups(group)
        for side in range(2):
            gain = load_gain(pl.ds(group * GROUP + side * half, half))
            normed = [fields[t][side] * inverse[t] for t in every]
            gained = [normed[t] * gain for t in every]
            for t, u in pairs:
                raw[t, u] = raw[t, u] + gained[t] * normed[u]
                grad[t, u] = grad[t, u] + ups[t][side] * fields[u][side]

    value_part, score_part = {}, {}
    for t in every:
        seen = range(t + 1)
        for u in seen:
            raw[t, u] = total(raw[t, u])
            grad[t, u] = total(grad[t, u]) * valid[t]
        scores = [raw[t, u] * score_scale + bias[u] for u in seen]
        largest = functools.reduce(jnp.maximum, scores)
        raised = [jnp.exp(score - largest) for score in scores]
        over = 1.0 / functools.reduce(jnp.add, raised)
        weights = [piece * over for piece in raised]
        mean_grad = functools.reduce(jnp.add, [weights[u] * grad[t, u] for u in seen])
        for u in seen:
            rounded = weights[u].astype(jnp.bfloat16).astype(jnp.float32)
            value_part[t, u] = (rounded + (1.0 if u == t else 0.0)) * valid[t]
            score_part[t, u] = weights[u] * (grad[t, u] - mean_grad) * score_scale

    both = {(t, u): score_part[t, u] * (2.0 if t == u else 1.0) for t, u in pairs}
    both.update({(u, t): both[t, u] for t, u in pairs})
    raw.update({(u, t): raw[t, u] for t, u in pairs})
    mean_part = [
        functools.reduce(jnp.add, [both[u, v] * raw[u, v] for v in every]) * (1.0 / feat)
        for u in every
    ]

    all_mixed = []
    for group in range(feat // GROUP):
        fields, ups = load_fields(group), load_ups(group)
        outs = [[] for _ in every]
        for side in range(2):
            rows = pl.ds(group * GROUP + side * half, half)
            gain = load_gain(rows)
            normed = [fields[t][side] * inverse[t] for t in every]
            mixed = jnp.zeros((half, lanes), jnp.float32)
            for u in every:
                crossed = functools.reduce(jnp.add, [both[u, v] * normed[v] for v in every])
                mixed = mixed + crossed * normed[u]
                from_norm = inverse[u] * (gain * crossed - normed[u] * mean_part[u])
                direct = functools.reduce(
                    jnp.add, [value_part[t, u] * ups[t][side] for t in range(u, frames)]
                )
                outs[u].append(direct + from_norm)
            all_mixed.append(mixed)
        for u in every:
            grad_ref[u, pl.ds(group * GROUP, GROUP), :] = jnp.concatenate(
                outs[u], axis=0
            ).astype(jnp.bfloat16)
    return jnp.concatenate(all_mixed, axis=0)


def temporal_kernel(frames, scalars, *refs):
    attended_refs, (upstream_ref, gain_ref) = refs[:frames], refs[frames : frames + 2]
    grad_refs, mixed_ref = refs[frames + 2 : 2 * frames + 2], refs[2 * frames + 2]
    attended, grads = refs[2 * frames + 3 :]
    parts, _, heads, _, lanes = upstream_ref.shape
    mixed_ref[...] = jnp.full(mixed_ref.shape, scalars[2].astype(jnp.float32))

    def step(head, carry):
        for distance, ref in enumerate(attended_refs):
            frame = partner(scalars, distance)
            for part in range(parts):
                attended[part, frame] = ref[head, :, pl.ds(part * lanes, lanes)]
        mixed = [
            temporal_part(
                scalars[1],
                attended.at[part],
                lambda t, rows: upstream_ref[part, t, head, rows, :],
                lambda rows: gain_ref[head, rows, :],
                grads.at[part],
            )
            for part in range(parts)
        ]
        summed = functools.reduce(jnp.add, mixed)
        mixed_ref[pl.ds(head, 1), :] = jnp.sum(summed.T, axis=0, keepdims=True) * 0.5
        for distance, ref in enumerate(grad_refs):
            frame = partner(scalars, distance)
            for part in range(parts):
                ref[head, :, pl.ds(part * lanes, lanes)] = grads[part, frame]
        return carry

    lax.fori_loop(0, heads, step, 0)


def temporal(scalars, attended, upstream, gain):
    spaces, frames, heads, feat, lanes = upstream.shape
    patches = spaces * lanes
    rows = -(-(heads + 1) // 8) * 8
    *grads, mixed = pl.pallas_call(
        functools.partial(temporal_kernel, frames),
        in_specs=[pl.BlockSpec(memory_space=pltpu.SMEM)]
        + [pl.BlockSpec(memory_space=pltpu.VMEM)] * (frames + 2),
        out_specs=[pl.BlockSpec(memory_space=pltpu.VMEM)] * (frames + 1),
        scratch_shapes=[pltpu.VMEM((spaces, frames, feat, lanes), jnp.bfloat16)] * 2,
        out_shape=[jax.ShapeDtypeStruct((heads, feat, patches), jnp.bfloat16)] * frames
        + [jax.ShapeDtypeStruct((rows, feat), jnp.float32)],
        compiler_params=params(patches),
        cost_estimate=cost(4),
        name="temporal",
    )(scalars, *attended, upstream, gain)
    return grads, mixed


def gain_gradients(heads, frames, clips, scalars, mixed_refs, gains_ref, grad_ref):
    tasks = gains_ref.shape[1]
    rows = sum(ref.shape[0] for ref in mixed_refs) // (frames * clips)
    each = mixed_refs[0].shape[0] // rows
    task_ids = lax.broadcasted_iota(jnp.int32, (tasks, HEAD_DIM), 0).astype(jnp.float32)
    for distance in range(frames):
        for head in range(heads):
            mixed = jnp.zeros((tasks, HEAD_DIM), jnp.float32)
            for clip in range(clips):
                block = distance * clips + clip
                ref, start = mixed_refs[block // each], block % each * rows
                task = ref[pl.ds(start + heads, 1), :]
                row = ref[pl.ds(start + head, 1), :]
                mixed = mixed + jnp.where(task_ids == task, row, 0.0)
            start = (partner(scalars, distance) * heads + head) * HEAD_DIM
            cols = pl.ds(pl.multiple_of(start, HEAD_DIM), HEAD_DIM)
            grad_ref[0, :, cols] = gains_ref[1, :, cols] * mixed
            grad_ref[1, :, cols] = gains_ref[0, :, cols] * mixed


def swap(field, axis, size, distance):
    return lax.ppermute(field, axis, [(i, i ^ distance) for i in range(size)])


def split_by_heads(
    query_heads, key_heads, value_heads, cotangent, task_ids, lengths, gains, clips, frames, spaces
):
    patches, feat = query_heads.shape[2:]
    heads = feat // HEAD_DIM
    own = heads // frames
    width = own * HEAD_DIM
    queries, key_rows, values = (
        field.reshape(patches, feat) for field in (query_heads, key_heads, value_heads)
    )
    frame = lax.axis_index("tm")
    scalars = jnp.stack([frame, lengths[0], task_ids[0]]).astype(jnp.int32)

    packed = pack(cotangent.reshape(cotangent.shape[2:]), frames, spaces)
    incoming = lax.all_to_all(packed, ("tm", "space"), split_axis=0, concat_axis=0, tiled=True)
    queries, _ = lax.optimization_barrier((queries, packed))
    fields = (queries, key_rows, values)
    weights, attended = forward(scalars, *fields, frames)
    for distance in reversed(range(1, frames)):
        attended[distance] = swap(attended[distance], "tm", frames, distance)
    incoming, _ = lax.optimization_barrier((incoming, weights))
    upstream = turn(incoming, frames, spaces)
    rows = lax.dynamic_index_in_dim(gains, task_ids[0], 1, keepdims=False)
    product = lax.dynamic_slice_in_dim(rows[0] * rows[1], frame * width, width, 0)
    gain = jnp.broadcast_to(
        product.reshape(own, HEAD_DIM, 1), (own, HEAD_DIM, patches // spaces)
    )
    grads, mixed = temporal(scalars, attended, upstream, gain)
    for distance in reversed(range(1, frames)):
        grads[distance] = swap(grads[distance], "tm", frames, distance)
    here = grads[0]
    for bit in range(clips.bit_length() - 1):
        other = swap(mixed, "dp", clips, 1 << bit)
        if bit == 0:
            here, other = lax.optimization_barrier((here, other))
        mixed = jnp.concatenate([mixed, other], axis=0)
    results = backward(scalars, fields, weights, [here], [0])
    mixed, results = lax.optimization_barrier((mixed, results))
    near, grads[1] = lax.optimization_barrier((mixed, grads[1]))
    mixed = [mixed, swap(near, "tm", frames, 1)] + [
        swap(mixed, "tm", frames, distance) for distance in range(2, frames)
    ]
    grad_queries, grad_keys, grad_gains = backward(
        scalars,
        fields,
        weights,
        grads[:0:-1],
        list(range(frames - 1, 0, -1)),
        results,
        mixed,
        gains,
        (own, frames, clips),
    )
    return (
        grad_queries.reshape(query_heads.shape),
        grad_keys.reshape(query_heads.shape),
        grad_gains,
    )


def temporal_grads(attended, upstream, gain_query, gain_keys, length):
    highest = lax.Precision.HIGHEST
    frames = attended.shape[0]
    score_scale = attended.shape[-1] ** (-0.5)
    floats = attended.astype(jnp.float32)
    inverse_rms = lax.rsqrt(jnp.mean(floats * floats, axis=-1, keepdims=True) + 1e-06)
    normed = floats * inverse_rms
    t_query = normed * gain_query
    t_keys = normed * gain_keys
    scores = jnp.einsum("txhd,uxhd->xhtu", t_query, t_keys, precision=highest) * score_scale
    frame_ids = jnp.arange(frames, dtype=jnp.int32)
    allowed = (frame_ids[None, :] <= frame_ids[:, None]) & (frame_ids[None, :] < length)
    scores = jnp.where(allowed, scores, -1e30)
    weights = jax.nn.softmax(scores, axis=-1)
    weights_low = lax.optimization_barrier(weights.astype(jnp.bfloat16)).astype(jnp.float32)
    valid_rows = (frame_ids < length).astype(jnp.float32)
    masked = upstream.astype(jnp.float32) * valid_rows[:, None, None, None]
    grad_weights = jnp.einsum("txhd,uxhd->xhtu", masked, floats, precision=highest)
    from_values = jnp.einsum("xhtu,txhd->uxhd", weights_low, masked, precision=highest)
    grad_scores = (
        weights
        * (grad_weights - jnp.sum(grad_weights * weights, axis=-1, keepdims=True))
        * score_scale
    )
    grad_tquery = jnp.einsum("xhtu,uxhd->txhd", grad_scores, t_keys, precision=highest)
    grad_tkeys = jnp.einsum("xhtu,txhd->uxhd", grad_scores, t_query, precision=highest)
    grad_normed = grad_tquery * gain_query + grad_tkeys * gain_keys
    grad_gain_query = jnp.sum(grad_tquery * normed, axis=(0, 1))
    grad_gain_keys = jnp.sum(grad_tkeys * normed, axis=(0, 1))
    from_norm = inverse_rms * (
        grad_normed - normed * jnp.mean(grad_normed * normed, axis=-1, keepdims=True)
    )
    grad_total = (masked + from_values + from_norm).astype(jnp.bfloat16)
    return (grad_total, grad_gain_query, grad_gain_keys)


def split_by_patches(query_heads, key_heads, value_heads, cotangent, task_ids, lengths, gains):
    patches, feat = query_heads.shape[2:]
    heads = feat // HEAD_DIM
    queries, key_rows, values = (
        field.reshape(patches, feat) for field in (query_heads, key_heads, value_heads)
    )
    scalars = jnp.zeros((1,), jnp.int32)
    fields = (queries, key_rows, values)
    weights, attended = forward(scalars, *fields, 1)
    attended_field = jnp.transpose(attended[0], (2, 0, 1)).reshape(1, 1, patches, feat)
    upstream = lax.all_to_all(
        lax.all_to_all(cotangent, "space", split_axis=3, concat_axis=2, tiled=True),
        "tm",
        split_axis=2,
        concat_axis=1,
        tiled=True,
    )
    frames_attended = lax.all_to_all(attended_field, "tm", split_axis=2, concat_axis=1, tiled=True)
    frames, local_patches = frames_attended.shape[1:3]
    selector = (task_ids[0] == jnp.arange(gains.shape[1], dtype=jnp.int32)).astype(jnp.float32)
    gain_query = jnp.sum(selector[:, None] * gains[0], axis=0).reshape(heads, HEAD_DIM)
    gain_keys = jnp.sum(selector[:, None] * gains[1], axis=0).reshape(heads, HEAD_DIM)
    grad_total, grad_gq, grad_gk = temporal_grads(
        frames_attended.reshape(frames, local_patches, heads, HEAD_DIM),
        upstream.reshape(frames, local_patches, heads, HEAD_DIM),
        gain_query,
        gain_keys,
        lengths[0],
    )
    gain_terms = jnp.stack(
        [
            selector[:, None] * grad_gq.reshape(1, feat),
            selector[:, None] * grad_gk.reshape(1, feat),
        ]
    )
    grad_gains = lax.psum(gain_terms, ("dp", "tm"))
    returned = lax.all_to_all(
        grad_total.reshape(1, frames, local_patches, feat),
        "tm",
        split_axis=1,
        concat_axis=2,
        tiled=True,
    )
    head_grads = jnp.transpose(returned.reshape(patches, heads, HEAD_DIM), (1, 2, 0))
    grad_queries, grad_keys = backward(scalars, fields, weights, [head_grads], [0])
    return (
        grad_queries.reshape(query_heads.shape),
        grad_keys.reshape(query_heads.shape),
        grad_gains,
    )


def solution(mesh):
    clips, frames, spaces = (mesh.shape[axis] for axis in ("dp", "tm", "space"))

    def local(query_heads, *others):
        heads = query_heads.shape[3] // HEAD_DIM
        powers = all(size & (size - 1) == 0 for size in (clips, frames))
        if powers and frames <= 4 and heads % frames == 0:
            return split_by_heads(query_heads, *others, clips, frames, spaces)
        return split_by_patches(query_heads, *others)

    return jax.shard_map(
        local,
        mesh=mesh,
        in_specs=(
            P("dp", "tm", None, "space"),
            P("dp", "tm", None, "space"),
            P("dp", "tm", None, "space"),
            P("dp", "tm", "space", None),
            P("dp"),
            P("dp"),
            P(None, None, "space"),
        ),
        out_specs=(
            P("dp", "tm", None, "space"),
            P("dp", "tm", None, "space"),
            P(None, None, "space"),
        ),
        check_vma=False,
    )
```

```python
import functools

import jax
import jax.numpy as jnp
from jax import lax
from jax.experimental import pallas as pl
from jax.experimental.pallas import tpu as pltpu
from jax.sharding import PartitionSpec as P

HEAD_DIM = 128
GROUP = 16
MIB = 1024 * 1024


def params(patches):
    return pltpu.CompilerParams(vmem_limit_bytes=(16 if patches <= 512 else 60) * MIB)


def cost(microseconds):
    return pl.CostEstimate(flops=int(microseconds * 1e8), bytes_accessed=0, transcendentals=0)


def columns_dot(left, right):
    return lax.dot_general(
        left, right, (((1,), (1,)), ((), ())), preferred_element_type=jnp.float32
    )


def dot(left, right):
    return jnp.dot(left, right, preferred_element_type=jnp.float32)


def partner(scalars, distance):
    return jnp.bitwise_xor(scalars[0], distance)


def forward_kernel(scalars, query_ref, key_ref, value_ref, weights_ref, *refs):
    (queries, key_rows, values, arrived), attended_refs = refs[-4:], refs[:-4]
    score_scale = HEAD_DIM ** (-0.5)
    groups, _, width = queries.shape
    own = width // HEAD_DIM
    copies = []
    for group in range(groups):
        cols = pl.ds(pl.multiple_of(partner(scalars, group) * width, HEAD_DIM), width)
        for field, (source, target) in enumerate(
            ((query_ref, queries), (key_ref, key_rows), (value_ref, values))
        ):
            copy = pltpu.make_async_copy(
                source.at[:, cols], target.at[group], arrived.at[group, field]
            )
            copy.start()
            copies.append(copy)
    for group in range(groups):
        for copy in copies[3 * group : 3 * group + 3]:
            copy.wait()
        for head in range(own):
            cols = pl.ds(head * HEAD_DIM, HEAD_DIM)
            scores = columns_dot(key_rows[group, :, cols], queries[group, :, cols])
            largest = jnp.max(scores, axis=0, keepdims=True)
            raised = jnp.exp((scores - largest) * score_scale)
            weights = raised * (1.0 / jnp.sum(raised, axis=0, keepdims=True))
            weights_ref[group * own + head] = weights
            attended = dot(values[group, :, cols].T, weights.astype(jnp.bfloat16))
            attended_refs[group][head] = attended.astype(jnp.bfloat16)


def forward(scalars, queries, key_rows, values, groups):
    patches, feat = queries.shape
    heads = feat // HEAD_DIM
    own = heads // groups
    fields = [
        pltpu.with_memory_space_constraint(field, pltpu.HBM) for field in (queries, key_rows, values)
    ]
    weights, *attended = pl.pallas_call(
        forward_kernel,
        in_specs=[pl.BlockSpec(memory_space=pltpu.SMEM)]
        + [pl.BlockSpec(memory_space=pltpu.HBM)] * 3,
        out_specs=[pl.BlockSpec(memory_space=pltpu.VMEM)] * (1 + groups),
        scratch_shapes=[pltpu.VMEM((groups, patches, feat // groups), jnp.bfloat16)] * 3
        + [pltpu.SemaphoreType.DMA((groups, 3))],
        out_shape=[jax.ShapeDtypeStruct((heads, patches, patches), jnp.float32)]
        + [jax.ShapeDtypeStruct((own, HEAD_DIM, patches), jnp.bfloat16)] * groups,
        compiler_params=params(patches),
        cost_estimate=cost(6),
        name="spatial_forward",
    )(scalars, *fields)
    return weights, attended


def backward_group(scalars, fields, weights_ref, grad_ref, distance, scratch, results, sent):
    query_ref, key_ref, value_ref = fields
    score_scale = HEAD_DIM ** (-0.5)
    own = grad_ref.shape[0]
    start = partner(scalars, distance) * (own * HEAD_DIM)
    columns = [
        pl.ds(pl.multiple_of(start + head * HEAD_DIM, HEAD_DIM), HEAD_DIM) for head in range(own)
    ]
    spatial_grads = [dot(value_ref[:, columns[head]], grad_ref[head]) for head in range(own)]
    all_scores = []
    for head, spatial_grad in enumerate(spatial_grads):
        weights = weights_ref[distance * own + head]
        row_sum = jnp.sum(spatial_grad * weights, axis=0, keepdims=True)
        scores = weights * (spatial_grad - row_sum) * score_scale
        all_scores.append(scores.astype(jnp.bfloat16))
    gq, gk = scratch
    for head, scores in enumerate(all_scores):
        cols = pl.ds(head * HEAD_DIM, HEAD_DIM)
        gk[:, cols] = dot(scores, query_ref[:, columns[head]]).astype(jnp.bfloat16)
        gq[:, cols] = dot(key_ref[:, columns[head]].T, scores).astype(jnp.bfloat16).T
    there = pl.ds(pl.multiple_of(start, HEAD_DIM), own * HEAD_DIM)
    copies = [
        pltpu.make_async_copy(source, target.at[:, there], sent.at[side])
        for side, (source, target) in enumerate(zip(scratch, results))
    ]
    for copy in copies:
        copy.start()
    return copies


def backward_kernel(distances, gains_of, scalars, *refs):
    fields, weights_ref, refs = refs[:3], refs[3], refs[4:]
    grad_refs, refs = refs[: len(distances)], refs[len(distances) :]
    *refs, gq, gk, sent = refs
    copies = []
    if gains_of:
        *mixed_refs, gains_ref, _, _, gq_ref, gk_ref, grad_gains_ref, grad_gains = refs
        gain_gradients(*gains_of, scalars, mixed_refs, gains_ref, grad_gains)
        copy = pltpu.make_async_copy(grad_gains, grad_gains_ref, sent.at[len(distances), 0])
        copy.start()
        copies.append(copy)
    else:
        gq_ref, gk_ref = refs
    for place, (distance, grad_ref) in enumerate(zip(distances, grad_refs)):
        copies += backward_group(
            scalars,
            fields,
            weights_ref,
            grad_ref,
            distance,
            (gq.at[place], gk.at[place]),
            (gq_ref, gk_ref),
            sent.at[place],
        )
    for copy in copies:
        copy.wait()


def backward(scalars, fields, weights, grads, distances, earlier=(), mixed=(), gains=None, gains_of=()):
    patches, feat = fields[0].shape
    own = grads[0].shape[0]
    operands = [*fields, weights, *grads] + ([*mixed, gains] if gains_of else [])
    block = pltpu.VMEM((len(distances), patches, own * HEAD_DIM), jnp.bfloat16)
    out_shape = [jax.ShapeDtypeStruct((patches, feat), jnp.bfloat16)] * 2
    scratch = [block, block, pltpu.SemaphoreType.DMA((len(distances) + 1, 2))]
    if gains_of:
        out_shape.append(jax.ShapeDtypeStruct(gains.shape, jnp.float32))
        scratch.insert(0, pltpu.VMEM(gains.shape, jnp.float32))
    return pl.pallas_call(
        functools.partial(backward_kernel, distances, gains_of),
        in_specs=[pl.BlockSpec(memory_space=pltpu.SMEM)]
        + [pl.BlockSpec(memory_space=pltpu.VMEM)] * len(operands)
        + [pl.BlockSpec(memory_space=pl.ANY)] * len(earlier),
        out_specs=[pl.BlockSpec(memory_space=pl.ANY)] * len(out_shape),
        scratch_shapes=scratch,
        out_shape=out_shape,
        input_output_aliases={len(operands) + 1 + index: index for index in range(len(earlier))},
        compiler_params=params(patches),
        cost_estimate=cost(2),
        name="spatial_backward",
    )(scalars, *operands, *earlier)


def pack_kernel(scalars, field_ref, *refs):
    *packed_refs, rows, arrived = refs
    chunks, size, _ = rows.shape
    spaces, _, width = packed_refs[0].shape
    copies = [
        pltpu.make_async_copy(
            field_ref.at[pl.ds(chunk * size, size), :], rows.at[chunk], arrived.at[chunk]
        )
        for chunk in range(chunks)
    ]
    for copy in copies:
        copy.start()
    for chunk, copy in enumerate(copies):
        copy.wait()
        for distance, packed_ref in enumerate(packed_refs):
            for space in range(spaces):
                start = (space * len(packed_refs) + partner(scalars, distance)) * width
                cols = pl.ds(pl.multiple_of(start, HEAD_DIM), width)
                packed_ref[space, pl.ds(chunk * size, size), :] = rows[chunk, :, cols]


def pack(scalars, field, frames, spaces):
    patches, feat = field.shape
    chunks = patches // GROUP
    shape = (spaces, patches, feat // (frames * spaces))
    return pl.pallas_call(
        pack_kernel,
        in_specs=[
            pl.BlockSpec(memory_space=pltpu.SMEM),
            pl.BlockSpec(memory_space=pltpu.HBM),
        ],
        out_specs=[pl.BlockSpec(memory_space=pltpu.VMEM)] * frames,
        out_shape=[jax.ShapeDtypeStruct(shape, field.dtype)] * frames,
        scratch_shapes=[
            pltpu.VMEM((chunks, patches // chunks, feat), field.dtype),
            pltpu.SemaphoreType.DMA((chunks,)),
        ],
        compiler_params=params(patches),
        cost_estimate=cost(1),
        name="pack_cotangent",
    )(scalars, pltpu.with_memory_space_constraint(field, pltpu.HBM))


def turn_kernel(frames, scalars, *refs):
    piece_refs, (own_ref, *other_refs), turned = refs[:frames], refs[frames:-1], refs[-1]
    spaces = piece_refs[0].shape[0]
    heads = own_ref.shape[1]
    for space in range(spaces):
        target = turned if space else own_ref
        source = jnp.bitwise_xor(scalars[1], space)
        for distance, ref in enumerate(piece_refs):
            frame = partner(scalars, distance)
            for head in range(heads):
                cols = pl.ds(head * HEAD_DIM, HEAD_DIM)
                target[frame, head] = ref[source, :, cols].T
        if space:
            half = frames // 2
            other_refs[2 * space - 2][...] = turned[:half]
            other_refs[2 * space - 1][...] = turned[half:]


def turn(scalars, pieces):
    spaces, patches, feat = pieces[0].shape
    frames, heads = len(pieces), feat // HEAD_DIM
    turned = (heads, HEAD_DIM, patches)
    sizes = [frames] + [frames // 2, frames - frames // 2] * (spaces - 1)
    return pl.pallas_call(
        functools.partial(turn_kernel, frames),
        in_specs=[pl.BlockSpec(memory_space=pltpu.SMEM)]
        + [pl.BlockSpec(memory_space=pltpu.VMEM)] * frames,
        out_specs=[pl.BlockSpec(memory_space=pltpu.VMEM)] * len(sizes),
        out_shape=[jax.ShapeDtypeStruct((size,) + turned, pieces[0].dtype) for size in sizes],
        scratch_shapes=[pltpu.VMEM((frames,) + turned, pieces[0].dtype)],
        compiler_params=params(patches),
        cost_estimate=cost(2),
        name="turn_cotangent",
    )(scalars, *pieces)


def temporal_part(length, attended_ref, load_upstream, load_gain, grad_ref):
    frames, feat, lanes = attended_ref.shape
    half = GROUP // 2
    score_scale = feat ** (-0.5)
    pairs = [(t, u) for t in range(frames) for u in range(t + 1)]
    every = range(frames)
    valid = [jnp.where(t < length, 1.0, 0.0).astype(jnp.float32) for t in every]
    bias = [jnp.where(u < length, 0.0, -1e30).astype(jnp.float32) for u in every]

    def split(block):
        block = block.astype(jnp.float32)
        return block[:half], block[half:]

    def load_fields(group):
        return [split(attended_ref[t, pl.ds(group * GROUP, GROUP), :]) for t in every]

    def load_ups(group):
        return [split(load_upstream(t, pl.ds(group * GROUP, GROUP))) for t in every]

    def total(piece):
        return jnp.broadcast_to(jnp.sum(piece, axis=0, keepdims=True), (half, lanes))

    squares = [jnp.zeros((half, lanes), jnp.float32) for _ in every]
    for group in range(feat // GROUP):
        for t, (low, high) in enumerate(load_fields(group)):
            squares[t] = squares[t] + (low * low + high * high)
    inverse = [lax.rsqrt(total(squares[t]) * (1.0 / feat) + 1e-06) for t in every]

    raw = {pair: jnp.zeros((half, lanes), jnp.float32) for pair in pairs}
    grad = {pair: jnp.zeros((half, lanes), jnp.float32) for pair in pairs}
    for group in range(feat // GROUP):
        fields, ups = load_fields(group), load_ups(group)
        for side in range(2):
            gain = load_gain(pl.ds(group * GROUP + side * half, half))
            normed = [fields[t][side] * inverse[t] for t in every]
            gained = [normed[t] * gain for t in every]
            for t, u in pairs:
                raw[t, u] = raw[t, u] + gained[t] * normed[u]
                grad[t, u] = grad[t, u] + ups[t][side] * fields[u][side]

    value_part, score_part = {}, {}
    for t in every:
        seen = range(t + 1)
        for u in seen:
            raw[t, u] = total(raw[t, u])
            grad[t, u] = total(grad[t, u]) * valid[t]
        scores = [raw[t, u] * score_scale + bias[u] for u in seen]
        largest = functools.reduce(jnp.maximum, scores)
        raised = [jnp.exp(score - largest) for score in scores]
        over = 1.0 / functools.reduce(jnp.add, raised)
        weights = [piece * over for piece in raised]
        mean_grad = functools.reduce(jnp.add, [weights[u] * grad[t, u] for u in seen])
        for u in seen:
            rounded = weights[u].astype(jnp.bfloat16).astype(jnp.float32)
            value_part[t, u] = (rounded + (1.0 if u == t else 0.0)) * valid[t]
            score_part[t, u] = weights[u] * (grad[t, u] - mean_grad) * score_scale

    both = {(t, u): score_part[t, u] * (2.0 if t == u else 1.0) for t, u in pairs}
    both.update({(u, t): both[t, u] for t, u in pairs})
    raw.update({(u, t): raw[t, u] for t, u in pairs})
    mean_part = [
        functools.reduce(jnp.add, [both[u, v] * raw[u, v] for v in every]) * (1.0 / feat)
        for u in every
    ]

    all_mixed = []
    for group in range(feat // GROUP):
        fields, ups = load_fields(group), load_ups(group)
        outs = [[] for _ in every]
        for side in range(2):
            rows = pl.ds(group * GROUP + side * half, half)
            gain = load_gain(rows)
            normed = [fields[t][side] * inverse[t] for t in every]
            mixed = jnp.zeros((half, lanes), jnp.float32)
            for u in every:
                crossed = functools.reduce(jnp.add, [both[u, v] * normed[v] for v in every])
                mixed = mixed + crossed * normed[u]
                from_norm = inverse[u] * (gain * crossed - normed[u] * mean_part[u])
                direct = functools.reduce(
                    jnp.add, [value_part[t, u] * ups[t][side] for t in range(u, frames)]
                )
                outs[u].append(direct + from_norm)
            all_mixed.append(mixed)
        for u in every:
            grad_ref[u, pl.ds(group * GROUP, GROUP), :] = jnp.concatenate(
                outs[u], axis=0
            ).astype(jnp.bfloat16)
    return jnp.concatenate(all_mixed, axis=0)


def temporal_kernel(frames, spaces, scalars, *refs):
    attended_refs, (gain_ref, own_ref, *other_refs), refs = (
        refs[:frames],
        refs[frames : frames + 2 * spaces],
        refs[frames + 2 * spaces :],
    )
    grad_refs, (mixed_ref, attended, grads) = refs[:frames], refs[frames:]
    heads, lanes = own_ref.shape[1], own_ref.shape[3]
    half = frames // 2
    mixed_ref[...] = jnp.full(mixed_ref.shape, scalars[3].astype(jnp.float32))

    def load_upstream(space, head, t, rows):
        if space == 0:
            return own_ref[t, head, rows, :]
        return other_refs[2 * space - 2 + t // half][t % half, head, rows, :]

    def step(head, carry):
        places = [
            pl.ds(pl.multiple_of(jnp.bitwise_xor(scalars[1], space) * lanes, lanes), lanes)
            for space in range(spaces)
        ]
        for distance, ref in enumerate(attended_refs):
            frame = partner(scalars, distance)
            for space, here in enumerate(places):
                attended[space, frame] = ref[head, :, here]
        mixed = [
            temporal_part(
                scalars[2],
                attended.at[space],
                functools.partial(load_upstream, space, head),
                lambda rows: gain_ref[head, rows, :],
                grads.at[space],
            )
            for space in range(spaces)
        ]
        summed = functools.reduce(jnp.add, mixed)
        mixed_ref[pl.ds(head, 1), :] = jnp.sum(summed.T, axis=0, keepdims=True) * 0.5
        for distance, ref in enumerate(grad_refs):
            frame = partner(scalars, distance)
            for space, here in enumerate(places):
                ref[head, :, here] = grads[space, frame]
        return carry

    lax.fori_loop(0, heads, step, 0)


def temporal(scalars, attended, upstream, gain):
    frames, heads, feat, lanes = upstream[0].shape
    spaces = (len(upstream) + 1) // 2
    patches = spaces * lanes
    rows = -(-(heads + 1) // 8) * 8
    operands = [*attended, gain, *upstream]
    *grads, mixed = pl.pallas_call(
        functools.partial(temporal_kernel, frames, spaces),
        in_specs=[pl.BlockSpec(memory_space=pltpu.SMEM)]
        + [pl.BlockSpec(memory_space=pltpu.VMEM)] * len(operands),
        out_specs=[pl.BlockSpec(memory_space=pltpu.VMEM)] * (frames + 1),
        scratch_shapes=[pltpu.VMEM((spaces, frames, feat, lanes), jnp.bfloat16)] * 2,
        out_shape=[jax.ShapeDtypeStruct((heads, feat, patches), jnp.bfloat16)] * frames
        + [jax.ShapeDtypeStruct((rows, feat), jnp.float32)],
        compiler_params=params(patches),
        cost_estimate=cost(4),
        name="temporal",
    )(scalars, *operands)
    return grads, mixed


def gain_gradients(heads, frames, clips, scalars, mixed_refs, gains_ref, grad_ref):
    tasks = gains_ref.shape[1]
    rows = sum(ref.shape[0] for ref in mixed_refs) // (frames * clips)
    each = mixed_refs[0].shape[0] // rows
    task_ids = lax.broadcasted_iota(jnp.int32, (tasks, HEAD_DIM), 0).astype(jnp.float32)
    for distance in range(frames):
        for head in range(heads):
            mixed = jnp.zeros((tasks, HEAD_DIM), jnp.float32)
            for clip in range(clips):
                block = distance * clips + clip
                ref, start = mixed_refs[block // each], block % each * rows
                task = ref[pl.ds(start + heads, 1), :]
                row = ref[pl.ds(start + head, 1), :]
                mixed = mixed + jnp.where(task_ids == task, row, 0.0)
            start = (partner(scalars, distance) * heads + head) * HEAD_DIM
            cols = pl.ds(pl.multiple_of(start, HEAD_DIM), HEAD_DIM)
            grad_ref[0, :, cols] = gains_ref[1, :, cols] * mixed
            grad_ref[1, :, cols] = gains_ref[0, :, cols] * mixed


def swap(field, axis, size, distance):
    return lax.ppermute(field, axis, [(i, i ^ distance) for i in range(size)])


def split_by_heads(
    query_heads, key_heads, value_heads, cotangent, task_ids, lengths, gains, clips, frames, spaces
):
    patches, feat = query_heads.shape[2:]
    heads = feat // HEAD_DIM
    own = heads // frames
    width = own * HEAD_DIM
    queries, key_rows, values = (
        field.reshape(patches, feat) for field in (query_heads, key_heads, value_heads)
    )
    frame, space = lax.axis_index("tm"), lax.axis_index("space")
    scalars = jnp.stack([frame, space, lengths[0], task_ids[0]]).astype(jnp.int32)

    pieces = pack(scalars, cotangent.reshape(cotangent.shape[2:]), frames, spaces)
    queries, pieces = lax.optimization_barrier((queries, list(pieces)))
    for distance in range(1, frames):
        pieces[distance] = swap(pieces[distance], "tm", frames, distance)
    fields = (queries, key_rows, values)
    weights, attended = forward(scalars, *fields, frames)
    for distance in range(1, frames):
        attended[distance] = swap(attended[distance], "tm", frames, distance)
    pieces, _ = lax.optimization_barrier((pieces, weights))
    upstream = list(turn(scalars, pieces))
    for index in range(1, len(upstream)):
        upstream[index] = swap(upstream[index], "space", spaces, (index + 1) // 2)
    rows = lax.dynamic_index_in_dim(gains, task_ids[0], 1, keepdims=False)
    product = lax.dynamic_slice_in_dim(rows[0] * rows[1], frame * width, width, 0)
    gain = jnp.broadcast_to(
        product.reshape(own, HEAD_DIM, 1), (own, HEAD_DIM, patches // spaces)
    )
    grads, mixed = temporal(scalars, attended, upstream, gain)
    for distance in reversed(range(1, frames)):
        grads[distance] = swap(grads[distance], "tm", frames, distance)
    here = grads[0]
    for bit in range(clips.bit_length() - 1):
        other = swap(mixed, "dp", clips, 1 << bit)
        if bit == 0:
            here, other = lax.optimization_barrier((here, other))
        mixed = jnp.concatenate([mixed, other], axis=0)
    results = backward(scalars, fields, weights, [here], [0])
    mixed, results = lax.optimization_barrier((mixed, results))
    near, grads[1] = lax.optimization_barrier((mixed, grads[1]))
    mixed = [mixed, swap(near, "tm", frames, 1)] + [
        swap(mixed, "tm", frames, distance) for distance in range(2, frames)
    ]
    grad_queries, grad_keys, grad_gains = backward(
        scalars,
        fields,
        weights,
        grads[:0:-1],
        list(range(frames - 1, 0, -1)),
        results,
        mixed,
        gains,
        (own, frames, clips),
    )
    return (
        grad_queries.reshape(query_heads.shape),
        grad_keys.reshape(query_heads.shape),
        grad_gains,
    )


def temporal_grads(attended, upstream, gain_query, gain_keys, length):
    highest = lax.Precision.HIGHEST
    frames = attended.shape[0]
    score_scale = attended.shape[-1] ** (-0.5)
    floats = attended.astype(jnp.float32)
    inverse_rms = lax.rsqrt(jnp.mean(floats * floats, axis=-1, keepdims=True) + 1e-06)
    normed = floats * inverse_rms
    t_query = normed * gain_query
    t_keys = normed * gain_keys
    scores = jnp.einsum("txhd,uxhd->xhtu", t_query, t_keys, precision=highest) * score_scale
    frame_ids = jnp.arange(frames, dtype=jnp.int32)
    allowed = (frame_ids[None, :] <= frame_ids[:, None]) & (frame_ids[None, :] < length)
    scores = jnp.where(allowed, scores, -1e30)
    weights = jax.nn.softmax(scores, axis=-1)
    weights_low = lax.optimization_barrier(weights.astype(jnp.bfloat16)).astype(jnp.float32)
    valid_rows = (frame_ids < length).astype(jnp.float32)
    masked = upstream.astype(jnp.float32) * valid_rows[:, None, None, None]
    grad_weights = jnp.einsum("txhd,uxhd->xhtu", masked, floats, precision=highest)
    from_values = jnp.einsum("xhtu,txhd->uxhd", weights_low, masked, precision=highest)
    grad_scores = (
        weights
        * (grad_weights - jnp.sum(grad_weights * weights, axis=-1, keepdims=True))
        * score_scale
    )
    grad_tquery = jnp.einsum("xhtu,uxhd->txhd", grad_scores, t_keys, precision=highest)
    grad_tkeys = jnp.einsum("xhtu,txhd->uxhd", grad_scores, t_query, precision=highest)
    grad_normed = grad_tquery * gain_query + grad_tkeys * gain_keys
    grad_gain_query = jnp.sum(grad_tquery * normed, axis=(0, 1))
    grad_gain_keys = jnp.sum(grad_tkeys * normed, axis=(0, 1))
    from_norm = inverse_rms * (
        grad_normed - normed * jnp.mean(grad_normed * normed, axis=-1, keepdims=True)
    )
    grad_total = (masked + from_values + from_norm).astype(jnp.bfloat16)
    return (grad_total, grad_gain_query, grad_gain_keys)


def split_by_patches(query_heads, key_heads, value_heads, cotangent, task_ids, lengths, gains):
    patches, feat = query_heads.shape[2:]
    heads = feat // HEAD_DIM
    queries, key_rows, values = (
        field.reshape(patches, feat) for field in (query_heads, key_heads, value_heads)
    )
    scalars = jnp.zeros((1,), jnp.int32)
    fields = (queries, key_rows, values)
    weights, attended = forward(scalars, *fields, 1)
    attended_field = jnp.transpose(attended[0], (2, 0, 1)).reshape(1, 1, patches, feat)
    upstream = lax.all_to_all(
        lax.all_to_all(cotangent, "space", split_axis=3, concat_axis=2, tiled=True),
        "tm",
        split_axis=2,
        concat_axis=1,
        tiled=True,
    )
    frames_attended = lax.all_to_all(attended_field, "tm", split_axis=2, concat_axis=1, tiled=True)
    frames, local_patches = frames_attended.shape[1:3]
    selector = (task_ids[0] == jnp.arange(gains.shape[1], dtype=jnp.int32)).astype(jnp.float32)
    gain_query = jnp.sum(selector[:, None] * gains[0], axis=0).reshape(heads, HEAD_DIM)
    gain_keys = jnp.sum(selector[:, None] * gains[1], axis=0).reshape(heads, HEAD_DIM)
    grad_total, grad_gq, grad_gk = temporal_grads(
        frames_attended.reshape(frames, local_patches, heads, HEAD_DIM),
        upstream.reshape(frames, local_patches, heads, HEAD_DIM),
        gain_query,
        gain_keys,
        lengths[0],
    )
    gain_terms = jnp.stack(
        [
            selector[:, None] * grad_gq.reshape(1, feat),
            selector[:, None] * grad_gk.reshape(1, feat),
        ]
    )
    grad_gains = lax.psum(gain_terms, ("dp", "tm"))
    returned = lax.all_to_all(
        grad_total.reshape(1, frames, local_patches, feat),
        "tm",
        split_axis=1,
        concat_axis=2,
        tiled=True,
    )
    head_grads = jnp.transpose(returned.reshape(patches, heads, HEAD_DIM), (1, 2, 0))
    grad_queries, grad_keys = backward(scalars, fields, weights, [head_grads], [0])
    return (
        grad_queries.reshape(query_heads.shape),
        grad_keys.reshape(query_heads.shape),
        grad_gains,
    )


def solution(mesh):
    clips, frames, spaces = (mesh.shape[axis] for axis in ("dp", "tm", "space"))

    def local(query_heads, *others):
        heads = query_heads.shape[3] // HEAD_DIM
        powers = all(size & (size - 1) == 0 for size in (clips, frames, spaces))
        if powers and 2 <= frames <= 4 and heads % frames == 0:
            return split_by_heads(query_heads, *others, clips, frames, spaces)
        return split_by_patches(query_heads, *others)

    return jax.shard_map(
        local,
        mesh=mesh,
        in_specs=(
            P("dp", "tm", None, "space"),
            P("dp", "tm", None, "space"),
            P("dp", "tm", None, "space"),
            P("dp", "tm", "space", None),
            P("dp"),
            P("dp"),
            P(None, None, "space"),
        ),
        out_specs=(
            P("dp", "tm", None, "space"),
            P("dp", "tm", None, "space"),
            P(None, None, "space"),
        ),
        check_vma=False,
    )
```

```python
import functools

import jax
import jax.numpy as jnp
from jax import lax
from jax.experimental import pallas as pl
from jax.experimental.pallas import tpu as pltpu
from jax.sharding import PartitionSpec as P

HEAD_DIM = 128
GROUP = 16
MIB = 1024 * 1024


def params(patches):
    return pltpu.CompilerParams(vmem_limit_bytes=(16 if patches <= 512 else 60) * MIB)


def cost(microseconds):
    return pl.CostEstimate(flops=int(microseconds * 1e8), bytes_accessed=0, transcendentals=0)


def in_hbm(field):
    return pltpu.with_memory_space_constraint(field, pltpu.HBM)


def columns_dot(left, right):
    return lax.dot_general(
        left, right, (((1,), (1,)), ((), ())), preferred_element_type=jnp.float32
    )


def dot(left, right):
    return jnp.dot(left, right, preferred_element_type=jnp.float32)


def partner(axis, distance):
    return distance if axis is None else jnp.bitwise_xor(lax.axis_index(axis), distance)


def forward_kernel(axis, query_ref, key_ref, value_ref, weights_ref, *refs):
    (queries, key_rows, values, arrived), attended_refs = refs[-4:], refs[:-4]
    score_scale = HEAD_DIM ** (-0.5)
    groups, _, width = queries.shape
    own = width // HEAD_DIM
    copies = []
    for group in range(groups):
        cols = pl.ds(pl.multiple_of(partner(axis, group) * width, HEAD_DIM), width)
        for field, (source, target) in enumerate(
            ((query_ref, queries), (key_ref, key_rows), (value_ref, values))
        ):
            copy = pltpu.make_async_copy(
                source.at[:, cols], target.at[group], arrived.at[group, field]
            )
            copy.start()
            copies.append(copy)
    for group in range(groups):
        for copy in copies[3 * group : 3 * group + 3]:
            copy.wait()
        for head in range(own):
            cols = pl.ds(head * HEAD_DIM, HEAD_DIM)
            scores = columns_dot(key_rows[group, :, cols], queries[group, :, cols])
            largest = jnp.max(scores, axis=0, keepdims=True)
            raised = jnp.exp((scores - largest) * score_scale)
            weights = raised * (1.0 / jnp.sum(raised, axis=0, keepdims=True))
            weights_ref[group * own + head] = weights
            attended = dot(values[group, :, cols].T, weights.astype(jnp.bfloat16))
            attended_refs[group][head] = attended.astype(jnp.bfloat16)


def forward(axis, queries, key_rows, values, groups):
    patches, feat = queries.shape
    heads = feat // HEAD_DIM
    own = heads // groups
    fields = [in_hbm(field) for field in (queries, key_rows, values)]
    weights, *attended = pl.pallas_call(
        functools.partial(forward_kernel, axis),
        in_specs=[pl.BlockSpec(memory_space=pltpu.HBM)] * 3,
        out_specs=[pl.BlockSpec(memory_space=pltpu.VMEM)] * (1 + groups),
        scratch_shapes=[pltpu.VMEM((groups, patches, feat // groups), jnp.bfloat16)] * 3
        + [pltpu.SemaphoreType.DMA((groups, 3))],
        out_shape=[jax.ShapeDtypeStruct((heads, patches, patches), jnp.float32)]
        + [jax.ShapeDtypeStruct((own, HEAD_DIM, patches), jnp.bfloat16)] * groups,
        compiler_params=params(patches),
        cost_estimate=cost(6),
        name="spatial_forward",
    )(*fields)
    return weights, attended


def backward_group(axis, fields, weights_ref, grad_ref, distance, scratch, results, sent):
    query_ref, key_ref, value_ref = fields
    score_scale = HEAD_DIM ** (-0.5)
    own = grad_ref.shape[0]
    start = partner(axis, distance) * (own * HEAD_DIM)
    columns = [
        pl.ds(pl.multiple_of(start + head * HEAD_DIM, HEAD_DIM), HEAD_DIM) for head in range(own)
    ]
    spatial_grads = [dot(value_ref[:, columns[head]], grad_ref[head]) for head in range(own)]
    all_scores = []
    for head, spatial_grad in enumerate(spatial_grads):
        weights = weights_ref[distance * own + head]
        row_sum = jnp.sum(spatial_grad * weights, axis=0, keepdims=True)
        scores = weights * (spatial_grad - row_sum) * score_scale
        all_scores.append(scores.astype(jnp.bfloat16))
    gq, gk = scratch
    for head, scores in enumerate(all_scores):
        cols = pl.ds(head * HEAD_DIM, HEAD_DIM)
        gk[:, cols] = dot(scores, query_ref[:, columns[head]]).astype(jnp.bfloat16)
        gq[:, cols] = dot(key_ref[:, columns[head]].T, scores).astype(jnp.bfloat16).T
    there = pl.ds(pl.multiple_of(start, HEAD_DIM), own * HEAD_DIM)
    copies = [
        pltpu.make_async_copy(source, target.at[:, there], sent.at[side])
        for side, (source, target) in enumerate(zip(scratch, results))
    ]
    for copy in copies:
        copy.start()
    return copies


def backward_kernel(axis, distances, gains_of, *refs):
    fields, weights_ref, refs = refs[:3], refs[3], refs[4:]
    grad_refs, refs = refs[: len(distances)], refs[len(distances) :]
    *refs, gq, gk, sent = refs
    copies = []
    if gains_of:
        *mixed_refs, gains_ref, _, _, gq_ref, gk_ref, grad_gains_ref, grad_gains = refs
        gain_gradients(axis, *gains_of, mixed_refs, gains_ref, grad_gains)
        copy = pltpu.make_async_copy(grad_gains, grad_gains_ref, sent.at[len(distances), 0])
        copy.start()
        copies.append(copy)
    else:
        gq_ref, gk_ref = refs
    for place, (distance, grad_ref) in enumerate(zip(distances, grad_refs)):
        copies += backward_group(
            axis,
            fields,
            weights_ref,
            grad_ref,
            distance,
            (gq.at[place], gk.at[place]),
            (gq_ref, gk_ref),
            sent.at[place],
        )
    for copy in copies:
        copy.wait()


def backward(axis, fields, weights, grads, distances, earlier=(), mixed=(), gains=None, gains_of=()):
    patches, feat = fields[0].shape
    own = grads[0].shape[0]
    operands = [*fields, weights, *grads] + ([*mixed, gains] if gains_of else [])
    block = pltpu.VMEM((len(distances), patches, own * HEAD_DIM), jnp.bfloat16)
    out_shape = [jax.ShapeDtypeStruct((patches, feat), jnp.bfloat16)] * 2
    scratch = [block, block, pltpu.SemaphoreType.DMA((len(distances) + 1, 2))]
    if gains_of:
        out_shape.append(jax.ShapeDtypeStruct(gains.shape, jnp.float32))
        scratch.insert(0, pltpu.VMEM(gains.shape, jnp.float32))
    return pl.pallas_call(
        functools.partial(backward_kernel, axis, distances, gains_of),
        in_specs=[pl.BlockSpec(memory_space=pltpu.VMEM)] * len(operands)
        + [pl.BlockSpec(memory_space=pl.ANY)] * len(earlier),
        out_specs=[pl.BlockSpec(memory_space=pl.ANY)] * len(out_shape),
        scratch_shapes=scratch,
        out_shape=out_shape,
        input_output_aliases={len(operands) + index: index for index in range(len(earlier))},
        compiler_params=params(patches),
        cost_estimate=cost(2),
        name="spatial_backward",
    )(*operands, *earlier)


def pack_kernel(field_ref, *refs):
    *packed_refs, rows, arrived = refs
    chunks, size, _ = rows.shape
    spaces, _, width = packed_refs[0].shape
    copies = [
        pltpu.make_async_copy(
            field_ref.at[pl.ds(chunk * size, size), :], rows.at[chunk], arrived.at[chunk]
        )
        for chunk in range(chunks)
    ]
    for copy in copies:
        copy.start()
    for chunk, copy in enumerate(copies):
        copy.wait()
        for distance, packed_ref in enumerate(packed_refs):
            for space in range(spaces):
                start = (space * len(packed_refs) + partner("tm", distance)) * width
                cols = pl.ds(pl.multiple_of(start, HEAD_DIM), width)
                packed_ref[space, pl.ds(chunk * size, size), :] = rows[chunk, :, cols]


def pack(field, frames, spaces):
    patches, feat = field.shape
    chunks = patches // GROUP
    shape = (spaces, patches, feat // (frames * spaces))
    return pl.pallas_call(
        pack_kernel,
        in_specs=[pl.BlockSpec(memory_space=pltpu.HBM)],
        out_specs=[pl.BlockSpec(memory_space=pltpu.VMEM)] * frames,
        out_shape=[jax.ShapeDtypeStruct(shape, field.dtype)] * frames,
        scratch_shapes=[
            pltpu.VMEM((chunks, patches // chunks, feat), field.dtype),
            pltpu.SemaphoreType.DMA((chunks,)),
        ],
        compiler_params=params(patches),
        cost_estimate=cost(1),
        name="pack_cotangent",
    )(in_hbm(field))


def turn_kernel(frames, *refs):
    piece_refs, (plane_ref, plane_out_ref, own_ref, *other_refs), turned = (
        refs[:frames][::-1],
        refs[frames:-1],
        refs[-1],
    )
    plane_out_ref[...] = plane_ref[...]
    spaces = piece_refs[0].shape[0]
    heads = own_ref.shape[1]
    for space in range(spaces):
        target = turned if space else own_ref
        source = partner("space", space)
        for distance, ref in enumerate(piece_refs):
            frame = partner("tm", distance)
            for head in range(heads):
                cols = pl.ds(head * HEAD_DIM, HEAD_DIM)
                target[frame, head] = ref[source, :, cols].T
        if space:
            half = frames // 2
            other_refs[2 * space - 2][...] = turned[:half]
            other_refs[2 * space - 1][...] = turned[half:]


def turn(pieces, plane):
    spaces, patches, feat = pieces[0].shape
    frames, heads = len(pieces), feat // HEAD_DIM
    turned = (heads, HEAD_DIM, patches)
    sizes = [frames] + [frames // 2, frames - frames // 2] * (spaces - 1)
    return pl.pallas_call(
        functools.partial(turn_kernel, frames),
        in_specs=[pl.BlockSpec(memory_space=pltpu.VMEM)] * (frames + 1),
        out_specs=[pl.BlockSpec(memory_space=pltpu.VMEM)] * (len(sizes) + 1),
        out_shape=[jax.ShapeDtypeStruct(plane.shape, plane.dtype)]
        + [jax.ShapeDtypeStruct((size,) + turned, pieces[0].dtype) for size in sizes],
        scratch_shapes=[pltpu.VMEM((frames,) + turned, pieces[0].dtype)],
        compiler_params=params(patches),
        cost_estimate=cost(2),
        name="turn_cotangent",
    )(*reversed(pieces), plane)


def temporal_part(length, attended_ref, load_upstream, load_gain, grad_ref):
    frames, feat, lanes = attended_ref.shape
    half = GROUP // 2
    score_scale = feat ** (-0.5)
    pairs = [(t, u) for t in range(frames) for u in range(t + 1)]
    every = range(frames)
    valid = [jnp.where(t < length, 1.0, 0.0).astype(jnp.float32) for t in every]
    bias = [jnp.where(u < length, 0.0, -1e30).astype(jnp.float32) for u in every]

    def split(block):
        block = block.astype(jnp.float32)
        return block[:half], block[half:]

    def load_fields(group):
        return [split(attended_ref[t, pl.ds(group * GROUP, GROUP), :]) for t in every]

    def load_ups(group):
        return [split(load_upstream(t, pl.ds(group * GROUP, GROUP))) for t in every]

    def total(piece):
        return jnp.broadcast_to(jnp.sum(piece, axis=0, keepdims=True), (half, lanes))

    squares = [jnp.zeros((half, lanes), jnp.float32) for _ in every]
    for group in range(feat // GROUP):
        for t, (low, high) in enumerate(load_fields(group)):
            squares[t] = squares[t] + (low * low + high * high)
    inverse = [lax.rsqrt(total(squares[t]) * (1.0 / feat) + 1e-06) for t in every]

    raw = {pair: jnp.zeros((half, lanes), jnp.float32) for pair in pairs}
    grad = {pair: jnp.zeros((half, lanes), jnp.float32) for pair in pairs}
    for group in range(feat // GROUP):
        fields, ups = load_fields(group), load_ups(group)
        for side in range(2):
            gain = load_gain(pl.ds(group * GROUP + side * half, half))
            normed = [fields[t][side] * inverse[t] for t in every]
            gained = [normed[t] * gain for t in every]
            for t, u in pairs:
                raw[t, u] = raw[t, u] + gained[t] * normed[u]
                grad[t, u] = grad[t, u] + ups[t][side] * fields[u][side]

    value_part, score_part = {}, {}
    for t in every:
        seen = range(t + 1)
        for u in seen:
            raw[t, u] = total(raw[t, u])
            grad[t, u] = total(grad[t, u]) * valid[t]
        scores = [raw[t, u] * score_scale + bias[u] for u in seen]
        largest = functools.reduce(jnp.maximum, scores)
        raised = [jnp.exp(score - largest) for score in scores]
        over = 1.0 / functools.reduce(jnp.add, raised)
        weights = [piece * over for piece in raised]
        mean_grad = functools.reduce(jnp.add, [weights[u] * grad[t, u] for u in seen])
        for u in seen:
            rounded = weights[u].astype(jnp.bfloat16).astype(jnp.float32)
            value_part[t, u] = (rounded + (1.0 if u == t else 0.0)) * valid[t]
            score_part[t, u] = weights[u] * (grad[t, u] - mean_grad) * score_scale

    both = {(t, u): score_part[t, u] * (2.0 if t == u else 1.0) for t, u in pairs}
    both.update({(u, t): both[t, u] for t, u in pairs})
    raw.update({(u, t): raw[t, u] for t, u in pairs})
    mean_part = [
        functools.reduce(jnp.add, [both[u, v] * raw[u, v] for v in every]) * (1.0 / feat)
        for u in every
    ]

    all_mixed = []
    for group in range(feat // GROUP):
        fields, ups = load_fields(group), load_ups(group)
        outs = [[] for _ in every]
        for side in range(2):
            rows = pl.ds(group * GROUP + side * half, half)
            gain = load_gain(rows)
            normed = [fields[t][side] * inverse[t] for t in every]
            mixed = jnp.zeros((half, lanes), jnp.float32)
            for u in every:
                crossed = functools.reduce(jnp.add, [both[u, v] * normed[v] for v in every])
                mixed = mixed + crossed * normed[u]
                from_norm = inverse[u] * (gain * crossed - normed[u] * mean_part[u])
                direct = functools.reduce(
                    jnp.add, [value_part[t, u] * ups[t][side] for t in range(u, frames)]
                )
                outs[u].append(direct + from_norm)
            all_mixed.append(mixed)
        for u in every:
            grad_ref[u, pl.ds(group * GROUP, GROUP), :] = jnp.concatenate(
                outs[u], axis=0
            ).astype(jnp.bfloat16)
    return jnp.concatenate(all_mixed, axis=0)


def temporal_kernel(frames, spaces, length_ref, task_ref, *refs):
    attended_refs, (gain_ref, own_ref, *other_refs), refs = (
        (refs[frames - 1], *refs[: frames - 1]),
        refs[frames : frames + 2 * spaces],
        refs[frames + 2 * spaces :],
    )
    field_refs, grad_refs, (mixed_ref, *kept_refs, attended, grads, arrived) = (
        refs[:3],
        refs[3 : frames + 3],
        refs[frames + 3 :],
    )
    copies = [
        pltpu.make_async_copy(source, target, arrived.at[index])
        for index, (source, target) in enumerate(zip(field_refs, kept_refs))
    ]
    for copy in copies:
        copy.start()
    heads, lanes = own_ref.shape[1], own_ref.shape[3]
    half = frames // 2
    mixed_ref[...] = jnp.full(mixed_ref.shape, task_ref[0].astype(jnp.float32))

    def load_upstream(space, head, t, rows):
        if space == 0:
            return own_ref[t, head, rows, :]
        return other_refs[2 * space - 2 + t // half][t % half, head, rows, :]

    def step(head, carry):
        places = [
            pl.ds(pl.multiple_of(partner("space", space) * lanes, lanes), lanes)
            for space in range(spaces)
        ]
        for distance, ref in enumerate(attended_refs):
            frame = partner("tm", distance)
            for space, here in enumerate(places):
                attended[space, frame] = ref[head, :, here]
        mixed = [
            temporal_part(
                length_ref[0],
                attended.at[space],
                functools.partial(load_upstream, space, head),
                lambda rows: gain_ref[head, rows, :],
                grads.at[space],
            )
            for space in range(spaces)
        ]
        summed = functools.reduce(jnp.add, mixed)
        mixed_ref[pl.ds(head, 1), :] = jnp.sum(summed.T, axis=0, keepdims=True) * 0.5
        for distance, ref in enumerate(grad_refs):
            frame = partner("tm", distance)
            for space, here in enumerate(places):
                ref[head, :, here] = grads[space, frame]
        return carry

    lax.fori_loop(0, heads, step, 0)
    for copy in copies:
        copy.wait()


def temporal(lengths, task_ids, attended, upstream, gain, fields):
    frames, heads, feat, lanes = upstream[0].shape
    spaces = (len(upstream) + 1) // 2
    patches = spaces * lanes
    rows = -(-(heads + 1) // 8) * 8
    operands = [*attended[1:], attended[0], gain, *upstream]
    results = pl.pallas_call(
        functools.partial(temporal_kernel, frames, spaces),
        in_specs=[pl.BlockSpec(memory_space=pltpu.SMEM)] * 2
        + [pl.BlockSpec(memory_space=pltpu.VMEM)] * len(operands)
        + [pl.BlockSpec(memory_space=pltpu.HBM)] * len(fields),
        out_specs=[pl.BlockSpec(memory_space=pltpu.VMEM)] * (frames + 1 + len(fields)),
        scratch_shapes=[pltpu.VMEM((spaces, frames, feat, lanes), jnp.bfloat16)] * 2
        + [pltpu.SemaphoreType.DMA((len(fields),))],
        out_shape=[jax.ShapeDtypeStruct((heads, feat, patches), jnp.bfloat16)] * frames
        + [jax.ShapeDtypeStruct((rows, feat), jnp.float32)]
        + [jax.ShapeDtypeStruct(field.shape, field.dtype) for field in fields],
        compiler_params=params(patches),
        cost_estimate=cost(4),
        name="temporal",
    )(lengths, task_ids, *operands, *[in_hbm(field) for field in fields])
    return list(results[:frames]), results[frames], results[frames + 1 :]


def gain_gradients(axis, heads, frames, clips, mixed_refs, gains_ref, grad_ref):
    tasks = gains_ref.shape[1]
    rows = sum(ref.shape[0] for ref in mixed_refs) // (frames * clips)
    each = mixed_refs[0].shape[0] // rows
    task_ids = lax.broadcasted_iota(jnp.int32, (tasks, HEAD_DIM), 0).astype(jnp.float32)
    for distance in range(frames):
        for head in range(heads):
            mixed = jnp.zeros((tasks, HEAD_DIM), jnp.float32)
            for clip in range(clips):
                block = distance * clips + clip
                ref, start = mixed_refs[block // each], block % each * rows
                task = ref[pl.ds(start + heads, 1), :]
                row = ref[pl.ds(start + head, 1), :]
                mixed = mixed + jnp.where(task_ids == task, row, 0.0)
            start = (partner(axis, distance) * heads + head) * HEAD_DIM
            cols = pl.ds(pl.multiple_of(start, HEAD_DIM), HEAD_DIM)
            grad_ref[0, :, cols] = gains_ref[1, :, cols] * mixed
            grad_ref[1, :, cols] = gains_ref[0, :, cols] * mixed


def swap(field, axis, size, distance):
    return lax.ppermute(field, axis, [(i, i ^ distance) for i in range(size)])


def split_by_heads(
    query_heads, key_heads, value_heads, cotangent, task_ids, lengths, gains, clips, frames, spaces
):
    patches, feat = query_heads.shape[2:]
    heads = feat // HEAD_DIM
    own = heads // frames
    width = own * HEAD_DIM
    queries, key_rows, values = (
        field.reshape(patches, feat) for field in (query_heads, key_heads, value_heads)
    )
    frame = lax.axis_index("tm")

    pieces = list(pack(cotangent.reshape(cotangent.shape[2:]), frames, spaces))
    queries, pieces = lax.optimization_barrier((queries, pieces))
    for distance in range(1, frames):
        pieces[distance] = swap(pieces[distance], "tm", frames, distance)
    fields = (queries, key_rows, values)
    weights, attended = forward("tm", *fields, frames)
    for distance in range(1, frames):
        attended[distance] = swap(attended[distance], "tm", frames, distance)
    backwards, _ = lax.optimization_barrier((pieces[::-1], weights))
    attended[0], *upstream = turn(backwards[::-1], attended[0])
    for index in range(1, len(upstream)):
        upstream[index] = swap(upstream[index], "space", spaces, (index + 1) // 2)
    rows = lax.dynamic_index_in_dim(gains, task_ids[0], 1, keepdims=False)
    product = lax.dynamic_slice_in_dim(rows[0] * rows[1], frame * width, width, 0)
    gain = jnp.broadcast_to(
        product.reshape(own, HEAD_DIM, 1), (own, HEAD_DIM, patches // spaces)
    )
    grads, mixed, kept = temporal(lengths, task_ids, attended, upstream, gain, fields)
    for distance in reversed(range(1, frames)):
        grads[distance] = swap(grads[distance], "tm", frames, distance)
    here = grads[0]
    for bit in range(clips.bit_length() - 1):
        other = swap(mixed, "dp", clips, 1 << bit)
        if bit == 0:
            here, other = lax.optimization_barrier((here, other))
        mixed = jnp.concatenate([mixed, other], axis=0)
    results = backward("tm", kept, weights, [here], [0])
    mixed, results = lax.optimization_barrier((mixed, results))
    near, grads[1] = lax.optimization_barrier((mixed, grads[1]))
    mixed = [mixed, swap(near, "tm", frames, 1)] + [
        swap(mixed, "tm", frames, distance) for distance in range(2, frames)
    ]
    grad_queries, grad_keys, grad_gains = backward(
        "tm",
        kept,
        weights,
        grads[:0:-1],
        list(range(frames - 1, 0, -1)),
        results,
        mixed,
        gains,
        (own, frames, clips),
    )
    return (
        grad_queries.reshape(query_heads.shape),
        grad_keys.reshape(query_heads.shape),
        grad_gains,
    )


def temporal_grads(attended, upstream, gain_query, gain_keys, length):
    highest = lax.Precision.HIGHEST
    frames = attended.shape[0]
    score_scale = attended.shape[-1] ** (-0.5)
    floats = attended.astype(jnp.float32)
    inverse_rms = lax.rsqrt(jnp.mean(floats * floats, axis=-1, keepdims=True) + 1e-06)
    normed = floats * inverse_rms
    t_query = normed * gain_query
    t_keys = normed * gain_keys
    scores = jnp.einsum("txhd,uxhd->xhtu", t_query, t_keys, precision=highest) * score_scale
    frame_ids = jnp.arange(frames, dtype=jnp.int32)
    allowed = (frame_ids[None, :] <= frame_ids[:, None]) & (frame_ids[None, :] < length)
    scores = jnp.where(allowed, scores, -1e30)
    weights = jax.nn.softmax(scores, axis=-1)
    weights_low = lax.optimization_barrier(weights.astype(jnp.bfloat16)).astype(jnp.float32)
    valid_rows = (frame_ids < length).astype(jnp.float32)
    masked = upstream.astype(jnp.float32) * valid_rows[:, None, None, None]
    grad_weights = jnp.einsum("txhd,uxhd->xhtu", masked, floats, precision=highest)
    from_values = jnp.einsum("xhtu,txhd->uxhd", weights_low, masked, precision=highest)
    grad_scores = (
        weights
        * (grad_weights - jnp.sum(grad_weights * weights, axis=-1, keepdims=True))
        * score_scale
    )
    grad_tquery = jnp.einsum("xhtu,uxhd->txhd", grad_scores, t_keys, precision=highest)
    grad_tkeys = jnp.einsum("xhtu,txhd->uxhd", grad_scores, t_query, precision=highest)
    grad_normed = grad_tquery * gain_query + grad_tkeys * gain_keys
    grad_gain_query = jnp.sum(grad_tquery * normed, axis=(0, 1))
    grad_gain_keys = jnp.sum(grad_tkeys * normed, axis=(0, 1))
    from_norm = inverse_rms * (
        grad_normed - normed * jnp.mean(grad_normed * normed, axis=-1, keepdims=True)
    )
    grad_total = (masked + from_values + from_norm).astype(jnp.bfloat16)
    return (grad_total, grad_gain_query, grad_gain_keys)


def split_by_patches(query_heads, key_heads, value_heads, cotangent, task_ids, lengths, gains):
    patches, feat = query_heads.shape[2:]
    heads = feat // HEAD_DIM
    queries, key_rows, values = (
        field.reshape(patches, feat) for field in (query_heads, key_heads, value_heads)
    )
    fields = (queries, key_rows, values)
    weights, attended = forward(None, *fields, 1)
    attended_field = jnp.transpose(attended[0], (2, 0, 1)).reshape(1, 1, patches, feat)
    upstream = lax.all_to_all(
        lax.all_to_all(cotangent, "space", split_axis=3, concat_axis=2, tiled=True),
        "tm",
        split_axis=2,
        concat_axis=1,
        tiled=True,
    )
    frames_attended = lax.all_to_all(attended_field, "tm", split_axis=2, concat_axis=1, tiled=True)
    frames, local_patches = frames_attended.shape[1:3]
    selector = (task_ids[0] == jnp.arange(gains.shape[1], dtype=jnp.int32)).astype(jnp.float32)
    gain_query = jnp.sum(selector[:, None] * gains[0], axis=0).reshape(heads, HEAD_DIM)
    gain_keys = jnp.sum(selector[:, None] * gains[1], axis=0).reshape(heads, HEAD_DIM)
    grad_total, grad_gq, grad_gk = temporal_grads(
        frames_attended.reshape(frames, local_patches, heads, HEAD_DIM),
        upstream.reshape(frames, local_patches, heads, HEAD_DIM),
        gain_query,
        gain_keys,
        lengths[0],
    )
    gain_terms = jnp.stack(
        [
            selector[:, None] * grad_gq.reshape(1, feat),
            selector[:, None] * grad_gk.reshape(1, feat),
        ]
    )
    grad_gains = lax.psum(gain_terms, ("dp", "tm"))
    returned = lax.all_to_all(
        grad_total.reshape(1, frames, local_patches, feat),
        "tm",
        split_axis=1,
        concat_axis=2,
        tiled=True,
    )
    head_grads = jnp.transpose(returned.reshape(patches, heads, HEAD_DIM), (1, 2, 0))
    grad_queries, grad_keys = backward(None, fields, weights, [head_grads], [0])
    return (
        grad_queries.reshape(query_heads.shape),
        grad_keys.reshape(query_heads.shape),
        grad_gains,
    )


def solution(mesh):
    clips, frames, spaces = (mesh.shape[axis] for axis in ("dp", "tm", "space"))

    def local(query_heads, *others):
        heads = query_heads.shape[3] // HEAD_DIM
        powers = all(size & (size - 1) == 0 for size in (clips, frames, spaces))
        if powers and 2 <= frames <= 4 and heads % frames == 0:
            return split_by_heads(query_heads, *others, clips, frames, spaces)
        return split_by_patches(query_heads, *others)

    return jax.shard_map(
        local,
        mesh=mesh,
        in_specs=(
            P("dp", "tm", None, "space"),
            P("dp", "tm", None, "space"),
            P("dp", "tm", None, "space"),
            P("dp", "tm", "space", None),
            P("dp"),
            P("dp"),
            P(None, None, "space"),
        ),
        out_specs=(
            P("dp", "tm", None, "space"),
            P("dp", "tm", None, "space"),
            P(None, None, "space"),
        ),
        check_vma=False,
    )
```

```python
import functools

import jax
import jax.numpy as jnp
from jax import lax
from jax.experimental import pallas as pl
from jax.experimental.pallas import tpu as pltpu
from jax.sharding import PartitionSpec as P

HEAD_DIM = 128
GROUP = 16
MIB = 1024 * 1024


def params(patches):
    return pltpu.CompilerParams(vmem_limit_bytes=(16 if patches <= 512 else 60) * MIB)


def cost(microseconds):
    return pl.CostEstimate(flops=int(microseconds * 1e8), bytes_accessed=0, transcendentals=0)


def in_hbm(field):
    return pltpu.with_memory_space_constraint(field, pltpu.HBM)


def columns_dot(left, right):
    return lax.dot_general(
        left, right, (((1,), (1,)), ((), ())), preferred_element_type=jnp.float32
    )


def dot(left, right):
    return jnp.dot(left, right, preferred_element_type=jnp.float32)


def partner(axis, distance):
    return distance if axis is None else jnp.bitwise_xor(lax.axis_index(axis), distance)


def forward_kernel(axis, query_ref, key_ref, value_ref, weights_ref, *refs):
    (queries, key_rows, values, arrived), attended_refs = refs[-4:], refs[:-4]
    score_scale = HEAD_DIM ** (-0.5)
    groups, _, width = queries.shape
    own = width // HEAD_DIM
    copies = []
    for group in range(groups):
        cols = pl.ds(pl.multiple_of(partner(axis, group) * width, HEAD_DIM), width)
        for field, (source, target) in enumerate(
            ((query_ref, queries), (key_ref, key_rows), (value_ref, values))
        ):
            copy = pltpu.make_async_copy(
                source.at[:, cols], target.at[group], arrived.at[group, field]
            )
            copy.start()
            copies.append(copy)
    for group in range(groups):
        for copy in copies[3 * group : 3 * group + 3]:
            copy.wait()
        for head in range(own):
            cols = pl.ds(head * HEAD_DIM, HEAD_DIM)
            scores = columns_dot(key_rows[group, :, cols], queries[group, :, cols])
            largest = jnp.max(scores, axis=0, keepdims=True)
            raised = jnp.exp((scores - largest) * score_scale)
            weights = raised * (1.0 / jnp.sum(raised, axis=0, keepdims=True))
            weights_ref[group * own + head] = weights
            attended = dot(values[group, :, cols].T, weights.astype(jnp.bfloat16))
            attended_refs[group][head] = attended.astype(jnp.bfloat16)


def forward(axis, queries, key_rows, values, groups):
    patches, feat = queries.shape
    heads = feat // HEAD_DIM
    own = heads // groups
    fields = [in_hbm(field) for field in (queries, key_rows, values)]
    weights, *attended = pl.pallas_call(
        functools.partial(forward_kernel, axis),
        in_specs=[pl.BlockSpec(memory_space=pltpu.HBM)] * 3,
        out_specs=[pl.BlockSpec(memory_space=pltpu.VMEM)] * (1 + groups),
        scratch_shapes=[pltpu.VMEM((groups, patches, feat // groups), jnp.bfloat16)] * 3
        + [pltpu.SemaphoreType.DMA((groups, 3))],
        out_shape=[jax.ShapeDtypeStruct((heads, patches, patches), jnp.float32)]
        + [jax.ShapeDtypeStruct((own, HEAD_DIM, patches), jnp.bfloat16)] * groups,
        compiler_params=params(patches),
        cost_estimate=cost(6),
        name="spatial_forward",
    )(*fields)
    return weights, attended


def backward_group(axis, fields, weights_ref, grad_ref, distance, scratch, results, sent):
    query_ref, key_ref, value_ref = fields
    score_scale = HEAD_DIM ** (-0.5)
    own = grad_ref.shape[0]
    start = partner(axis, distance) * (own * HEAD_DIM)
    columns = [
        pl.ds(pl.multiple_of(start + head * HEAD_DIM, HEAD_DIM), HEAD_DIM) for head in range(own)
    ]
    spatial_grads = [dot(value_ref[:, columns[head]], grad_ref[head]) for head in range(own)]
    all_scores = []
    for head, spatial_grad in enumerate(spatial_grads):
        weights = weights_ref[distance * own + head]
        row_sum = jnp.sum(spatial_grad * weights, axis=0, keepdims=True)
        scores = weights * (spatial_grad - row_sum) * score_scale
        all_scores.append(scores.astype(jnp.bfloat16))
    gq, gk = scratch
    for head, scores in enumerate(all_scores):
        cols = pl.ds(head * HEAD_DIM, HEAD_DIM)
        gk[:, cols] = dot(scores, query_ref[:, columns[head]]).astype(jnp.bfloat16)
        gq[:, cols] = dot(key_ref[:, columns[head]].T, scores).astype(jnp.bfloat16).T
    there = pl.ds(pl.multiple_of(start, HEAD_DIM), own * HEAD_DIM)
    copies = [
        pltpu.make_async_copy(source, target.at[:, there], sent.at[side])
        for side, (source, target) in enumerate(zip(scratch, results))
    ]
    for copy in copies:
        copy.start()
    return copies


def backward_kernel(axis, distances, gains_of, *refs):
    fields, weights_ref, refs = refs[:3], refs[3], refs[4:]
    grad_refs, refs = refs[: len(distances)], refs[len(distances) :]
    *refs, gq, gk, sent = refs
    copies = []
    if gains_of:
        *mixed_refs, gains_ref, _, _, gq_ref, gk_ref, grad_gains_ref, grad_gains = refs
        gain_gradients(axis, *gains_of, mixed_refs, gains_ref, grad_gains)
        copy = pltpu.make_async_copy(grad_gains, grad_gains_ref, sent.at[len(distances), 0])
        copy.start()
        copies.append(copy)
    else:
        gq_ref, gk_ref = refs
    for place, (distance, grad_ref) in enumerate(zip(distances, grad_refs)):
        copies += backward_group(
            axis,
            fields,
            weights_ref,
            grad_ref,
            distance,
            (gq.at[place], gk.at[place]),
            (gq_ref, gk_ref),
            sent.at[place],
        )
    for copy in copies:
        copy.wait()


def backward(axis, fields, weights, grads, distances, earlier=(), mixed=(), gains=None, gains_of=()):
    patches, feat = fields[0].shape
    own = grads[0].shape[0]
    operands = [*fields, weights, *grads] + ([*mixed, gains] if gains_of else [])
    block = pltpu.VMEM((len(distances), patches, own * HEAD_DIM), jnp.bfloat16)
    out_shape = [jax.ShapeDtypeStruct((patches, feat), jnp.bfloat16)] * 2
    scratch = [block, block, pltpu.SemaphoreType.DMA((len(distances) + 1, 2))]
    if gains_of:
        out_shape.append(jax.ShapeDtypeStruct(gains.shape, jnp.float32))
        scratch.insert(0, pltpu.VMEM(gains.shape, jnp.float32))
    return pl.pallas_call(
        functools.partial(backward_kernel, axis, distances, gains_of),
        in_specs=[pl.BlockSpec(memory_space=pltpu.VMEM)] * len(operands)
        + [pl.BlockSpec(memory_space=pl.ANY)] * len(earlier),
        out_specs=[pl.BlockSpec(memory_space=pl.ANY)] * len(out_shape),
        scratch_shapes=scratch,
        out_shape=out_shape,
        input_output_aliases={len(operands) + index: index for index in range(len(earlier))},
        compiler_params=params(patches),
        cost_estimate=cost(2),
        name="spatial_backward",
    )(*operands, *earlier)


def pack_kernel(field_ref, *refs):
    *packed_refs, rows, arrived = refs
    chunks, size, _ = rows.shape
    spaces, _, width = packed_refs[0].shape
    copies = [
        pltpu.make_async_copy(
            field_ref.at[pl.ds(chunk * size, size), :], rows.at[chunk], arrived.at[chunk]
        )
        for chunk in range(chunks)
    ]
    for copy in copies:
        copy.start()
    for chunk, copy in enumerate(copies):
        copy.wait()
        for distance, packed_ref in enumerate(packed_refs):
            for space in range(spaces):
                start = (space * len(packed_refs) + partner("tm", distance)) * width
                cols = pl.ds(pl.multiple_of(start, HEAD_DIM), width)
                packed_ref[space, pl.ds(chunk * size, size), :] = rows[chunk, :, cols]


def pack(field, frames, spaces):
    patches, feat = field.shape
    chunks = patches // GROUP
    shape = (spaces, patches, feat // (frames * spaces))
    return pl.pallas_call(
        pack_kernel,
        in_specs=[pl.BlockSpec(memory_space=pltpu.HBM)],
        out_specs=[pl.BlockSpec(memory_space=pltpu.VMEM)] * frames,
        out_shape=[jax.ShapeDtypeStruct(shape, field.dtype)] * frames,
        scratch_shapes=[
            pltpu.VMEM((chunks, patches // chunks, feat), field.dtype),
            pltpu.SemaphoreType.DMA((chunks,)),
        ],
        compiler_params=params(patches),
        cost_estimate=cost(1),
        name="pack_cotangent",
    )(in_hbm(field))


def turn_kernel(frames, *refs):
    piece_refs, (plane_ref, own_ref, *other_refs), turned = (
        refs[:frames][::-1],
        refs[frames:-1],
        refs[-1],
    )
    spaces, lanes, _ = piece_refs[0].shape
    for space in range(spaces):
        place = pl.multiple_of(partner("space", space) * lanes, lanes)
        own_ref[frames + space] = plane_ref[:, :, pl.ds(place, lanes)]
    heads = own_ref.shape[1]
    for space in range(spaces):
        target = turned if space else own_ref
        source = partner("space", space)
        for distance, ref in enumerate(piece_refs):
            frame = partner("tm", distance)
            for head in range(heads):
                cols = pl.ds(head * HEAD_DIM, HEAD_DIM)
                target[frame, head] = ref[source, :, cols].T
        if space:
            half = frames // 2
            other_refs[2 * space - 2][...] = turned[:half]
            other_refs[2 * space - 1][...] = turned[half:]


def turn(pieces, plane):
    spaces, patches, feat = pieces[0].shape
    frames, heads = len(pieces), feat // HEAD_DIM
    turned = (heads, HEAD_DIM, patches)
    sizes = [frames + spaces] + [frames // 2, frames - frames // 2] * (spaces - 1)
    return pl.pallas_call(
        functools.partial(turn_kernel, frames),
        in_specs=[pl.BlockSpec(memory_space=pltpu.VMEM)] * (frames + 1),
        out_specs=[pl.BlockSpec(memory_space=pltpu.VMEM)] * len(sizes),
        out_shape=[jax.ShapeDtypeStruct((size,) + turned, pieces[0].dtype) for size in sizes],
        scratch_shapes=[pltpu.VMEM((frames,) + turned, pieces[0].dtype)],
        compiler_params=params(patches),
        cost_estimate=cost(2),
        name="turn_cotangent",
    )(*reversed(pieces), plane)


def temporal_part(length, load_attended, load_upstream, load_gain, fields, ups, normed, grad_ref):
    frames, feat, lanes = grad_ref.shape
    half = GROUP // 2
    score_scale = feat ** (-0.5)
    pairs = [(t, u) for t in range(frames) for u in range(t + 1)]
    every = range(frames)
    valid = [jnp.where(t < length, 1.0, 0.0).astype(jnp.float32) for t in every]
    bias = [jnp.where(u < length, 0.0, -1e30).astype(jnp.float32) for u in every]

    def total(piece):
        return jnp.broadcast_to(jnp.sum(piece, axis=0, keepdims=True), (half, lanes))

    squares = [jnp.zeros((half, lanes), jnp.float32) for _ in every]
    for group in range(feat // GROUP):
        rows = pl.ds(group * GROUP, GROUP)
        for t in every:
            field = load_attended(t, rows).astype(jnp.float32)
            fields[t, rows, :] = field
            ups[t, rows, :] = load_upstream(t, rows).astype(jnp.float32)
            low, high = field[:half], field[half:]
            squares[t] = squares[t] + (low * low + high * high)
    inverse = [lax.rsqrt(total(squares[t]) * (1.0 / feat) + 1e-06) for t in every]

    raw = {pair: jnp.zeros((half, lanes), jnp.float32) for pair in pairs}
    grad = {pair: jnp.zeros((half, lanes), jnp.float32) for pair in pairs}
    for group in range(feat // half):
        rows = pl.ds(group * half, half)
        gain = load_gain(rows)
        here = [fields[t, rows, :] for t in every]
        above = [ups[t, rows, :] for t in every]
        scaled = [here[t] * inverse[t] for t in every]
        gained = [scaled[t] * gain for t in every]
        for t in every:
            normed[t, rows, :] = scaled[t]
        for t, u in pairs:
            raw[t, u] = raw[t, u] + gained[t] * scaled[u]
            grad[t, u] = grad[t, u] + above[t] * here[u]

    value_part, score_part = {}, {}
    for t in every:
        seen = range(t + 1)
        for u in seen:
            raw[t, u] = total(raw[t, u])
            grad[t, u] = total(grad[t, u]) * valid[t]
        scores = [raw[t, u] * score_scale + bias[u] for u in seen]
        largest = functools.reduce(jnp.maximum, scores)
        raised = [jnp.exp(score - largest) for score in scores]
        over = 1.0 / functools.reduce(jnp.add, raised)
        weights = [piece * over for piece in raised]
        mean_grad = functools.reduce(jnp.add, [weights[u] * grad[t, u] for u in seen])
        for u in seen:
            rounded = weights[u].astype(jnp.bfloat16).astype(jnp.float32)
            value_part[t, u] = (rounded + (1.0 if u == t else 0.0)) * valid[t]
            score_part[t, u] = weights[u] * (grad[t, u] - mean_grad) * score_scale

    both = {(t, u): score_part[t, u] * (2.0 if t == u else 1.0) for t, u in pairs}
    both.update({(u, t): both[t, u] for t, u in pairs})
    raw.update({(u, t): raw[t, u] for t, u in pairs})
    mean_part = [
        functools.reduce(jnp.add, [both[u, v] * raw[u, v] for v in every]) * (1.0 / feat)
        for u in every
    ]

    all_mixed = []
    for group in range(feat // GROUP):
        outs = [[] for _ in every]
        for side in range(2):
            rows = pl.ds(group * GROUP + side * half, half)
            gain = load_gain(rows)
            scaled = [normed[t, rows, :] for t in every]
            above = [ups[t, rows, :] for t in every]
            mixed = jnp.zeros((half, lanes), jnp.float32)
            for u in every:
                crossed = functools.reduce(jnp.add, [both[u, v] * scaled[v] for v in every])
                mixed = mixed + crossed * scaled[u]
                from_norm = inverse[u] * (gain * crossed - scaled[u] * mean_part[u])
                direct = functools.reduce(
                    jnp.add, [value_part[t, u] * above[t] for t in range(u, frames)]
                )
                outs[u].append(direct + from_norm)
            all_mixed.append(mixed)
        for u in every:
            grad_ref[u, pl.ds(group * GROUP, GROUP), :] = jnp.concatenate(
                outs[u], axis=0
            ).astype(jnp.bfloat16)
    return jnp.concatenate(all_mixed, axis=0)


def temporal_kernel(frames, spaces, length_ref, task_ref, *refs):
    attended_refs, (gain_ref, own_ref, *other_refs), refs = (
        refs[: frames - 1],
        refs[frames - 1 : frames - 1 + 2 * spaces],
        refs[frames - 1 + 2 * spaces :],
    )
    field_refs, grad_refs, (mixed_ref, *kept_refs, attended, grads, wide, arrived) = (
        refs[:3],
        refs[3 : frames + 3],
        refs[frames + 3 :],
    )
    copies = [
        pltpu.make_async_copy(source, target, arrived.at[index])
        for index, (source, target) in enumerate(zip(field_refs, kept_refs))
    ]
    for copy in copies:
        copy.start()
    heads, lanes = own_ref.shape[1], own_ref.shape[3]
    half = frames // 2
    mixed_ref[...] = jnp.full(mixed_ref.shape, task_ref[0].astype(jnp.float32))

    def load_upstream(space, head, t, rows):
        if space == 0:
            return own_ref[t, head, rows, :]
        return other_refs[2 * space - 2 + t // half][t % half, head, rows, :]

    def step(head, carry):
        places = [
            pl.ds(pl.multiple_of(partner("space", space) * lanes, lanes), lanes)
            for space in range(spaces)
        ]
        for space, here in enumerate(places):
            attended[space, partner("tm", 0)] = own_ref[frames + space, head]
            for distance, ref in enumerate(attended_refs):
                attended[space, partner("tm", distance + 1)] = ref[head, :, here]
        mixed = [
            temporal_part(
                length_ref[0],
                lambda t, rows: attended[space, t, rows, :],
                functools.partial(load_upstream, space, head),
                lambda rows: gain_ref[head, rows, :],
                wide.at[space, 0],
                wide.at[space, 1],
                wide.at[space, 2],
                grads.at[space],
            )
            for space in range(spaces)
        ]
        summed = functools.reduce(jnp.add, mixed)
        mixed_ref[pl.ds(head, 1), :] = jnp.sum(summed.T, axis=0, keepdims=True) * 0.5
        for distance, ref in enumerate(grad_refs):
            frame = partner("tm", distance)
            for space, here in enumerate(places):
                ref[head, :, here] = grads[space, frame]
        return carry

    lax.fori_loop(0, heads, step, 0)
    for copy in copies:
        copy.wait()


def temporal(lengths, task_ids, attended, upstream, gain, fields):
    _, heads, feat, lanes = upstream[0].shape
    frames, spaces = len(attended) + 1, (len(upstream) + 1) // 2
    patches = spaces * lanes
    rows = -(-(heads + 1) // 8) * 8
    operands = [*attended, gain, *upstream]
    results = pl.pallas_call(
        functools.partial(temporal_kernel, frames, spaces),
        in_specs=[pl.BlockSpec(memory_space=pltpu.SMEM)] * 2
        + [pl.BlockSpec(memory_space=pltpu.VMEM)] * len(operands)
        + [pl.BlockSpec(memory_space=pltpu.HBM)] * len(fields),
        out_specs=[pl.BlockSpec(memory_space=pltpu.VMEM)] * (frames + 1 + len(fields)),
        scratch_shapes=[pltpu.VMEM((spaces, frames, feat, lanes), jnp.bfloat16)] * 2
        + [pltpu.VMEM((spaces, 3, frames, feat, lanes), jnp.float32)]
        + [pltpu.SemaphoreType.DMA((len(fields),))],
        out_shape=[jax.ShapeDtypeStruct((heads, feat, patches), jnp.bfloat16)] * frames
        + [jax.ShapeDtypeStruct((rows, feat), jnp.float32)]
        + [jax.ShapeDtypeStruct(field.shape, field.dtype) for field in fields],
        compiler_params=params(patches),
        cost_estimate=cost(4),
        name="temporal",
    )(lengths, task_ids, *operands, *[in_hbm(field) for field in fields])
    return list(results[:frames]), results[frames], results[frames + 1 :]


def gain_gradients(axis, heads, frames, clips, mixed_refs, gains_ref, grad_ref):
    tasks = gains_ref.shape[1]
    rows = sum(ref.shape[0] for ref in mixed_refs) // (frames * clips)
    each = mixed_refs[0].shape[0] // rows
    task_ids = lax.broadcasted_iota(jnp.int32, (tasks, HEAD_DIM), 0).astype(jnp.float32)
    for distance in range(frames):
        for head in range(heads):
            mixed = jnp.zeros((tasks, HEAD_DIM), jnp.float32)
            for clip in range(clips):
                block = distance * clips + clip
                ref, start = mixed_refs[block // each], block % each * rows
                task = ref[pl.ds(start + heads, 1), :]
                row = ref[pl.ds(start + head, 1), :]
                mixed = mixed + jnp.where(task_ids == task, row, 0.0)
            start = (partner(axis, distance) * heads + head) * HEAD_DIM
            cols = pl.ds(pl.multiple_of(start, HEAD_DIM), HEAD_DIM)
            grad_ref[0, :, cols] = gains_ref[1, :, cols] * mixed
            grad_ref[1, :, cols] = gains_ref[0, :, cols] * mixed


def swap(field, axis, size, distance):
    return lax.ppermute(field, axis, [(i, i ^ distance) for i in range(size)])


def split_by_heads(
    query_heads, key_heads, value_heads, cotangent, task_ids, lengths, gains, clips, frames, spaces
):
    patches, feat = query_heads.shape[2:]
    heads = feat // HEAD_DIM
    own = heads // frames
    width = own * HEAD_DIM
    queries, key_rows, values = (
        field.reshape(patches, feat) for field in (query_heads, key_heads, value_heads)
    )
    frame = lax.axis_index("tm")

    pieces = list(pack(cotangent.reshape(cotangent.shape[2:]), frames, spaces))
    queries, pieces = lax.optimization_barrier((queries, pieces))
    for distance in range(1, frames):
        pieces[distance] = swap(pieces[distance], "tm", frames, distance)
    fields = (queries, key_rows, values)
    weights, attended = forward("tm", *fields, frames)
    for distance in range(1, frames):
        attended[distance] = swap(attended[distance], "tm", frames, distance)
    backwards, _ = lax.optimization_barrier((pieces[::-1], weights))
    upstream = list(turn(backwards[::-1], attended[0]))
    for index in range(1, len(upstream)):
        upstream[index] = swap(upstream[index], "space", spaces, (index + 1) // 2)
    rows = lax.dynamic_index_in_dim(gains, task_ids[0], 1, keepdims=False)
    product = lax.dynamic_slice_in_dim(rows[0] * rows[1], frame * width, width, 0)
    gain = jnp.broadcast_to(
        product.reshape(own, HEAD_DIM, 1), (own, HEAD_DIM, patches // spaces)
    )
    grads, mixed, kept = temporal(
        lengths, task_ids, attended[1:], upstream, gain, fields
    )
    for distance in reversed(range(1, frames)):
        grads[distance] = swap(grads[distance], "tm", frames, distance)
    here = grads[0]
    for bit in range(clips.bit_length() - 1):
        other = swap(mixed, "dp", clips, 1 << bit)
        if bit == 0:
            here, other = lax.optimization_barrier((here, other))
        mixed = jnp.concatenate([mixed, other], axis=0)
    results = backward("tm", kept, weights, [here], [0])
    mixed, results = lax.optimization_barrier((mixed, results))
    near, grads[1] = lax.optimization_barrier((mixed, grads[1]))
    mixed = [mixed, swap(near, "tm", frames, 1)] + [
        swap(mixed, "tm", frames, distance) for distance in range(2, frames)
    ]
    grad_queries, grad_keys, grad_gains = backward(
        "tm",
        kept,
        weights,
        grads[:0:-1],
        list(range(frames - 1, 0, -1)),
        results,
        mixed,
        gains,
        (own, frames, clips),
    )
    return (
        grad_queries.reshape(query_heads.shape),
        grad_keys.reshape(query_heads.shape),
        grad_gains,
    )


def temporal_grads(attended, upstream, gain_query, gain_keys, length):
    highest = lax.Precision.HIGHEST
    frames = attended.shape[0]
    score_scale = attended.shape[-1] ** (-0.5)
    floats = attended.astype(jnp.float32)
    inverse_rms = lax.rsqrt(jnp.mean(floats * floats, axis=-1, keepdims=True) + 1e-06)
    normed = floats * inverse_rms
    t_query = normed * gain_query
    t_keys = normed * gain_keys
    scores = jnp.einsum("txhd,uxhd->xhtu", t_query, t_keys, precision=highest) * score_scale
    frame_ids = jnp.arange(frames, dtype=jnp.int32)
    allowed = (frame_ids[None, :] <= frame_ids[:, None]) & (frame_ids[None, :] < length)
    scores = jnp.where(allowed, scores, -1e30)
    weights = jax.nn.softmax(scores, axis=-1)
    weights_low = lax.optimization_barrier(weights.astype(jnp.bfloat16)).astype(jnp.float32)
    valid_rows = (frame_ids < length).astype(jnp.float32)
    masked = upstream.astype(jnp.float32) * valid_rows[:, None, None, None]
    grad_weights = jnp.einsum("txhd,uxhd->xhtu", masked, floats, precision=highest)
    from_values = jnp.einsum("xhtu,txhd->uxhd", weights_low, masked, precision=highest)
    grad_scores = (
        weights
        * (grad_weights - jnp.sum(grad_weights * weights, axis=-1, keepdims=True))
        * score_scale
    )
    grad_tquery = jnp.einsum("xhtu,uxhd->txhd", grad_scores, t_keys, precision=highest)
    grad_tkeys = jnp.einsum("xhtu,txhd->uxhd", grad_scores, t_query, precision=highest)
    grad_normed = grad_tquery * gain_query + grad_tkeys * gain_keys
    grad_gain_query = jnp.sum(grad_tquery * normed, axis=(0, 1))
    grad_gain_keys = jnp.sum(grad_tkeys * normed, axis=(0, 1))
    from_norm = inverse_rms * (
        grad_normed - normed * jnp.mean(grad_normed * normed, axis=-1, keepdims=True)
    )
    grad_total = (masked + from_values + from_norm).astype(jnp.bfloat16)
    return (grad_total, grad_gain_query, grad_gain_keys)


def split_by_patches(query_heads, key_heads, value_heads, cotangent, task_ids, lengths, gains):
    patches, feat = query_heads.shape[2:]
    heads = feat // HEAD_DIM
    queries, key_rows, values = (
        field.reshape(patches, feat) for field in (query_heads, key_heads, value_heads)
    )
    fields = (queries, key_rows, values)
    weights, attended = forward(None, *fields, 1)
    attended_field = jnp.transpose(attended[0], (2, 0, 1)).reshape(1, 1, patches, feat)
    upstream = lax.all_to_all(
        lax.all_to_all(cotangent, "space", split_axis=3, concat_axis=2, tiled=True),
        "tm",
        split_axis=2,
        concat_axis=1,
        tiled=True,
    )
    frames_attended = lax.all_to_all(attended_field, "tm", split_axis=2, concat_axis=1, tiled=True)
    frames, local_patches = frames_attended.shape[1:3]
    selector = (task_ids[0] == jnp.arange(gains.shape[1], dtype=jnp.int32)).astype(jnp.float32)
    gain_query = jnp.sum(selector[:, None] * gains[0], axis=0).reshape(heads, HEAD_DIM)
    gain_keys = jnp.sum(selector[:, None] * gains[1], axis=0).reshape(heads, HEAD_DIM)
    grad_total, grad_gq, grad_gk = temporal_grads(
        frames_attended.reshape(frames, local_patches, heads, HEAD_DIM),
        upstream.reshape(frames, local_patches, heads, HEAD_DIM),
        gain_query,
        gain_keys,
        lengths[0],
    )
    gain_terms = jnp.stack(
        [
            selector[:, None] * grad_gq.reshape(1, feat),
            selector[:, None] * grad_gk.reshape(1, feat),
        ]
    )
    grad_gains = lax.psum(gain_terms, ("dp", "tm"))
    returned = lax.all_to_all(
        grad_total.reshape(1, frames, local_patches, feat),
        "tm",
        split_axis=1,
        concat_axis=2,
        tiled=True,
    )
    head_grads = jnp.transpose(returned.reshape(patches, heads, HEAD_DIM), (1, 2, 0))
    grad_queries, grad_keys = backward(None, fields, weights, [head_grads], [0])
    return (
        grad_queries.reshape(query_heads.shape),
        grad_keys.reshape(query_heads.shape),
        grad_gains,
    )


def solution(mesh):
    clips, frames, spaces = (mesh.shape[axis] for axis in ("dp", "tm", "space"))

    def local(query_heads, *others):
        heads = query_heads.shape[3] // HEAD_DIM
        powers = all(size & (size - 1) == 0 for size in (clips, frames, spaces))
        if powers and 2 <= frames <= 4 and heads % frames == 0:
            return split_by_heads(query_heads, *others, clips, frames, spaces)
        return split_by_patches(query_heads, *others)

    return jax.shard_map(
        local,
        mesh=mesh,
        in_specs=(
            P("dp", "tm", None, "space"),
            P("dp", "tm", None, "space"),
            P("dp", "tm", None, "space"),
            P("dp", "tm", "space", None),
            P("dp"),
            P("dp"),
            P(None, None, "space"),
        ),
        out_specs=(
            P("dp", "tm", None, "space"),
            P("dp", "tm", None, "space"),
            P(None, None, "space"),
        ),
        check_vma=False,
    )
```

```python
import functools

import jax
import jax.numpy as jnp
from jax import lax
from jax.experimental import pallas as pl
from jax.experimental.pallas import tpu as pltpu
from jax.sharding import PartitionSpec as P

HEAD_DIM = 128
GROUP = 16
MIB = 1024 * 1024


def params(patches):
    return pltpu.CompilerParams(vmem_limit_bytes=(16 if patches <= 512 else 60) * MIB)


def cost(microseconds):
    return pl.CostEstimate(flops=int(microseconds * 1e8), bytes_accessed=0, transcendentals=0)


def in_hbm(field):
    return pltpu.with_memory_space_constraint(field, pltpu.HBM)


def columns_dot(left, right):
    return lax.dot_general(
        left, right, (((1,), (1,)), ((), ())), preferred_element_type=jnp.float32
    )


def dot(left, right):
    return jnp.dot(left, right, preferred_element_type=jnp.float32)


def partner(axis, distance):
    return distance if axis is None else jnp.bitwise_xor(lax.axis_index(axis), distance)


def forward_kernel(axis, query_ref, key_ref, value_ref, weights_ref, *refs):
    (queries, key_rows, values, arrived), attended_refs = refs[-4:], refs[:-4]
    score_scale = HEAD_DIM ** (-0.5)
    groups, _, width = queries.shape
    own = width // HEAD_DIM
    copies = []
    for group in range(groups):
        cols = pl.ds(pl.multiple_of(partner(axis, group) * width, HEAD_DIM), width)
        for field, (source, target) in enumerate(
            ((query_ref, queries), (key_ref, key_rows), (value_ref, values))
        ):
            copy = pltpu.make_async_copy(
                source.at[:, cols], target.at[group], arrived.at[group, field]
            )
            copy.start()
            copies.append(copy)
    for group in range(groups):
        for copy in copies[3 * group : 3 * group + 3]:
            copy.wait()
        for head in range(own):
            cols = pl.ds(head * HEAD_DIM, HEAD_DIM)
            scores = columns_dot(key_rows[group, :, cols], queries[group, :, cols])
            largest = jnp.max(scores, axis=0, keepdims=True)
            raised = jnp.exp((scores - largest) * score_scale)
            weights = raised * (1.0 / jnp.sum(raised, axis=0, keepdims=True))
            weights_ref[group * own + head] = weights
            attended = dot(values[group, :, cols].T, weights.astype(jnp.bfloat16))
            attended_refs[group][head] = attended.astype(jnp.bfloat16)


def forward(axis, queries, key_rows, values, groups):
    patches, feat = queries.shape
    heads = feat // HEAD_DIM
    own = heads // groups
    fields = [in_hbm(field) for field in (queries, key_rows, values)]
    weights, *attended = pl.pallas_call(
        functools.partial(forward_kernel, axis),
        in_specs=[pl.BlockSpec(memory_space=pltpu.HBM)] * 3,
        out_specs=[pl.BlockSpec(memory_space=pltpu.VMEM)] * (1 + groups),
        scratch_shapes=[pltpu.VMEM((groups, patches, feat // groups), jnp.bfloat16)] * 3
        + [pltpu.SemaphoreType.DMA((groups, 3))],
        out_shape=[jax.ShapeDtypeStruct((heads, patches, patches), jnp.float32)]
        + [jax.ShapeDtypeStruct((own, HEAD_DIM, patches), jnp.bfloat16)] * groups,
        compiler_params=params(patches),
        cost_estimate=cost(6),
        name="spatial_forward",
    )(*fields)
    return weights, attended


def backward_group(axis, fields, weights_ref, grad_ref, distance, scratch, results, sent):
    query_ref, key_ref, value_ref = fields
    score_scale = HEAD_DIM ** (-0.5)
    own = grad_ref.shape[0]
    start = partner(axis, distance) * (own * HEAD_DIM)
    columns = [
        pl.ds(pl.multiple_of(start + head * HEAD_DIM, HEAD_DIM), HEAD_DIM) for head in range(own)
    ]
    spatial_grads = [dot(value_ref[:, columns[head]], grad_ref[head]) for head in range(own)]
    all_scores = []
    for head, spatial_grad in enumerate(spatial_grads):
        weights = weights_ref[distance * own + head]
        row_sum = jnp.sum(spatial_grad * weights, axis=0, keepdims=True)
        scores = weights * (spatial_grad - row_sum) * score_scale
        all_scores.append(scores.astype(jnp.bfloat16))
    gq, gk = scratch
    for head, scores in enumerate(all_scores):
        cols = pl.ds(head * HEAD_DIM, HEAD_DIM)
        gk[:, cols] = dot(scores, query_ref[:, columns[head]]).astype(jnp.bfloat16)
        gq[:, cols] = dot(key_ref[:, columns[head]].T, scores).astype(jnp.bfloat16).T
    there = pl.ds(pl.multiple_of(start, HEAD_DIM), own * HEAD_DIM)
    copies = [
        pltpu.make_async_copy(source, target.at[:, there], sent.at[side])
        for side, (source, target) in enumerate(zip(scratch, results))
    ]
    for copy in copies:
        copy.start()
    return copies


def backward_kernel(axis, distances, gains_of, *refs):
    fields, weights_ref, refs = refs[:3], refs[3], refs[4:]
    grad_refs, refs = refs[: len(distances)], refs[len(distances) :]
    *refs, gq, gk, sent = refs
    copies = []
    if gains_of:
        *mixed_refs, gains_ref, _, _, gq_ref, gk_ref, grad_gains_ref, grad_gains = refs
        gain_gradients(axis, *gains_of, mixed_refs, gains_ref, grad_gains)
        copy = pltpu.make_async_copy(grad_gains, grad_gains_ref, sent.at[len(distances), 0])
        copy.start()
        copies.append(copy)
    else:
        gq_ref, gk_ref = refs[-2:]
    for place, (distance, grad_ref) in enumerate(zip(distances, grad_refs)):
        copies += backward_group(
            axis,
            fields,
            weights_ref,
            grad_ref,
            distance,
            (gq.at[place], gk.at[place]),
            (gq_ref, gk_ref),
            sent.at[place],
        )
    for copy in copies:
        copy.wait()


def backward(axis, fields, weights, grads, distances, earlier=(), mixed=(), gains=None, gains_of=()):
    patches, feat = fields[0].shape
    own = grads[0].shape[0]
    operands = [*fields, weights, *grads] + ([*mixed, gains] if gains_of else [])
    block = pltpu.VMEM((len(distances), patches, own * HEAD_DIM), jnp.bfloat16)
    out_shape = [jax.ShapeDtypeStruct((patches, feat), jnp.bfloat16)] * 2
    scratch = [block, block, pltpu.SemaphoreType.DMA((len(distances) + 1, 2))]
    if gains_of:
        out_shape.append(jax.ShapeDtypeStruct(gains.shape, jnp.float32))
        scratch.insert(0, pltpu.VMEM(gains.shape, jnp.float32))
    return pl.pallas_call(
        functools.partial(backward_kernel, axis, distances, gains_of),
        in_specs=[pl.BlockSpec(memory_space=pltpu.VMEM)] * len(operands)
        + [pl.BlockSpec(memory_space=pl.ANY)] * len(earlier),
        out_specs=[pl.BlockSpec(memory_space=pl.ANY)] * len(out_shape),
        scratch_shapes=scratch,
        out_shape=out_shape,
        input_output_aliases={len(operands) + index: index for index in range(len(earlier))},
        compiler_params=params(patches),
        cost_estimate=cost(2),
        name="spatial_backward",
    )(*operands, *earlier)


def pack_kernel(field_ref, *refs):
    *packed_refs, rows, arrived = refs
    chunks, size, _ = rows.shape
    spaces, _, width = packed_refs[0].shape
    copies = [
        pltpu.make_async_copy(
            field_ref.at[pl.ds(chunk * size, size), :], rows.at[chunk], arrived.at[chunk]
        )
        for chunk in range(chunks)
    ]
    for copy in copies:
        copy.start()
    for chunk, copy in enumerate(copies):
        copy.wait()
        for distance, packed_ref in enumerate(packed_refs):
            for space in range(spaces):
                start = (space * len(packed_refs) + partner("tm", distance)) * width
                cols = pl.ds(pl.multiple_of(start, HEAD_DIM), width)
                packed_ref[space, pl.ds(chunk * size, size), :] = rows[chunk, :, cols]


def pack(field, frames, spaces):
    patches, feat = field.shape
    chunks = patches // GROUP
    shape = (spaces, patches, feat // (frames * spaces))
    return pl.pallas_call(
        pack_kernel,
        in_specs=[pl.BlockSpec(memory_space=pltpu.HBM)],
        out_specs=[pl.BlockSpec(memory_space=pltpu.VMEM)] * frames,
        out_shape=[jax.ShapeDtypeStruct(shape, field.dtype)] * frames,
        scratch_shapes=[
            pltpu.VMEM((chunks, patches // chunks, feat), field.dtype),
            pltpu.SemaphoreType.DMA((chunks,)),
        ],
        compiler_params=params(patches),
        cost_estimate=cost(1),
        name="pack_cotangent",
    )(in_hbm(field))


def turn_kernel(frames, *refs):
    piece_refs, (plane_ref, own_hbm, *other_refs), (turned, own_ref, sent) = (
        refs[:frames][::-1],
        refs[frames:-3],
        refs[-3:],
    )
    spaces, lanes, _ = piece_refs[0].shape
    for space in range(spaces):
        place = pl.multiple_of(partner("space", space) * lanes, lanes)
        own_ref[frames + space] = plane_ref[:, :, pl.ds(place, lanes)]
    heads = own_ref.shape[1]
    for space in range(spaces):
        target = turned if space else own_ref
        source = partner("space", space)
        for distance, ref in enumerate(piece_refs):
            frame = partner("tm", distance)
            for head in range(heads):
                cols = pl.ds(head * HEAD_DIM, HEAD_DIM)
                target[frame, head] = ref[source, :, cols].T
        if space == 0:
            copy = pltpu.make_async_copy(own_ref, own_hbm, sent)
            copy.start()
        else:
            half = frames // 2
            other_refs[2 * space - 2][...] = turned[:half]
            other_refs[2 * space - 1][...] = turned[half:]
    copy.wait()


def turn(pieces, plane):
    spaces, patches, feat = pieces[0].shape
    frames, heads = len(pieces), feat // HEAD_DIM
    turned = (heads, HEAD_DIM, patches)
    sizes = [frames + spaces] + [frames // 2, frames - frames // 2] * (spaces - 1)
    return pl.pallas_call(
        functools.partial(turn_kernel, frames),
        in_specs=[pl.BlockSpec(memory_space=pltpu.VMEM)] * (frames + 1),
        out_specs=[pl.BlockSpec(memory_space=pltpu.HBM)]
        + [pl.BlockSpec(memory_space=pltpu.VMEM)] * (len(sizes) - 1),
        out_shape=[jax.ShapeDtypeStruct((size,) + turned, pieces[0].dtype) for size in sizes],
        scratch_shapes=[
            pltpu.VMEM((frames,) + turned, pieces[0].dtype),
            pltpu.VMEM((frames + spaces,) + turned, pieces[0].dtype),
            pltpu.SemaphoreType.DMA,
        ],
        compiler_params=params(patches),
        cost_estimate=cost(2),
        name="turn_cotangent",
    )(*reversed(pieces), plane)


def temporal_part(length, load_attended, load_upstream, load_gain, fields, ups, normed, grad_ref):
    frames, feat, lanes = grad_ref.shape
    half = GROUP // 2
    score_scale = feat ** (-0.5)
    pairs = [(t, u) for t in range(frames) for u in range(t + 1)]
    every = range(frames)
    valid = [jnp.where(t < length, 1.0, 0.0).astype(jnp.float32) for t in every]
    bias = [jnp.where(u < length, 0.0, -1e30).astype(jnp.float32) for u in every]

    def total(piece):
        return jnp.broadcast_to(jnp.sum(piece, axis=0, keepdims=True), (half, lanes))

    squares = [jnp.zeros((half, lanes), jnp.float32) for _ in every]
    for group in range(feat // GROUP):
        rows = pl.ds(group * GROUP, GROUP)
        for t in every:
            field = load_attended(t, rows).astype(jnp.float32)
            fields[t, rows, :] = field
            ups[t, rows, :] = load_upstream(t, rows).astype(jnp.float32)
            low, high = field[:half], field[half:]
            squares[t] = squares[t] + (low * low + high * high)
    inverse = [lax.rsqrt(total(squares[t]) * (1.0 / feat) + 1e-06) for t in every]

    raw = {pair: jnp.zeros((half, lanes), jnp.float32) for pair in pairs}
    grad = {pair: jnp.zeros((half, lanes), jnp.float32) for pair in pairs}
    for group in range(feat // half):
        rows = pl.ds(group * half, half)
        gain = load_gain(rows)
        here = [fields[t, rows, :] for t in every]
        above = [ups[t, rows, :] for t in every]
        scaled = [here[t] * inverse[t] for t in every]
        gained = [scaled[t] * gain for t in every]
        for t in every:
            normed[t, rows, :] = scaled[t]
        for t, u in pairs:
            raw[t, u] = raw[t, u] + gained[t] * scaled[u]
            grad[t, u] = grad[t, u] + above[t] * here[u]

    value_part, score_part = {}, {}
    for t in every:
        seen = range(t + 1)
        for u in seen:
            raw[t, u] = total(raw[t, u])
            grad[t, u] = total(grad[t, u]) * valid[t]
        scores = [raw[t, u] * score_scale + bias[u] for u in seen]
        largest = functools.reduce(jnp.maximum, scores)
        raised = [jnp.exp(score - largest) for score in scores]
        over = 1.0 / functools.reduce(jnp.add, raised)
        weights = [piece * over for piece in raised]
        mean_grad = functools.reduce(jnp.add, [weights[u] * grad[t, u] for u in seen])
        for u in seen:
            rounded = weights[u].astype(jnp.bfloat16).astype(jnp.float32)
            value_part[t, u] = (rounded + (1.0 if u == t else 0.0)) * valid[t]
            score_part[t, u] = weights[u] * (grad[t, u] - mean_grad) * score_scale

    both = {(t, u): score_part[t, u] * (2.0 if t == u else 1.0) for t, u in pairs}
    both.update({(u, t): both[t, u] for t, u in pairs})
    raw.update({(u, t): raw[t, u] for t, u in pairs})
    mean_part = [
        functools.reduce(jnp.add, [both[u, v] * raw[u, v] for v in every]) * (1.0 / feat)
        for u in every
    ]

    all_mixed = []
    for group in range(feat // GROUP):
        outs = [[] for _ in every]
        for side in range(2):
            rows = pl.ds(group * GROUP + side * half, half)
            gain = load_gain(rows)
            scaled = [normed[t, rows, :] for t in every]
            above = [ups[t, rows, :] for t in every]
            mixed = jnp.zeros((half, lanes), jnp.float32)
            for u in every:
                crossed = functools.reduce(jnp.add, [both[u, v] * scaled[v] for v in every])
                mixed = mixed + crossed * scaled[u]
                from_norm = inverse[u] * (gain * crossed - scaled[u] * mean_part[u])
                direct = functools.reduce(
                    jnp.add, [value_part[t, u] * above[t] for t in range(u, frames)]
                )
                outs[u].append(direct + from_norm)
            all_mixed.append(mixed)
        for u in every:
            grad_ref[u, pl.ds(group * GROUP, GROUP), :] = jnp.concatenate(
                outs[u], axis=0
            ).astype(jnp.bfloat16)
    return jnp.concatenate(all_mixed, axis=0)


def temporal_kernel(frames, spaces, length_ref, task_ref, *refs):
    attended_refs, (gain_ref, *other_refs), refs = (
        refs[: frames - 1],
        refs[frames - 1 : frames - 2 + 2 * spaces],
        refs[frames - 2 + 2 * spaces :],
    )
    (own_hbm, *field_refs), grad_refs, refs = refs[:4], refs[4 : frames + 4], refs[frames + 4 :]
    mixed_ref, *kept_refs, attended, grads, wide, own_ref, arrived = refs
    heads, lanes = own_ref.shape[1], own_ref.shape[3]
    copies = [
        pltpu.make_async_copy(own_hbm.at[:, head], own_ref.at[:, head], arrived.at[head])
        for head in range(heads)
    ] + [
        pltpu.make_async_copy(source, target, arrived.at[heads + index])
        for index, (source, target) in enumerate(zip(field_refs, kept_refs))
    ]
    for copy in copies:
        copy.start()
    half = frames // 2
    mixed_ref[...] = jnp.full(mixed_ref.shape, task_ref[0].astype(jnp.float32))

    def load_upstream(space, head, t, rows):
        if space == 0:
            return own_ref[t, head, rows, :]
        return other_refs[2 * space - 2 + t // half][t % half, head, rows, :]

    places = [
        pl.ds(pl.multiple_of(partner("space", space) * lanes, lanes), lanes)
        for space in range(spaces)
    ]
    for head in range(heads):
        copies[head].wait()
        for space, here in enumerate(places):
            attended[head, space, partner("tm", 0)] = own_ref[frames + space, head]
            for distance, ref in enumerate(attended_refs):
                attended[head, space, partner("tm", distance + 1)] = ref[head, :, here]
        mixed = [
            temporal_part(
                length_ref[0],
                lambda t, rows: attended[head, space, t, rows, :],
                functools.partial(load_upstream, space, head),
                lambda rows: gain_ref[head, rows, :],
                wide.at[head % 2, space, 0],
                wide.at[head % 2, space, 1],
                wide.at[head % 2, space, 2],
                grads.at[head, space],
            )
            for space in range(spaces)
        ]
        summed = functools.reduce(jnp.add, mixed)
        mixed_ref[pl.ds(head, 1), :] = jnp.sum(summed.T, axis=0, keepdims=True) * 0.5
        for distance, ref in enumerate(grad_refs):
            frame = partner("tm", distance)
            for space, here in enumerate(places):
                ref[head, :, here] = grads[head, space, frame]
    for copy in copies[heads:]:
        copy.wait()


def temporal(lengths, task_ids, attended, upstream, gain, fields):
    _, heads, feat, lanes = upstream[0].shape
    frames, spaces = len(attended) + 1, (len(upstream) + 1) // 2
    patches = spaces * lanes
    rows = -(-(heads + 1) // 8) * 8
    operands = [*attended, gain, *upstream[1:]]
    in_place = [in_hbm(field) for field in (upstream[0], *fields)]
    block = (heads, spaces, frames, feat, lanes)
    results = pl.pallas_call(
        functools.partial(temporal_kernel, frames, spaces),
        in_specs=[pl.BlockSpec(memory_space=pltpu.SMEM)] * 2
        + [pl.BlockSpec(memory_space=pltpu.VMEM)] * len(operands)
        + [pl.BlockSpec(memory_space=pltpu.HBM)] * len(in_place),
        out_specs=[pl.BlockSpec(memory_space=pltpu.VMEM)] * (frames + 1 + len(fields)),
        scratch_shapes=[
            pltpu.VMEM(block, jnp.bfloat16),
            pltpu.VMEM(block, jnp.bfloat16),
            pltpu.VMEM((2, spaces, 3, frames, feat, lanes), jnp.float32),
            pltpu.VMEM(upstream[0].shape, upstream[0].dtype),
            pltpu.SemaphoreType.DMA((heads + len(fields),)),
        ],
        out_shape=[jax.ShapeDtypeStruct((heads, feat, patches), jnp.bfloat16)] * frames
        + [jax.ShapeDtypeStruct((rows, feat), jnp.float32)]
        + [jax.ShapeDtypeStruct(field.shape, field.dtype) for field in fields],
        compiler_params=params(patches),
        cost_estimate=cost(4),
        name="temporal",
    )(lengths, task_ids, *operands, *in_place)
    return list(results[:frames]), results[frames], results[frames + 1 :]


def gain_gradients(axis, heads, frames, clips, mixed_refs, gains_ref, grad_ref):
    tasks = gains_ref.shape[1]
    rows = sum(ref.shape[0] for ref in mixed_refs) // (frames * clips)
    each = mixed_refs[0].shape[0] // rows
    task_ids = lax.broadcasted_iota(jnp.int32, (tasks, HEAD_DIM), 0).astype(jnp.float32)
    for distance in range(frames):
        for head in range(heads):
            mixed = jnp.zeros((tasks, HEAD_DIM), jnp.float32)
            for clip in range(clips):
                block = distance * clips + clip
                ref, start = mixed_refs[block // each], block % each * rows
                task = ref[pl.ds(start + heads, 1), :]
                row = ref[pl.ds(start + head, 1), :]
                mixed = mixed + jnp.where(task_ids == task, row, 0.0)
            start = (partner(axis, distance) * heads + head) * HEAD_DIM
            cols = pl.ds(pl.multiple_of(start, HEAD_DIM), HEAD_DIM)
            grad_ref[0, :, cols] = gains_ref[1, :, cols] * mixed
            grad_ref[1, :, cols] = gains_ref[0, :, cols] * mixed


def swap(field, axis, size, distance):
    return lax.ppermute(field, axis, [(i, i ^ distance) for i in range(size)])


def split_by_heads(
    query_heads, key_heads, value_heads, cotangent, task_ids, lengths, gains, clips, frames, spaces
):
    patches, feat = query_heads.shape[2:]
    heads = feat // HEAD_DIM
    own = heads // frames
    width = own * HEAD_DIM
    queries, key_rows, values = (
        field.reshape(patches, feat) for field in (query_heads, key_heads, value_heads)
    )
    frame = lax.axis_index("tm")

    pieces = list(pack(cotangent.reshape(cotangent.shape[2:]), frames, spaces))
    queries, pieces = lax.optimization_barrier((queries, pieces))
    for distance in range(1, frames):
        pieces[distance] = swap(pieces[distance], "tm", frames, distance)
    fields = (queries, key_rows, values)
    weights, attended = forward("tm", *fields, frames)
    for distance in range(1, frames):
        attended[distance] = swap(attended[distance], "tm", frames, distance)
    backwards, _ = lax.optimization_barrier((pieces[::-1], weights))
    upstream = list(turn(backwards[::-1], attended[0]))
    for index in range(1, len(upstream)):
        upstream[index] = swap(upstream[index], "space", spaces, (index + 1) // 2)
    rows = lax.dynamic_index_in_dim(gains, task_ids[0], 1, keepdims=False)
    product = lax.dynamic_slice_in_dim(rows[0] * rows[1], frame * width, width, 0)
    gain = jnp.broadcast_to(
        product.reshape(own, HEAD_DIM, 1), (own, HEAD_DIM, patches // spaces)
    )
    grads, mixed, kept = temporal(
        lengths, task_ids, attended[1:], upstream, gain, fields
    )
    for distance in reversed(range(1, frames)):
        grads[distance] = swap(grads[distance], "tm", frames, distance)
    here = grads[0]
    for bit in range(clips.bit_length() - 1):
        other = swap(mixed, "dp", clips, 1 << bit)
        if bit == 0:
            here, other = lax.optimization_barrier((here, other))
        mixed = jnp.concatenate([mixed, other], axis=0)
    results = backward("tm", kept, weights, [here], [0])
    mixed, results = lax.optimization_barrier((mixed, results))
    near, grads[1] = lax.optimization_barrier((mixed, grads[1]))
    mixed = [mixed, swap(near, "tm", frames, 1)] + [
        swap(mixed, "tm", frames, distance) for distance in range(2, frames)
    ]
    last = range(frames - 1, 0, -1)
    if frames > 2:
        results = backward("tm", kept, weights, [grads[1]], [1], results)
        last = range(frames - 1, 1, -1)
    grad_queries, grad_keys, grad_gains = backward(
        "tm",
        kept,
        weights,
        [grads[distance] for distance in last],
        list(last),
        results,
        mixed,
        gains,
        (own, frames, clips),
    )
    return (
        grad_queries.reshape(query_heads.shape),
        grad_keys.reshape(query_heads.shape),
        grad_gains,
    )


def temporal_grads(attended, upstream, gain_query, gain_keys, length):
    highest = lax.Precision.HIGHEST
    frames = attended.shape[0]
    score_scale = attended.shape[-1] ** (-0.5)
    floats = attended.astype(jnp.float32)
    inverse_rms = lax.rsqrt(jnp.mean(floats * floats, axis=-1, keepdims=True) + 1e-06)
    normed = floats * inverse_rms
    t_query = normed * gain_query
    t_keys = normed * gain_keys
    scores = jnp.einsum("txhd,uxhd->xhtu", t_query, t_keys, precision=highest) * score_scale
    frame_ids = jnp.arange(frames, dtype=jnp.int32)
    allowed = (frame_ids[None, :] <= frame_ids[:, None]) & (frame_ids[None, :] < length)
    scores = jnp.where(allowed, scores, -1e30)
    weights = jax.nn.softmax(scores, axis=-1)
    weights_low = lax.optimization_barrier(weights.astype(jnp.bfloat16)).astype(jnp.float32)
    valid_rows = (frame_ids < length).astype(jnp.float32)
    masked = upstream.astype(jnp.float32) * valid_rows[:, None, None, None]
    grad_weights = jnp.einsum("txhd,uxhd->xhtu", masked, floats, precision=highest)
    from_values = jnp.einsum("xhtu,txhd->uxhd", weights_low, masked, precision=highest)
    grad_scores = (
        weights
        * (grad_weights - jnp.sum(grad_weights * weights, axis=-1, keepdims=True))
        * score_scale
    )
    grad_tquery = jnp.einsum("xhtu,uxhd->txhd", grad_scores, t_keys, precision=highest)
    grad_tkeys = jnp.einsum("xhtu,txhd->uxhd", grad_scores, t_query, precision=highest)
    grad_normed = grad_tquery * gain_query + grad_tkeys * gain_keys
    grad_gain_query = jnp.sum(grad_tquery * normed, axis=(0, 1))
    grad_gain_keys = jnp.sum(grad_tkeys * normed, axis=(0, 1))
    from_norm = inverse_rms * (
        grad_normed - normed * jnp.mean(grad_normed * normed, axis=-1, keepdims=True)
    )
    grad_total = (masked + from_values + from_norm).astype(jnp.bfloat16)
    return (grad_total, grad_gain_query, grad_gain_keys)


def split_by_patches(query_heads, key_heads, value_heads, cotangent, task_ids, lengths, gains):
    patches, feat = query_heads.shape[2:]
    heads = feat // HEAD_DIM
    queries, key_rows, values = (
        field.reshape(patches, feat) for field in (query_heads, key_heads, value_heads)
    )
    fields = (queries, key_rows, values)
    weights, attended = forward(None, *fields, 1)
    attended_field = jnp.transpose(attended[0], (2, 0, 1)).reshape(1, 1, patches, feat)
    upstream = lax.all_to_all(
        lax.all_to_all(cotangent, "space", split_axis=3, concat_axis=2, tiled=True),
        "tm",
        split_axis=2,
        concat_axis=1,
        tiled=True,
    )
    frames_attended = lax.all_to_all(attended_field, "tm", split_axis=2, concat_axis=1, tiled=True)
    frames, local_patches = frames_attended.shape[1:3]
    selector = (task_ids[0] == jnp.arange(gains.shape[1], dtype=jnp.int32)).astype(jnp.float32)
    gain_query = jnp.sum(selector[:, None] * gains[0], axis=0).reshape(heads, HEAD_DIM)
    gain_keys = jnp.sum(selector[:, None] * gains[1], axis=0).reshape(heads, HEAD_DIM)
    grad_total, grad_gq, grad_gk = temporal_grads(
        frames_attended.reshape(frames, local_patches, heads, HEAD_DIM),
        upstream.reshape(frames, local_patches, heads, HEAD_DIM),
        gain_query,
        gain_keys,
        lengths[0],
    )
    gain_terms = jnp.stack(
        [
            selector[:, None] * grad_gq.reshape(1, feat),
            selector[:, None] * grad_gk.reshape(1, feat),
        ]
    )
    grad_gains = lax.psum(gain_terms, ("dp", "tm"))
    returned = lax.all_to_all(
        grad_total.reshape(1, frames, local_patches, feat),
        "tm",
        split_axis=1,
        concat_axis=2,
        tiled=True,
    )
    head_grads = jnp.transpose(returned.reshape(patches, heads, HEAD_DIM), (1, 2, 0))
    grad_queries, grad_keys = backward(None, fields, weights, [head_grads], [0])
    return (
        grad_queries.reshape(query_heads.shape),
        grad_keys.reshape(query_heads.shape),
        grad_gains,
    )


def solution(mesh):
    clips, frames, spaces = (mesh.shape[axis] for axis in ("dp", "tm", "space"))

    def local(query_heads, *others):
        heads = query_heads.shape[3] // HEAD_DIM
        powers = all(size & (size - 1) == 0 for size in (clips, frames, spaces))
        if powers and 2 <= frames <= 4 and heads % frames == 0:
            return split_by_heads(query_heads, *others, clips, frames, spaces)
        return split_by_patches(query_heads, *others)

    return jax.shard_map(
        local,
        mesh=mesh,
        in_specs=(
            P("dp", "tm", None, "space"),
            P("dp", "tm", None, "space"),
            P("dp", "tm", None, "space"),
            P("dp", "tm", "space", None),
            P("dp"),
            P("dp"),
            P(None, None, "space"),
        ),
        out_specs=(
            P("dp", "tm", None, "space"),
            P("dp", "tm", None, "space"),
            P(None, None, "space"),
        ),
        check_vma=False,
    )
```

```python
import functools

import jax
import jax.numpy as jnp
from jax import lax
from jax.experimental import pallas as pl
from jax.experimental.pallas import tpu as pltpu
from jax.sharding import PartitionSpec as P

HEAD_DIM = 128
GROUP = 16
MIB = 1024 * 1024


def params(patches):
    return pltpu.CompilerParams(vmem_limit_bytes=(16 if patches <= 512 else 60) * MIB)


def cost(microseconds):
    return pl.CostEstimate(flops=int(microseconds * 1e8), bytes_accessed=0, transcendentals=0)


def in_hbm(field):
    return pltpu.with_memory_space_constraint(field, pltpu.HBM)


def columns_dot(left, right):
    return lax.dot_general(
        left, right, (((1,), (1,)), ((), ())), preferred_element_type=jnp.float32
    )


def dot(left, right):
    return jnp.dot(left, right, preferred_element_type=jnp.float32)


def partner(axis, distance):
    return distance if axis is None else jnp.bitwise_xor(lax.axis_index(axis), distance)


def forward_kernel(axis, chunks, query_ref, key_ref, value_ref, weights_ref, *refs):
    (queries, key_rows, values, arrived), attended_refs = refs[-4:], refs[:-4]
    score_scale = HEAD_DIM ** (-0.5)
    groups, _, width = queries.shape
    own = width // HEAD_DIM
    copies = []
    for group in range(groups):
        cols = pl.ds(pl.multiple_of(partner(axis, group) * width, HEAD_DIM), width)
        for field, (source, target) in enumerate(
            ((query_ref, queries), (key_ref, key_rows), (value_ref, values))
        ):
            copy = pltpu.make_async_copy(
                source.at[:, cols], target.at[group], arrived.at[group, field]
            )
            copy.start()
            copies.append(copy)
    for group in range(groups):
        for copy in copies[3 * group : 3 * group + 3]:
            copy.wait()
        for head in range(own):
            cols = pl.ds(head * HEAD_DIM, HEAD_DIM)
            scores = columns_dot(key_rows[group, :, cols], queries[group, :, cols])
            largest = jnp.max(scores, axis=0, keepdims=True)
            raised = jnp.exp((scores - largest) * score_scale)
            weights = raised * (1.0 / jnp.sum(raised, axis=0, keepdims=True))
            weights_ref[group * own + head] = weights
            attended = dot(values[group, :, cols].T, weights.astype(jnp.bfloat16))
            part, place = (0, head) if head < chunks[group][0] else (1, head - chunks[group][0])
            ref = attended_refs[sum(len(sizes) for sizes in chunks[:group]) + part]
            ref[place] = attended.astype(jnp.bfloat16)


def forward(axis, queries, key_rows, values, chunks):
    patches, feat = queries.shape
    heads, groups = feat // HEAD_DIM, len(chunks)
    fields = [in_hbm(field) for field in (queries, key_rows, values)]
    weights, *attended = pl.pallas_call(
        functools.partial(forward_kernel, axis, chunks),
        in_specs=[pl.BlockSpec(memory_space=pltpu.HBM)] * 3,
        out_specs=[pl.BlockSpec(memory_space=pltpu.VMEM)] * (1 + sum(map(len, chunks))),
        scratch_shapes=[pltpu.VMEM((groups, patches, feat // groups), jnp.bfloat16)] * 3
        + [pltpu.SemaphoreType.DMA((groups, 3))],
        out_shape=[jax.ShapeDtypeStruct((heads, patches, patches), jnp.float32)]
        + [
            jax.ShapeDtypeStruct((size, HEAD_DIM, patches), jnp.bfloat16)
            for sizes in chunks
            for size in sizes
        ],
        compiler_params=params(patches),
        cost_estimate=cost(6),
        name="spatial_forward",
    )(*fields)
    attended = iter(attended)
    return weights, [[next(attended) for _ in sizes] for sizes in chunks]


def backward_group(axis, whole, first, fields, weights_ref, grad_refs, distance, scratch, results, sent):
    query_ref, key_ref, value_ref = fields
    score_scale = HEAD_DIM ** (-0.5)
    grads = [(ref, place) for ref in grad_refs for place in range(ref.shape[0])]
    own = len(grads)
    start = (partner(axis, distance) * whole + first) * HEAD_DIM
    columns = [
        pl.ds(pl.multiple_of(start + head * HEAD_DIM, HEAD_DIM), HEAD_DIM) for head in range(own)
    ]
    spatial_grads = [
        dot(value_ref[:, columns[head]], ref[place]) for head, (ref, place) in enumerate(grads)
    ]
    all_scores = []
    for head, spatial_grad in enumerate(spatial_grads):
        weights = weights_ref[distance * whole + first + head]
        row_sum = jnp.sum(spatial_grad * weights, axis=0, keepdims=True)
        scores = weights * (spatial_grad - row_sum) * score_scale
        all_scores.append(scores.astype(jnp.bfloat16))
    gq, gk = scratch
    for head, scores in enumerate(all_scores):
        cols = pl.ds(head * HEAD_DIM, HEAD_DIM)
        gk[:, cols] = dot(scores, query_ref[:, columns[head]]).astype(jnp.bfloat16)
        gq[:, cols] = dot(key_ref[:, columns[head]].T, scores).astype(jnp.bfloat16).T
    there = pl.ds(pl.multiple_of(start, HEAD_DIM), own * HEAD_DIM)
    copies = [
        pltpu.make_async_copy(source, target.at[:, there], sent.at[side])
        for side, (source, target) in enumerate(zip(scratch, results))
    ]
    for copy in copies:
        copy.start()
    return copies


def backward_kernel(axis, distances, arrays, whole, first, gains_of, *refs):
    fields, weights_ref, refs = refs[:3], refs[3], refs[4:]
    ends = [sum(arrays[: place + 1]) for place in range(len(arrays))]
    grad_refs = [refs[end - size : end] for end, size in zip(ends, arrays)]
    refs = refs[ends[-1] :]
    *refs, gq, gk, sent = refs
    copies = []
    if gains_of:
        *mixed_refs, gains_ref, _, _, gq_ref, gk_ref, grad_gains_ref, grad_gains = refs
        gain_gradients(axis, *gains_of, mixed_refs, gains_ref, grad_gains)
        copy = pltpu.make_async_copy(grad_gains, grad_gains_ref, sent.at[len(distances), 0])
        copy.start()
        copies.append(copy)
    else:
        gq_ref, gk_ref = refs[-2:]
    for place, distance in enumerate(distances):
        copies += backward_group(
            axis,
            whole,
            first,
            fields,
            weights_ref,
            grad_refs[place],
            distance,
            (gq.at[place], gk.at[place]),
            (gq_ref, gk_ref),
            sent.at[place],
        )
    for copy in copies:
        copy.wait()


def backward(
    axis, fields, weights, grads, distances, whole, first=0, earlier=(), mixed=(), gains=None, gains_of=()
):
    patches, feat = fields[0].shape
    own = sum(part.shape[0] for part in grads[0])
    arrays = [len(parts) for parts in grads]
    operands = [*fields, weights, *sum(grads, [])] + ([*mixed, gains] if gains_of else [])
    block = pltpu.VMEM((len(distances), patches, own * HEAD_DIM), jnp.bfloat16)
    out_shape = [jax.ShapeDtypeStruct((patches, feat), jnp.bfloat16)] * 2
    scratch = [block, block, pltpu.SemaphoreType.DMA((len(distances) + 1, 2))]
    if gains_of:
        out_shape.append(jax.ShapeDtypeStruct(gains.shape, jnp.float32))
        scratch.insert(0, pltpu.VMEM(gains.shape, jnp.float32))
    return pl.pallas_call(
        functools.partial(backward_kernel, axis, distances, arrays, whole, first, gains_of),
        in_specs=[pl.BlockSpec(memory_space=pltpu.VMEM)] * len(operands)
        + [pl.BlockSpec(memory_space=pl.ANY)] * len(earlier),
        out_specs=[pl.BlockSpec(memory_space=pl.ANY)] * len(out_shape),
        scratch_shapes=scratch,
        out_shape=out_shape,
        input_output_aliases={len(operands) + index: index for index in range(len(earlier))},
        compiler_params=params(patches),
        cost_estimate=cost(2),
        name="spatial_backward",
    )(*operands, *earlier)


def pack_kernel(field_ref, *refs):
    *packed_refs, rows, arrived = refs
    chunks, size, _ = rows.shape
    spaces, _, width = packed_refs[0].shape
    copies = [
        pltpu.make_async_copy(
            field_ref.at[pl.ds(chunk * size, size), :], rows.at[chunk], arrived.at[chunk]
        )
        for chunk in range(chunks)
    ]
    for copy in copies:
        copy.start()
    for chunk, copy in enumerate(copies):
        copy.wait()
        for distance, packed_ref in enumerate(packed_refs):
            for space in range(spaces):
                start = (space * len(packed_refs) + partner("tm", distance)) * width
                cols = pl.ds(pl.multiple_of(start, HEAD_DIM), width)
                packed_ref[space, pl.ds(chunk * size, size), :] = rows[chunk, :, cols]


def pack(field, frames, spaces):
    patches, feat = field.shape
    chunks = patches // GROUP
    shape = (spaces, patches, feat // (frames * spaces))
    return pl.pallas_call(
        pack_kernel,
        in_specs=[pl.BlockSpec(memory_space=pltpu.HBM)],
        out_specs=[pl.BlockSpec(memory_space=pltpu.VMEM)] * frames,
        out_shape=[jax.ShapeDtypeStruct(shape, field.dtype)] * frames,
        scratch_shapes=[
            pltpu.VMEM((chunks, patches // chunks, feat), field.dtype),
            pltpu.SemaphoreType.DMA((chunks,)),
        ],
        compiler_params=params(patches),
        cost_estimate=cost(1),
        name="pack_cotangent",
    )(in_hbm(field))


def turn_kernel(frames, *refs):
    piece_refs, (plane_ref, own_hbm, *other_refs), (turned, own_ref, sent) = (
        refs[:frames][::-1],
        refs[frames:-3],
        refs[-3:],
    )
    spaces, lanes, _ = piece_refs[0].shape
    for space in range(spaces):
        place = pl.multiple_of(partner("space", space) * lanes, lanes)
        own_ref[frames + space] = plane_ref[:, :, pl.ds(place, lanes)]
    heads = own_ref.shape[1]
    for space in range(spaces):
        target = turned if space else own_ref
        source = partner("space", space)
        for distance, ref in enumerate(piece_refs):
            frame = partner("tm", distance)
            for head in range(heads):
                cols = pl.ds(head * HEAD_DIM, HEAD_DIM)
                target[frame, head] = ref[source, :, cols].T
        if space == 0:
            copy = pltpu.make_async_copy(own_ref, own_hbm, sent)
            copy.start()
        else:
            for head in range(heads):
                other_refs[(space - 1) * heads + head][:, 0] = turned[:, head]
    copy.wait()


def turn(pieces, plane):
    spaces, patches, feat = pieces[0].shape
    frames, heads = len(pieces), feat // HEAD_DIM
    turned = (heads, HEAD_DIM, patches)
    others = heads * (spaces - 1)
    other = jax.ShapeDtypeStruct((frames, 1, HEAD_DIM, patches), pieces[0].dtype)
    return pl.pallas_call(
        functools.partial(turn_kernel, frames),
        in_specs=[pl.BlockSpec(memory_space=pltpu.VMEM)] * (frames + 1),
        out_specs=[pl.BlockSpec(memory_space=pltpu.HBM)]
        + [pl.BlockSpec(memory_space=pltpu.VMEM)] * others,
        out_shape=[jax.ShapeDtypeStruct((frames + spaces,) + turned, pieces[0].dtype)]
        + [other] * others,
        scratch_shapes=[
            pltpu.VMEM((frames,) + turned, pieces[0].dtype),
            pltpu.VMEM((frames + spaces,) + turned, pieces[0].dtype),
            pltpu.SemaphoreType.DMA,
        ],
        compiler_params=params(patches),
        cost_estimate=cost(2),
        name="turn_cotangent",
    )(*reversed(pieces), plane)


def temporal_part(length, load_attended, load_upstream, load_gain, fields, ups, normed, grad_ref):
    frames, feat, lanes = grad_ref.shape
    half = GROUP // 2
    score_scale = feat ** (-0.5)
    pairs = [(t, u) for t in range(frames) for u in range(t + 1)]
    every = range(frames)
    valid = [jnp.where(t < length, 1.0, 0.0).astype(jnp.float32) for t in every]
    bias = [jnp.where(u < length, 0.0, -1e30).astype(jnp.float32) for u in every]

    def total(piece):
        return jnp.broadcast_to(jnp.sum(piece, axis=0, keepdims=True), (half, lanes))

    squares = [jnp.zeros((half, lanes), jnp.float32) for _ in every]
    for group in range(feat // GROUP):
        rows = pl.ds(group * GROUP, GROUP)
        for t in every:
            field = load_attended(t, rows).astype(jnp.float32)
            fields[t, rows, :] = field
            ups[t, rows, :] = load_upstream(t, rows).astype(jnp.float32)
            low, high = field[:half], field[half:]
            squares[t] = squares[t] + (low * low + high * high)
    inverse = [lax.rsqrt(total(squares[t]) * (1.0 / feat) + 1e-06) for t in every]

    raw = {pair: jnp.zeros((half, lanes), jnp.float32) for pair in pairs}
    grad = {pair: jnp.zeros((half, lanes), jnp.float32) for pair in pairs}
    for group in range(feat // half):
        rows = pl.ds(group * half, half)
        gain = load_gain(rows)
        here = [fields[t, rows, :] for t in every]
        above = [ups[t, rows, :] for t in every]
        scaled = [here[t] * inverse[t] for t in every]
        gained = [scaled[t] * gain for t in every]
        for t in every:
            normed[t, rows, :] = scaled[t]
        for t, u in pairs:
            raw[t, u] = raw[t, u] + gained[t] * scaled[u]
            grad[t, u] = grad[t, u] + above[t] * here[u]

    value_part, score_part = {}, {}
    for t in every:
        seen = range(t + 1)
        for u in seen:
            raw[t, u] = total(raw[t, u])
            grad[t, u] = total(grad[t, u]) * valid[t]
        scores = [raw[t, u] * score_scale + bias[u] for u in seen]
        largest = functools.reduce(jnp.maximum, scores)
        raised = [jnp.exp(score - largest) for score in scores]
        over = 1.0 / functools.reduce(jnp.add, raised)
        weights = [piece * over for piece in raised]
        mean_grad = functools.reduce(jnp.add, [weights[u] * grad[t, u] for u in seen])
        for u in seen:
            rounded = weights[u].astype(jnp.bfloat16).astype(jnp.float32)
            value_part[t, u] = (rounded + (1.0 if u == t else 0.0)) * valid[t]
            score_part[t, u] = weights[u] * (grad[t, u] - mean_grad) * score_scale

    both = {(t, u): score_part[t, u] * (2.0 if t == u else 1.0) for t, u in pairs}
    both.update({(u, t): both[t, u] for t, u in pairs})
    raw.update({(u, t): raw[t, u] for t, u in pairs})
    mean_part = [
        functools.reduce(jnp.add, [both[u, v] * raw[u, v] for v in every]) * (1.0 / feat)
        for u in every
    ]

    all_mixed = []
    for group in range(feat // GROUP):
        outs = [[] for _ in every]
        for side in range(2):
            rows = pl.ds(group * GROUP + side * half, half)
            gain = load_gain(rows)
            scaled = [normed[t, rows, :] for t in every]
            above = [ups[t, rows, :] for t in every]
            mixed = jnp.zeros((half, lanes), jnp.float32)
            for u in every:
                crossed = functools.reduce(jnp.add, [both[u, v] * scaled[v] for v in every])
                mixed = mixed + crossed * scaled[u]
                from_norm = inverse[u] * (gain * crossed - scaled[u] * mean_part[u])
                direct = functools.reduce(
                    jnp.add, [value_part[t, u] * above[t] for t in range(u, frames)]
                )
                outs[u].append(direct + from_norm)
            all_mixed.append(mixed)
        for u in every:
            grad_ref[u, pl.ds(group * GROUP, GROUP), :] = jnp.concatenate(
                outs[u], axis=0
            ).astype(jnp.bfloat16)
    return jnp.concatenate(all_mixed, axis=0)


def temporal_kernel(frames, spaces, heads, length_ref, task_ref, *refs):
    first, count, whole = heads
    refs = list(refs)

    def take(number):
        taken, refs[:] = refs[:number], refs[number:]
        return taken

    attended_refs, (gain_ref,), other_refs = take(frames - 1), take(1), take((spaces - 1) * count)
    earlier_refs = take(3 if first else 0)
    (own_hbm,), field_refs = take(1), take(0 if first else 3)
    grad_refs, (mixed_ref,), kept_refs = take(frames), take(1), take(len(field_refs))
    attended, grads, wide, own_ref, arrived = refs
    lanes = own_ref.shape[3]
    own_copies = [
        pltpu.make_async_copy(
            own_hbm.at[:, first + place], own_ref.at[:, place], arrived.at[place]
        )
        for place in range(count)
    ]
    copies = [
        pltpu.make_async_copy(source, target, arrived.at[count + index])
        for index, (source, target) in enumerate(zip(field_refs, kept_refs))
    ]
    for copy in own_copies + copies:
        copy.start()
    if first:
        *plane_refs, rows_ref = earlier_refs
        mixed_ref[...] = rows_ref[...]
        for ref, earlier_ref in zip(grad_refs, plane_refs):
            ref[:first] = earlier_ref[...]
    else:
        mixed_ref[...] = jnp.full(mixed_ref.shape, task_ref[0].astype(jnp.float32))

    def load_upstream(space, place, t, rows):
        if space == 0:
            return own_ref[t, place, rows, :]
        return other_refs[(space - 1) * count + place][t, 0, rows, :]

    places = [
        pl.ds(pl.multiple_of(partner("space", space) * lanes, lanes), lanes)
        for space in range(spaces)
    ]
    for place in range(count):
        own_copies[place].wait()
        for space, here in enumerate(places):
            attended[place, space, partner("tm", 0)] = own_ref[frames + space, place]
            for distance, ref in enumerate(attended_refs):
                source = place + (first if ref.shape[0] == whole else 0)
                attended[place, space, partner("tm", distance + 1)] = ref[source, :, here]
        mixed = [
            temporal_part(
                length_ref[0],
                lambda t, rows: attended[place, space, t, rows, :],
                functools.partial(load_upstream, space, place),
                lambda rows: gain_ref[first + place, rows, :],
                wide.at[place % 2, space, 0],
                wide.at[place % 2, space, 1],
                wide.at[place % 2, space, 2],
                grads.at[place, space],
            )
            for space in range(spaces)
        ]
        summed = functools.reduce(jnp.add, mixed)
        mixed_ref[pl.ds(first + place, 1), :] = jnp.sum(summed.T, axis=0, keepdims=True) * 0.5
        for distance, ref in enumerate(grad_refs):
            frame = partner("tm", distance)
            target = place + (first if ref.shape[0] == whole else 0)
            for space, here in enumerate(places):
                ref[target, :, here] = grads[place, space, frame]
    for copy in copies:
        copy.wait()


def temporal(lengths, task_ids, attended, upstream, gain, fields, heads, earlier):
    feat, lanes = upstream[0].shape[2:]
    first, count, whole = heads
    frames, spaces = len(attended) + 1, 1 + (len(upstream) - 1) // whole
    patches = spaces * lanes
    others = [
        upstream[1 + (space - 1) * whole + first + place]
        for space in range(1, spaces)
        for place in range(count)
    ]
    rows = -(-(whole + 1) // 8) * 8
    sizes = [whole if first else count] * 2 + [count] * (frames - 2)
    operands = [*attended, gain, *others, *earlier]
    fields = [] if first else fields
    in_place = [in_hbm(field) for field in (upstream[0], *fields)]
    block = (count, spaces, frames, feat, lanes)
    own = (upstream[0].shape[0], count, feat, lanes)
    results = pl.pallas_call(
        functools.partial(temporal_kernel, frames, spaces, heads),
        in_specs=[pl.BlockSpec(memory_space=pltpu.SMEM)] * 2
        + [pl.BlockSpec(memory_space=pltpu.VMEM)] * len(operands)
        + [pl.BlockSpec(memory_space=pltpu.HBM)] * len(in_place),
        out_specs=[pl.BlockSpec(memory_space=pltpu.VMEM)] * (frames + 1 + len(fields)),
        scratch_shapes=[
            pltpu.VMEM(block, jnp.bfloat16),
            pltpu.VMEM(block, jnp.bfloat16),
            pltpu.VMEM((2, spaces, 3, frames, feat, lanes), jnp.float32),
            pltpu.VMEM(own, upstream[0].dtype),
            pltpu.SemaphoreType.DMA((count + len(fields),)),
        ],
        out_shape=[jax.ShapeDtypeStruct((size, feat, patches), jnp.bfloat16) for size in sizes]
        + [jax.ShapeDtypeStruct((rows, feat), jnp.float32)]
        + [jax.ShapeDtypeStruct(field.shape, field.dtype) for field in fields],
        compiler_params=params(patches),
        cost_estimate=cost(2000),
        name="temporal",
    )(lengths, task_ids, *operands, *in_place)
    return list(results[:frames]), results[frames], results[frames + 1 :]


def gain_gradients(axis, heads, frames, clips, mixed_refs, gains_ref, grad_ref):
    tasks = gains_ref.shape[1]
    rows = sum(ref.shape[0] for ref in mixed_refs) // (frames * clips)
    each = mixed_refs[0].shape[0] // rows
    task_ids = lax.broadcasted_iota(jnp.int32, (tasks, HEAD_DIM), 0).astype(jnp.float32)
    for distance in range(frames):
        for head in range(heads):
            mixed = jnp.zeros((tasks, HEAD_DIM), jnp.float32)
            for clip in range(clips):
                block = distance * clips + clip
                ref, start = mixed_refs[block // each], block % each * rows
                task = ref[pl.ds(start + heads, 1), :]
                row = ref[pl.ds(start + head, 1), :]
                mixed = mixed + jnp.where(task_ids == task, row, 0.0)
            start = (partner(axis, distance) * heads + head) * HEAD_DIM
            cols = pl.ds(pl.multiple_of(start, HEAD_DIM), HEAD_DIM)
            grad_ref[0, :, cols] = gains_ref[1, :, cols] * mixed
            grad_ref[1, :, cols] = gains_ref[0, :, cols] * mixed


def swap(field, axis, size, distance):
    return lax.ppermute(field, axis, [(i, i ^ distance) for i in range(size)])


def split_by_heads(
    query_heads, key_heads, value_heads, cotangent, task_ids, lengths, gains, clips, frames, spaces
):
    patches, feat = query_heads.shape[2:]
    heads = feat // HEAD_DIM
    own = heads // frames
    width = own * HEAD_DIM
    queries, key_rows, values = (
        field.reshape(patches, feat) for field in (query_heads, key_heads, value_heads)
    )
    frame = lax.axis_index("tm")

    pieces = list(pack(cotangent.reshape(cotangent.shape[2:]), frames, spaces))
    queries, pieces = lax.optimization_barrier((queries, pieces))
    for distance in range(1, frames):
        pieces[distance] = swap(pieces[distance], "tm", frames, distance)
    fields = (queries, key_rows, values)
    early = max(1, own - 1)
    late = own - early
    weights, attended = forward(
        "tm", *fields, [(own,), (own,)] + [(early, late)] * (frames - 2)
    )
    plane, near, *far = [parts[0] for parts in attended]
    late_far = [parts[1] for parts in attended[2:]]
    near = swap(near, "tm", frames, 1)
    far = [swap(part, "tm", frames, distance) for distance, part in enumerate(far, 2)]
    backwards, _ = lax.optimization_barrier((pieces[::-1], weights))
    upstream = list(turn(backwards[::-1], plane))
    late_far, upstream[0] = lax.optimization_barrier((late_far, upstream[0]))
    for index in range(1, len(upstream)):
        upstream[index] = swap(upstream[index], "space", spaces, 1 + (index - 1) // own)
    late_far = [swap(part, "tm", frames, distance) for distance, part in enumerate(late_far, 2)]
    rows = lax.dynamic_index_in_dim(gains, task_ids[0], 1, keepdims=False)
    product = lax.dynamic_slice_in_dim(rows[0] * rows[1], frame * width, width, 0)
    gain = jnp.broadcast_to(
        product.reshape(own, HEAD_DIM, 1), (own, HEAD_DIM, patches // spaces)
    )
    (own_part, near_part, *far_grads), mixed, kept = temporal(
        lengths, task_ids, [near, *far], upstream, gain, fields, (0, early, own), ()
    )
    far_grads = [swap(part, "tm", frames, distance) for distance, part in enumerate(far_grads, 2)]
    (here, near_grads, *late_grads), mixed, _ = temporal(
        lengths,
        task_ids,
        [near, *late_far],
        upstream,
        gain,
        fields,
        (early, late, own),
        (own_part, near_part, mixed),
    )
    late_grads = [
        swap(part, "tm", frames, distance) for distance, part in enumerate(late_grads, 2)
    ]
    near_grads = swap(near_grads, "tm", frames, 1)
    grads = [[here], [near_grads]] + [list(parts) for parts in zip(far_grads, late_grads)]
    here = grads[0]
    for bit in range(clips.bit_length() - 1):
        other = swap(mixed, "dp", clips, 1 << bit)
        if bit == 0:
            here, far_grads, other = lax.optimization_barrier((here, far_grads, other))
        mixed = jnp.concatenate([mixed, other], axis=0)
    results = backward("tm", kept, weights, [here], [0], own)
    mixed, results = lax.optimization_barrier((mixed, results))
    close, grads[1] = lax.optimization_barrier((mixed, grads[1]))
    mixed = [mixed, swap(close, "tm", frames, 1)] + [
        swap(mixed, "tm", frames, distance) for distance in range(2, frames)
    ]
    if frames > 2:
        results = backward(
            "tm", kept, weights, [[part] for part in far_grads], list(range(2, frames)), own, 0, results
        )
        results = backward("tm", kept, weights, [grads[1]], [1], own, 0, results)
    last = list(range(frames - 1, 1, -1)) or [1]
    grad_queries, grad_keys, grad_gains = backward(
        "tm",
        kept,
        weights,
        [grads[distance][-1:] for distance in last],
        last,
        own,
        early if frames > 2 else 0,
        results,
        mixed,
        gains,
        (own, frames, clips),
    )
    return (
        grad_queries.reshape(query_heads.shape),
        grad_keys.reshape(query_heads.shape),
        grad_gains,
    )


def temporal_grads(attended, upstream, gain_query, gain_keys, length):
    highest = lax.Precision.HIGHEST
    frames = attended.shape[0]
    score_scale = attended.shape[-1] ** (-0.5)
    floats = attended.astype(jnp.float32)
    inverse_rms = lax.rsqrt(jnp.mean(floats * floats, axis=-1, keepdims=True) + 1e-06)
    normed = floats * inverse_rms
    t_query = normed * gain_query
    t_keys = normed * gain_keys
    scores = jnp.einsum("txhd,uxhd->xhtu", t_query, t_keys, precision=highest) * score_scale
    frame_ids = jnp.arange(frames, dtype=jnp.int32)
    allowed = (frame_ids[None, :] <= frame_ids[:, None]) & (frame_ids[None, :] < length)
    scores = jnp.where(allowed, scores, -1e30)
    weights = jax.nn.softmax(scores, axis=-1)
    weights_low = lax.optimization_barrier(weights.astype(jnp.bfloat16)).astype(jnp.float32)
    valid_rows = (frame_ids < length).astype(jnp.float32)
    masked = upstream.astype(jnp.float32) * valid_rows[:, None, None, None]
    grad_weights = jnp.einsum("txhd,uxhd->xhtu", masked, floats, precision=highest)
    from_values = jnp.einsum("xhtu,txhd->uxhd", weights_low, masked, precision=highest)
    grad_scores = (
        weights
        * (grad_weights - jnp.sum(grad_weights * weights, axis=-1, keepdims=True))
        * score_scale
    )
    grad_tquery = jnp.einsum("xhtu,uxhd->txhd", grad_scores, t_keys, precision=highest)
    grad_tkeys = jnp.einsum("xhtu,txhd->uxhd", grad_scores, t_query, precision=highest)
    grad_normed = grad_tquery * gain_query + grad_tkeys * gain_keys
    grad_gain_query = jnp.sum(grad_tquery * normed, axis=(0, 1))
    grad_gain_keys = jnp.sum(grad_tkeys * normed, axis=(0, 1))
    from_norm = inverse_rms * (
        grad_normed - normed * jnp.mean(grad_normed * normed, axis=-1, keepdims=True)
    )
    grad_total = (masked + from_values + from_norm).astype(jnp.bfloat16)
    return (grad_total, grad_gain_query, grad_gain_keys)


def split_by_patches(query_heads, key_heads, value_heads, cotangent, task_ids, lengths, gains):
    patches, feat = query_heads.shape[2:]
    heads = feat // HEAD_DIM
    queries, key_rows, values = (
        field.reshape(patches, feat) for field in (query_heads, key_heads, value_heads)
    )
    fields = (queries, key_rows, values)
    weights, attended = forward(None, *fields, [(heads,)])
    attended_field = jnp.transpose(attended[0][0], (2, 0, 1)).reshape(1, 1, patches, feat)
    upstream = lax.all_to_all(
        lax.all_to_all(cotangent, "space", split_axis=3, concat_axis=2, tiled=True),
        "tm",
        split_axis=2,
        concat_axis=1,
        tiled=True,
    )
    frames_attended = lax.all_to_all(attended_field, "tm", split_axis=2, concat_axis=1, tiled=True)
    frames, local_patches = frames_attended.shape[1:3]
    selector = (task_ids[0] == jnp.arange(gains.shape[1], dtype=jnp.int32)).astype(jnp.float32)
    gain_query = jnp.sum(selector[:, None] * gains[0], axis=0).reshape(heads, HEAD_DIM)
    gain_keys = jnp.sum(selector[:, None] * gains[1], axis=0).reshape(heads, HEAD_DIM)
    grad_total, grad_gq, grad_gk = temporal_grads(
        frames_attended.reshape(frames, local_patches, heads, HEAD_DIM),
        upstream.reshape(frames, local_patches, heads, HEAD_DIM),
        gain_query,
        gain_keys,
        lengths[0],
    )
    gain_terms = jnp.stack(
        [
            selector[:, None] * grad_gq.reshape(1, feat),
            selector[:, None] * grad_gk.reshape(1, feat),
        ]
    )
    grad_gains = lax.psum(gain_terms, ("dp", "tm"))
    returned = lax.all_to_all(
        grad_total.reshape(1, frames, local_patches, feat),
        "tm",
        split_axis=1,
        concat_axis=2,
        tiled=True,
    )
    head_grads = jnp.transpose(returned.reshape(patches, heads, HEAD_DIM), (1, 2, 0))
    grad_queries, grad_keys = backward(None, fields, weights, [[head_grads]], [0], heads)
    return (
        grad_queries.reshape(query_heads.shape),
        grad_keys.reshape(query_heads.shape),
        grad_gains,
    )


def solution(mesh):
    clips, frames, spaces = (mesh.shape[axis] for axis in ("dp", "tm", "space"))

    def local(query_heads, *others):
        heads = query_heads.shape[3] // HEAD_DIM
        powers = all(size & (size - 1) == 0 for size in (clips, frames, spaces))
        if powers and 2 <= frames <= 4 and heads % frames == 0 and heads > frames:
            return split_by_heads(query_heads, *others, clips, frames, spaces)
        return split_by_patches(query_heads, *others)

    return jax.shard_map(
        local,
        mesh=mesh,
        in_specs=(
            P("dp", "tm", None, "space"),
            P("dp", "tm", None, "space"),
            P("dp", "tm", None, "space"),
            P("dp", "tm", "space", None),
            P("dp"),
            P("dp"),
            P(None, None, "space"),
        ),
        out_specs=(
            P("dp", "tm", None, "space"),
            P("dp", "tm", None, "space"),
            P(None, None, "space"),
        ),
        check_vma=False,
    )
```

```python
import functools

import jax
import jax.numpy as jnp
from jax import lax
from jax.experimental import pallas as pl
from jax.experimental.pallas import tpu as pltpu
from jax.sharding import PartitionSpec as P

HEAD_DIM = 128
GROUP = 16
MIB = 1024 * 1024


def params(patches):
    return pltpu.CompilerParams(vmem_limit_bytes=(16 if patches <= 512 else 60) * MIB)


def cost(microseconds):
    return pl.CostEstimate(flops=int(microseconds * 1e8), bytes_accessed=0, transcendentals=0)


def in_hbm(field):
    return pltpu.with_memory_space_constraint(field, pltpu.HBM)


def columns_dot(left, right):
    return lax.dot_general(
        left, right, (((1,), (1,)), ((), ())), preferred_element_type=jnp.float32
    )


def dot(left, right):
    return jnp.dot(left, right, preferred_element_type=jnp.float32)


def partner(axis, distance):
    return distance if axis is None else jnp.bitwise_xor(lax.axis_index(axis), distance)


def forward_kernel(axis, query_ref, key_ref, value_ref, weights_ref, *refs):
    (queries, key_rows, values, arrived), attended_refs = refs[-4:], refs[:-4]
    score_scale = HEAD_DIM ** (-0.5)
    groups, _, width = queries.shape
    own = width // HEAD_DIM
    copies = []
    for group in range(groups):
        cols = pl.ds(pl.multiple_of(partner(axis, group) * width, HEAD_DIM), width)
        for field, (source, target) in enumerate(
            ((query_ref, queries), (key_ref, key_rows), (value_ref, values))
        ):
            copy = pltpu.make_async_copy(
                source.at[:, cols], target.at[group], arrived.at[group, field]
            )
            copy.start()
            copies.append(copy)
    for group in range(groups):
        for copy in copies[3 * group : 3 * group + 3]:
            copy.wait()
        for head in range(own):
            cols = pl.ds(head * HEAD_DIM, HEAD_DIM)
            scores = columns_dot(key_rows[group, :, cols], queries[group, :, cols])
            largest = jnp.max(scores, axis=0, keepdims=True)
            raised = jnp.exp((scores - largest) * score_scale)
            weights = raised * (1.0 / jnp.sum(raised, axis=0, keepdims=True))
            weights_ref[group * own + head] = weights
            attended = dot(values[group, :, cols].T, weights.astype(jnp.bfloat16))
            attended_refs[group][head] = attended.astype(jnp.bfloat16)


def forward(axis, queries, key_rows, values, groups):
    patches, feat = queries.shape
    heads = feat // HEAD_DIM
    own = heads // groups
    fields = [in_hbm(field) for field in (queries, key_rows, values)]
    weights, *attended = pl.pallas_call(
        functools.partial(forward_kernel, axis),
        in_specs=[pl.BlockSpec(memory_space=pltpu.HBM)] * 3,
        out_specs=[pl.BlockSpec(memory_space=pltpu.VMEM)] * (1 + groups),
        scratch_shapes=[pltpu.VMEM((groups, patches, feat // groups), jnp.bfloat16)] * 3
        + [pltpu.SemaphoreType.DMA((groups, 3))],
        out_shape=[jax.ShapeDtypeStruct((heads, patches, patches), jnp.float32)]
        + [jax.ShapeDtypeStruct((own, HEAD_DIM, patches), jnp.bfloat16)] * groups,
        compiler_params=params(patches),
        cost_estimate=cost(6),
        name="spatial_forward",
    )(*fields)
    return weights, attended


def backward_group(axis, fields, weights_ref, grad_ref, distance, scratch, results, sent):
    query_ref, key_ref, value_ref = fields
    score_scale = HEAD_DIM ** (-0.5)
    own = grad_ref.shape[0]
    start = partner(axis, distance) * (own * HEAD_DIM)
    columns = [
        pl.ds(pl.multiple_of(start + head * HEAD_DIM, HEAD_DIM), HEAD_DIM) for head in range(own)
    ]
    spatial_grads = [dot(value_ref[:, columns[head]], grad_ref[head]) for head in range(own)]
    all_scores = []
    for head, spatial_grad in enumerate(spatial_grads):
        weights = weights_ref[distance * own + head]
        row_sum = jnp.sum(spatial_grad * weights, axis=0, keepdims=True)
        scores = weights * (spatial_grad - row_sum) * score_scale
        all_scores.append(scores.astype(jnp.bfloat16))
    gq, gk = scratch
    for head, scores in enumerate(all_scores):
        cols = pl.ds(head * HEAD_DIM, HEAD_DIM)
        gk[:, cols] = dot(scores, query_ref[:, columns[head]]).astype(jnp.bfloat16)
        gq[:, cols] = dot(key_ref[:, columns[head]].T, scores).astype(jnp.bfloat16).T
    there = pl.ds(pl.multiple_of(start, HEAD_DIM), own * HEAD_DIM)
    copies = [
        pltpu.make_async_copy(source, target.at[:, there], sent.at[side])
        for side, (source, target) in enumerate(zip(scratch, results))
    ]
    for copy in copies:
        copy.start()
    return copies


def backward_kernel(axis, distances, gains_of, *refs):
    fields, weights_ref, refs = refs[:3], refs[3], refs[4:]
    grad_refs, refs = refs[: len(distances)], refs[len(distances) :]
    *refs, gq, gk, sent = refs
    copies = []
    if gains_of:
        *mixed_refs, gains_ref, _, _, gq_ref, gk_ref, grad_gains_ref, grad_gains = refs
        gain_gradients(axis, *gains_of, mixed_refs, gains_ref, grad_gains)
        copy = pltpu.make_async_copy(grad_gains, grad_gains_ref, sent.at[len(distances), 0])
        copy.start()
        copies.append(copy)
    else:
        gq_ref, gk_ref = refs[-2:]
    for place, (distance, grad_ref) in enumerate(zip(distances, grad_refs)):
        copies += backward_group(
            axis,
            fields,
            weights_ref,
            grad_ref,
            distance,
            (gq.at[place], gk.at[place]),
            (gq_ref, gk_ref),
            sent.at[place],
        )
    for copy in copies:
        copy.wait()


def backward(axis, fields, weights, grads, distances, earlier=(), mixed=(), gains=None, gains_of=()):
    patches, feat = fields[0].shape
    own = grads[0].shape[0]
    operands = [*fields, weights, *grads] + ([*mixed, gains] if gains_of else [])
    block = pltpu.VMEM((len(distances), patches, own * HEAD_DIM), jnp.bfloat16)
    out_shape = [jax.ShapeDtypeStruct((patches, feat), jnp.bfloat16)] * 2
    scratch = [block, block, pltpu.SemaphoreType.DMA((len(distances) + 1, 2))]
    if gains_of:
        out_shape.append(jax.ShapeDtypeStruct(gains.shape, jnp.float32))
        scratch.insert(0, pltpu.VMEM(gains.shape, jnp.float32))
    return pl.pallas_call(
        functools.partial(backward_kernel, axis, distances, gains_of),
        in_specs=[pl.BlockSpec(memory_space=pltpu.VMEM)] * len(operands)
        + [pl.BlockSpec(memory_space=pl.ANY)] * len(earlier),
        out_specs=[pl.BlockSpec(memory_space=pl.ANY)] * len(out_shape),
        scratch_shapes=scratch,
        out_shape=out_shape,
        input_output_aliases={len(operands) + index: index for index in range(len(earlier))},
        compiler_params=params(patches),
        cost_estimate=cost(2),
        name="spatial_backward",
    )(*operands, *earlier)


def pack_kernel(field_ref, *refs):
    *packed_refs, rows, arrived = refs
    chunks, size, _ = rows.shape
    spaces, _, width = packed_refs[0].shape
    copies = [
        pltpu.make_async_copy(
            field_ref.at[pl.ds(chunk * size, size), :], rows.at[chunk], arrived.at[chunk]
        )
        for chunk in range(chunks)
    ]
    for copy in copies:
        copy.start()
    for chunk, copy in enumerate(copies):
        copy.wait()
        for distance, packed_ref in enumerate(packed_refs):
            for space in range(spaces):
                start = (space * len(packed_refs) + partner("tm", distance)) * width
                cols = pl.ds(pl.multiple_of(start, HEAD_DIM), width)
                packed_ref[space, pl.ds(chunk * size, size), :] = rows[chunk, :, cols]


def pack(field, frames, spaces):
    patches, feat = field.shape
    chunks = patches // GROUP
    shape = (spaces, patches, feat // (frames * spaces))
    return pl.pallas_call(
        pack_kernel,
        in_specs=[pl.BlockSpec(memory_space=pltpu.HBM)],
        out_specs=[pl.BlockSpec(memory_space=pltpu.VMEM)] * frames,
        out_shape=[jax.ShapeDtypeStruct(shape, field.dtype)] * frames,
        scratch_shapes=[
            pltpu.VMEM((chunks, patches // chunks, feat), field.dtype),
            pltpu.SemaphoreType.DMA((chunks,)),
        ],
        compiler_params=params(patches),
        cost_estimate=cost(1),
        name="pack_cotangent",
    )(in_hbm(field))


def turn_kernel(frames, *refs):
    piece_refs, (plane_ref, own_hbm, *other_refs), (turned, own_ref, sent) = (
        refs[:frames][::-1],
        refs[frames:-3],
        refs[-3:],
    )
    spaces, lanes, _ = piece_refs[0].shape
    for space in range(spaces):
        place = pl.multiple_of(partner("space", space) * lanes, lanes)
        own_ref[frames + space] = plane_ref[:, :, pl.ds(place, lanes)]
    heads = own_ref.shape[1]
    for space in range(spaces):
        target = turned if space else own_ref
        source = partner("space", space)
        for distance, ref in enumerate(piece_refs):
            frame = partner("tm", distance)
            for head in range(heads):
                cols = pl.ds(head * HEAD_DIM, HEAD_DIM)
                target[frame, head] = ref[source, :, cols].T
        if space == 0:
            copy = pltpu.make_async_copy(own_ref, own_hbm, sent)
            copy.start()
        else:
            half = frames // 2
            other_refs[2 * space - 2][...] = turned[:half]
            other_refs[2 * space - 1][...] = turned[half:]
    copy.wait()


def turn(pieces, plane):
    spaces, patches, feat = pieces[0].shape
    frames, heads = len(pieces), feat // HEAD_DIM
    turned = (heads, HEAD_DIM, patches)
    sizes = [frames + spaces] + [frames // 2, frames - frames // 2] * (spaces - 1)
    return pl.pallas_call(
        functools.partial(turn_kernel, frames),
        in_specs=[pl.BlockSpec(memory_space=pltpu.VMEM)] * (frames + 1),
        out_specs=[pl.BlockSpec(memory_space=pltpu.HBM)]
        + [pl.BlockSpec(memory_space=pltpu.VMEM)] * (len(sizes) - 1),
        out_shape=[jax.ShapeDtypeStruct((size,) + turned, pieces[0].dtype) for size in sizes],
        scratch_shapes=[
            pltpu.VMEM((frames,) + turned, pieces[0].dtype),
            pltpu.VMEM((frames + spaces,) + turned, pieces[0].dtype),
            pltpu.SemaphoreType.DMA,
        ],
        compiler_params=params(patches),
        cost_estimate=cost(2),
        name="turn_cotangent",
    )(*reversed(pieces), plane)


def temporal_part(length, load_attended, load_upstream, load_gain, fields, ups, normed, grad_ref):
    frames, feat, lanes = grad_ref.shape
    half = GROUP // 2
    score_scale = feat ** (-0.5)
    pairs = [(t, u) for t in range(frames) for u in range(t + 1)]
    every = range(frames)
    valid = [jnp.where(t < length, 1.0, 0.0).astype(jnp.float32) for t in every]
    bias = [jnp.where(u < length, 0.0, -1e30).astype(jnp.float32) for u in every]

    def total(piece):
        return jnp.broadcast_to(jnp.sum(piece, axis=0, keepdims=True), (half, lanes))

    squares = [jnp.zeros((half, lanes), jnp.float32) for _ in every]
    for group in range(feat // GROUP):
        rows = pl.ds(group * GROUP, GROUP)
        for t in every:
            field = load_attended(t, rows).astype(jnp.float32)
            fields[t, rows, :] = field
            ups[t, rows, :] = load_upstream(t, rows).astype(jnp.float32)
            low, high = field[:half], field[half:]
            squares[t] = squares[t] + (low * low + high * high)
    inverse = [lax.rsqrt(total(squares[t]) * (1.0 / feat) + 1e-06) for t in every]

    raw = {pair: jnp.zeros((half, lanes), jnp.float32) for pair in pairs}
    grad = {pair: jnp.zeros((half, lanes), jnp.float32) for pair in pairs}
    for group in range(feat // half):
        rows = pl.ds(group * half, half)
        gain = load_gain(rows)
        here = [fields[t, rows, :] for t in every]
        above = [ups[t, rows, :] for t in every]
        scaled = [here[t] * inverse[t] for t in every]
        gained = [scaled[t] * gain for t in every]
        for t in every:
            normed[t, rows, :] = scaled[t]
        for t, u in pairs:
            raw[t, u] = raw[t, u] + gained[t] * scaled[u]
            grad[t, u] = grad[t, u] + above[t] * here[u]

    value_part, score_part = {}, {}
    for t in every:
        seen = range(t + 1)
        for u in seen:
            raw[t, u] = total(raw[t, u])
            grad[t, u] = total(grad[t, u]) * valid[t]
        scores = [raw[t, u] * score_scale + bias[u] for u in seen]
        largest = functools.reduce(jnp.maximum, scores)
        raised = [jnp.exp(score - largest) for score in scores]
        over = 1.0 / functools.reduce(jnp.add, raised)
        weights = [piece * over for piece in raised]
        mean_grad = functools.reduce(jnp.add, [weights[u] * grad[t, u] for u in seen])
        for u in seen:
            rounded = weights[u].astype(jnp.bfloat16).astype(jnp.float32)
            value_part[t, u] = (rounded + (1.0 if u == t else 0.0)) * valid[t]
            score_part[t, u] = weights[u] * (grad[t, u] - mean_grad) * score_scale

    both = {(t, u): score_part[t, u] * (2.0 if t == u else 1.0) for t, u in pairs}
    both.update({(u, t): both[t, u] for t, u in pairs})
    raw.update({(u, t): raw[t, u] for t, u in pairs})
    mean_part = [
        functools.reduce(jnp.add, [both[u, v] * raw[u, v] for v in every]) * (1.0 / feat)
        for u in every
    ]

    all_mixed = []
    for group in range(feat // GROUP):
        outs = [[] for _ in every]
        for side in range(2):
            rows = pl.ds(group * GROUP + side * half, half)
            gain = load_gain(rows)
            scaled = [normed[t, rows, :] for t in every]
            above = [ups[t, rows, :] for t in every]
            mixed = jnp.zeros((half, lanes), jnp.float32)
            for u in every:
                crossed = functools.reduce(jnp.add, [both[u, v] * scaled[v] for v in every])
                mixed = mixed + crossed * scaled[u]
                from_norm = inverse[u] * (gain * crossed - scaled[u] * mean_part[u])
                direct = functools.reduce(
                    jnp.add, [value_part[t, u] * above[t] for t in range(u, frames)]
                )
                outs[u].append(direct + from_norm)
            all_mixed.append(mixed)
        for u in every:
            grad_ref[u, pl.ds(group * GROUP, GROUP), :] = jnp.concatenate(
                outs[u], axis=0
            ).astype(jnp.bfloat16)
    return jnp.concatenate(all_mixed, axis=0)


def fetch_kernel(source_ref, target_ref, arrived):
    copies = [
        pltpu.make_async_copy(source_ref.at[index], target_ref.at[index], arrived.at[index])
        for index in range(source_ref.shape[0])
    ]
    for copy in copies:
        copy.start()
    for copy in copies:
        copy.wait()


def fetch(field):
    return pl.pallas_call(
        fetch_kernel,
        in_specs=[pl.BlockSpec(memory_space=pltpu.HBM)],
        out_specs=pl.BlockSpec(memory_space=pltpu.VMEM),
        out_shape=jax.ShapeDtypeStruct(field.shape, field.dtype),
        scratch_shapes=[pltpu.SemaphoreType.DMA((field.shape[0],))],
        compiler_params=params(0),
        cost_estimate=cost(1),
        name="fetch_own",
    )(in_hbm(field))


def temporal_kernel(frames, spaces, length_ref, task_ref, *refs):
    attended_refs, (gain_ref, own_ref, *other_refs), refs = (
        refs[: frames - 1],
        refs[frames - 1 : frames - 1 + 2 * spaces],
        refs[frames - 1 + 2 * spaces :],
    )
    field_refs, grad_refs, refs = refs[:3], refs[3 : frames + 3], refs[frames + 3 :]
    mixed_ref, *kept_refs, attended, grads, wide, arrived = refs
    heads, lanes = own_ref.shape[1], own_ref.shape[3]
    copies = [
        pltpu.make_async_copy(source, target, arrived.at[index])
        for index, (source, target) in enumerate(zip(field_refs, kept_refs))
    ]
    for copy in copies:
        copy.start()
    half = frames // 2
    mixed_ref[...] = jnp.full(mixed_ref.shape, task_ref[0].astype(jnp.float32))

    def load_upstream(space, head, t, rows):
        if space == 0:
            return own_ref[t, head, rows, :]
        return other_refs[2 * space - 2 + t // half][t % half, head, rows, :]

    places = [
        pl.ds(pl.multiple_of(partner("space", space) * lanes, lanes), lanes)
        for space in range(spaces)
    ]
    for head in range(heads):
        for space, here in enumerate(places):
            attended[head, space, partner("tm", 0)] = own_ref[frames + space, head]
            for distance, ref in enumerate(attended_refs):
                attended[head, space, partner("tm", distance + 1)] = ref[head, :, here]
        mixed = [
            temporal_part(
                length_ref[0],
                lambda t, rows: attended[head, space, t, rows, :],
                functools.partial(load_upstream, space, head),
                lambda rows: gain_ref[head, rows, :],
                wide.at[head % 2, space, 0],
                wide.at[head % 2, space, 1],
                wide.at[head % 2, space, 2],
                grads.at[head, space],
            )
            for space in range(spaces)
        ]
        summed = functools.reduce(jnp.add, mixed)
        mixed_ref[pl.ds(head, 1), :] = jnp.sum(summed.T, axis=0, keepdims=True) * 0.5
        for distance, ref in enumerate(grad_refs):
            frame = partner("tm", distance)
            for space, here in enumerate(places):
                ref[head, :, here] = grads[head, space, frame]
    for copy in copies:
        copy.wait()


def temporal(lengths, task_ids, attended, upstream, gain, fields):
    _, heads, feat, lanes = upstream[0].shape
    frames, spaces = len(attended) + 1, (len(upstream) + 1) // 2
    patches = spaces * lanes
    rows = -(-(heads + 1) // 8) * 8
    operands = [*attended, gain, *upstream]
    in_place = [in_hbm(field) for field in fields]
    block = (heads, spaces, frames, feat, lanes)
    results = pl.pallas_call(
        functools.partial(temporal_kernel, frames, spaces),
        in_specs=[pl.BlockSpec(memory_space=pltpu.SMEM)] * 2
        + [pl.BlockSpec(memory_space=pltpu.VMEM)] * len(operands)
        + [pl.BlockSpec(memory_space=pltpu.HBM)] * len(in_place),
        out_specs=[pl.BlockSpec(memory_space=pltpu.VMEM)] * (frames + 1 + len(fields)),
        scratch_shapes=[
            pltpu.VMEM(block, jnp.bfloat16),
            pltpu.VMEM(block, jnp.bfloat16),
            pltpu.VMEM((2, spaces, 3, frames, feat, lanes), jnp.float32),
            pltpu.SemaphoreType.DMA((len(fields),)),
        ],
        out_shape=[jax.ShapeDtypeStruct((heads, feat, patches), jnp.bfloat16)] * frames
        + [jax.ShapeDtypeStruct((rows, feat), jnp.float32)]
        + [jax.ShapeDtypeStruct(field.shape, field.dtype) for field in fields],
        compiler_params=params(patches),
        cost_estimate=cost(4),
        name="temporal",
    )(lengths, task_ids, *operands, *in_place)
    return list(results[:frames]), results[frames], results[frames + 1 :]


def gain_gradients(axis, heads, frames, clips, mixed_refs, gains_ref, grad_ref):
    tasks = gains_ref.shape[1]
    rows = sum(ref.shape[0] for ref in mixed_refs) // (frames * clips)
    each = mixed_refs[0].shape[0] // rows
    task_ids = lax.broadcasted_iota(jnp.int32, (tasks, HEAD_DIM), 0).astype(jnp.float32)
    for distance in range(frames):
        for head in range(heads):
            mixed = jnp.zeros((tasks, HEAD_DIM), jnp.float32)
            for clip in range(clips):
                block = distance * clips + clip
                ref, start = mixed_refs[block // each], block % each * rows
                task = ref[pl.ds(start + heads, 1), :]
                row = ref[pl.ds(start + head, 1), :]
                mixed = mixed + jnp.where(task_ids == task, row, 0.0)
            start = (partner(axis, distance) * heads + head) * HEAD_DIM
            cols = pl.ds(pl.multiple_of(start, HEAD_DIM), HEAD_DIM)
            grad_ref[0, :, cols] = gains_ref[1, :, cols] * mixed
            grad_ref[1, :, cols] = gains_ref[0, :, cols] * mixed


def swap(field, axis, size, distance):
    return lax.ppermute(field, axis, [(i, i ^ distance) for i in range(size)])


def split_by_heads(
    query_heads, key_heads, value_heads, cotangent, task_ids, lengths, gains, clips, frames, spaces
):
    patches, feat = query_heads.shape[2:]
    heads = feat // HEAD_DIM
    own = heads // frames
    width = own * HEAD_DIM
    queries, key_rows, values = (
        field.reshape(patches, feat) for field in (query_heads, key_heads, value_heads)
    )
    frame = lax.axis_index("tm")

    pieces = list(pack(cotangent.reshape(cotangent.shape[2:]), frames, spaces))
    queries, pieces = lax.optimization_barrier((queries, pieces))
    for distance in range(1, frames):
        pieces[distance] = swap(pieces[distance], "tm", frames, distance)
    fields = (queries, key_rows, values)
    weights, attended = forward("tm", *fields, frames)
    for distance in range(1, frames):
        attended[distance] = swap(attended[distance], "tm", frames, distance)
    backwards, _ = lax.optimization_barrier((pieces[::-1], weights))
    upstream = list(turn(backwards[::-1], attended[0]))
    for index in range(1, len(upstream)):
        upstream[index] = swap(upstream[index], "space", spaces, (index + 1) // 2)
    rows = lax.dynamic_index_in_dim(gains, task_ids[0], 1, keepdims=False)
    product = lax.dynamic_slice_in_dim(rows[0] * rows[1], frame * width, width, 0)
    gain = jnp.broadcast_to(
        product.reshape(own, HEAD_DIM, 1), (own, HEAD_DIM, patches // spaces)
    )
    attended[1], upstream[0] = lax.optimization_barrier((attended[1], upstream[0]))
    upstream[0] = fetch(upstream[0])
    grads, mixed, kept = temporal(
        lengths, task_ids, attended[1:], upstream, gain, fields
    )
    for distance in reversed(range(1, frames)):
        grads[distance] = swap(grads[distance], "tm", frames, distance)
    here = grads[0]
    for bit in range(clips.bit_length() - 1):
        other = swap(mixed, "dp", clips, 1 << bit)
        if bit == 0:
            here, other = lax.optimization_barrier((here, other))
        mixed = jnp.concatenate([mixed, other], axis=0)
    results = backward("tm", kept, weights, [here], [0])
    mixed, results = lax.optimization_barrier((mixed, results))
    near, grads[1] = lax.optimization_barrier((mixed, grads[1]))
    mixed = [mixed, swap(near, "tm", frames, 1)] + [
        swap(mixed, "tm", frames, distance) for distance in range(2, frames)
    ]
    last = range(frames - 1, 0, -1)
    if frames > 2:
        results = backward("tm", kept, weights, [grads[1]], [1], results)
        last = range(frames - 1, 1, -1)
    grad_queries, grad_keys, grad_gains = backward(
        "tm",
        kept,
        weights,
        [grads[distance] for distance in last],
        list(last),
        results,
        mixed,
        gains,
        (own, frames, clips),
    )
    return (
        grad_queries.reshape(query_heads.shape),
        grad_keys.reshape(query_heads.shape),
        grad_gains,
    )


def temporal_grads(attended, upstream, gain_query, gain_keys, length):
    highest = lax.Precision.HIGHEST
    frames = attended.shape[0]
    score_scale = attended.shape[-1] ** (-0.5)
    floats = attended.astype(jnp.float32)
    inverse_rms = lax.rsqrt(jnp.mean(floats * floats, axis=-1, keepdims=True) + 1e-06)
    normed = floats * inverse_rms
    t_query = normed * gain_query
    t_keys = normed * gain_keys
    scores = jnp.einsum("txhd,uxhd->xhtu", t_query, t_keys, precision=highest) * score_scale
    frame_ids = jnp.arange(frames, dtype=jnp.int32)
    allowed = (frame_ids[None, :] <= frame_ids[:, None]) & (frame_ids[None, :] < length)
    scores = jnp.where(allowed, scores, -1e30)
    weights = jax.nn.softmax(scores, axis=-1)
    weights_low = lax.optimization_barrier(weights.astype(jnp.bfloat16)).astype(jnp.float32)
    valid_rows = (frame_ids < length).astype(jnp.float32)
    masked = upstream.astype(jnp.float32) * valid_rows[:, None, None, None]
    grad_weights = jnp.einsum("txhd,uxhd->xhtu", masked, floats, precision=highest)
    from_values = jnp.einsum("xhtu,txhd->uxhd", weights_low, masked, precision=highest)
    grad_scores = (
        weights
        * (grad_weights - jnp.sum(grad_weights * weights, axis=-1, keepdims=True))
        * score_scale
    )
    grad_tquery = jnp.einsum("xhtu,uxhd->txhd", grad_scores, t_keys, precision=highest)
    grad_tkeys = jnp.einsum("xhtu,txhd->uxhd", grad_scores, t_query, precision=highest)
    grad_normed = grad_tquery * gain_query + grad_tkeys * gain_keys
    grad_gain_query = jnp.sum(grad_tquery * normed, axis=(0, 1))
    grad_gain_keys = jnp.sum(grad_tkeys * normed, axis=(0, 1))
    from_norm = inverse_rms * (
        grad_normed - normed * jnp.mean(grad_normed * normed, axis=-1, keepdims=True)
    )
    grad_total = (masked + from_values + from_norm).astype(jnp.bfloat16)
    return (grad_total, grad_gain_query, grad_gain_keys)


def split_by_patches(query_heads, key_heads, value_heads, cotangent, task_ids, lengths, gains):
    patches, feat = query_heads.shape[2:]
    heads = feat // HEAD_DIM
    queries, key_rows, values = (
        field.reshape(patches, feat) for field in (query_heads, key_heads, value_heads)
    )
    fields = (queries, key_rows, values)
    weights, attended = forward(None, *fields, 1)
    attended_field = jnp.transpose(attended[0], (2, 0, 1)).reshape(1, 1, patches, feat)
    upstream = lax.all_to_all(
        lax.all_to_all(cotangent, "space", split_axis=3, concat_axis=2, tiled=True),
        "tm",
        split_axis=2,
        concat_axis=1,
        tiled=True,
    )
    frames_attended = lax.all_to_all(attended_field, "tm", split_axis=2, concat_axis=1, tiled=True)
    frames, local_patches = frames_attended.shape[1:3]
    selector = (task_ids[0] == jnp.arange(gains.shape[1], dtype=jnp.int32)).astype(jnp.float32)
    gain_query = jnp.sum(selector[:, None] * gains[0], axis=0).reshape(heads, HEAD_DIM)
    gain_keys = jnp.sum(selector[:, None] * gains[1], axis=0).reshape(heads, HEAD_DIM)
    grad_total, grad_gq, grad_gk = temporal_grads(
        frames_attended.reshape(frames, local_patches, heads, HEAD_DIM),
        upstream.reshape(frames, local_patches, heads, HEAD_DIM),
        gain_query,
        gain_keys,
        lengths[0],
    )
    gain_terms = jnp.stack(
        [
            selector[:, None] * grad_gq.reshape(1, feat),
            selector[:, None] * grad_gk.reshape(1, feat),
        ]
    )
    grad_gains = lax.psum(gain_terms, ("dp", "tm"))
    returned = lax.all_to_all(
        grad_total.reshape(1, frames, local_patches, feat),
        "tm",
        split_axis=1,
        concat_axis=2,
        tiled=True,
    )
    head_grads = jnp.transpose(returned.reshape(patches, heads, HEAD_DIM), (1, 2, 0))
    grad_queries, grad_keys = backward(None, fields, weights, [head_grads], [0])
    return (
        grad_queries.reshape(query_heads.shape),
        grad_keys.reshape(query_heads.shape),
        grad_gains,
    )


def solution(mesh):
    clips, frames, spaces = (mesh.shape[axis] for axis in ("dp", "tm", "space"))

    def local(query_heads, *others):
        heads = query_heads.shape[3] // HEAD_DIM
        powers = all(size & (size - 1) == 0 for size in (clips, frames, spaces))
        if powers and 2 <= frames <= 4 and heads % frames == 0:
            return split_by_heads(query_heads, *others, clips, frames, spaces)
        return split_by_patches(query_heads, *others)

    return jax.shard_map(
        local,
        mesh=mesh,
        in_specs=(
            P("dp", "tm", None, "space"),
            P("dp", "tm", None, "space"),
            P("dp", "tm", None, "space"),
            P("dp", "tm", "space", None),
            P("dp"),
            P("dp"),
            P(None, None, "space"),
        ),
        out_specs=(
            P("dp", "tm", None, "space"),
            P("dp", "tm", None, "space"),
            P(None, None, "space"),
        ),
        check_vma=False,
    )
```

```python
import functools

import jax
import jax.numpy as jnp
from jax import lax
from jax.experimental import pallas as pl
from jax.experimental.pallas import tpu as pltpu
from jax.sharding import PartitionSpec as P

HEAD_DIM = 128
GROUP = 16
MIB = 1024 * 1024


def params(patches):
    return pltpu.CompilerParams(vmem_limit_bytes=(16 if patches <= 512 else 60) * MIB)


def cost(microseconds):
    return pl.CostEstimate(flops=int(microseconds * 1e8), bytes_accessed=0, transcendentals=0)


def in_hbm(field):
    return pltpu.with_memory_space_constraint(field, pltpu.HBM)


def columns_dot(left, right):
    return lax.dot_general(
        left, right, (((1,), (1,)), ((), ())), preferred_element_type=jnp.float32
    )


def dot(left, right):
    return jnp.dot(left, right, preferred_element_type=jnp.float32)


def partner(axis, distance):
    return distance if axis is None else jnp.bitwise_xor(lax.axis_index(axis), distance)


def forward_kernel(axis, query_ref, key_ref, value_ref, weights_ref, *refs):
    (queries, key_rows, values, arrived), attended_refs = refs[-4:], refs[:-4]
    score_scale = HEAD_DIM ** (-0.5)
    groups, _, width = queries.shape
    own = width // HEAD_DIM
    copies = []
    for group in range(groups):
        cols = pl.ds(pl.multiple_of(partner(axis, group) * width, HEAD_DIM), width)
        for field, (source, target) in enumerate(
            ((query_ref, queries), (key_ref, key_rows), (value_ref, values))
        ):
            copy = pltpu.make_async_copy(
                source.at[:, cols], target.at[group], arrived.at[group, field]
            )
            copy.start()
            copies.append(copy)
    for group in range(groups):
        for copy in copies[3 * group : 3 * group + 3]:
            copy.wait()
        for head in range(own):
            cols = pl.ds(head * HEAD_DIM, HEAD_DIM)
            scores = columns_dot(key_rows[group, :, cols], queries[group, :, cols])
            largest = jnp.max(scores, axis=0, keepdims=True)
            raised = jnp.exp((scores - largest) * score_scale)
            weights = raised * (1.0 / jnp.sum(raised, axis=0, keepdims=True))
            weights_ref[group * own + head] = weights
            attended = dot(values[group, :, cols].T, weights.astype(jnp.bfloat16))
            attended_refs[group][head] = attended.astype(jnp.bfloat16)


def forward(axis, queries, key_rows, values, groups):
    patches, feat = queries.shape
    heads = feat // HEAD_DIM
    own = heads // groups
    fields = [in_hbm(field) for field in (queries, key_rows, values)]
    weights, *attended = pl.pallas_call(
        functools.partial(forward_kernel, axis),
        in_specs=[pl.BlockSpec(memory_space=pltpu.HBM)] * 3,
        out_specs=[pl.BlockSpec(memory_space=pltpu.VMEM)] * (1 + groups),
        scratch_shapes=[pltpu.VMEM((groups, patches, feat // groups), jnp.bfloat16)] * 3
        + [pltpu.SemaphoreType.DMA((groups, 3))],
        out_shape=[jax.ShapeDtypeStruct((heads, patches, patches), jnp.float32)]
        + [jax.ShapeDtypeStruct((own, HEAD_DIM, patches), jnp.bfloat16)] * groups,
        compiler_params=params(patches),
        cost_estimate=cost(6),
        name="spatial_forward",
    )(*fields)
    return weights, attended


def backward_group(axis, fields, weights_ref, grad_ref, distance, scratch, results, sent):
    query_ref, key_ref, value_ref = fields
    score_scale = HEAD_DIM ** (-0.5)
    own = grad_ref.shape[0]
    start = partner(axis, distance) * (own * HEAD_DIM)
    columns = [
        pl.ds(pl.multiple_of(start + head * HEAD_DIM, HEAD_DIM), HEAD_DIM) for head in range(own)
    ]
    spatial_grads = [dot(value_ref[:, columns[head]], grad_ref[head]) for head in range(own)]
    all_scores = []
    for head, spatial_grad in enumerate(spatial_grads):
        weights = weights_ref[distance * own + head]
        row_sum = jnp.sum(spatial_grad * weights, axis=0, keepdims=True)
        scores = weights * (spatial_grad - row_sum) * score_scale
        all_scores.append(scores.astype(jnp.bfloat16))
    gq, gk = scratch
    for head, scores in enumerate(all_scores):
        cols = pl.ds(head * HEAD_DIM, HEAD_DIM)
        gk[:, cols] = dot(scores, query_ref[:, columns[head]]).astype(jnp.bfloat16)
        gq[:, cols] = dot(key_ref[:, columns[head]].T, scores).astype(jnp.bfloat16).T
    there = pl.ds(pl.multiple_of(start, HEAD_DIM), own * HEAD_DIM)
    copies = [
        pltpu.make_async_copy(source, target.at[:, there], sent.at[side])
        for side, (source, target) in enumerate(zip(scratch, results))
    ]
    for copy in copies:
        copy.start()
    return copies


def backward_kernel(axis, distances, gains_of, *refs):
    fields, weights_ref, refs = refs[:3], refs[3], refs[4:]
    grad_refs, refs = refs[: len(distances)], refs[len(distances) :]
    *refs, gq, gk, sent = refs
    copies = []
    if gains_of:
        *mixed_refs, gains_ref, _, _, gq_ref, gk_ref, grad_gains_ref, grad_gains = refs
        gain_gradients(axis, *gains_of, mixed_refs, gains_ref, grad_gains)
        copy = pltpu.make_async_copy(grad_gains, grad_gains_ref, sent.at[len(distances), 0])
        copy.start()
        copies.append(copy)
    else:
        gq_ref, gk_ref = refs[-2:]
    for place, (distance, grad_ref) in enumerate(zip(distances, grad_refs)):
        copies += backward_group(
            axis,
            fields,
            weights_ref,
            grad_ref,
            distance,
            (gq.at[place], gk.at[place]),
            (gq_ref, gk_ref),
            sent.at[place],
        )
    for copy in copies:
        copy.wait()


def backward(axis, fields, weights, grads, distances, earlier=(), mixed=(), gains=None, gains_of=()):
    patches, feat = fields[0].shape
    own = grads[0].shape[0]
    operands = [*fields, weights, *grads] + ([*mixed, gains] if gains_of else [])
    block = pltpu.VMEM((len(distances), patches, own * HEAD_DIM), jnp.bfloat16)
    out_shape = [jax.ShapeDtypeStruct((patches, feat), jnp.bfloat16)] * 2
    scratch = [block, block, pltpu.SemaphoreType.DMA((len(distances) + 1, 2))]
    if gains_of:
        out_shape.append(jax.ShapeDtypeStruct(gains.shape, jnp.float32))
        scratch.insert(0, pltpu.VMEM(gains.shape, jnp.float32))
    return pl.pallas_call(
        functools.partial(backward_kernel, axis, distances, gains_of),
        in_specs=[pl.BlockSpec(memory_space=pltpu.VMEM)] * len(operands)
        + [pl.BlockSpec(memory_space=pl.ANY)] * len(earlier),
        out_specs=[pl.BlockSpec(memory_space=pl.ANY)] * len(out_shape),
        scratch_shapes=scratch,
        out_shape=out_shape,
        input_output_aliases={len(operands) + index: index for index in range(len(earlier))},
        compiler_params=params(patches),
        cost_estimate=cost(2),
        name="spatial_backward",
    )(*operands, *earlier)


def pack_kernel(field_ref, *refs):
    *packed_refs, rows, arrived = refs
    chunks, size, _ = rows.shape
    spaces, _, width = packed_refs[0].shape
    copies = [
        pltpu.make_async_copy(
            field_ref.at[pl.ds(chunk * size, size), :], rows.at[chunk], arrived.at[chunk]
        )
        for chunk in range(chunks)
    ]
    for copy in copies:
        copy.start()
    for chunk, copy in enumerate(copies):
        copy.wait()
        for distance, packed_ref in enumerate(packed_refs):
            for space in range(spaces):
                start = (space * len(packed_refs) + partner("tm", distance)) * width
                cols = pl.ds(pl.multiple_of(start, HEAD_DIM), width)
                packed_ref[space, pl.ds(chunk * size, size), :] = rows[chunk, :, cols]


def pack(field, frames, spaces):
    patches, feat = field.shape
    chunks = patches // GROUP
    shape = (spaces, patches, feat // (frames * spaces))
    return pl.pallas_call(
        pack_kernel,
        in_specs=[pl.BlockSpec(memory_space=pltpu.HBM)],
        out_specs=[pl.BlockSpec(memory_space=pltpu.VMEM)] * frames,
        out_shape=[jax.ShapeDtypeStruct(shape, field.dtype)] * frames,
        scratch_shapes=[
            pltpu.VMEM((chunks, patches // chunks, feat), field.dtype),
            pltpu.SemaphoreType.DMA((chunks,)),
        ],
        compiler_params=params(patches),
        cost_estimate=cost(1),
        name="pack_cotangent",
    )(in_hbm(field))


def turn_kernel(frames, *refs):
    piece_refs, (plane_ref, own_hbm, *other_refs), (turned, own_ref, sent) = (
        refs[:frames][::-1],
        refs[frames:-3],
        refs[-3:],
    )
    spaces, lanes, _ = piece_refs[0].shape
    for space in range(spaces):
        place = pl.multiple_of(partner("space", space) * lanes, lanes)
        own_ref[frames + space] = plane_ref[:, :, pl.ds(place, lanes)]
    heads = own_ref.shape[1]
    for space in range(spaces):
        target = turned if space else own_ref
        source = partner("space", space)
        for distance, ref in enumerate(piece_refs):
            frame = partner("tm", distance)
            for head in range(heads):
                cols = pl.ds(head * HEAD_DIM, HEAD_DIM)
                target[frame, head] = ref[source, :, cols].T
        if space == 0:
            copy = pltpu.make_async_copy(own_ref, own_hbm, sent)
            copy.start()
        else:
            half = frames // 2
            other_refs[2 * space - 2][...] = turned[:half]
            other_refs[2 * space - 1][...] = turned[half:]
    copy.wait()


def turn(pieces, plane):
    spaces, patches, feat = pieces[0].shape
    frames, heads = len(pieces), feat // HEAD_DIM
    turned = (heads, HEAD_DIM, patches)
    sizes = [frames + spaces] + [frames // 2, frames - frames // 2] * (spaces - 1)
    return pl.pallas_call(
        functools.partial(turn_kernel, frames),
        in_specs=[pl.BlockSpec(memory_space=pltpu.VMEM)] * (frames + 1),
        out_specs=[pl.BlockSpec(memory_space=pltpu.HBM)]
        + [pl.BlockSpec(memory_space=pltpu.VMEM)] * (len(sizes) - 1),
        out_shape=[jax.ShapeDtypeStruct((size,) + turned, pieces[0].dtype) for size in sizes],
        scratch_shapes=[
            pltpu.VMEM((frames,) + turned, pieces[0].dtype),
            pltpu.VMEM((frames + spaces,) + turned, pieces[0].dtype),
            pltpu.SemaphoreType.DMA,
        ],
        compiler_params=params(patches),
        cost_estimate=cost(2),
        name="turn_cotangent",
    )(*reversed(pieces), plane)


def temporal_part(length, load_attended, load_upstream, load_gain, fields, ups, normed, grad_ref):
    frames, feat, lanes = grad_ref.shape
    half = GROUP // 2
    score_scale = feat ** (-0.5)
    pairs = [(t, u) for t in range(frames) for u in range(t + 1)]
    every = range(frames)
    valid = [jnp.where(t < length, 1.0, 0.0).astype(jnp.float32) for t in every]
    bias = [jnp.where(u < length, 0.0, -1e30).astype(jnp.float32) for u in every]

    def total(piece):
        return jnp.broadcast_to(jnp.sum(piece, axis=0, keepdims=True), (half, lanes))

    squares = [jnp.zeros((half, lanes), jnp.float32) for _ in every]
    for group in range(feat // GROUP):
        rows = pl.ds(group * GROUP, GROUP)
        for t in every:
            field = load_attended(t, rows).astype(jnp.float32)
            fields[t, rows, :] = field
            ups[t, rows, :] = load_upstream(t, rows).astype(jnp.float32)
            low, high = field[:half], field[half:]
            squares[t] = squares[t] + (low * low + high * high)
    inverse = [lax.rsqrt(total(squares[t]) * (1.0 / feat) + 1e-06) for t in every]

    raw = {pair: jnp.zeros((half, lanes), jnp.float32) for pair in pairs}
    grad = {pair: jnp.zeros((half, lanes), jnp.float32) for pair in pairs}
    for group in range(feat // half):
        rows = pl.ds(group * half, half)
        gain = load_gain(rows)
        here = [fields[t, rows, :] for t in every]
        above = [ups[t, rows, :] for t in every]
        scaled = [here[t] * inverse[t] for t in every]
        gained = [scaled[t] * gain for t in every]
        for t in every:
            normed[t, rows, :] = scaled[t]
        for t, u in pairs:
            raw[t, u] = raw[t, u] + gained[t] * scaled[u]
            grad[t, u] = grad[t, u] + above[t] * here[u]

    value_part, score_part = {}, {}
    for t in every:
        seen = range(t + 1)
        for u in seen:
            raw[t, u] = total(raw[t, u])
            grad[t, u] = total(grad[t, u]) * valid[t]
        scores = [raw[t, u] * score_scale + bias[u] for u in seen]
        largest = functools.reduce(jnp.maximum, scores)
        raised = [jnp.exp(score - largest) for score in scores]
        over = 1.0 / functools.reduce(jnp.add, raised)
        weights = [piece * over for piece in raised]
        mean_grad = functools.reduce(jnp.add, [weights[u] * grad[t, u] for u in seen])
        for u in seen:
            rounded = weights[u].astype(jnp.bfloat16).astype(jnp.float32)
            value_part[t, u] = (rounded + (1.0 if u == t else 0.0)) * valid[t]
            score_part[t, u] = weights[u] * (grad[t, u] - mean_grad) * score_scale

    both = {(t, u): score_part[t, u] * (2.0 if t == u else 1.0) for t, u in pairs}
    both.update({(u, t): both[t, u] for t, u in pairs})
    raw.update({(u, t): raw[t, u] for t, u in pairs})
    mean_part = [
        functools.reduce(jnp.add, [both[u, v] * raw[u, v] for v in every]) * (1.0 / feat)
        for u in every
    ]

    all_mixed = []
    for group in range(feat // GROUP):
        outs = [[] for _ in every]
        for side in range(2):
            rows = pl.ds(group * GROUP + side * half, half)
            gain = load_gain(rows)
            scaled = [normed[t, rows, :] for t in every]
            above = [ups[t, rows, :] for t in every]
            mixed = jnp.zeros((half, lanes), jnp.float32)
            for u in every:
                crossed = functools.reduce(jnp.add, [both[u, v] * scaled[v] for v in every])
                mixed = mixed + crossed * scaled[u]
                from_norm = inverse[u] * (gain * crossed - scaled[u] * mean_part[u])
                direct = functools.reduce(
                    jnp.add, [value_part[t, u] * above[t] for t in range(u, frames)]
                )
                outs[u].append(direct + from_norm)
            all_mixed.append(mixed)
        for u in every:
            grad_ref[u, pl.ds(group * GROUP, GROUP), :] = jnp.concatenate(
                outs[u], axis=0
            ).astype(jnp.bfloat16)
    return jnp.concatenate(all_mixed, axis=0)


def fetch_kernel(*refs):
    *refs, arrived = refs
    number = len(refs) // 2
    copies = [
        pltpu.make_async_copy(source, target, arrived.at[index])
        for index, (source, target) in enumerate(zip(refs[:number], refs[number:]))
    ]
    for copy in copies:
        copy.start()
    for copy in copies:
        copy.wait()


def fetch(*fields):
    return pl.pallas_call(
        fetch_kernel,
        in_specs=[pl.BlockSpec(memory_space=pltpu.HBM)] * len(fields),
        out_specs=[pl.BlockSpec(memory_space=pltpu.VMEM)] * len(fields),
        out_shape=[jax.ShapeDtypeStruct(field.shape, field.dtype) for field in fields],
        scratch_shapes=[pltpu.SemaphoreType.DMA((len(fields),))],
        compiler_params=params(0),
        cost_estimate=cost(1),
        name="fetch",
    )(*[in_hbm(field) for field in fields])


def temporal_kernel(frames, spaces, length_ref, task_ref, *refs):
    attended_refs, (gain_ref, own_ref, *other_refs), refs = (
        refs[: frames - 1],
        refs[frames - 1 : frames - 1 + 2 * spaces],
        refs[frames - 1 + 2 * spaces :],
    )
    grad_refs, (mixed_ref, attended, grads, wide) = refs[:frames], refs[frames:]
    heads, lanes = own_ref.shape[1], own_ref.shape[3]
    half = frames // 2
    mixed_ref[...] = jnp.full(mixed_ref.shape, task_ref[0].astype(jnp.float32))

    def load_upstream(space, head, t, rows):
        if space == 0:
            return own_ref[t, head, rows, :]
        return other_refs[2 * space - 2 + t // half][t % half, head, rows, :]

    places = [
        pl.ds(pl.multiple_of(partner("space", space) * lanes, lanes), lanes)
        for space in range(spaces)
    ]
    for head in range(heads):
        for space, here in enumerate(places):
            attended[head, space, partner("tm", 0)] = own_ref[frames + space, head]
            for distance, ref in enumerate(attended_refs):
                attended[head, space, partner("tm", distance + 1)] = ref[head, :, here]
        mixed = [
            temporal_part(
                length_ref[0],
                lambda t, rows: attended[head, space, t, rows, :],
                functools.partial(load_upstream, space, head),
                lambda rows: gain_ref[head, rows, :],
                wide.at[head % 2, space, 0],
                wide.at[head % 2, space, 1],
                wide.at[head % 2, space, 2],
                grads.at[head, space],
            )
            for space in range(spaces)
        ]
        summed = functools.reduce(jnp.add, mixed)
        mixed_ref[pl.ds(head, 1), :] = jnp.sum(summed.T, axis=0, keepdims=True) * 0.5
        for distance, ref in enumerate(grad_refs):
            frame = partner("tm", distance)
            for space, here in enumerate(places):
                ref[head, :, here] = grads[head, space, frame]


def temporal(lengths, task_ids, attended, upstream, gain):
    _, heads, feat, lanes = upstream[0].shape
    frames, spaces = len(attended) + 1, (len(upstream) + 1) // 2
    patches = spaces * lanes
    rows = -(-(heads + 1) // 8) * 8
    operands = [*attended, gain, *upstream]
    block = (heads, spaces, frames, feat, lanes)
    results = pl.pallas_call(
        functools.partial(temporal_kernel, frames, spaces),
        in_specs=[pl.BlockSpec(memory_space=pltpu.SMEM)] * 2
        + [pl.BlockSpec(memory_space=pltpu.VMEM)] * len(operands),
        out_specs=[pl.BlockSpec(memory_space=pltpu.VMEM)] * (frames + 1),
        scratch_shapes=[
            pltpu.VMEM(block, jnp.bfloat16),
            pltpu.VMEM(block, jnp.bfloat16),
            pltpu.VMEM((2, spaces, 3, frames, feat, lanes), jnp.float32),
        ],
        out_shape=[jax.ShapeDtypeStruct((heads, feat, patches), jnp.bfloat16)] * frames
        + [jax.ShapeDtypeStruct((rows, feat), jnp.float32)],
        compiler_params=params(patches),
        cost_estimate=cost(4),
        name="temporal",
    )(lengths, task_ids, *operands)
    return list(results[:frames]), results[frames]


def gain_gradients(axis, heads, frames, clips, mixed_refs, gains_ref, grad_ref):
    tasks = gains_ref.shape[1]
    rows = sum(ref.shape[0] for ref in mixed_refs) // (frames * clips)
    each = mixed_refs[0].shape[0] // rows
    task_ids = lax.broadcasted_iota(jnp.int32, (tasks, HEAD_DIM), 0).astype(jnp.float32)
    for distance in range(frames):
        for head in range(heads):
            mixed = jnp.zeros((tasks, HEAD_DIM), jnp.float32)
            for clip in range(clips):
                block = distance * clips + clip
                ref, start = mixed_refs[block // each], block % each * rows
                task = ref[pl.ds(start + heads, 1), :]
                row = ref[pl.ds(start + head, 1), :]
                mixed = mixed + jnp.where(task_ids == task, row, 0.0)
            start = (partner(axis, distance) * heads + head) * HEAD_DIM
            cols = pl.ds(pl.multiple_of(start, HEAD_DIM), HEAD_DIM)
            grad_ref[0, :, cols] = gains_ref[1, :, cols] * mixed
            grad_ref[1, :, cols] = gains_ref[0, :, cols] * mixed


def swap(field, axis, size, distance):
    return lax.ppermute(field, axis, [(i, i ^ distance) for i in range(size)])


def split_by_heads(
    query_heads, key_heads, value_heads, cotangent, task_ids, lengths, gains, clips, frames, spaces
):
    patches, feat = query_heads.shape[2:]
    heads = feat // HEAD_DIM
    own = heads // frames
    width = own * HEAD_DIM
    queries, key_rows, values = (
        field.reshape(patches, feat) for field in (query_heads, key_heads, value_heads)
    )
    frame = lax.axis_index("tm")

    pieces = list(pack(cotangent.reshape(cotangent.shape[2:]), frames, spaces))
    queries, pieces = lax.optimization_barrier((queries, pieces))
    for distance in range(1, frames):
        pieces[distance] = swap(pieces[distance], "tm", frames, distance)
    fields = (queries, key_rows, values)
    weights, attended = forward("tm", *fields, frames)
    for distance in range(1, frames):
        attended[distance] = swap(attended[distance], "tm", frames, distance)
    backwards, _ = lax.optimization_barrier((pieces[::-1], weights))
    upstream = list(turn(backwards[::-1], attended[0]))
    for index in range(1, len(upstream)):
        upstream[index] = swap(upstream[index], "space", spaces, (index + 1) // 2)
    rows = lax.dynamic_index_in_dim(gains, task_ids[0], 1, keepdims=False)
    product = lax.dynamic_slice_in_dim(rows[0] * rows[1], frame * width, width, 0)
    gain = jnp.broadcast_to(
        product.reshape(own, HEAD_DIM, 1), (own, HEAD_DIM, patches // spaces)
    )
    attended[1], gain, upstream[0] = lax.optimization_barrier((attended[1], gain, upstream[0]))
    upstream[0], *kept = fetch(upstream[0], *fields)
    grads, mixed = temporal(lengths, task_ids, attended[1:], upstream, gain)
    for distance in reversed(range(1, frames)):
        grads[distance] = swap(grads[distance], "tm", frames, distance)
    here = grads[0]
    for bit in range(clips.bit_length() - 1):
        other = swap(mixed, "dp", clips, 1 << bit)
        if bit == 0:
            here, other = lax.optimization_barrier((here, other))
        mixed = jnp.concatenate([mixed, other], axis=0)
    results = backward("tm", kept, weights, [here], [0])
    mixed, results = lax.optimization_barrier((mixed, results))
    near, grads[1] = lax.optimization_barrier((mixed, grads[1]))
    mixed = [mixed, swap(near, "tm", frames, 1)] + [
        swap(mixed, "tm", frames, distance) for distance in range(2, frames)
    ]
    last = range(frames - 1, 0, -1)
    if frames > 2:
        results = backward("tm", kept, weights, [grads[1]], [1], results)
        last = range(frames - 1, 1, -1)
    grad_queries, grad_keys, grad_gains = backward(
        "tm",
        kept,
        weights,
        [grads[distance] for distance in last],
        list(last),
        results,
        mixed,
        gains,
        (own, frames, clips),
    )
    return (
        grad_queries.reshape(query_heads.shape),
        grad_keys.reshape(query_heads.shape),
        grad_gains,
    )


def temporal_grads(attended, upstream, gain_query, gain_keys, length):
    highest = lax.Precision.HIGHEST
    frames = attended.shape[0]
    score_scale = attended.shape[-1] ** (-0.5)
    floats = attended.astype(jnp.float32)
    inverse_rms = lax.rsqrt(jnp.mean(floats * floats, axis=-1, keepdims=True) + 1e-06)
    normed = floats * inverse_rms
    t_query = normed * gain_query
    t_keys = normed * gain_keys
    scores = jnp.einsum("txhd,uxhd->xhtu", t_query, t_keys, precision=highest) * score_scale
    frame_ids = jnp.arange(frames, dtype=jnp.int32)
    allowed = (frame_ids[None, :] <= frame_ids[:, None]) & (frame_ids[None, :] < length)
    scores = jnp.where(allowed, scores, -1e30)
    weights = jax.nn.softmax(scores, axis=-1)
    weights_low = lax.optimization_barrier(weights.astype(jnp.bfloat16)).astype(jnp.float32)
    valid_rows = (frame_ids < length).astype(jnp.float32)
    masked = upstream.astype(jnp.float32) * valid_rows[:, None, None, None]
    grad_weights = jnp.einsum("txhd,uxhd->xhtu", masked, floats, precision=highest)
    from_values = jnp.einsum("xhtu,txhd->uxhd", weights_low, masked, precision=highest)
    grad_scores = (
        weights
        * (grad_weights - jnp.sum(grad_weights * weights, axis=-1, keepdims=True))
        * score_scale
    )
    grad_tquery = jnp.einsum("xhtu,uxhd->txhd", grad_scores, t_keys, precision=highest)
    grad_tkeys = jnp.einsum("xhtu,txhd->uxhd", grad_scores, t_query, precision=highest)
    grad_normed = grad_tquery * gain_query + grad_tkeys * gain_keys
    grad_gain_query = jnp.sum(grad_tquery * normed, axis=(0, 1))
    grad_gain_keys = jnp.sum(grad_tkeys * normed, axis=(0, 1))
    from_norm = inverse_rms * (
        grad_normed - normed * jnp.mean(grad_normed * normed, axis=-1, keepdims=True)
    )
    grad_total = (masked + from_values + from_norm).astype(jnp.bfloat16)
    return (grad_total, grad_gain_query, grad_gain_keys)


def split_by_patches(query_heads, key_heads, value_heads, cotangent, task_ids, lengths, gains):
    patches, feat = query_heads.shape[2:]
    heads = feat // HEAD_DIM
    queries, key_rows, values = (
        field.reshape(patches, feat) for field in (query_heads, key_heads, value_heads)
    )
    fields = (queries, key_rows, values)
    weights, attended = forward(None, *fields, 1)
    attended_field = jnp.transpose(attended[0], (2, 0, 1)).reshape(1, 1, patches, feat)
    upstream = lax.all_to_all(
        lax.all_to_all(cotangent, "space", split_axis=3, concat_axis=2, tiled=True),
        "tm",
        split_axis=2,
        concat_axis=1,
        tiled=True,
    )
    frames_attended = lax.all_to_all(attended_field, "tm", split_axis=2, concat_axis=1, tiled=True)
    frames, local_patches = frames_attended.shape[1:3]
    selector = (task_ids[0] == jnp.arange(gains.shape[1], dtype=jnp.int32)).astype(jnp.float32)
    gain_query = jnp.sum(selector[:, None] * gains[0], axis=0).reshape(heads, HEAD_DIM)
    gain_keys = jnp.sum(selector[:, None] * gains[1], axis=0).reshape(heads, HEAD_DIM)
    grad_total, grad_gq, grad_gk = temporal_grads(
        frames_attended.reshape(frames, local_patches, heads, HEAD_DIM),
        upstream.reshape(frames, local_patches, heads, HEAD_DIM),
        gain_query,
        gain_keys,
        lengths[0],
    )
    gain_terms = jnp.stack(
        [
            selector[:, None] * grad_gq.reshape(1, feat),
            selector[:, None] * grad_gk.reshape(1, feat),
        ]
    )
    grad_gains = lax.psum(gain_terms, ("dp", "tm"))
    returned = lax.all_to_all(
        grad_total.reshape(1, frames, local_patches, feat),
        "tm",
        split_axis=1,
        concat_axis=2,
        tiled=True,
    )
    head_grads = jnp.transpose(returned.reshape(patches, heads, HEAD_DIM), (1, 2, 0))
    grad_queries, grad_keys = backward(None, fields, weights, [head_grads], [0])
    return (
        grad_queries.reshape(query_heads.shape),
        grad_keys.reshape(query_heads.shape),
        grad_gains,
    )


def solution(mesh):
    clips, frames, spaces = (mesh.shape[axis] for axis in ("dp", "tm", "space"))

    def local(query_heads, *others):
        heads = query_heads.shape[3] // HEAD_DIM
        powers = all(size & (size - 1) == 0 for size in (clips, frames, spaces))
        if powers and 2 <= frames <= 4 and heads % frames == 0:
            return split_by_heads(query_heads, *others, clips, frames, spaces)
        return split_by_patches(query_heads, *others)

    return jax.shard_map(
        local,
        mesh=mesh,
        in_specs=(
            P("dp", "tm", None, "space"),
            P("dp", "tm", None, "space"),
            P("dp", "tm", None, "space"),
            P("dp", "tm", "space", None),
            P("dp"),
            P("dp"),
            P(None, None, "space"),
        ),
        out_specs=(
            P("dp", "tm", None, "space"),
            P("dp", "tm", None, "space"),
            P(None, None, "space"),
        ),
        check_vma=False,
    )
```

```python
import functools

import jax
import jax.numpy as jnp
from jax import lax
from jax.experimental import pallas as pl
from jax.experimental.pallas import tpu as pltpu
from jax.sharding import PartitionSpec as P

HEAD_DIM = 128
GROUP = 16
MIB = 1024 * 1024


def params(patches):
    return pltpu.CompilerParams(vmem_limit_bytes=(16 if patches <= 512 else 60) * MIB)


def cost(microseconds):
    return pl.CostEstimate(flops=int(microseconds * 1e8), bytes_accessed=0, transcendentals=0)


def in_hbm(field):
    return pltpu.with_memory_space_constraint(field, pltpu.HBM)


def columns_dot(left, right):
    return lax.dot_general(
        left, right, (((1,), (1,)), ((), ())), preferred_element_type=jnp.float32
    )


def dot(left, right):
    return jnp.dot(left, right, preferred_element_type=jnp.float32)


def partner(axis, distance):
    return distance if axis is None else jnp.bitwise_xor(lax.axis_index(axis), distance)


def forward_kernel(axis, query_ref, key_ref, value_ref, weights_ref, *refs):
    (queries, key_rows, values, arrived), attended_refs = refs[-4:], refs[:-4]
    score_scale = HEAD_DIM ** (-0.5)
    groups, _, width = queries.shape
    own = width // HEAD_DIM
    copies = []
    for group in range(groups):
        cols = pl.ds(pl.multiple_of(partner(axis, group) * width, HEAD_DIM), width)
        for field, (source, target) in enumerate(
            ((query_ref, queries), (key_ref, key_rows), (value_ref, values))
        ):
            copy = pltpu.make_async_copy(
                source.at[:, cols], target.at[group], arrived.at[group, field]
            )
            copy.start()
            copies.append(copy)
    for group in range(groups):
        for copy in copies[3 * group : 3 * group + 3]:
            copy.wait()
        for head in range(own):
            cols = pl.ds(head * HEAD_DIM, HEAD_DIM)
            scores = columns_dot(key_rows[group, :, cols], queries[group, :, cols])
            largest = jnp.max(scores, axis=0, keepdims=True)
            raised = jnp.exp((scores - largest) * score_scale)
            weights = raised * (1.0 / jnp.sum(raised, axis=0, keepdims=True))
            weights_ref[group * own + head] = weights
            attended = dot(values[group, :, cols].T, weights.astype(jnp.bfloat16))
            attended_refs[group][head] = attended.astype(jnp.bfloat16)


def forward(axis, queries, key_rows, values, groups):
    patches, feat = queries.shape
    heads = feat // HEAD_DIM
    own = heads // groups
    fields = [in_hbm(field) for field in (queries, key_rows, values)]
    weights, *attended = pl.pallas_call(
        functools.partial(forward_kernel, axis),
        in_specs=[pl.BlockSpec(memory_space=pltpu.HBM)] * 3,
        out_specs=[pl.BlockSpec(memory_space=pltpu.VMEM)] * (1 + groups),
        scratch_shapes=[pltpu.VMEM((groups, patches, feat // groups), jnp.bfloat16)] * 3
        + [pltpu.SemaphoreType.DMA((groups, 3))],
        out_shape=[jax.ShapeDtypeStruct((heads, patches, patches), jnp.float32)]
        + [jax.ShapeDtypeStruct((own, HEAD_DIM, patches), jnp.bfloat16)] * groups,
        compiler_params=params(patches),
        cost_estimate=cost(6),
        name="spatial_forward",
    )(*fields)
    return weights, attended


def backward_group(axis, fields, weights_ref, grad_ref, distance, scratch, results, sent):
    query_ref, key_ref, value_ref = fields
    score_scale = HEAD_DIM ** (-0.5)
    own = grad_ref.shape[0]
    start = partner(axis, distance) * (own * HEAD_DIM)
    columns = [
        pl.ds(pl.multiple_of(start + head * HEAD_DIM, HEAD_DIM), HEAD_DIM) for head in range(own)
    ]
    spatial_grads = [dot(value_ref[:, columns[head]], grad_ref[head]) for head in range(own)]
    all_scores = []
    for head, spatial_grad in enumerate(spatial_grads):
        weights = weights_ref[distance * own + head]
        row_sum = jnp.sum(spatial_grad * weights, axis=0, keepdims=True)
        scores = weights * (spatial_grad - row_sum) * score_scale
        all_scores.append(scores.astype(jnp.bfloat16))
    gq, gk = scratch
    for head, scores in enumerate(all_scores):
        cols = pl.ds(head * HEAD_DIM, HEAD_DIM)
        gk[:, cols] = dot(scores, query_ref[:, columns[head]]).astype(jnp.bfloat16)
        gq[:, cols] = dot(key_ref[:, columns[head]].T, scores).astype(jnp.bfloat16).T
    there = pl.ds(pl.multiple_of(start, HEAD_DIM), own * HEAD_DIM)
    copies = [
        pltpu.make_async_copy(source, target.at[:, there], sent.at[side])
        for side, (source, target) in enumerate(zip(scratch, results))
    ]
    for copy in copies:
        copy.start()
    return copies


def backward_kernel(axis, distances, gains_of, *refs):
    fields, weights_ref, refs = refs[:3], refs[3], refs[4:]
    grad_refs, refs = refs[: len(distances)], refs[len(distances) :]
    *refs, gq, gk, sent = refs
    copies = []
    if gains_of:
        *mixed_refs, gains_ref, _, _, gq_ref, gk_ref, grad_gains_ref, grad_gains = refs
        gain_gradients(axis, *gains_of, mixed_refs, gains_ref, grad_gains)
        copy = pltpu.make_async_copy(grad_gains, grad_gains_ref, sent.at[len(distances), 0])
        copy.start()
        copies.append(copy)
    else:
        gq_ref, gk_ref = refs[-2:]
    for place, (distance, grad_ref) in enumerate(zip(distances, grad_refs)):
        copies += backward_group(
            axis,
            fields,
            weights_ref,
            grad_ref,
            distance,
            (gq.at[place], gk.at[place]),
            (gq_ref, gk_ref),
            sent.at[place],
        )
    for copy in copies:
        copy.wait()


def backward(axis, fields, weights, grads, distances, earlier=(), mixed=(), gains=None, gains_of=()):
    patches, feat = fields[0].shape
    own = grads[0].shape[0]
    operands = [*fields, weights, *grads] + ([*mixed, gains] if gains_of else [])
    block = pltpu.VMEM((len(distances), patches, own * HEAD_DIM), jnp.bfloat16)
    out_shape = [jax.ShapeDtypeStruct((patches, feat), jnp.bfloat16)] * 2
    scratch = [block, block, pltpu.SemaphoreType.DMA((len(distances) + 1, 2))]
    if gains_of:
        out_shape.append(jax.ShapeDtypeStruct(gains.shape, jnp.float32))
        scratch.insert(0, pltpu.VMEM(gains.shape, jnp.float32))
    return pl.pallas_call(
        functools.partial(backward_kernel, axis, distances, gains_of),
        in_specs=[pl.BlockSpec(memory_space=pltpu.VMEM)] * len(operands)
        + [pl.BlockSpec(memory_space=pl.ANY)] * len(earlier),
        out_specs=[pl.BlockSpec(memory_space=pl.ANY)] * len(out_shape),
        scratch_shapes=scratch,
        out_shape=out_shape,
        input_output_aliases={len(operands) + index: index for index in range(len(earlier))},
        compiler_params=params(patches),
        cost_estimate=cost(2),
        name="spatial_backward",
    )(*operands, *earlier)


def pack_kernel(field_ref, *refs):
    *packed_refs, rows, arrived = refs
    chunks, size, _ = rows.shape
    spaces, _, width = packed_refs[0].shape
    copies = [
        pltpu.make_async_copy(
            field_ref.at[pl.ds(chunk * size, size), :], rows.at[chunk], arrived.at[chunk]
        )
        for chunk in range(chunks)
    ]
    for copy in copies:
        copy.start()
    for chunk, copy in enumerate(copies):
        copy.wait()
        for distance, packed_ref in enumerate(packed_refs):
            for space in range(spaces):
                start = (space * len(packed_refs) + partner("tm", distance)) * width
                cols = pl.ds(pl.multiple_of(start, HEAD_DIM), width)
                packed_ref[space, pl.ds(chunk * size, size), :] = rows[chunk, :, cols]


def pack(field, frames, spaces):
    patches, feat = field.shape
    chunks = patches // GROUP
    shape = (spaces, patches, feat // (frames * spaces))
    return pl.pallas_call(
        pack_kernel,
        in_specs=[pl.BlockSpec(memory_space=pltpu.HBM)],
        out_specs=[pl.BlockSpec(memory_space=pltpu.VMEM)] * frames,
        out_shape=[jax.ShapeDtypeStruct(shape, field.dtype)] * frames,
        scratch_shapes=[
            pltpu.VMEM((chunks, patches // chunks, feat), field.dtype),
            pltpu.SemaphoreType.DMA((chunks,)),
        ],
        compiler_params=params(patches),
        cost_estimate=cost(1),
        name="pack_cotangent",
    )(in_hbm(field))


def turn_kernel(frames, *refs):
    piece_refs, (plane_ref, own_hbm, *other_refs), (turned, own_ref, sent) = (
        refs[:frames][::-1],
        refs[frames:-3],
        refs[-3:],
    )
    spaces, lanes, _ = piece_refs[0].shape
    for space in range(spaces):
        place = pl.multiple_of(partner("space", space) * lanes, lanes)
        own_ref[frames + space] = plane_ref[:, :, pl.ds(place, lanes)]
    heads = own_ref.shape[1]
    for space in range(spaces):
        target = turned if space else own_ref
        source = partner("space", space)
        for distance, ref in enumerate(piece_refs):
            frame = partner("tm", distance)
            for head in range(heads):
                cols = pl.ds(head * HEAD_DIM, HEAD_DIM)
                target[frame, head] = ref[source, :, cols].T
        if space == 0:
            copy = pltpu.make_async_copy(own_ref, own_hbm, sent)
            copy.start()
        else:
            half = frames // 2
            other_refs[2 * space - 2][...] = turned[:half]
            other_refs[2 * space - 1][...] = turned[half:]
    copy.wait()


def turn(pieces, plane):
    spaces, patches, feat = pieces[0].shape
    frames, heads = len(pieces), feat // HEAD_DIM
    turned = (heads, HEAD_DIM, patches)
    sizes = [frames + spaces] + [frames // 2, frames - frames // 2] * (spaces - 1)
    return pl.pallas_call(
        functools.partial(turn_kernel, frames),
        in_specs=[pl.BlockSpec(memory_space=pltpu.VMEM)] * (frames + 1),
        out_specs=[pl.BlockSpec(memory_space=pltpu.HBM)]
        + [pl.BlockSpec(memory_space=pltpu.VMEM)] * (len(sizes) - 1),
        out_shape=[jax.ShapeDtypeStruct((size,) + turned, pieces[0].dtype) for size in sizes],
        scratch_shapes=[
            pltpu.VMEM((frames,) + turned, pieces[0].dtype),
            pltpu.VMEM((frames + spaces,) + turned, pieces[0].dtype),
            pltpu.SemaphoreType.DMA,
        ],
        compiler_params=params(patches),
        cost_estimate=cost(2),
        name="turn_cotangent",
    )(*reversed(pieces), plane)


class Block:
    def __init__(self, length, load_attended, load_upstream, load_gain, scratch, grad_ref):
        self.load_attended, self.load_upstream = load_attended, load_upstream
        self.load_gain, self.grad_ref = load_gain, grad_ref
        self.fields, self.ups, self.normed = (scratch.at[index] for index in range(3))
        self.frames, self.feat, self.lanes = grad_ref.shape
        self.half = GROUP // 2
        self.every = range(self.frames)
        self.pairs = [(t, u) for t in self.every for u in range(t + 1)]
        self.valid = [jnp.where(t < length, 1.0, 0.0).astype(jnp.float32) for t in self.every]
        self.bias = [jnp.where(u < length, 0.0, -1e30).astype(jnp.float32) for u in self.every]

    def total(self, piece):
        return jnp.broadcast_to(jnp.sum(piece, axis=0, keepdims=True), (self.half, self.lanes))

    def zeros(self):
        return jnp.zeros((self.half, self.lanes), jnp.float32)

    def widen(self):
        squares = [self.zeros() for _ in self.every]
        for group in range(self.feat // GROUP):
            rows = pl.ds(group * GROUP, GROUP)
            for t in self.every:
                field = self.load_attended(t, rows).astype(jnp.float32)
                self.fields[t, rows, :] = field
                self.ups[t, rows, :] = self.load_upstream(t, rows).astype(jnp.float32)
                low, high = field[: self.half], field[self.half :]
                squares[t] = squares[t] + (low * low + high * high)
        self.inverse = [
            lax.rsqrt(self.total(square) * (1.0 / self.feat) + 1e-06) for square in squares
        ]

    def sums(self):
        raw = {pair: self.zeros() for pair in self.pairs}
        grad = {pair: self.zeros() for pair in self.pairs}
        for group in range(self.feat // self.half):
            rows = pl.ds(group * self.half, self.half)
            gain = self.load_gain(rows)
            here = [self.fields[t, rows, :] for t in self.every]
            above = [self.ups[t, rows, :] for t in self.every]
            scaled = [here[t] * self.inverse[t] for t in self.every]
            gained = [scaled[t] * gain for t in self.every]
            for t in self.every:
                self.normed[t, rows, :] = scaled[t]
            for t, u in self.pairs:
                raw[t, u] = raw[t, u] + gained[t] * scaled[u]
                grad[t, u] = grad[t, u] + above[t] * here[u]
        self.raw = {pair: self.total(raw[pair]) for pair in self.pairs}
        self.grad = {pair: self.total(grad[pair]) * self.valid[pair[0]] for pair in self.pairs}

    def weigh(self):
        score_scale = self.feat ** (-0.5)
        raw, grad = self.raw, self.grad
        self.value_part, score_part = {}, {}
        for t in self.every:
            seen = range(t + 1)
            scores = [raw[t, u] * score_scale + self.bias[u] for u in seen]
            largest = functools.reduce(jnp.maximum, scores)
            raised = [jnp.exp(score - largest) for score in scores]
            over = 1.0 / functools.reduce(jnp.add, raised)
            weights = [piece * over for piece in raised]
            mean_grad = functools.reduce(jnp.add, [weights[u] * grad[t, u] for u in seen])
            for u in seen:
                rounded = weights[u].astype(jnp.bfloat16).astype(jnp.float32)
                self.value_part[t, u] = (rounded + (1.0 if u == t else 0.0)) * self.valid[t]
                score_part[t, u] = weights[u] * (grad[t, u] - mean_grad) * score_scale
        both = {(t, u): score_part[t, u] * (2.0 if t == u else 1.0) for t, u in self.pairs}
        both.update({(u, t): both[t, u] for t, u in self.pairs})
        raw.update({(u, t): raw[t, u] for t, u in self.pairs})
        self.both = both
        self.mean_part = [
            functools.reduce(jnp.add, [both[u, v] * raw[u, v] for v in self.every])
            * (1.0 / self.feat)
            for u in self.every
        ]

    def gradients(self):
        all_mixed = []
        for group in range(self.feat // GROUP):
            outs = [[] for _ in self.every]
            for side in range(2):
                rows = pl.ds(group * GROUP + side * self.half, self.half)
                gain = self.load_gain(rows)
                scaled = [self.normed[t, rows, :] for t in self.every]
                above = [self.ups[t, rows, :] for t in self.every]
                mixed = self.zeros()
                for u in self.every:
                    crossed = functools.reduce(
                        jnp.add, [self.both[u, v] * scaled[v] for v in self.every]
                    )
                    mixed = mixed + crossed * scaled[u]
                    from_norm = self.inverse[u] * (gain * crossed - scaled[u] * self.mean_part[u])
                    direct = functools.reduce(
                        jnp.add, [self.value_part[t, u] * above[t] for t in range(u, self.frames)]
                    )
                    outs[u].append(direct + from_norm)
                all_mixed.append(mixed)
            for u in self.every:
                self.grad_ref[u, pl.ds(group * GROUP, GROUP), :] = jnp.concatenate(
                    outs[u], axis=0
                ).astype(jnp.bfloat16)
        return jnp.concatenate(all_mixed, axis=0)


def fetch_kernel(*refs):
    *refs, arrived = refs
    number = len(refs) // 2
    copies = [
        pltpu.make_async_copy(source, target, arrived.at[index])
        for index, (source, target) in enumerate(zip(refs[:number], refs[number:]))
    ]
    for copy in copies:
        copy.start()
    for copy in copies:
        copy.wait()


def fetch(*fields):
    return pl.pallas_call(
        fetch_kernel,
        in_specs=[pl.BlockSpec(memory_space=pltpu.HBM)] * len(fields),
        out_specs=[pl.BlockSpec(memory_space=pltpu.VMEM)] * len(fields),
        out_shape=[jax.ShapeDtypeStruct(field.shape, field.dtype) for field in fields],
        scratch_shapes=[pltpu.SemaphoreType.DMA((len(fields),))],
        compiler_params=params(0),
        cost_estimate=cost(1),
        name="fetch",
    )(*[in_hbm(field) for field in fields])


def temporal_kernel(frames, spaces, length_ref, task_ref, *refs):
    attended_refs, (gain_ref, own_ref, *other_refs), refs = (
        refs[: frames - 1],
        refs[frames - 1 : frames - 1 + 2 * spaces],
        refs[frames - 1 + 2 * spaces :],
    )
    grad_refs, (mixed_ref, attended, grads, wide) = refs[:frames], refs[frames:]
    heads, lanes = own_ref.shape[1], own_ref.shape[3]
    half = frames // 2
    mixed_ref[...] = jnp.full(mixed_ref.shape, task_ref[0].astype(jnp.float32))

    def load_upstream(space, head, t, rows):
        if space == 0:
            return own_ref[t, head, rows, :]
        return other_refs[2 * space - 2 + t // half][t % half, head, rows, :]

    places = [
        pl.ds(pl.multiple_of(partner("space", space) * lanes, lanes), lanes)
        for space in range(spaces)
    ]
    for head in range(heads):
        for space, here in enumerate(places):
            attended[head, space, partner("tm", 0)] = own_ref[frames + space, head]
            for distance, ref in enumerate(attended_refs):
                attended[head, space, partner("tm", distance + 1)] = ref[head, :, here]
    blocks = [
        Block(
            length_ref[0],
            functools.partial(lambda head, space, t, rows: attended[head, space, t, rows, :], head, space),
            functools.partial(load_upstream, space, head),
            functools.partial(lambda head, rows: gain_ref[head, rows, :], head),
            wide.at[head, space],
            grads.at[head, space],
        )
        for head in range(heads)
        for space in range(spaces)
    ]
    for block in blocks:
        block.widen()
    blocks[0].sums()
    mixed = []
    for block, later in zip(blocks, blocks[1:] + [None]):
        block.weigh()
        if later:
            later.sums()
        mixed.append(block.gradients())
    for head in range(heads):
        summed = functools.reduce(jnp.add, mixed[head * spaces : (head + 1) * spaces])
        mixed_ref[pl.ds(head, 1), :] = jnp.sum(summed.T, axis=0, keepdims=True) * 0.5
    for distance, ref in enumerate(grad_refs):
        frame = partner("tm", distance)
        for head in range(heads):
            for space, here in enumerate(places):
                ref[head, :, here] = grads[head, space, frame]


def temporal(lengths, task_ids, attended, upstream, gain):
    _, heads, feat, lanes = upstream[0].shape
    frames, spaces = len(attended) + 1, (len(upstream) + 1) // 2
    patches = spaces * lanes
    rows = -(-(heads + 1) // 8) * 8
    operands = [*attended, gain, *upstream]
    block = (heads, spaces, frames, feat, lanes)
    results = pl.pallas_call(
        functools.partial(temporal_kernel, frames, spaces),
        in_specs=[pl.BlockSpec(memory_space=pltpu.SMEM)] * 2
        + [pl.BlockSpec(memory_space=pltpu.VMEM)] * len(operands),
        out_specs=[pl.BlockSpec(memory_space=pltpu.VMEM)] * (frames + 1),
        scratch_shapes=[
            pltpu.VMEM(block, jnp.bfloat16),
            pltpu.VMEM(block, jnp.bfloat16),
            pltpu.VMEM((heads, spaces, 3, frames, feat, lanes), jnp.float32),
        ],
        out_shape=[jax.ShapeDtypeStruct((heads, feat, patches), jnp.bfloat16)] * frames
        + [jax.ShapeDtypeStruct((rows, feat), jnp.float32)],
        compiler_params=params(patches),
        cost_estimate=cost(4),
        name="temporal",
    )(lengths, task_ids, *operands)
    return list(results[:frames]), results[frames]


def gain_gradients(axis, heads, frames, clips, mixed_refs, gains_ref, grad_ref):
    tasks = gains_ref.shape[1]
    rows = sum(ref.shape[0] for ref in mixed_refs) // (frames * clips)
    each = mixed_refs[0].shape[0] // rows
    task_ids = lax.broadcasted_iota(jnp.int32, (tasks, HEAD_DIM), 0).astype(jnp.float32)
    for distance in range(frames):
        for head in range(heads):
            mixed = jnp.zeros((tasks, HEAD_DIM), jnp.float32)
            for clip in range(clips):
                block = distance * clips + clip
                ref, start = mixed_refs[block // each], block % each * rows
                task = ref[pl.ds(start + heads, 1), :]
                row = ref[pl.ds(start + head, 1), :]
                mixed = mixed + jnp.where(task_ids == task, row, 0.0)
            start = (partner(axis, distance) * heads + head) * HEAD_DIM
            cols = pl.ds(pl.multiple_of(start, HEAD_DIM), HEAD_DIM)
            grad_ref[0, :, cols] = gains_ref[1, :, cols] * mixed
            grad_ref[1, :, cols] = gains_ref[0, :, cols] * mixed


def swap(field, axis, size, distance):
    return lax.ppermute(field, axis, [(i, i ^ distance) for i in range(size)])


def split_by_heads(
    query_heads, key_heads, value_heads, cotangent, task_ids, lengths, gains, clips, frames, spaces
):
    patches, feat = query_heads.shape[2:]
    heads = feat // HEAD_DIM
    own = heads // frames
    width = own * HEAD_DIM
    queries, key_rows, values = (
        field.reshape(patches, feat) for field in (query_heads, key_heads, value_heads)
    )
    frame = lax.axis_index("tm")

    pieces = list(pack(cotangent.reshape(cotangent.shape[2:]), frames, spaces))
    queries, pieces = lax.optimization_barrier((queries, pieces))
    for distance in range(1, frames):
        pieces[distance] = swap(pieces[distance], "tm", frames, distance)
    fields = (queries, key_rows, values)
    weights, attended = forward("tm", *fields, frames)
    for distance in range(1, frames):
        attended[distance] = swap(attended[distance], "tm", frames, distance)
    backwards, _ = lax.optimization_barrier((pieces[::-1], weights))
    upstream = list(turn(backwards[::-1], attended[0]))
    for index in range(1, len(upstream)):
        upstream[index] = swap(upstream[index], "space", spaces, (index + 1) // 2)
    rows = lax.dynamic_index_in_dim(gains, task_ids[0], 1, keepdims=False)
    product = lax.dynamic_slice_in_dim(rows[0] * rows[1], frame * width, width, 0)
    gain = jnp.broadcast_to(
        product.reshape(own, HEAD_DIM, 1), (own, HEAD_DIM, patches // spaces)
    )
    attended[1], gain, upstream[0] = lax.optimization_barrier((attended[1], gain, upstream[0]))
    upstream[0], *kept = fetch(upstream[0], *fields)
    grads, mixed = temporal(lengths, task_ids, attended[1:], upstream, gain)
    for distance in reversed(range(1, frames)):
        grads[distance] = swap(grads[distance], "tm", frames, distance)
    here = grads[0]
    for bit in range(clips.bit_length() - 1):
        other = swap(mixed, "dp", clips, 1 << bit)
        if bit == 0:
            here, other = lax.optimization_barrier((here, other))
        mixed = jnp.concatenate([mixed, other], axis=0)
    results = backward("tm", kept, weights, [here], [0])
    mixed, results = lax.optimization_barrier((mixed, results))
    near, grads[1] = lax.optimization_barrier((mixed, grads[1]))
    mixed = [mixed, swap(near, "tm", frames, 1)] + [
        swap(mixed, "tm", frames, distance) for distance in range(2, frames)
    ]
    last = range(frames - 1, 0, -1)
    if frames > 2:
        results = backward("tm", kept, weights, [grads[1]], [1], results)
        last = range(frames - 1, 1, -1)
    grad_queries, grad_keys, grad_gains = backward(
        "tm",
        kept,
        weights,
        [grads[distance] for distance in last],
        list(last),
        results,
        mixed,
        gains,
        (own, frames, clips),
    )
    return (
        grad_queries.reshape(query_heads.shape),
        grad_keys.reshape(query_heads.shape),
        grad_gains,
    )


def temporal_grads(attended, upstream, gain_query, gain_keys, length):
    highest = lax.Precision.HIGHEST
    frames = attended.shape[0]
    score_scale = attended.shape[-1] ** (-0.5)
    floats = attended.astype(jnp.float32)
    inverse_rms = lax.rsqrt(jnp.mean(floats * floats, axis=-1, keepdims=True) + 1e-06)
    normed = floats * inverse_rms
    t_query = normed * gain_query
    t_keys = normed * gain_keys
    scores = jnp.einsum("txhd,uxhd->xhtu", t_query, t_keys, precision=highest) * score_scale
    frame_ids = jnp.arange(frames, dtype=jnp.int32)
    allowed = (frame_ids[None, :] <= frame_ids[:, None]) & (frame_ids[None, :] < length)
    scores = jnp.where(allowed, scores, -1e30)
    weights = jax.nn.softmax(scores, axis=-1)
    weights_low = lax.optimization_barrier(weights.astype(jnp.bfloat16)).astype(jnp.float32)
    valid_rows = (frame_ids < length).astype(jnp.float32)
    masked = upstream.astype(jnp.float32) * valid_rows[:, None, None, None]
    grad_weights = jnp.einsum("txhd,uxhd->xhtu", masked, floats, precision=highest)
    from_values = jnp.einsum("xhtu,txhd->uxhd", weights_low, masked, precision=highest)
    grad_scores = (
        weights
        * (grad_weights - jnp.sum(grad_weights * weights, axis=-1, keepdims=True))
        * score_scale
    )
    grad_tquery = jnp.einsum("xhtu,uxhd->txhd", grad_scores, t_keys, precision=highest)
    grad_tkeys = jnp.einsum("xhtu,txhd->uxhd", grad_scores, t_query, precision=highest)
    grad_normed = grad_tquery * gain_query + grad_tkeys * gain_keys
    grad_gain_query = jnp.sum(grad_tquery * normed, axis=(0, 1))
    grad_gain_keys = jnp.sum(grad_tkeys * normed, axis=(0, 1))
    from_norm = inverse_rms * (
        grad_normed - normed * jnp.mean(grad_normed * normed, axis=-1, keepdims=True)
    )
    grad_total = (masked + from_values + from_norm).astype(jnp.bfloat16)
    return (grad_total, grad_gain_query, grad_gain_keys)


def split_by_patches(query_heads, key_heads, value_heads, cotangent, task_ids, lengths, gains):
    patches, feat = query_heads.shape[2:]
    heads = feat // HEAD_DIM
    queries, key_rows, values = (
        field.reshape(patches, feat) for field in (query_heads, key_heads, value_heads)
    )
    fields = (queries, key_rows, values)
    weights, attended = forward(None, *fields, 1)
    attended_field = jnp.transpose(attended[0], (2, 0, 1)).reshape(1, 1, patches, feat)
    upstream = lax.all_to_all(
        lax.all_to_all(cotangent, "space", split_axis=3, concat_axis=2, tiled=True),
        "tm",
        split_axis=2,
        concat_axis=1,
        tiled=True,
    )
    frames_attended = lax.all_to_all(attended_field, "tm", split_axis=2, concat_axis=1, tiled=True)
    frames, local_patches = frames_attended.shape[1:3]
    selector = (task_ids[0] == jnp.arange(gains.shape[1], dtype=jnp.int32)).astype(jnp.float32)
    gain_query = jnp.sum(selector[:, None] * gains[0], axis=0).reshape(heads, HEAD_DIM)
    gain_keys = jnp.sum(selector[:, None] * gains[1], axis=0).reshape(heads, HEAD_DIM)
    grad_total, grad_gq, grad_gk = temporal_grads(
        frames_attended.reshape(frames, local_patches, heads, HEAD_DIM),
        upstream.reshape(frames, local_patches, heads, HEAD_DIM),
        gain_query,
        gain_keys,
        lengths[0],
    )
    gain_terms = jnp.stack(
        [
            selector[:, None] * grad_gq.reshape(1, feat),
            selector[:, None] * grad_gk.reshape(1, feat),
        ]
    )
    grad_gains = lax.psum(gain_terms, ("dp", "tm"))
    returned = lax.all_to_all(
        grad_total.reshape(1, frames, local_patches, feat),
        "tm",
        split_axis=1,
        concat_axis=2,
        tiled=True,
    )
    head_grads = jnp.transpose(returned.reshape(patches, heads, HEAD_DIM), (1, 2, 0))
    grad_queries, grad_keys = backward(None, fields, weights, [head_grads], [0])
    return (
        grad_queries.reshape(query_heads.shape),
        grad_keys.reshape(query_heads.shape),
        grad_gains,
    )


def solution(mesh):
    clips, frames, spaces = (mesh.shape[axis] for axis in ("dp", "tm", "space"))

    def local(query_heads, *others):
        heads = query_heads.shape[3] // HEAD_DIM
        powers = all(size & (size - 1) == 0 for size in (clips, frames, spaces))
        if powers and 2 <= frames <= 4 and heads % frames == 0:
            return split_by_heads(query_heads, *others, clips, frames, spaces)
        return split_by_patches(query_heads, *others)

    return jax.shard_map(
        local,
        mesh=mesh,
        in_specs=(
            P("dp", "tm", None, "space"),
            P("dp", "tm", None, "space"),
            P("dp", "tm", None, "space"),
            P("dp", "tm", "space", None),
            P("dp"),
            P("dp"),
            P(None, None, "space"),
        ),
        out_specs=(
            P("dp", "tm", None, "space"),
            P("dp", "tm", None, "space"),
            P(None, None, "space"),
        ),
        check_vma=False,
    )
```

```python
import functools

import jax
import jax.numpy as jnp
from jax import lax
from jax.experimental import pallas as pl
from jax.experimental.pallas import tpu as pltpu
from jax.sharding import PartitionSpec as P

HEAD_DIM = 128
GROUP = 16
MIB = 1024 * 1024


def params(patches):
    return pltpu.CompilerParams(vmem_limit_bytes=(16 if patches <= 512 else 60) * MIB)


def cost(microseconds):
    return pl.CostEstimate(flops=int(microseconds * 1e8), bytes_accessed=0, transcendentals=0)


def in_hbm(field):
    return pltpu.with_memory_space_constraint(field, pltpu.HBM)


def columns_dot(left, right):
    return lax.dot_general(
        left, right, (((1,), (1,)), ((), ())), preferred_element_type=jnp.float32
    )


def dot(left, right):
    return jnp.dot(left, right, preferred_element_type=jnp.float32)


def partner(axis, distance):
    return distance if axis is None else jnp.bitwise_xor(lax.axis_index(axis), distance)


def forward_kernel(axis, query_ref, key_ref, value_ref, weights_ref, *refs):
    (queries, key_rows, values, arrived), attended_refs = refs[-4:], refs[:-4]
    score_scale = HEAD_DIM ** (-0.5)
    groups, _, width = queries.shape
    own = width // HEAD_DIM
    copies = []
    for group in range(groups):
        cols = pl.ds(pl.multiple_of(partner(axis, group) * width, HEAD_DIM), width)
        for field, (source, target) in enumerate(
            ((query_ref, queries), (key_ref, key_rows), (value_ref, values))
        ):
            copy = pltpu.make_async_copy(
                source.at[:, cols], target.at[group], arrived.at[group, field]
            )
            copy.start()
            copies.append(copy)
    for group in range(groups):
        for copy in copies[3 * group : 3 * group + 3]:
            copy.wait()
        for head in range(own):
            cols = pl.ds(head * HEAD_DIM, HEAD_DIM)
            scores = columns_dot(key_rows[group, :, cols], queries[group, :, cols])
            largest = jnp.max(scores, axis=0, keepdims=True)
            raised = jnp.exp((scores - largest) * score_scale)
            weights = raised * (1.0 / jnp.sum(raised, axis=0, keepdims=True))
            weights_ref[group * own + head] = weights
            attended = dot(values[group, :, cols].T, weights.astype(jnp.bfloat16))
            attended_refs[group][head] = attended.astype(jnp.bfloat16)


def forward(axis, queries, key_rows, values, groups):
    patches, feat = queries.shape
    heads = feat // HEAD_DIM
    own = heads // groups
    fields = [in_hbm(field) for field in (queries, key_rows, values)]
    weights, *attended = pl.pallas_call(
        functools.partial(forward_kernel, axis),
        in_specs=[pl.BlockSpec(memory_space=pltpu.HBM)] * 3,
        out_specs=[pl.BlockSpec(memory_space=pltpu.VMEM)] * (1 + groups),
        scratch_shapes=[pltpu.VMEM((groups, patches, feat // groups), jnp.bfloat16)] * 3
        + [pltpu.SemaphoreType.DMA((groups, 3))],
        out_shape=[jax.ShapeDtypeStruct((heads, patches, patches), jnp.float32)]
        + [jax.ShapeDtypeStruct((own, HEAD_DIM, patches), jnp.bfloat16)] * groups,
        compiler_params=params(patches),
        cost_estimate=cost(6),
        name="spatial_forward",
    )(*fields)
    return weights, attended


def backward_group(axis, fields, weights_ref, grad_ref, distance, scratch, results, sent):
    query_ref, key_ref, value_ref = fields
    score_scale = HEAD_DIM ** (-0.5)
    own = grad_ref.shape[0]
    start = partner(axis, distance) * (own * HEAD_DIM)
    columns = [
        pl.ds(pl.multiple_of(start + head * HEAD_DIM, HEAD_DIM), HEAD_DIM) for head in range(own)
    ]
    spatial_grads = [dot(value_ref[:, columns[head]], grad_ref[head]) for head in range(own)]
    all_scores = []
    for head, spatial_grad in enumerate(spatial_grads):
        weights = weights_ref[distance * own + head]
        row_sum = jnp.sum(spatial_grad * weights, axis=0, keepdims=True)
        scores = weights * (spatial_grad - row_sum) * score_scale
        all_scores.append(scores.astype(jnp.bfloat16))
    gq, gk = scratch
    for head, scores in enumerate(all_scores):
        cols = pl.ds(head * HEAD_DIM, HEAD_DIM)
        gk[:, cols] = dot(scores, query_ref[:, columns[head]]).astype(jnp.bfloat16)
        gq[:, cols] = dot(key_ref[:, columns[head]].T, scores).astype(jnp.bfloat16).T
    there = pl.ds(pl.multiple_of(start, HEAD_DIM), own * HEAD_DIM)
    copies = [
        pltpu.make_async_copy(source, target.at[:, there], sent.at[side])
        for side, (source, target) in enumerate(zip(scratch, results))
    ]
    for copy in copies:
        copy.start()
    return copies


def backward_kernel(axis, distances, gains_of, *refs):
    fields, weights_ref, refs = refs[:3], refs[3], refs[4:]
    grad_refs, refs = refs[: len(distances)], refs[len(distances) :]
    *refs, gq, gk, sent = refs
    copies = []
    if gains_of:
        *mixed_refs, gains_ref, _, _, gq_ref, gk_ref, grad_gains_ref, grad_gains = refs
        gain_gradients(axis, *gains_of, mixed_refs, gains_ref, grad_gains)
        copy = pltpu.make_async_copy(grad_gains, grad_gains_ref, sent.at[len(distances), 0])
        copy.start()
        copies.append(copy)
    else:
        gq_ref, gk_ref = refs[-2:]
    for place, (distance, grad_ref) in enumerate(zip(distances, grad_refs)):
        copies += backward_group(
            axis,
            fields,
            weights_ref,
            grad_ref,
            distance,
            (gq.at[place], gk.at[place]),
            (gq_ref, gk_ref),
            sent.at[place],
        )
    for copy in copies:
        copy.wait()


def backward(axis, fields, weights, grads, distances, earlier=(), mixed=(), gains=None, gains_of=()):
    patches, feat = fields[0].shape
    own = grads[0].shape[0]
    operands = [*fields, weights, *grads] + ([*mixed, gains] if gains_of else [])
    block = pltpu.VMEM((len(distances), patches, own * HEAD_DIM), jnp.bfloat16)
    out_shape = [jax.ShapeDtypeStruct((patches, feat), jnp.bfloat16)] * 2
    scratch = [block, block, pltpu.SemaphoreType.DMA((len(distances) + 1, 2))]
    if gains_of:
        out_shape.append(jax.ShapeDtypeStruct(gains.shape, jnp.float32))
        scratch.insert(0, pltpu.VMEM(gains.shape, jnp.float32))
    return pl.pallas_call(
        functools.partial(backward_kernel, axis, distances, gains_of),
        in_specs=[pl.BlockSpec(memory_space=pltpu.VMEM)] * len(operands)
        + [pl.BlockSpec(memory_space=pl.ANY)] * len(earlier),
        out_specs=[pl.BlockSpec(memory_space=pl.ANY)] * len(out_shape),
        scratch_shapes=scratch,
        out_shape=out_shape,
        input_output_aliases={len(operands) + index: index for index in range(len(earlier))},
        compiler_params=params(patches),
        cost_estimate=cost(2),
        name="spatial_backward",
    )(*operands, *earlier)


def pack_kernel(field_ref, *refs):
    *packed_refs, rows, arrived = refs
    chunks, size, _ = rows.shape
    spaces, _, width = packed_refs[0].shape
    copies = [
        pltpu.make_async_copy(
            field_ref.at[pl.ds(chunk * size, size), :], rows.at[chunk], arrived.at[chunk]
        )
        for chunk in range(chunks)
    ]
    for copy in copies:
        copy.start()
    for chunk, copy in enumerate(copies):
        copy.wait()
        for distance, packed_ref in enumerate(packed_refs):
            for space in range(spaces):
                start = (space * len(packed_refs) + partner("tm", distance)) * width
                cols = pl.ds(pl.multiple_of(start, HEAD_DIM), width)
                packed_ref[space, pl.ds(chunk * size, size), :] = rows[chunk, :, cols]


def pack(field, frames, spaces):
    patches, feat = field.shape
    chunks = patches // GROUP
    shape = (spaces, patches, feat // (frames * spaces))
    return pl.pallas_call(
        pack_kernel,
        in_specs=[pl.BlockSpec(memory_space=pltpu.HBM)],
        out_specs=[pl.BlockSpec(memory_space=pltpu.VMEM)] * frames,
        out_shape=[jax.ShapeDtypeStruct(shape, field.dtype)] * frames,
        scratch_shapes=[
            pltpu.VMEM((chunks, patches // chunks, feat), field.dtype),
            pltpu.SemaphoreType.DMA((chunks,)),
        ],
        compiler_params=params(patches),
        cost_estimate=cost(1),
        name="pack_cotangent",
    )(in_hbm(field))


def turn_kernel(frames, *refs):
    piece_refs, (plane_ref, own_hbm, *other_refs), (turned, own_ref, sent) = (
        refs[:frames][::-1],
        refs[frames:-3],
        refs[-3:],
    )
    spaces, lanes, _ = piece_refs[0].shape
    for space in range(spaces):
        place = pl.multiple_of(partner("space", space) * lanes, lanes)
        own_ref[frames + space] = plane_ref[:, :, pl.ds(place, lanes)]
    heads = own_ref.shape[1]
    for space in range(spaces):
        target = turned if space else own_ref
        source = partner("space", space)
        for distance, ref in enumerate(piece_refs):
            frame = partner("tm", distance)
            for head in range(heads):
                cols = pl.ds(head * HEAD_DIM, HEAD_DIM)
                target[frame, head] = ref[source, :, cols].T
        if space == 0:
            copy = pltpu.make_async_copy(own_ref, own_hbm, sent)
            copy.start()
        else:
            half = frames // 2
            other_refs[2 * space - 2][...] = turned[:half]
            other_refs[2 * space - 1][...] = turned[half:]
    copy.wait()


def turn(pieces, plane):
    spaces, patches, feat = pieces[0].shape
    frames, heads = len(pieces), feat // HEAD_DIM
    turned = (heads, HEAD_DIM, patches)
    sizes = [frames + spaces] + [frames // 2, frames - frames // 2] * (spaces - 1)
    return pl.pallas_call(
        functools.partial(turn_kernel, frames),
        in_specs=[pl.BlockSpec(memory_space=pltpu.VMEM)] * (frames + 1),
        out_specs=[pl.BlockSpec(memory_space=pltpu.HBM)]
        + [pl.BlockSpec(memory_space=pltpu.VMEM)] * (len(sizes) - 1),
        out_shape=[jax.ShapeDtypeStruct((size,) + turned, pieces[0].dtype) for size in sizes],
        scratch_shapes=[
            pltpu.VMEM((frames,) + turned, pieces[0].dtype),
            pltpu.VMEM((frames + spaces,) + turned, pieces[0].dtype),
            pltpu.SemaphoreType.DMA,
        ],
        compiler_params=params(patches),
        cost_estimate=cost(2),
        name="turn_cotangent",
    )(*reversed(pieces), plane)


def temporal_part(length, load_attended, load_upstream, load_gain, fields, ups, normed, grad_ref):
    frames, feat, lanes = grad_ref.shape
    half = GROUP // 2
    score_scale = feat ** (-0.5)
    pairs = [(t, u) for t in range(frames) for u in range(t + 1)]
    every = range(frames)
    valid = [jnp.where(t < length, 1.0, 0.0).astype(jnp.float32) for t in every]
    bias = [jnp.where(u < length, 0.0, -1e30).astype(jnp.float32) for u in every]

    def total(piece):
        return jnp.broadcast_to(jnp.sum(piece, axis=0, keepdims=True), (half, lanes))

    squares = [jnp.zeros((half, lanes), jnp.float32) for _ in every]
    for group in range(feat // GROUP):
        rows = pl.ds(group * GROUP, GROUP)
        for t in every:
            field = load_attended(t, rows).astype(jnp.float32)
            fields[t, rows, :] = field
            ups[t, rows, :] = load_upstream(t, rows).astype(jnp.float32)
            low, high = field[:half], field[half:]
            squares[t] = squares[t] + (low * low + high * high)
    inverse = [lax.rsqrt(total(squares[t]) * (1.0 / feat) + 1e-06) for t in every]

    raw = {pair: jnp.zeros((half, lanes), jnp.float32) for pair in pairs}
    grad = {pair: jnp.zeros((half, lanes), jnp.float32) for pair in pairs}
    for group in range(feat // half):
        rows = pl.ds(group * half, half)
        gain = load_gain(rows)
        here = [fields[t, rows, :] for t in every]
        above = [ups[t, rows, :] for t in every]
        scaled = [here[t] * inverse[t] for t in every]
        gained = [scaled[t] * gain for t in every]
        for t in every:
            normed[t, rows, :] = scaled[t]
        for t, u in pairs:
            raw[t, u] = raw[t, u] + gained[t] * scaled[u]
            grad[t, u] = grad[t, u] + above[t] * here[u]

    value_part, score_part = {}, {}
    for t in every:
        seen = range(t + 1)
        for u in seen:
            raw[t, u] = total(raw[t, u])
            grad[t, u] = total(grad[t, u]) * valid[t]
        scores = [raw[t, u] * score_scale + bias[u] for u in seen]
        largest = functools.reduce(jnp.maximum, scores)
        raised = [jnp.exp(score - largest) for score in scores]
        over = 1.0 / functools.reduce(jnp.add, raised)
        weights = [piece * over for piece in raised]
        mean_grad = functools.reduce(jnp.add, [weights[u] * grad[t, u] for u in seen])
        for u in seen:
            rounded = weights[u].astype(jnp.bfloat16).astype(jnp.float32)
            value_part[t, u] = (rounded + (1.0 if u == t else 0.0)) * valid[t]
            score_part[t, u] = weights[u] * (grad[t, u] - mean_grad) * score_scale

    both = {(t, u): score_part[t, u] * (2.0 if t == u else 1.0) for t, u in pairs}
    both.update({(u, t): both[t, u] for t, u in pairs})
    raw.update({(u, t): raw[t, u] for t, u in pairs})
    mean_part = [
        functools.reduce(jnp.add, [both[u, v] * raw[u, v] for v in every]) * (1.0 / feat)
        for u in every
    ]

    all_mixed = []
    for group in range(feat // GROUP):
        outs = [[] for _ in every]
        for side in range(2):
            rows = pl.ds(group * GROUP + side * half, half)
            gain = load_gain(rows)
            scaled = [normed[t, rows, :] for t in every]
            above = [ups[t, rows, :] for t in every]
            mixed = jnp.zeros((half, lanes), jnp.float32)
            for u in every:
                crossed = functools.reduce(jnp.add, [both[u, v] * scaled[v] for v in every])
                mixed = mixed + crossed * scaled[u]
                from_norm = inverse[u] * (gain * crossed - scaled[u] * mean_part[u])
                direct = functools.reduce(
                    jnp.add, [value_part[t, u] * above[t] for t in range(u, frames)]
                )
                outs[u].append(direct + from_norm)
            all_mixed.append(mixed)
        for u in every:
            grad_ref[u, pl.ds(group * GROUP, GROUP), :] = jnp.concatenate(
                outs[u], axis=0
            ).astype(jnp.bfloat16)
    return jnp.concatenate(all_mixed, axis=0)


def fetch_kernel(*refs):
    *refs, arrived = refs
    number = len(refs) // 2
    copies = [
        pltpu.make_async_copy(source, target, arrived.at[index])
        for index, (source, target) in enumerate(zip(refs[:number], refs[number:]))
    ]
    for copy in copies:
        copy.start()
    for copy in copies:
        copy.wait()


def fetch(*fields):
    return pl.pallas_call(
        fetch_kernel,
        in_specs=[pl.BlockSpec(memory_space=pltpu.HBM)] * len(fields),
        out_specs=[pl.BlockSpec(memory_space=pltpu.VMEM)] * len(fields),
        out_shape=[jax.ShapeDtypeStruct(field.shape, field.dtype) for field in fields],
        scratch_shapes=[pltpu.SemaphoreType.DMA((len(fields),))],
        compiler_params=params(0),
        cost_estimate=cost(1),
        name="fetch",
    )(*[in_hbm(field) for field in fields])


def temporal_kernel(frames, spaces, length_ref, task_ref, *refs):
    attended_refs, (gain_ref, own_ref, *other_refs), refs = (
        (refs[frames - 2], *refs[: frames - 2]),
        refs[frames - 1 : frames - 1 + 2 * spaces],
        refs[frames - 1 + 2 * spaces :],
    )
    grad_refs, (mixed_ref, attended, grads, wide) = refs[:frames], refs[frames:]
    heads, lanes = own_ref.shape[1], own_ref.shape[3]
    half = frames // 2
    mixed_ref[...] = jnp.full(mixed_ref.shape, task_ref[0].astype(jnp.float32))

    def load_upstream(space, head, t, rows):
        if space == 0:
            return own_ref[t, head, rows, :]
        return other_refs[2 * space - 2 + t // half][t % half, head, rows, :]

    places = [
        pl.ds(pl.multiple_of(partner("space", space) * lanes, lanes), lanes)
        for space in range(spaces)
    ]
    for head in range(heads):
        for space, here in enumerate(places):
            attended[head, space, partner("tm", 0)] = own_ref[frames + space, head]
            for distance, ref in enumerate(attended_refs):
                attended[head, space, partner("tm", distance + 1)] = ref[head, :, here]
        mixed = [
            temporal_part(
                length_ref[0],
                lambda t, rows: attended[head, space, t, rows, :],
                functools.partial(load_upstream, space, head),
                lambda rows: gain_ref[head, rows, :],
                wide.at[head % 2, space, 0],
                wide.at[head % 2, space, 1],
                wide.at[head % 2, space, 2],
                grads.at[head, space],
            )
            for space in range(spaces)
        ]
        summed = functools.reduce(jnp.add, mixed)
        mixed_ref[pl.ds(head, 1), :] = jnp.sum(summed.T, axis=0, keepdims=True) * 0.5
        for distance, ref in enumerate(grad_refs):
            frame = partner("tm", distance)
            for space, here in enumerate(places):
                ref[head, :, here] = grads[head, space, frame]


def temporal(lengths, task_ids, attended, upstream, gain):
    _, heads, feat, lanes = upstream[0].shape
    frames, spaces = len(attended) + 1, (len(upstream) + 1) // 2
    patches = spaces * lanes
    rows = -(-(heads + 1) // 8) * 8
    operands = [*attended[1:], attended[0], gain, *upstream]
    block = (heads, spaces, frames, feat, lanes)
    results = pl.pallas_call(
        functools.partial(temporal_kernel, frames, spaces),
        in_specs=[pl.BlockSpec(memory_space=pltpu.SMEM)] * 2
        + [pl.BlockSpec(memory_space=pltpu.VMEM)] * len(operands),
        out_specs=[pl.BlockSpec(memory_space=pltpu.VMEM)] * (frames + 1),
        scratch_shapes=[
            pltpu.VMEM(block, jnp.bfloat16),
            pltpu.VMEM(block, jnp.bfloat16),
            pltpu.VMEM((2, spaces, 3, frames, feat, lanes), jnp.float32),
        ],
        out_shape=[jax.ShapeDtypeStruct((heads, feat, patches), jnp.bfloat16)] * frames
        + [jax.ShapeDtypeStruct((rows, feat), jnp.float32)],
        compiler_params=params(patches),
        cost_estimate=cost(4),
        name="temporal",
    )(lengths, task_ids, *operands)
    return list(results[:frames]), results[frames]


def gain_gradients(axis, heads, frames, clips, mixed_refs, gains_ref, grad_ref):
    tasks = gains_ref.shape[1]
    rows = sum(ref.shape[0] for ref in mixed_refs) // (frames * clips)
    each = mixed_refs[0].shape[0] // rows
    task_ids = lax.broadcasted_iota(jnp.int32, (tasks, HEAD_DIM), 0).astype(jnp.float32)
    for distance in range(frames):
        for head in range(heads):
            mixed = jnp.zeros((tasks, HEAD_DIM), jnp.float32)
            for clip in range(clips):
                block = distance * clips + clip
                ref, start = mixed_refs[block // each], block % each * rows
                task = ref[pl.ds(start + heads, 1), :]
                row = ref[pl.ds(start + head, 1), :]
                mixed = mixed + jnp.where(task_ids == task, row, 0.0)
            start = (partner(axis, distance) * heads + head) * HEAD_DIM
            cols = pl.ds(pl.multiple_of(start, HEAD_DIM), HEAD_DIM)
            grad_ref[0, :, cols] = gains_ref[1, :, cols] * mixed
            grad_ref[1, :, cols] = gains_ref[0, :, cols] * mixed


def swap(field, axis, size, distance):
    return lax.ppermute(field, axis, [(i, i ^ distance) for i in range(size)])


def split_by_heads(
    query_heads, key_heads, value_heads, cotangent, task_ids, lengths, gains, clips, frames, spaces
):
    patches, feat = query_heads.shape[2:]
    heads = feat // HEAD_DIM
    own = heads // frames
    width = own * HEAD_DIM
    queries, key_rows, values = (
        field.reshape(patches, feat) for field in (query_heads, key_heads, value_heads)
    )
    frame = lax.axis_index("tm")

    pieces = list(pack(cotangent.reshape(cotangent.shape[2:]), frames, spaces))
    queries, pieces = lax.optimization_barrier((queries, pieces))
    for distance in range(1, frames):
        pieces[distance] = swap(pieces[distance], "tm", frames, distance)
    fields = (queries, key_rows, values)
    weights, attended = forward("tm", *fields, frames)
    for distance in range(1, frames):
        attended[distance] = swap(attended[distance], "tm", frames, distance)
    backwards, _ = lax.optimization_barrier((pieces[::-1], weights))
    upstream = list(turn(backwards[::-1], attended[0]))
    for index in range(1, len(upstream)):
        upstream[index] = swap(upstream[index], "space", spaces, (index + 1) // 2)
    rows = lax.dynamic_index_in_dim(gains, task_ids[0], 1, keepdims=False)
    product = lax.dynamic_slice_in_dim(rows[0] * rows[1], frame * width, width, 0)
    gain = jnp.broadcast_to(
        product.reshape(own, HEAD_DIM, 1), (own, HEAD_DIM, patches // spaces)
    )
    attended[-2], gain, upstream[0] = lax.optimization_barrier((attended[-2], gain, upstream[0]))
    upstream[0], *kept = fetch(upstream[0], *fields)
    grads, mixed = temporal(lengths, task_ids, attended[1:], upstream, gain)
    for distance in reversed(range(1, frames)):
        grads[distance] = swap(grads[distance], "tm", frames, distance)
    here = grads[0]
    for bit in range(clips.bit_length() - 1):
        other = swap(mixed, "dp", clips, 1 << bit)
        if bit == 0:
            here, other = lax.optimization_barrier((here, other))
        mixed = jnp.concatenate([mixed, other], axis=0)
    results = backward("tm", kept, weights, [here], [0])
    mixed, results = lax.optimization_barrier((mixed, results))
    near, grads[1] = lax.optimization_barrier((mixed, grads[1]))
    mixed = [mixed, swap(near, "tm", frames, 1)] + [
        swap(mixed, "tm", frames, distance) for distance in range(2, frames)
    ]
    last = range(frames - 1, 0, -1)
    if frames > 2:
        results = backward("tm", kept, weights, [grads[1]], [1], results)
        last = range(frames - 1, 1, -1)
    grad_queries, grad_keys, grad_gains = backward(
        "tm",
        kept,
        weights,
        [grads[distance] for distance in last],
        list(last),
        results,
        mixed,
        gains,
        (own, frames, clips),
    )
    return (
        grad_queries.reshape(query_heads.shape),
        grad_keys.reshape(query_heads.shape),
        grad_gains,
    )


def temporal_grads(attended, upstream, gain_query, gain_keys, length):
    highest = lax.Precision.HIGHEST
    frames = attended.shape[0]
    score_scale = attended.shape[-1] ** (-0.5)
    floats = attended.astype(jnp.float32)
    inverse_rms = lax.rsqrt(jnp.mean(floats * floats, axis=-1, keepdims=True) + 1e-06)
    normed = floats * inverse_rms
    t_query = normed * gain_query
    t_keys = normed * gain_keys
    scores = jnp.einsum("txhd,uxhd->xhtu", t_query, t_keys, precision=highest) * score_scale
    frame_ids = jnp.arange(frames, dtype=jnp.int32)
    allowed = (frame_ids[None, :] <= frame_ids[:, None]) & (frame_ids[None, :] < length)
    scores = jnp.where(allowed, scores, -1e30)
    weights = jax.nn.softmax(scores, axis=-1)
    weights_low = lax.optimization_barrier(weights.astype(jnp.bfloat16)).astype(jnp.float32)
    valid_rows = (frame_ids < length).astype(jnp.float32)
    masked = upstream.astype(jnp.float32) * valid_rows[:, None, None, None]
    grad_weights = jnp.einsum("txhd,uxhd->xhtu", masked, floats, precision=highest)
    from_values = jnp.einsum("xhtu,txhd->uxhd", weights_low, masked, precision=highest)
    grad_scores = (
        weights
        * (grad_weights - jnp.sum(grad_weights * weights, axis=-1, keepdims=True))
        * score_scale
    )
    grad_tquery = jnp.einsum("xhtu,uxhd->txhd", grad_scores, t_keys, precision=highest)
    grad_tkeys = jnp.einsum("xhtu,txhd->uxhd", grad_scores, t_query, precision=highest)
    grad_normed = grad_tquery * gain_query + grad_tkeys * gain_keys
    grad_gain_query = jnp.sum(grad_tquery * normed, axis=(0, 1))
    grad_gain_keys = jnp.sum(grad_tkeys * normed, axis=(0, 1))
    from_norm = inverse_rms * (
        grad_normed - normed * jnp.mean(grad_normed * normed, axis=-1, keepdims=True)
    )
    grad_total = (masked + from_values + from_norm).astype(jnp.bfloat16)
    return (grad_total, grad_gain_query, grad_gain_keys)


def split_by_patches(query_heads, key_heads, value_heads, cotangent, task_ids, lengths, gains):
    patches, feat = query_heads.shape[2:]
    heads = feat // HEAD_DIM
    queries, key_rows, values = (
        field.reshape(patches, feat) for field in (query_heads, key_heads, value_heads)
    )
    fields = (queries, key_rows, values)
    weights, attended = forward(None, *fields, 1)
    attended_field = jnp.transpose(attended[0], (2, 0, 1)).reshape(1, 1, patches, feat)
    upstream = lax.all_to_all(
        lax.all_to_all(cotangent, "space", split_axis=3, concat_axis=2, tiled=True),
        "tm",
        split_axis=2,
        concat_axis=1,
        tiled=True,
    )
    frames_attended = lax.all_to_all(attended_field, "tm", split_axis=2, concat_axis=1, tiled=True)
    frames, local_patches = frames_attended.shape[1:3]
    selector = (task_ids[0] == jnp.arange(gains.shape[1], dtype=jnp.int32)).astype(jnp.float32)
    gain_query = jnp.sum(selector[:, None] * gains[0], axis=0).reshape(heads, HEAD_DIM)
    gain_keys = jnp.sum(selector[:, None] * gains[1], axis=0).reshape(heads, HEAD_DIM)
    grad_total, grad_gq, grad_gk = temporal_grads(
        frames_attended.reshape(frames, local_patches, heads, HEAD_DIM),
        upstream.reshape(frames, local_patches, heads, HEAD_DIM),
        gain_query,
        gain_keys,
        lengths[0],
    )
    gain_terms = jnp.stack(
        [
            selector[:, None] * grad_gq.reshape(1, feat),
            selector[:, None] * grad_gk.reshape(1, feat),
        ]
    )
    grad_gains = lax.psum(gain_terms, ("dp", "tm"))
    returned = lax.all_to_all(
        grad_total.reshape(1, frames, local_patches, feat),
        "tm",
        split_axis=1,
        concat_axis=2,
        tiled=True,
    )
    head_grads = jnp.transpose(returned.reshape(patches, heads, HEAD_DIM), (1, 2, 0))
    grad_queries, grad_keys = backward(None, fields, weights, [head_grads], [0])
    return (
        grad_queries.reshape(query_heads.shape),
        grad_keys.reshape(query_heads.shape),
        grad_gains,
    )


def solution(mesh):
    clips, frames, spaces = (mesh.shape[axis] for axis in ("dp", "tm", "space"))

    def local(query_heads, *others):
        heads = query_heads.shape[3] // HEAD_DIM
        powers = all(size & (size - 1) == 0 for size in (clips, frames, spaces))
        if powers and 2 <= frames <= 4 and heads % frames == 0:
            return split_by_heads(query_heads, *others, clips, frames, spaces)
        return split_by_patches(query_heads, *others)

    return jax.shard_map(
        local,
        mesh=mesh,
        in_specs=(
            P("dp", "tm", None, "space"),
            P("dp", "tm", None, "space"),
            P("dp", "tm", None, "space"),
            P("dp", "tm", "space", None),
            P("dp"),
            P("dp"),
            P(None, None, "space"),
        ),
        out_specs=(
            P("dp", "tm", None, "space"),
            P("dp", "tm", None, "space"),
            P(None, None, "space"),
        ),
        check_vma=False,
    )
```

```python
import functools

import jax
import jax.numpy as jnp
from jax import lax
from jax.experimental import pallas as pl
from jax.experimental.pallas import tpu as pltpu
from jax.sharding import PartitionSpec as P

HEAD_DIM = 128
GROUP = 16
MIB = 1024 * 1024


def params(patches):
    return pltpu.CompilerParams(vmem_limit_bytes=(16 if patches <= 512 else 60) * MIB)


def cost(microseconds):
    return pl.CostEstimate(flops=int(microseconds * 1e8), bytes_accessed=0, transcendentals=0)


def in_hbm(field):
    return pltpu.with_memory_space_constraint(field, pltpu.HBM)


def columns_dot(left, right):
    return lax.dot_general(
        left, right, (((1,), (1,)), ((), ())), preferred_element_type=jnp.float32
    )


def dot(left, right):
    return jnp.dot(left, right, preferred_element_type=jnp.float32)


def partner(axis, distance):
    return distance if axis is None else jnp.bitwise_xor(lax.axis_index(axis), distance)


def forward_kernel(axis, query_ref, key_ref, value_ref, weights_ref, *refs):
    (queries, key_rows, values, arrived), attended_refs = refs[-4:], refs[:-4]
    score_scale = HEAD_DIM ** (-0.5)
    groups, _, width = queries.shape
    own = width // HEAD_DIM
    copies = []
    for group in range(groups):
        cols = pl.ds(pl.multiple_of(partner(axis, group) * width, HEAD_DIM), width)
        for field, (source, target) in enumerate(
            ((query_ref, queries), (key_ref, key_rows), (value_ref, values))
        ):
            copy = pltpu.make_async_copy(
                source.at[:, cols], target.at[group], arrived.at[group, field]
            )
            copy.start()
            copies.append(copy)
    for group in range(groups):
        for copy in copies[3 * group : 3 * group + 3]:
            copy.wait()
        for head in range(own):
            cols = pl.ds(head * HEAD_DIM, HEAD_DIM)
            scores = columns_dot(key_rows[group, :, cols], queries[group, :, cols])
            largest = jnp.max(scores, axis=0, keepdims=True)
            raised = jnp.exp((scores - largest) * score_scale)
            weights = raised * (1.0 / jnp.sum(raised, axis=0, keepdims=True))
            weights_ref[group * own + head] = weights
            attended = dot(values[group, :, cols].T, weights.astype(jnp.bfloat16))
            attended_refs[group][head] = attended.astype(jnp.bfloat16)


def forward(axis, queries, key_rows, values, groups):
    patches, feat = queries.shape
    heads = feat // HEAD_DIM
    own = heads // groups
    fields = [in_hbm(field) for field in (queries, key_rows, values)]
    weights, *attended = pl.pallas_call(
        functools.partial(forward_kernel, axis),
        in_specs=[pl.BlockSpec(memory_space=pltpu.HBM)] * 3,
        out_specs=[pl.BlockSpec(memory_space=pltpu.VMEM)] * (1 + groups),
        scratch_shapes=[pltpu.VMEM((groups, patches, feat // groups), jnp.bfloat16)] * 3
        + [pltpu.SemaphoreType.DMA((groups, 3))],
        out_shape=[jax.ShapeDtypeStruct((heads, patches, patches), jnp.float32)]
        + [jax.ShapeDtypeStruct((own, HEAD_DIM, patches), jnp.bfloat16)] * groups,
        compiler_params=params(patches),
        cost_estimate=cost(6),
        name="spatial_forward",
    )(*fields)
    return weights, attended


def backward_group(axis, fields, weights_ref, grad_ref, distance, scratch, results, sent):
    query_ref, key_ref, value_ref = fields
    score_scale = HEAD_DIM ** (-0.5)
    own = grad_ref.shape[0]
    start = partner(axis, distance) * (own * HEAD_DIM)
    columns = [
        pl.ds(pl.multiple_of(start + head * HEAD_DIM, HEAD_DIM), HEAD_DIM) for head in range(own)
    ]
    spatial_grads = [dot(value_ref[:, columns[head]], grad_ref[head]) for head in range(own)]
    all_scores = []
    for head, spatial_grad in enumerate(spatial_grads):
        weights = weights_ref[distance * own + head]
        row_sum = jnp.sum(spatial_grad * weights, axis=0, keepdims=True)
        scores = weights * (spatial_grad - row_sum) * score_scale
        all_scores.append(scores.astype(jnp.bfloat16))
    gq, gk = scratch
    for head, scores in enumerate(all_scores):
        cols = pl.ds(head * HEAD_DIM, HEAD_DIM)
        gk[:, cols] = dot(scores, query_ref[:, columns[head]]).astype(jnp.bfloat16)
        gq[:, cols] = dot(key_ref[:, columns[head]].T, scores).astype(jnp.bfloat16).T
    there = pl.ds(pl.multiple_of(start, HEAD_DIM), own * HEAD_DIM)
    copies = [
        pltpu.make_async_copy(source, target.at[:, there], sent.at[side])
        for side, (source, target) in enumerate(zip(scratch, results))
    ]
    for copy in copies:
        copy.start()
    return copies


def backward_kernel(axis, distances, gains_of, *refs):
    fields, weights_ref, refs = refs[:3], refs[3], refs[4:]
    grad_refs, refs = refs[: len(distances)], refs[len(distances) :]
    *refs, gq, gk, sent = refs
    copies = []
    if gains_of:
        *mixed_refs, gains_ref, _, _, gq_ref, gk_ref, grad_gains_ref, grad_gains = refs
        gain_gradients(axis, *gains_of, mixed_refs, gains_ref, grad_gains)
        copy = pltpu.make_async_copy(grad_gains, grad_gains_ref, sent.at[len(distances), 0])
        copy.start()
        copies.append(copy)
    else:
        gq_ref, gk_ref = refs[-2:]
    for place, (distance, grad_ref) in enumerate(zip(distances, grad_refs)):
        copies += backward_group(
            axis,
            fields,
            weights_ref,
            grad_ref,
            distance,
            (gq.at[place], gk.at[place]),
            (gq_ref, gk_ref),
            sent.at[place],
        )
    for copy in copies:
        copy.wait()


def backward(axis, fields, weights, grads, distances, earlier=(), mixed=(), gains=None, gains_of=()):
    patches, feat = fields[0].shape
    own = grads[0].shape[0]
    operands = [*fields, weights, *grads] + ([*mixed, gains] if gains_of else [])
    block = pltpu.VMEM((len(distances), patches, own * HEAD_DIM), jnp.bfloat16)
    out_shape = [jax.ShapeDtypeStruct((patches, feat), jnp.bfloat16)] * 2
    scratch = [block, block, pltpu.SemaphoreType.DMA((len(distances) + 1, 2))]
    if gains_of:
        out_shape.append(jax.ShapeDtypeStruct(gains.shape, jnp.float32))
        scratch.insert(0, pltpu.VMEM(gains.shape, jnp.float32))
    return pl.pallas_call(
        functools.partial(backward_kernel, axis, distances, gains_of),
        in_specs=[pl.BlockSpec(memory_space=pltpu.VMEM)] * len(operands)
        + [pl.BlockSpec(memory_space=pl.ANY)] * len(earlier),
        out_specs=[pl.BlockSpec(memory_space=pl.ANY)] * len(out_shape),
        scratch_shapes=scratch,
        out_shape=out_shape,
        input_output_aliases={len(operands) + index: index for index in range(len(earlier))},
        compiler_params=params(patches),
        cost_estimate=cost(2),
        name="spatial_backward",
    )(*operands, *earlier)


def pack_kernel(field_ref, *refs):
    *packed_refs, rows, arrived = refs
    chunks, size, _ = rows.shape
    spaces, _, width = packed_refs[0].shape
    copies = [
        pltpu.make_async_copy(
            field_ref.at[pl.ds(chunk * size, size), :], rows.at[chunk], arrived.at[chunk]
        )
        for chunk in range(chunks)
    ]
    for copy in copies:
        copy.start()
    for chunk, copy in enumerate(copies):
        copy.wait()
        for distance, packed_ref in enumerate(packed_refs):
            for space in range(spaces):
                start = (space * len(packed_refs) + partner("tm", distance)) * width
                cols = pl.ds(pl.multiple_of(start, HEAD_DIM), width)
                packed_ref[space, pl.ds(chunk * size, size), :] = rows[chunk, :, cols]


def pack(field, frames, spaces):
    patches, feat = field.shape
    chunks = patches // GROUP
    shape = (spaces, patches, feat // (frames * spaces))
    return pl.pallas_call(
        pack_kernel,
        in_specs=[pl.BlockSpec(memory_space=pltpu.HBM)],
        out_specs=[pl.BlockSpec(memory_space=pltpu.VMEM)] * frames,
        out_shape=[jax.ShapeDtypeStruct(shape, field.dtype)] * frames,
        scratch_shapes=[
            pltpu.VMEM((chunks, patches // chunks, feat), field.dtype),
            pltpu.SemaphoreType.DMA((chunks,)),
        ],
        compiler_params=params(patches),
        cost_estimate=cost(1),
        name="pack_cotangent",
    )(in_hbm(field))


def turn_kernel(frames, *refs):
    piece_refs, (plane_ref, own_hbm, *other_refs), (turned, own_ref, sent) = (
        refs[:frames][::-1],
        refs[frames:-3],
        refs[-3:],
    )
    spaces, lanes, _ = piece_refs[0].shape
    for space in range(spaces):
        place = pl.multiple_of(partner("space", space) * lanes, lanes)
        own_ref[frames + space] = plane_ref[:, :, pl.ds(place, lanes)]
    heads = own_ref.shape[1]
    for space in range(spaces):
        target = turned if space else own_ref
        source = partner("space", space)
        for distance, ref in enumerate(piece_refs):
            frame = partner("tm", distance)
            for head in range(heads):
                cols = pl.ds(head * HEAD_DIM, HEAD_DIM)
                target[frame, head] = ref[source, :, cols].T
        if space == 0:
            copy = pltpu.make_async_copy(own_ref, own_hbm, sent)
            copy.start()
        else:
            half = frames // 2
            other_refs[2 * space - 2][...] = turned[:half]
            other_refs[2 * space - 1][...] = turned[half:]
    copy.wait()


def turn(pieces, plane):
    spaces, patches, feat = pieces[0].shape
    frames, heads = len(pieces), feat // HEAD_DIM
    turned = (heads, HEAD_DIM, patches)
    sizes = [frames + spaces] + [frames // 2, frames - frames // 2] * (spaces - 1)
    return pl.pallas_call(
        functools.partial(turn_kernel, frames),
        in_specs=[pl.BlockSpec(memory_space=pltpu.VMEM)] * (frames + 1),
        out_specs=[pl.BlockSpec(memory_space=pltpu.HBM)]
        + [pl.BlockSpec(memory_space=pltpu.VMEM)] * (len(sizes) - 1),
        out_shape=[jax.ShapeDtypeStruct((size,) + turned, pieces[0].dtype) for size in sizes],
        scratch_shapes=[
            pltpu.VMEM((frames,) + turned, pieces[0].dtype),
            pltpu.VMEM((frames + spaces,) + turned, pieces[0].dtype),
            pltpu.SemaphoreType.DMA,
        ],
        compiler_params=params(patches),
        cost_estimate=cost(2),
        name="turn_cotangent",
    )(*reversed(pieces), plane)


HALF = GROUP // 2


def total(piece):
    return jnp.broadcast_to(jnp.sum(piece, axis=0, keepdims=True), piece.shape)


def groups(feat):
    return [pl.ds(start, HALF) for start in range(0, feat, HALF)]


def normalize(field_ref, normed_ref):
    feat = field_ref.shape[0]
    squares = functools.reduce(
        jnp.add, [field_ref[rows, :] * field_ref[rows, :] for rows in groups(feat)]
    )
    inverse = lax.rsqrt(total(squares) * (1.0 / feat) + 1e-06)
    for rows in groups(feat):
        normed_ref[rows, :] = field_ref[rows, :] * inverse
    return inverse


def weigh(length, raw, grad, frames, feat):
    score_scale = feat ** (-0.5)
    every = range(frames)
    pairs = [(t, u) for t in every for u in range(t + 1)]
    valid = [jnp.where(t < length, 1.0, 0.0).astype(jnp.float32) for t in every]
    bias = [jnp.where(u < length, 0.0, -1e30).astype(jnp.float32) for u in every]
    value_part, score_part = {}, {}
    for t in every:
        seen = range(t + 1)
        masked = [grad[t, u] * valid[t] for u in seen]
        scores = [raw[t, u] * score_scale + bias[u] for u in seen]
        largest = functools.reduce(jnp.maximum, scores)
        raised = [jnp.exp(score - largest) for score in scores]
        over = 1.0 / functools.reduce(jnp.add, raised)
        weights = [piece * over for piece in raised]
        mean_grad = functools.reduce(jnp.add, [weights[u] * masked[u] for u in seen])
        for u in seen:
            rounded = weights[u].astype(jnp.bfloat16).astype(jnp.float32)
            value_part[t, u] = (rounded + (1.0 if u == t else 0.0)) * valid[t]
            score_part[t, u] = weights[u] * (masked[u] - mean_grad) * score_scale
    both = {(t, u): score_part[t, u] * (2.0 if t == u else 1.0) for t, u in pairs}
    both.update({(u, t): both[t, u] for t, u in pairs})
    raw = {**raw, **{(u, t): raw[t, u] for t, u in pairs}}
    mean_part = [
        functools.reduce(jnp.add, [both[u, v] * raw[u, v] for v in every]) * (1.0 / feat)
        for u in every
    ]
    return value_part, both, mean_part


def gradients(parts, inverse, normed_ref, ups_ref, load_gain, grad_ref):
    value_part, both, mean_part = parts
    frames, feat, _ = grad_ref.shape
    every = range(frames)
    all_mixed = []
    for start in range(0, feat, GROUP):
        outs = [[] for _ in every]
        for rows in (pl.ds(start, HALF), pl.ds(start + HALF, HALF)):
            gain = load_gain(rows)
            scaled = [normed_ref[t, rows, :] for t in every]
            above = [ups_ref[t, rows, :] for t in every]
            mixed = []
            for u in every:
                crossed = functools.reduce(jnp.add, [both[u, v] * scaled[v] for v in every])
                mixed.append(crossed * scaled[u])
                from_norm = inverse[u] * (gain * crossed - scaled[u] * mean_part[u])
                direct = functools.reduce(
                    jnp.add, [value_part[t, u] * above[t] for t in range(u, frames)]
                )
                outs[u].append(direct + from_norm)
            all_mixed.append(functools.reduce(jnp.add, mixed))
        for u in every:
            grad_ref[u, pl.ds(start, GROUP), :] = jnp.concatenate(outs[u], axis=0).astype(
                jnp.bfloat16
            )
    return jnp.concatenate(all_mixed, axis=0)


def fetch_kernel(*refs):
    *refs, arrived = refs
    number = len(refs) // 2
    copies = [
        pltpu.make_async_copy(source, target, arrived.at[index])
        for index, (source, target) in enumerate(zip(refs[:number], refs[number:]))
    ]
    for copy in copies:
        copy.start()
    for copy in copies:
        copy.wait()


def fetch(*fields):
    return pl.pallas_call(
        fetch_kernel,
        in_specs=[pl.BlockSpec(memory_space=pltpu.HBM)] * len(fields),
        out_specs=[pl.BlockSpec(memory_space=pltpu.VMEM)] * len(fields),
        out_shape=[jax.ShapeDtypeStruct(field.shape, field.dtype) for field in fields],
        scratch_shapes=[pltpu.SemaphoreType.DMA((len(fields),))],
        compiler_params=params(0),
        cost_estimate=cost(0),
        name="fetch",
    )(*[in_hbm(field) for field in fields])


def order(frame, other):
    return jnp.maximum(frame, other), jnp.minimum(frame, other)


def early_kernel(frames, spaces, *refs):
    last = frames - 1
    attended_refs, (gain_ref, own_ref), outs = refs[: last - 1], refs[last - 1 : -5], refs[-5:]
    ups, fields, normed, sums, inverse = outs
    heads, feat, lanes = own_ref.shape[1:]
    mine = [partner("tm", distance) for distance in range(last)]
    for head in range(heads):
        for space in range(spaces):
            block = head * spaces + space
            here = pl.ds(pl.multiple_of(partner("space", space) * lanes, lanes), lanes)
            if space == 0:
                ups[head] = own_ref[:frames, head].astype(jnp.float32)
            for distance in range(last):
                if distance == 0:
                    field = own_ref[frames + space, head]
                else:
                    field = attended_refs[distance - 1][head, :, here]
                fields[block, distance] = field.astype(jnp.float32)
                inverse[block, mine[distance]] = normalize(
                    fields.at[block, distance], normed.at[block, distance]
                )
            pairs = [(x, y) for x in range(last) for y in range(x + 1)]
            raw = {pair: jnp.zeros((HALF, lanes), jnp.float32) for pair in pairs}
            grad = dict(raw)
            for rows in groups(feat):
                gain = gain_ref[head, rows, :]
                scaled = [normed[block, distance, rows, :] for distance in range(last)]
                gained = [piece * gain for piece in scaled]
                for x, y in pairs:
                    raw[x, y] = raw[x, y] + gained[x] * scaled[y]
                    if space == 0:
                        later, _ = order(mine[x], mine[y])
                        lower = jnp.where(mine[x] < mine[y], x, y)
                        product = ups[head, later, rows, :] * fields[block, lower, rows, :]
                        grad[x, y] = grad[x, y] + product
            for x, y in pairs:
                later, earlier = order(mine[x], mine[y])
                sums[block, 0, later * frames + earlier] = total(raw[x, y])
                if space == 0:
                    sums[block, 1, later * frames + earlier] = total(grad[x, y])


def late_kernel(frames, spaces, length_ref, task_ref, *refs):
    last = frames - 1
    (attended_ref, gain_ref, own_ups, fields, normed, sums, inverse), refs = refs[:7], refs[7:]
    other_refs, refs = refs[: 2 * spaces - 2], refs[2 * spaces - 2 :]
    grad_refs, (mixed_ref, own_field, own_normed, whole, table, inverses, grads, other_ups) = (
        refs[:frames],
        refs[frames:],
    )
    heads, feat, _ = attended_ref.shape
    lanes = own_ups.shape[-1]
    half = frames // 2
    mine = [partner("tm", distance) for distance in range(frames)]
    mixed_ref[...] = jnp.full(mixed_ref.shape, task_ref[0].astype(jnp.float32))
    for head in range(heads):
        mixed = []
        for space in range(spaces):
            block = head * spaces + space
            here = pl.ds(pl.multiple_of(partner("space", space) * lanes, lanes), lanes)
            field_ref, normed_ref = own_field.at[block], own_normed.at[block]
            field_ref[...] = attended_ref[head, :, here].astype(jnp.float32)
            table[block] = sums[block]
            inverses[block] = inverse[block]
            inverses[block, mine[last]] = normalize(field_ref, normed_ref)
            for distance in range(last):
                whole[block, mine[distance]] = normed[block, distance]
            whole[block, mine[last]] = normed_ref[...]
            if space == 0:
                ups = own_ups.at[head]
            else:
                ups = other_ups.at[block]
                for t in range(frames):
                    upstream = other_refs[2 * space - 2 + t // half][t % half, head]
                    ups[t] = upstream.astype(jnp.float32)
            near = [(x, y) for x in range(last) for y in range(x + 1)] if space else []
            nearer = {pair: jnp.zeros((HALF, lanes), jnp.float32) for pair in near}
            raw = [jnp.zeros((HALF, lanes), jnp.float32) for _ in range(frames)]
            grad = list(raw)
            for rows in groups(feat):
                for x, y in near:
                    later, _ = order(mine[x], mine[y])
                    lower = jnp.where(mine[x] < mine[y], x, y)
                    nearer[x, y] = nearer[x, y] + ups[later, rows, :] * fields[block, lower, rows, :]
                field, scaled = field_ref[rows, :], normed_ref[rows, :]
                gained = scaled * gain_ref[head, rows, :]
                for distance in range(frames):
                    later, _ = order(mine[last], mine[distance])
                    if distance < last:
                        other = normed[block, distance, rows, :]
                        lower = jnp.where(
                            mine[last] < mine[distance], field, fields[block, distance, rows, :]
                        )
                    else:
                        other, lower = scaled, field
                    raw[distance] = raw[distance] + gained * other
                    grad[distance] = grad[distance] + ups[later, rows, :] * lower
            for distance in range(frames):
                later, earlier = order(mine[last], mine[distance])
                table[block, 0, later * frames + earlier] = total(raw[distance])
                table[block, 1, later * frames + earlier] = total(grad[distance])
            for x, y in near:
                later, earlier = order(mine[x], mine[y])
                table[block, 1, later * frames + earlier] = total(nearer[x, y])
            pairs = [(t, u) for t in range(frames) for u in range(t + 1)]
            parts = weigh(
                length_ref[0],
                {(t, u): table[block, 0, t * frames + u] for t, u in pairs},
                {(t, u): table[block, 1, t * frames + u] for t, u in pairs},
                frames,
                feat,
            )
            mixed.append(
                gradients(
                    parts,
                    [inverses[block, t] for t in range(frames)],
                    whole.at[block],
                    ups,
                    lambda rows: gain_ref[head, rows, :],
                    grads.at[block],
                )
            )
            for distance, ref in enumerate(grad_refs):
                ref[head, :, here] = grads[block, mine[distance]]
        summed = functools.reduce(jnp.add, mixed)
        mixed_ref[pl.ds(head, 1), :] = jnp.sum(summed.T, axis=0, keepdims=True) * 0.5


def temporal_early(attended, upstream, gain):
    planes, heads, feat, lanes = upstream.shape
    frames = len(attended) + 2
    spaces = planes - frames
    blocks = heads * spaces
    operands = [*attended, gain, upstream]
    shapes = [
        (heads, frames, feat, lanes),
        (blocks, frames - 1, feat, lanes),
        (blocks, frames - 1, feat, lanes),
        (blocks, 2, frames * frames, HALF, lanes),
        (blocks, frames, HALF, lanes),
    ]
    return pl.pallas_call(
        functools.partial(early_kernel, frames, spaces),
        in_specs=[pl.BlockSpec(memory_space=pltpu.VMEM)] * len(operands),
        out_specs=[pl.BlockSpec(memory_space=pltpu.VMEM)] * len(shapes),
        out_shape=[jax.ShapeDtypeStruct(shape, jnp.float32) for shape in shapes],
        compiler_params=params(spaces * lanes),
        cost_estimate=cost(0),
        name="temporal_early",
    )(*operands)


def temporal_late(lengths, task_ids, attended, upstream, gain, early):
    heads, frames, feat, lanes = early[0].shape
    blocks, patches = early[1].shape[0], attended.shape[2]
    spaces = blocks // heads
    rows = -(-(heads + 1) // 8) * 8
    operands = [attended, gain, *early, *upstream]
    block = (blocks, feat, lanes)
    results = pl.pallas_call(
        functools.partial(late_kernel, frames, spaces),
        in_specs=[pl.BlockSpec(memory_space=pltpu.SMEM)] * 2
        + [pl.BlockSpec(memory_space=pltpu.VMEM)] * len(operands),
        out_specs=[pl.BlockSpec(memory_space=pltpu.VMEM)] * (frames + 1),
        scratch_shapes=[
            pltpu.VMEM(block, jnp.float32),
            pltpu.VMEM(block, jnp.float32),
            pltpu.VMEM((blocks, frames, feat, lanes), jnp.float32),
            pltpu.VMEM(early[3].shape, jnp.float32),
            pltpu.VMEM(early[4].shape, jnp.float32),
            pltpu.VMEM((blocks, frames, feat, lanes), jnp.bfloat16),
            pltpu.VMEM((blocks, frames, feat, lanes), jnp.float32),
        ],
        out_shape=[jax.ShapeDtypeStruct((heads, feat, patches), jnp.bfloat16)] * frames
        + [jax.ShapeDtypeStruct((rows, feat), jnp.float32)],
        compiler_params=params(patches),
        cost_estimate=cost(4),
        name="temporal_late",
    )(lengths, task_ids, *operands)
    return list(results[:frames]), results[frames]


def gain_gradients(axis, heads, frames, clips, mixed_refs, gains_ref, grad_ref):
    tasks = gains_ref.shape[1]
    rows = sum(ref.shape[0] for ref in mixed_refs) // (frames * clips)
    each = mixed_refs[0].shape[0] // rows
    task_ids = lax.broadcasted_iota(jnp.int32, (tasks, HEAD_DIM), 0).astype(jnp.float32)
    for distance in range(frames):
        for head in range(heads):
            mixed = jnp.zeros((tasks, HEAD_DIM), jnp.float32)
            for clip in range(clips):
                block = distance * clips + clip
                ref, start = mixed_refs[block // each], block % each * rows
                task = ref[pl.ds(start + heads, 1), :]
                row = ref[pl.ds(start + head, 1), :]
                mixed = mixed + jnp.where(task_ids == task, row, 0.0)
            start = (partner(axis, distance) * heads + head) * HEAD_DIM
            cols = pl.ds(pl.multiple_of(start, HEAD_DIM), HEAD_DIM)
            grad_ref[0, :, cols] = gains_ref[1, :, cols] * mixed
            grad_ref[1, :, cols] = gains_ref[0, :, cols] * mixed


def swap(field, axis, size, distance):
    return lax.ppermute(field, axis, [(i, i ^ distance) for i in range(size)])


def split_by_heads(
    query_heads, key_heads, value_heads, cotangent, task_ids, lengths, gains, clips, frames, spaces
):
    patches, feat = query_heads.shape[2:]
    heads = feat // HEAD_DIM
    own = heads // frames
    width = own * HEAD_DIM
    queries, key_rows, values = (
        field.reshape(patches, feat) for field in (query_heads, key_heads, value_heads)
    )
    frame = lax.axis_index("tm")

    pieces = list(pack(cotangent.reshape(cotangent.shape[2:]), frames, spaces))
    queries, pieces = lax.optimization_barrier((queries, pieces))
    for distance in range(1, frames):
        pieces[distance] = swap(pieces[distance], "tm", frames, distance)
    fields = (queries, key_rows, values)
    weights, attended = forward("tm", *fields, frames)
    for distance in range(1, frames):
        attended[distance] = swap(attended[distance], "tm", frames, distance)
    backwards, _ = lax.optimization_barrier((pieces[::-1], weights))
    upstream = list(turn(backwards[::-1], attended[0]))
    for index in range(1, len(upstream)):
        upstream[index] = swap(upstream[index], "space", spaces, (index + 1) // 2)
    rows = lax.dynamic_index_in_dim(gains, task_ids[0], 1, keepdims=False)
    product = lax.dynamic_slice_in_dim(rows[0] * rows[1], frame * width, width, 0)
    gain = jnp.broadcast_to(
        product.reshape(own, HEAD_DIM, 1), (own, HEAD_DIM, patches // spaces)
    )
    attended[1], gain, upstream[0] = lax.optimization_barrier((attended[1], gain, upstream[0]))
    upstream[0], *kept = fetch(upstream[0], *fields)
    early = temporal_early(attended[1:-1], upstream[0], gain)
    grads, mixed = temporal_late(lengths, task_ids, attended[-1], upstream[1:], gain, early)
    for distance in reversed(range(2, frames)):
        grads[distance] = swap(grads[distance], "tm", frames, distance)
    here = grads[0]
    for bit in range(clips.bit_length() - 1):
        other = swap(mixed, "dp", clips, 1 << bit)
        if bit == 0:
            here, grads[1], other = lax.optimization_barrier((here, grads[1], other))
        mixed = jnp.concatenate([mixed, other], axis=0)
    grads[1] = swap(grads[1], "tm", frames, 1)
    results = backward("tm", kept, weights, [here], [0])
    mixed, results = lax.optimization_barrier((mixed, results))
    near, grads[1] = lax.optimization_barrier((mixed, grads[1]))
    mixed = [mixed, swap(near, "tm", frames, 1)] + [
        swap(mixed, "tm", frames, distance) for distance in range(2, frames)
    ]
    last = range(frames - 1, 0, -1)
    if frames > 2:
        results = backward("tm", kept, weights, [grads[1]], [1], results)
        last = range(frames - 1, 1, -1)
    grad_queries, grad_keys, grad_gains = backward(
        "tm",
        kept,
        weights,
        [grads[distance] for distance in last],
        list(last),
        results,
        mixed,
        gains,
        (own, frames, clips),
    )
    return (
        grad_queries.reshape(query_heads.shape),
        grad_keys.reshape(query_heads.shape),
        grad_gains,
    )


def temporal_grads(attended, upstream, gain_query, gain_keys, length):
    highest = lax.Precision.HIGHEST
    frames = attended.shape[0]
    score_scale = attended.shape[-1] ** (-0.5)
    floats = attended.astype(jnp.float32)
    inverse_rms = lax.rsqrt(jnp.mean(floats * floats, axis=-1, keepdims=True) + 1e-06)
    normed = floats * inverse_rms
    t_query = normed * gain_query
    t_keys = normed * gain_keys
    scores = jnp.einsum("txhd,uxhd->xhtu", t_query, t_keys, precision=highest) * score_scale
    frame_ids = jnp.arange(frames, dtype=jnp.int32)
    allowed = (frame_ids[None, :] <= frame_ids[:, None]) & (frame_ids[None, :] < length)
    scores = jnp.where(allowed, scores, -1e30)
    weights = jax.nn.softmax(scores, axis=-1)
    weights_low = lax.optimization_barrier(weights.astype(jnp.bfloat16)).astype(jnp.float32)
    valid_rows = (frame_ids < length).astype(jnp.float32)
    masked = upstream.astype(jnp.float32) * valid_rows[:, None, None, None]
    grad_weights = jnp.einsum("txhd,uxhd->xhtu", masked, floats, precision=highest)
    from_values = jnp.einsum("xhtu,txhd->uxhd", weights_low, masked, precision=highest)
    grad_scores = (
        weights
        * (grad_weights - jnp.sum(grad_weights * weights, axis=-1, keepdims=True))
        * score_scale
    )
    grad_tquery = jnp.einsum("xhtu,uxhd->txhd", grad_scores, t_keys, precision=highest)
    grad_tkeys = jnp.einsum("xhtu,txhd->uxhd", grad_scores, t_query, precision=highest)
    grad_normed = grad_tquery * gain_query + grad_tkeys * gain_keys
    grad_gain_query = jnp.sum(grad_tquery * normed, axis=(0, 1))
    grad_gain_keys = jnp.sum(grad_tkeys * normed, axis=(0, 1))
    from_norm = inverse_rms * (
        grad_normed - normed * jnp.mean(grad_normed * normed, axis=-1, keepdims=True)
    )
    grad_total = (masked + from_values + from_norm).astype(jnp.bfloat16)
    return (grad_total, grad_gain_query, grad_gain_keys)


def split_by_patches(query_heads, key_heads, value_heads, cotangent, task_ids, lengths, gains):
    patches, feat = query_heads.shape[2:]
    heads = feat // HEAD_DIM
    queries, key_rows, values = (
        field.reshape(patches, feat) for field in (query_heads, key_heads, value_heads)
    )
    fields = (queries, key_rows, values)
    weights, attended = forward(None, *fields, 1)
    attended_field = jnp.transpose(attended[0], (2, 0, 1)).reshape(1, 1, patches, feat)
    upstream = lax.all_to_all(
        lax.all_to_all(cotangent, "space", split_axis=3, concat_axis=2, tiled=True),
        "tm",
        split_axis=2,
        concat_axis=1,
        tiled=True,
    )
    frames_attended = lax.all_to_all(attended_field, "tm", split_axis=2, concat_axis=1, tiled=True)
    frames, local_patches = frames_attended.shape[1:3]
    selector = (task_ids[0] == jnp.arange(gains.shape[1], dtype=jnp.int32)).astype(jnp.float32)
    gain_query = jnp.sum(selector[:, None] * gains[0], axis=0).reshape(heads, HEAD_DIM)
    gain_keys = jnp.sum(selector[:, None] * gains[1], axis=0).reshape(heads, HEAD_DIM)
    grad_total, grad_gq, grad_gk = temporal_grads(
        frames_attended.reshape(frames, local_patches, heads, HEAD_DIM),
        upstream.reshape(frames, local_patches, heads, HEAD_DIM),
        gain_query,
        gain_keys,
        lengths[0],
    )
    gain_terms = jnp.stack(
        [
            selector[:, None] * grad_gq.reshape(1, feat),
            selector[:, None] * grad_gk.reshape(1, feat),
        ]
    )
    grad_gains = lax.psum(gain_terms, ("dp", "tm"))
    returned = lax.all_to_all(
        grad_total.reshape(1, frames, local_patches, feat),
        "tm",
        split_axis=1,
        concat_axis=2,
        tiled=True,
    )
    head_grads = jnp.transpose(returned.reshape(patches, heads, HEAD_DIM), (1, 2, 0))
    grad_queries, grad_keys = backward(None, fields, weights, [head_grads], [0])
    return (
        grad_queries.reshape(query_heads.shape),
        grad_keys.reshape(query_heads.shape),
        grad_gains,
    )


def solution(mesh):
    clips, frames, spaces = (mesh.shape[axis] for axis in ("dp", "tm", "space"))

    def local(query_heads, *others):
        heads = query_heads.shape[3] // HEAD_DIM
        powers = all(size & (size - 1) == 0 for size in (clips, frames, spaces))
        if powers and frames == 4 and heads % frames == 0:
            return split_by_heads(query_heads, *others, clips, frames, spaces)
        return split_by_patches(query_heads, *others)

    return jax.shard_map(
        local,
        mesh=mesh,
        in_specs=(
            P("dp", "tm", None, "space"),
            P("dp", "tm", None, "space"),
            P("dp", "tm", None, "space"),
            P("dp", "tm", "space", None),
            P("dp"),
            P("dp"),
            P(None, None, "space"),
        ),
        out_specs=(
            P("dp", "tm", None, "space"),
            P("dp", "tm", None, "space"),
            P(None, None, "space"),
        ),
        check_vma=False,
    )
```

```python
import functools

import jax
import jax.numpy as jnp
from jax import lax
from jax.experimental import pallas as pl
from jax.experimental.pallas import tpu as pltpu
from jax.sharding import PartitionSpec as P

HEAD_DIM = 128
GROUP = 16
MIB = 1024 * 1024


def params(patches):
    return pltpu.CompilerParams(vmem_limit_bytes=(16 if patches <= 512 else 60) * MIB)


def cost(microseconds):
    return pl.CostEstimate(flops=int(microseconds * 1e8), bytes_accessed=0, transcendentals=0)


def in_hbm(field):
    return pltpu.with_memory_space_constraint(field, pltpu.HBM)


def columns_dot(left, right):
    return lax.dot_general(
        left, right, (((1,), (1,)), ((), ())), preferred_element_type=jnp.float32
    )


def dot(left, right):
    return jnp.dot(left, right, preferred_element_type=jnp.float32)


def partner(axis, distance):
    return distance if axis is None else jnp.bitwise_xor(lax.axis_index(axis), distance)


def forward_kernel(axis, query_ref, key_ref, value_ref, weights_ref, *refs):
    (queries, key_rows, values, arrived), attended_refs = refs[-4:], refs[:-4]
    score_scale = HEAD_DIM ** (-0.5)
    groups, _, width = queries.shape
    own = width // HEAD_DIM
    copies = []
    for group in range(groups):
        cols = pl.ds(pl.multiple_of(partner(axis, group) * width, HEAD_DIM), width)
        for field, (source, target) in enumerate(
            ((query_ref, queries), (key_ref, key_rows), (value_ref, values))
        ):
            copy = pltpu.make_async_copy(
                source.at[:, cols], target.at[group], arrived.at[group, field]
            )
            copy.start()
            copies.append(copy)
    for group in range(groups):
        for copy in copies[3 * group : 3 * group + 3]:
            copy.wait()
        for head in range(own):
            cols = pl.ds(head * HEAD_DIM, HEAD_DIM)
            scores = columns_dot(key_rows[group, :, cols], queries[group, :, cols])
            largest = jnp.max(scores, axis=0, keepdims=True)
            raised = jnp.exp((scores - largest) * score_scale)
            weights = raised * (1.0 / jnp.sum(raised, axis=0, keepdims=True))
            weights_ref[group * own + head] = weights
            attended = dot(values[group, :, cols].T, weights.astype(jnp.bfloat16))
            attended_refs[group][head] = attended.astype(jnp.bfloat16)


def forward(axis, queries, key_rows, values, groups):
    patches, feat = queries.shape
    heads = feat // HEAD_DIM
    own = heads // groups
    fields = [in_hbm(field) for field in (queries, key_rows, values)]
    weights, *attended = pl.pallas_call(
        functools.partial(forward_kernel, axis),
        in_specs=[pl.BlockSpec(memory_space=pltpu.HBM)] * 3,
        out_specs=[pl.BlockSpec(memory_space=pltpu.VMEM)] * (1 + groups),
        scratch_shapes=[pltpu.VMEM((groups, patches, feat // groups), jnp.bfloat16)] * 3
        + [pltpu.SemaphoreType.DMA((groups, 3))],
        out_shape=[jax.ShapeDtypeStruct((heads, patches, patches), jnp.float32)]
        + [jax.ShapeDtypeStruct((own, HEAD_DIM, patches), jnp.bfloat16)] * groups,
        compiler_params=params(patches),
        cost_estimate=cost(6),
        name="spatial_forward",
    )(*fields)
    return weights, attended


def backward_group(axis, fields, weights_ref, grad_ref, distance, scratch, results, sent):
    query_ref, key_ref, value_ref = fields
    score_scale = HEAD_DIM ** (-0.5)
    own = grad_ref.shape[0]
    start = partner(axis, distance) * (own * HEAD_DIM)
    columns = [
        pl.ds(pl.multiple_of(start + head * HEAD_DIM, HEAD_DIM), HEAD_DIM) for head in range(own)
    ]
    spatial_grads = [dot(value_ref[:, columns[head]], grad_ref[head]) for head in range(own)]
    all_scores = []
    for head, spatial_grad in enumerate(spatial_grads):
        weights = weights_ref[distance * own + head]
        row_sum = jnp.sum(spatial_grad * weights, axis=0, keepdims=True)
        scores = weights * (spatial_grad - row_sum) * score_scale
        all_scores.append(scores.astype(jnp.bfloat16))
    gq, gk = scratch
    for head, scores in enumerate(all_scores):
        cols = pl.ds(head * HEAD_DIM, HEAD_DIM)
        gk[:, cols] = dot(scores, query_ref[:, columns[head]]).astype(jnp.bfloat16)
        gq[:, cols] = dot(key_ref[:, columns[head]].T, scores).astype(jnp.bfloat16).T
    there = pl.ds(pl.multiple_of(start, HEAD_DIM), own * HEAD_DIM)
    copies = [
        pltpu.make_async_copy(source, target.at[:, there], sent.at[side])
        for side, (source, target) in enumerate(zip(scratch, results))
    ]
    for copy in copies:
        copy.start()
    return copies


def backward_kernel(axis, distances, gains_of, *refs):
    fields, weights_ref, refs = refs[:3], refs[3], refs[4:]
    grad_refs, refs = refs[: len(distances)], refs[len(distances) :]
    *refs, gq, gk, sent = refs
    copies = []
    if gains_of:
        *mixed_refs, gains_ref, _, _, gq_ref, gk_ref, grad_gains_ref, grad_gains = refs
        gain_gradients(axis, *gains_of, mixed_refs, gains_ref, grad_gains)
        copy = pltpu.make_async_copy(grad_gains, grad_gains_ref, sent.at[len(distances), 0])
        copy.start()
        copies.append(copy)
    else:
        gq_ref, gk_ref = refs[-2:]
    for place, (distance, grad_ref) in enumerate(zip(distances, grad_refs)):
        copies += backward_group(
            axis,
            fields,
            weights_ref,
            grad_ref,
            distance,
            (gq.at[place], gk.at[place]),
            (gq_ref, gk_ref),
            sent.at[place],
        )
    for copy in copies:
        copy.wait()


def backward(axis, fields, weights, grads, distances, earlier=(), mixed=(), gains=None, gains_of=()):
    patches, feat = fields[0].shape
    own = grads[0].shape[0]
    operands = [*fields, weights, *grads] + ([*mixed, gains] if gains_of else [])
    block = pltpu.VMEM((len(distances), patches, own * HEAD_DIM), jnp.bfloat16)
    out_shape = [jax.ShapeDtypeStruct((patches, feat), jnp.bfloat16)] * 2
    scratch = [block, block, pltpu.SemaphoreType.DMA((len(distances) + 1, 2))]
    if gains_of:
        out_shape.append(jax.ShapeDtypeStruct(gains.shape, jnp.float32))
        scratch.insert(0, pltpu.VMEM(gains.shape, jnp.float32))
    return pl.pallas_call(
        functools.partial(backward_kernel, axis, distances, gains_of),
        in_specs=[pl.BlockSpec(memory_space=pltpu.VMEM)] * len(operands)
        + [pl.BlockSpec(memory_space=pl.ANY)] * len(earlier),
        out_specs=[pl.BlockSpec(memory_space=pl.ANY)] * len(out_shape),
        scratch_shapes=scratch,
        out_shape=out_shape,
        input_output_aliases={len(operands) + index: index for index in range(len(earlier))},
        compiler_params=params(patches),
        cost_estimate=cost(2),
        name="spatial_backward",
    )(*operands, *earlier)


def pack_kernel(field_ref, *refs):
    *packed_refs, rows, arrived = refs
    chunks, size, _ = rows.shape
    spaces, _, width = packed_refs[0].shape
    copies = [
        pltpu.make_async_copy(
            field_ref.at[pl.ds(chunk * size, size), :], rows.at[chunk], arrived.at[chunk]
        )
        for chunk in range(chunks)
    ]
    for copy in copies:
        copy.start()
    for chunk, copy in enumerate(copies):
        copy.wait()
        for distance, packed_ref in enumerate(packed_refs):
            for space in range(spaces):
                start = (space * len(packed_refs) + partner("tm", distance)) * width
                cols = pl.ds(pl.multiple_of(start, HEAD_DIM), width)
                packed_ref[space, pl.ds(chunk * size, size), :] = rows[chunk, :, cols]


def pack(field, frames, spaces):
    patches, feat = field.shape
    chunks = patches // GROUP
    shape = (spaces, patches, feat // (frames * spaces))
    return pl.pallas_call(
        pack_kernel,
        in_specs=[pl.BlockSpec(memory_space=pltpu.HBM)],
        out_specs=[pl.BlockSpec(memory_space=pltpu.VMEM)] * frames,
        out_shape=[jax.ShapeDtypeStruct(shape, field.dtype)] * frames,
        scratch_shapes=[
            pltpu.VMEM((chunks, patches // chunks, feat), field.dtype),
            pltpu.SemaphoreType.DMA((chunks,)),
        ],
        compiler_params=params(patches),
        cost_estimate=cost(1),
        name="pack_cotangent",
    )(in_hbm(field))


def turn_kernel(frames, *refs):
    piece_refs, (plane_ref, own_hbm, *other_refs), (turned, own_ref, sent) = (
        refs[:frames][::-1],
        refs[frames:-3],
        refs[-3:],
    )
    spaces, lanes, _ = piece_refs[0].shape
    for space in range(spaces):
        place = pl.multiple_of(partner("space", space) * lanes, lanes)
        own_ref[frames + space] = plane_ref[:, :, pl.ds(place, lanes)]
    heads = own_ref.shape[1]
    for space in range(spaces):
        target = turned if space else own_ref
        source = partner("space", space)
        for distance, ref in enumerate(piece_refs):
            frame = partner("tm", distance)
            for head in range(heads):
                cols = pl.ds(head * HEAD_DIM, HEAD_DIM)
                target[frame, head] = ref[source, :, cols].T
        if space == 0:
            copy = pltpu.make_async_copy(own_ref, own_hbm, sent)
            copy.start()
        else:
            half = frames // 2
            other_refs[2 * space - 2][...] = turned[:half]
            other_refs[2 * space - 1][...] = turned[half:]
    copy.wait()


def turn(pieces, plane):
    spaces, patches, feat = pieces[0].shape
    frames, heads = len(pieces), feat // HEAD_DIM
    turned = (heads, HEAD_DIM, patches)
    sizes = [frames + spaces] + [frames // 2, frames - frames // 2] * (spaces - 1)
    return pl.pallas_call(
        functools.partial(turn_kernel, frames),
        in_specs=[pl.BlockSpec(memory_space=pltpu.VMEM)] * (frames + 1),
        out_specs=[pl.BlockSpec(memory_space=pltpu.HBM)]
        + [pl.BlockSpec(memory_space=pltpu.VMEM)] * (len(sizes) - 1),
        out_shape=[jax.ShapeDtypeStruct((size,) + turned, pieces[0].dtype) for size in sizes],
        scratch_shapes=[
            pltpu.VMEM((frames,) + turned, pieces[0].dtype),
            pltpu.VMEM((frames + spaces,) + turned, pieces[0].dtype),
            pltpu.SemaphoreType.DMA,
        ],
        compiler_params=params(patches),
        cost_estimate=cost(2),
        name="turn_cotangent",
    )(*reversed(pieces), plane)


def temporal_part(length, load_attended, load_upstream, load_gain, fields, ups, normed, grad_ref):
    frames, feat, lanes = grad_ref.shape
    half = GROUP // 2
    score_scale = feat ** (-0.5)
    pairs = [(t, u) for t in range(frames) for u in range(t + 1)]
    every = range(frames)
    valid = [jnp.where(t < length, 1.0, 0.0).astype(jnp.float32) for t in every]
    bias = [jnp.where(u < length, 0.0, -1e30).astype(jnp.float32) for u in every]

    def total(piece):
        return jnp.broadcast_to(jnp.sum(piece, axis=0, keepdims=True), (half, lanes))

    squares = [jnp.zeros((half, lanes), jnp.float32) for _ in every]
    for group in range(feat // GROUP):
        rows = pl.ds(group * GROUP, GROUP)
        for t in every:
            field = load_attended(t, rows).astype(jnp.float32)
            fields[t, rows, :] = field
            ups[t, rows, :] = load_upstream(t, rows).astype(jnp.float32)
            low, high = field[:half], field[half:]
            squares[t] = squares[t] + (low * low + high * high)
    inverse = [lax.rsqrt(total(squares[t]) * (1.0 / feat) + 1e-06) for t in every]

    raw = {pair: jnp.zeros((half, lanes), jnp.float32) for pair in pairs}
    grad = {pair: jnp.zeros((half, lanes), jnp.float32) for pair in pairs}
    for group in range(feat // half):
        rows = pl.ds(group * half, half)
        gain = load_gain(rows)
        here = [fields[t, rows, :] for t in every]
        above = [ups[t, rows, :] for t in every]
        scaled = [here[t] * inverse[t] for t in every]
        gained = [scaled[t] * gain for t in every]
        for t in every:
            normed[t, rows, :] = scaled[t]
        for t, u in pairs:
            raw[t, u] = raw[t, u] + gained[t] * scaled[u]
            grad[t, u] = grad[t, u] + above[t] * here[u]

    value_part, score_part = {}, {}
    for t in every:
        seen = range(t + 1)
        for u in seen:
            raw[t, u] = total(raw[t, u])
            grad[t, u] = total(grad[t, u]) * valid[t]
        scores = [raw[t, u] * score_scale + bias[u] for u in seen]
        largest = functools.reduce(jnp.maximum, scores)
        raised = [jnp.exp(score - largest) for score in scores]
        over = 1.0 / functools.reduce(jnp.add, raised)
        weights = [piece * over for piece in raised]
        mean_grad = functools.reduce(jnp.add, [weights[u] * grad[t, u] for u in seen])
        for u in seen:
            rounded = weights[u].astype(jnp.bfloat16).astype(jnp.float32)
            value_part[t, u] = (rounded + (1.0 if u == t else 0.0)) * valid[t]
            score_part[t, u] = weights[u] * (grad[t, u] - mean_grad) * score_scale

    both = {(t, u): score_part[t, u] * (2.0 if t == u else 1.0) for t, u in pairs}
    both.update({(u, t): both[t, u] for t, u in pairs})
    raw.update({(u, t): raw[t, u] for t, u in pairs})
    mean_part = [
        functools.reduce(jnp.add, [both[u, v] * raw[u, v] for v in every]) * (1.0 / feat)
        for u in every
    ]

    all_mixed = []
    for group in range(feat // GROUP):
        outs = [[] for _ in every]
        for side in range(2):
            rows = pl.ds(group * GROUP + side * half, half)
            gain = load_gain(rows)
            scaled = [normed[t, rows, :] for t in every]
            above = [ups[t, rows, :] for t in every]
            mixed = jnp.zeros((half, lanes), jnp.float32)
            for u in every:
                crossed = functools.reduce(jnp.add, [both[u, v] * scaled[v] for v in every])
                mixed = mixed + crossed * scaled[u]
                from_norm = inverse[u] * (gain * crossed - scaled[u] * mean_part[u])
                direct = functools.reduce(
                    jnp.add, [value_part[t, u] * above[t] for t in range(u, frames)]
                )
                outs[u].append(direct + from_norm)
            all_mixed.append(mixed)
        for u in every:
            grad_ref[u, pl.ds(group * GROUP, GROUP), :] = jnp.concatenate(
                outs[u], axis=0
            ).astype(jnp.bfloat16)
    return jnp.concatenate(all_mixed, axis=0)


def fetch_kernel(*refs):
    *refs, arrived = refs
    number = len(refs) // 2
    copies = [
        pltpu.make_async_copy(source, target, arrived.at[index])
        for index, (source, target) in enumerate(zip(refs[:number], refs[number:]))
    ]
    for copy in copies:
        copy.start()
    for copy in copies:
        copy.wait()


def fetch(*fields):
    return pl.pallas_call(
        fetch_kernel,
        in_specs=[pl.BlockSpec(memory_space=pltpu.HBM)] * len(fields),
        out_specs=[pl.BlockSpec(memory_space=pltpu.VMEM)] * len(fields),
        out_shape=[jax.ShapeDtypeStruct(field.shape, field.dtype) for field in fields],
        scratch_shapes=[pltpu.SemaphoreType.DMA((len(fields),))],
        compiler_params=params(0),
        cost_estimate=cost(1),
        name="fetch",
    )(*[in_hbm(field) for field in fields])


def temporal_kernel(frames, spaces, length_ref, task_ref, *refs):
    attended_refs, (gain_ref, own_ref, *other_refs), refs = (
        refs[: frames - 1],
        refs[frames - 1 : frames - 1 + 2 * spaces],
        refs[frames - 1 + 2 * spaces :],
    )
    grad_refs, (mixed_ref, attended, grads, wide) = refs[:frames], refs[frames:]
    heads, lanes = own_ref.shape[1], own_ref.shape[3]
    half = frames // 2
    mixed_ref[...] = jnp.full(mixed_ref.shape, task_ref[0].astype(jnp.float32))

    def load_upstream(space, head, t, rows):
        if space == 0:
            return own_ref[t, head, rows, :]
        return other_refs[2 * space - 2 + t // half][t % half, head, rows, :]

    places = [
        pl.ds(pl.multiple_of(partner("space", space) * lanes, lanes), lanes)
        for space in range(spaces)
    ]
    for head in range(heads):
        for space, here in enumerate(places):
            attended[head, space, partner("tm", 0)] = own_ref[frames + space, head]
            for distance, ref in enumerate(attended_refs):
                attended[head, space, partner("tm", distance + 1)] = ref[head, :, here]
        mixed = [
            temporal_part(
                length_ref[0],
                lambda t, rows: attended[head, space, t, rows, :],
                functools.partial(load_upstream, space, head),
                lambda rows: gain_ref[head, rows, :],
                wide.at[head % 2, space, 0],
                wide.at[head % 2, space, 1],
                wide.at[head % 2, space, 2],
                grads.at[head, space],
            )
            for space in range(spaces)
        ]
        summed = functools.reduce(jnp.add, mixed)
        mixed_ref[pl.ds(head, 1), :] = jnp.sum(summed.T, axis=0, keepdims=True) * 0.5
        for distance, ref in enumerate(grad_refs):
            frame = partner("tm", distance)
            for space, here in enumerate(places):
                ref[head, :, here] = grads[head, space, frame]


def temporal(lengths, task_ids, attended, upstream, gain):
    _, heads, feat, lanes = upstream[0].shape
    frames, spaces = len(attended) + 1, (len(upstream) + 1) // 2
    patches = spaces * lanes
    rows = -(-(heads + 1) // 8) * 8
    operands = [*attended, gain, *upstream]
    block = (heads, spaces, frames, feat, lanes)
    results = pl.pallas_call(
        functools.partial(temporal_kernel, frames, spaces),
        in_specs=[pl.BlockSpec(memory_space=pltpu.SMEM)] * 2
        + [pl.BlockSpec(memory_space=pltpu.VMEM)] * len(operands),
        out_specs=[pl.BlockSpec(memory_space=pltpu.VMEM)] * (frames + 1),
        scratch_shapes=[
            pltpu.VMEM(block, jnp.bfloat16),
            pltpu.VMEM(block, jnp.bfloat16),
            pltpu.VMEM((2, spaces, 3, frames, feat, lanes), jnp.float32),
        ],
        out_shape=[jax.ShapeDtypeStruct((heads, feat, patches), jnp.bfloat16)] * frames
        + [jax.ShapeDtypeStruct((rows, feat), jnp.float32)],
        compiler_params=params(patches),
        cost_estimate=cost(4),
        name="temporal",
    )(lengths, task_ids, *operands)
    return list(results[:frames]), results[frames]


def gain_gradients(axis, heads, frames, clips, mixed_refs, gains_ref, grad_ref):
    tasks = gains_ref.shape[1]
    rows = sum(ref.shape[0] for ref in mixed_refs) // (frames * clips)
    each = mixed_refs[0].shape[0] // rows
    task_ids = lax.broadcasted_iota(jnp.int32, (tasks, HEAD_DIM), 0).astype(jnp.float32)
    for distance in range(frames):
        for head in range(heads):
            mixed = jnp.zeros((tasks, HEAD_DIM), jnp.float32)
            for clip in range(clips):
                block = distance * clips + clip
                ref, start = mixed_refs[block // each], block % each * rows
                task = ref[pl.ds(start + heads, 1), :]
                row = ref[pl.ds(start + head, 1), :]
                mixed = mixed + jnp.where(task_ids == task, row, 0.0)
            start = (partner(axis, distance) * heads + head) * HEAD_DIM
            cols = pl.ds(pl.multiple_of(start, HEAD_DIM), HEAD_DIM)
            grad_ref[0, :, cols] = gains_ref[1, :, cols] * mixed
            grad_ref[1, :, cols] = gains_ref[0, :, cols] * mixed


def swap(field, axis, size, distance):
    return lax.ppermute(field, axis, [(i, i ^ distance) for i in range(size)])


def split_by_heads(
    query_heads, key_heads, value_heads, cotangent, task_ids, lengths, gains, clips, frames, spaces
):
    patches, feat = query_heads.shape[2:]
    heads = feat // HEAD_DIM
    own = heads // frames
    width = own * HEAD_DIM
    queries, key_rows, values = (
        field.reshape(patches, feat) for field in (query_heads, key_heads, value_heads)
    )
    frame = lax.axis_index("tm")

    pieces = list(pack(cotangent.reshape(cotangent.shape[2:]), frames, spaces))
    queries, pieces = lax.optimization_barrier((queries, pieces))
    for distance in range(1, frames):
        pieces[distance] = swap(pieces[distance], "tm", frames, distance)
    fields = (queries, key_rows, values)
    weights, attended = forward("tm", *fields, frames)
    for distance in range(1, frames):
        attended[distance] = swap(attended[distance], "tm", frames, distance)
    backwards, _ = lax.optimization_barrier((pieces[::-1], weights))
    upstream = list(turn(backwards[::-1], attended[0]))
    for index in range(1, len(upstream)):
        upstream[index] = swap(upstream[index], "space", spaces, (index + 1) // 2)
    rows = lax.dynamic_index_in_dim(gains, task_ids[0], 1, keepdims=False)
    product = lax.dynamic_slice_in_dim(rows[0] * rows[1], frame * width, width, 0)
    gain = jnp.broadcast_to(
        product.reshape(own, HEAD_DIM, 1), (own, HEAD_DIM, patches // spaces)
    )
    attended[1], gain, upstream[0] = lax.optimization_barrier((attended[1], gain, upstream[0]))
    upstream[0], *kept = fetch(upstream[0], *fields)
    grads, mixed = temporal(lengths, task_ids, attended[1:], upstream, gain)
    for distance in reversed(range(2, frames)):
        grads[distance] = swap(grads[distance], "tm", frames, distance)
    here = grads[0]
    for bit in range(clips.bit_length() - 1):
        other = swap(mixed, "dp", clips, 1 << bit)
        if bit == 0:
            here, grads[1], other = lax.optimization_barrier((here, grads[1], other))
        mixed = jnp.concatenate([mixed, other], axis=0)
    grads[1] = swap(grads[1], "tm", frames, 1)
    results = backward("tm", kept, weights, [here], [0])
    mixed, results = lax.optimization_barrier((mixed, results))
    near, grads[1] = lax.optimization_barrier((mixed, grads[1]))
    mixed = [mixed, swap(near, "tm", frames, 1)] + [
        swap(mixed, "tm", frames, distance) for distance in range(2, frames)
    ]
    last = range(frames - 1, 0, -1)
    if frames > 2:
        for distance in [1, *range(3, frames)]:
            results = backward("tm", kept, weights, [grads[distance]], [distance], results)
        last = [2]
    grad_queries, grad_keys, grad_gains = backward(
        "tm",
        kept,
        weights,
        [grads[distance] for distance in last],
        list(last),
        results,
        mixed,
        gains,
        (own, frames, clips),
    )
    return (
        grad_queries.reshape(query_heads.shape),
        grad_keys.reshape(query_heads.shape),
        grad_gains,
    )


def temporal_grads(attended, upstream, gain_query, gain_keys, length):
    highest = lax.Precision.HIGHEST
    frames = attended.shape[0]
    score_scale = attended.shape[-1] ** (-0.5)
    floats = attended.astype(jnp.float32)
    inverse_rms = lax.rsqrt(jnp.mean(floats * floats, axis=-1, keepdims=True) + 1e-06)
    normed = floats * inverse_rms
    t_query = normed * gain_query
    t_keys = normed * gain_keys
    scores = jnp.einsum("txhd,uxhd->xhtu", t_query, t_keys, precision=highest) * score_scale
    frame_ids = jnp.arange(frames, dtype=jnp.int32)
    allowed = (frame_ids[None, :] <= frame_ids[:, None]) & (frame_ids[None, :] < length)
    scores = jnp.where(allowed, scores, -1e30)
    weights = jax.nn.softmax(scores, axis=-1)
    weights_low = lax.optimization_barrier(weights.astype(jnp.bfloat16)).astype(jnp.float32)
    valid_rows = (frame_ids < length).astype(jnp.float32)
    masked = upstream.astype(jnp.float32) * valid_rows[:, None, None, None]
    grad_weights = jnp.einsum("txhd,uxhd->xhtu", masked, floats, precision=highest)
    from_values = jnp.einsum("xhtu,txhd->uxhd", weights_low, masked, precision=highest)
    grad_scores = (
        weights
        * (grad_weights - jnp.sum(grad_weights * weights, axis=-1, keepdims=True))
        * score_scale
    )
    grad_tquery = jnp.einsum("xhtu,uxhd->txhd", grad_scores, t_keys, precision=highest)
    grad_tkeys = jnp.einsum("xhtu,txhd->uxhd", grad_scores, t_query, precision=highest)
    grad_normed = grad_tquery * gain_query + grad_tkeys * gain_keys
    grad_gain_query = jnp.sum(grad_tquery * normed, axis=(0, 1))
    grad_gain_keys = jnp.sum(grad_tkeys * normed, axis=(0, 1))
    from_norm = inverse_rms * (
        grad_normed - normed * jnp.mean(grad_normed * normed, axis=-1, keepdims=True)
    )
    grad_total = (masked + from_values + from_norm).astype(jnp.bfloat16)
    return (grad_total, grad_gain_query, grad_gain_keys)


def split_by_patches(query_heads, key_heads, value_heads, cotangent, task_ids, lengths, gains):
    patches, feat = query_heads.shape[2:]
    heads = feat // HEAD_DIM
    queries, key_rows, values = (
        field.reshape(patches, feat) for field in (query_heads, key_heads, value_heads)
    )
    fields = (queries, key_rows, values)
    weights, attended = forward(None, *fields, 1)
    attended_field = jnp.transpose(attended[0], (2, 0, 1)).reshape(1, 1, patches, feat)
    upstream = lax.all_to_all(
        lax.all_to_all(cotangent, "space", split_axis=3, concat_axis=2, tiled=True),
        "tm",
        split_axis=2,
        concat_axis=1,
        tiled=True,
    )
    frames_attended = lax.all_to_all(attended_field, "tm", split_axis=2, concat_axis=1, tiled=True)
    frames, local_patches = frames_attended.shape[1:3]
    selector = (task_ids[0] == jnp.arange(gains.shape[1], dtype=jnp.int32)).astype(jnp.float32)
    gain_query = jnp.sum(selector[:, None] * gains[0], axis=0).reshape(heads, HEAD_DIM)
    gain_keys = jnp.sum(selector[:, None] * gains[1], axis=0).reshape(heads, HEAD_DIM)
    grad_total, grad_gq, grad_gk = temporal_grads(
        frames_attended.reshape(frames, local_patches, heads, HEAD_DIM),
        upstream.reshape(frames, local_patches, heads, HEAD_DIM),
        gain_query,
        gain_keys,
        lengths[0],
    )
    gain_terms = jnp.stack(
        [
            selector[:, None] * grad_gq.reshape(1, feat),
            selector[:, None] * grad_gk.reshape(1, feat),
        ]
    )
    grad_gains = lax.psum(gain_terms, ("dp", "tm"))
    returned = lax.all_to_all(
        grad_total.reshape(1, frames, local_patches, feat),
        "tm",
        split_axis=1,
        concat_axis=2,
        tiled=True,
    )
    head_grads = jnp.transpose(returned.reshape(patches, heads, HEAD_DIM), (1, 2, 0))
    grad_queries, grad_keys = backward(None, fields, weights, [head_grads], [0])
    return (
        grad_queries.reshape(query_heads.shape),
        grad_keys.reshape(query_heads.shape),
        grad_gains,
    )


def solution(mesh):
    clips, frames, spaces = (mesh.shape[axis] for axis in ("dp", "tm", "space"))

    def local(query_heads, *others):
        heads = query_heads.shape[3] // HEAD_DIM
        powers = all(size & (size - 1) == 0 for size in (clips, frames, spaces))
        if powers and 2 <= frames <= 4 and heads % frames == 0:
            return split_by_heads(query_heads, *others, clips, frames, spaces)
        return split_by_patches(query_heads, *others)

    return jax.shard_map(
        local,
        mesh=mesh,
        in_specs=(
            P("dp", "tm", None, "space"),
            P("dp", "tm", None, "space"),
            P("dp", "tm", None, "space"),
            P("dp", "tm", "space", None),
            P("dp"),
            P("dp"),
            P(None, None, "space"),
        ),
        out_specs=(
            P("dp", "tm", None, "space"),
            P("dp", "tm", None, "space"),
            P(None, None, "space"),
        ),
        check_vma=False,
    )
```

```python
import functools

import jax
import jax.numpy as jnp
from jax import lax
from jax.experimental import pallas as pl
from jax.experimental.pallas import tpu as pltpu
from jax.sharding import PartitionSpec as P

HEAD_DIM = 128
GROUP = 16
MIB = 1024 * 1024


def params(patches):
    return pltpu.CompilerParams(vmem_limit_bytes=(16 if patches <= 512 else 60) * MIB)


def cost(microseconds):
    return pl.CostEstimate(flops=int(microseconds * 1e8), bytes_accessed=0, transcendentals=0)


def in_hbm(field):
    return pltpu.with_memory_space_constraint(field, pltpu.HBM)


def columns_dot(left, right):
    return lax.dot_general(
        left, right, (((1,), (1,)), ((), ())), preferred_element_type=jnp.float32
    )


def dot(left, right):
    return jnp.dot(left, right, preferred_element_type=jnp.float32)


def partner(axis, distance):
    return distance if axis is None else jnp.bitwise_xor(lax.axis_index(axis), distance)


def forward_kernel(axis, query_ref, key_ref, value_ref, weights_ref, *refs):
    (queries, key_rows, values, arrived), attended_refs = refs[-4:], refs[:-4]
    score_scale = HEAD_DIM ** (-0.5)
    groups, _, width = queries.shape
    own = width // HEAD_DIM
    copies = []
    for group in range(groups):
        cols = pl.ds(pl.multiple_of(partner(axis, group) * width, HEAD_DIM), width)
        for field, (source, target) in enumerate(
            ((query_ref, queries), (key_ref, key_rows), (value_ref, values))
        ):
            copy = pltpu.make_async_copy(
                source.at[:, cols], target.at[group], arrived.at[group, field]
            )
            copy.start()
            copies.append(copy)
    for group in range(groups):
        for copy in copies[3 * group : 3 * group + 3]:
            copy.wait()
        for head in range(own):
            cols = pl.ds(head * HEAD_DIM, HEAD_DIM)
            scores = columns_dot(key_rows[group, :, cols], queries[group, :, cols])
            largest = jnp.max(scores, axis=0, keepdims=True)
            raised = jnp.exp((scores - largest) * score_scale)
            weights = raised * (1.0 / jnp.sum(raised, axis=0, keepdims=True))
            weights_ref[group * own + head] = weights
            attended = dot(values[group, :, cols].T, weights.astype(jnp.bfloat16))
            attended_refs[group][head] = attended.astype(jnp.bfloat16)


def forward(axis, queries, key_rows, values, groups):
    patches, feat = queries.shape
    heads = feat // HEAD_DIM
    own = heads // groups
    fields = [in_hbm(field) for field in (queries, key_rows, values)]
    weights, *attended = pl.pallas_call(
        functools.partial(forward_kernel, axis),
        in_specs=[pl.BlockSpec(memory_space=pltpu.HBM)] * 3,
        out_specs=[pl.BlockSpec(memory_space=pltpu.VMEM)] * (1 + groups),
        scratch_shapes=[pltpu.VMEM((groups, patches, feat // groups), jnp.bfloat16)] * 3
        + [pltpu.SemaphoreType.DMA((groups, 3))],
        out_shape=[jax.ShapeDtypeStruct((heads, patches, patches), jnp.float32)]
        + [jax.ShapeDtypeStruct((own, HEAD_DIM, patches), jnp.bfloat16)] * groups,
        compiler_params=params(patches),
        cost_estimate=cost(6),
        name="spatial_forward",
    )(*fields)
    return weights, attended


def backward_kernel(axis, distances, gains_of, *refs):
    (query_ref, key_ref, value_ref), weights_ref, refs = refs[:3], refs[3], refs[4:]
    grad_refs, refs = refs[: len(distances)], refs[len(distances) :]
    *refs, gq, gk, sent = refs
    score_scale = HEAD_DIM ** (-0.5)
    own = grad_refs[0].shape[0]
    copies = []

    def send(source, target, semaphore):
        copy = pltpu.make_async_copy(source, target, semaphore)
        copy.start()
        copies.append(copy)

    if gains_of:
        *mixed_refs, gains_ref, _, _, gq_ref, gk_ref, grad_gains_ref, grad_gains = refs
        gain_gradients(axis, *gains_of, mixed_refs, gains_ref, grad_gains)
        send(grad_gains, grad_gains_ref, sent.at[len(distances), 0])
    else:
        gq_ref, gk_ref = refs[-2:]
    starts = [partner(axis, distance) * (own * HEAD_DIM) for distance in distances]
    heads = [(group, head) for group in range(len(distances)) for head in range(own)]
    columns = [
        pl.ds(pl.multiple_of(starts[group] + head * HEAD_DIM, HEAD_DIM), HEAD_DIM)
        for group, head in heads
    ]
    spatial_grads = [
        dot(value_ref[:, cols], grad_refs[group][head])
        for cols, (group, head) in zip(columns, heads)
    ]
    all_scores = []
    for spatial_grad, (group, head) in zip(spatial_grads, heads):
        weights = weights_ref[distances[group] * own + head]
        row_sum = jnp.sum(spatial_grad * weights, axis=0, keepdims=True)
        scores = weights * (spatial_grad - row_sum) * score_scale
        all_scores.append(scores.astype(jnp.bfloat16))
    there = [pl.ds(pl.multiple_of(start, HEAD_DIM), own * HEAD_DIM) for start in starts]
    for scores, cols, (group, head) in zip(all_scores, columns, heads):
        here = pl.ds(head * HEAD_DIM, HEAD_DIM)
        gk[group, :, here] = dot(scores, query_ref[:, cols]).astype(jnp.bfloat16)
    for group, cols in enumerate(there):
        send(gk.at[group], gk_ref.at[:, cols], sent.at[group, 1])
    for scores, cols, (group, head) in zip(all_scores, columns, heads):
        here = pl.ds(head * HEAD_DIM, HEAD_DIM)
        gq[group, :, here] = dot(key_ref[:, cols].T, scores).astype(jnp.bfloat16).T
    for group, cols in enumerate(there):
        send(gq.at[group], gq_ref.at[:, cols], sent.at[group, 0])
    for copy in copies:
        copy.wait()


def backward(axis, fields, weights, grads, distances, earlier=(), mixed=(), gains=None, gains_of=()):
    patches, feat = fields[0].shape
    own = grads[0].shape[0]
    operands = [*fields, weights, *grads] + ([*mixed, gains] if gains_of else [])
    block = pltpu.VMEM((len(distances), patches, own * HEAD_DIM), jnp.bfloat16)
    out_shape = [jax.ShapeDtypeStruct((patches, feat), jnp.bfloat16)] * 2
    scratch = [block, block, pltpu.SemaphoreType.DMA((len(distances) + 1, 2))]
    if gains_of:
        out_shape.append(jax.ShapeDtypeStruct(gains.shape, jnp.float32))
        scratch.insert(0, pltpu.VMEM(gains.shape, jnp.float32))
    return pl.pallas_call(
        functools.partial(backward_kernel, axis, distances, gains_of),
        in_specs=[pl.BlockSpec(memory_space=pltpu.VMEM)] * len(operands)
        + [pl.BlockSpec(memory_space=pl.ANY)] * len(earlier),
        out_specs=[pl.BlockSpec(memory_space=pl.ANY)] * len(out_shape),
        scratch_shapes=scratch,
        out_shape=out_shape,
        input_output_aliases={len(operands) + index: index for index in range(len(earlier))},
        compiler_params=params(patches),
        cost_estimate=cost(2),
        name="spatial_backward",
    )(*operands, *earlier)


def pack_kernel(field_ref, *refs):
    *packed_refs, rows, arrived = refs
    chunks, size, _ = rows.shape
    spaces, _, width = packed_refs[0].shape
    copies = [
        pltpu.make_async_copy(
            field_ref.at[pl.ds(chunk * size, size), :], rows.at[chunk], arrived.at[chunk]
        )
        for chunk in range(chunks)
    ]
    for copy in copies:
        copy.start()
    for chunk, copy in enumerate(copies):
        copy.wait()
        for distance, packed_ref in enumerate(packed_refs):
            for space in range(spaces):
                start = (space * len(packed_refs) + partner("tm", distance)) * width
                cols = pl.ds(pl.multiple_of(start, HEAD_DIM), width)
                packed_ref[space, pl.ds(chunk * size, size), :] = rows[chunk, :, cols]


def pack(field, frames, spaces):
    patches, feat = field.shape
    chunks = patches // GROUP
    shape = (spaces, patches, feat // (frames * spaces))
    return pl.pallas_call(
        pack_kernel,
        in_specs=[pl.BlockSpec(memory_space=pltpu.HBM)],
        out_specs=[pl.BlockSpec(memory_space=pltpu.VMEM)] * frames,
        out_shape=[jax.ShapeDtypeStruct(shape, field.dtype)] * frames,
        scratch_shapes=[
            pltpu.VMEM((chunks, patches // chunks, feat), field.dtype),
            pltpu.SemaphoreType.DMA((chunks,)),
        ],
        compiler_params=params(patches),
        cost_estimate=cost(1),
        name="pack_cotangent",
    )(in_hbm(field))


def turn_kernel(frames, *refs):
    piece_refs, (plane_ref, own_hbm, *other_refs), (turned, own_ref, sent) = (
        refs[:frames][::-1],
        refs[frames:-3],
        refs[-3:],
    )
    spaces, lanes, _ = piece_refs[0].shape
    for space in range(spaces):
        place = pl.multiple_of(partner("space", space) * lanes, lanes)
        own_ref[frames + space] = plane_ref[:, :, pl.ds(place, lanes)]
    heads = own_ref.shape[1]
    for space in range(spaces):
        target = turned if space else own_ref
        source = partner("space", space)
        for distance, ref in enumerate(piece_refs):
            frame = partner("tm", distance)
            for head in range(heads):
                cols = pl.ds(head * HEAD_DIM, HEAD_DIM)
                target[frame, head] = ref[source, :, cols].T
        if space == 0:
            copy = pltpu.make_async_copy(own_ref, own_hbm, sent)
            copy.start()
        else:
            half = frames // 2
            other_refs[2 * space - 2][...] = turned[:half]
            other_refs[2 * space - 1][...] = turned[half:]
    copy.wait()


def turn(pieces, plane):
    spaces, patches, feat = pieces[0].shape
    frames, heads = len(pieces), feat // HEAD_DIM
    turned = (heads, HEAD_DIM, patches)
    sizes = [frames + spaces] + [frames // 2, frames - frames // 2] * (spaces - 1)
    return pl.pallas_call(
        functools.partial(turn_kernel, frames),
        in_specs=[pl.BlockSpec(memory_space=pltpu.VMEM)] * (frames + 1),
        out_specs=[pl.BlockSpec(memory_space=pltpu.HBM)]
        + [pl.BlockSpec(memory_space=pltpu.VMEM)] * (len(sizes) - 1),
        out_shape=[jax.ShapeDtypeStruct((size,) + turned, pieces[0].dtype) for size in sizes],
        scratch_shapes=[
            pltpu.VMEM((frames,) + turned, pieces[0].dtype),
            pltpu.VMEM((frames + spaces,) + turned, pieces[0].dtype),
            pltpu.SemaphoreType.DMA,
        ],
        compiler_params=params(patches),
        cost_estimate=cost(2),
        name="turn_cotangent",
    )(*reversed(pieces), plane)


def temporal_part(length, load_attended, load_upstream, load_gain, fields, ups, normed, grad_ref):
    frames, feat, lanes = grad_ref.shape
    half = GROUP // 2
    score_scale = feat ** (-0.5)
    pairs = [(t, u) for t in range(frames) for u in range(t + 1)]
    every = range(frames)
    valid = [jnp.where(t < length, 1.0, 0.0).astype(jnp.float32) for t in every]
    bias = [jnp.where(u < length, 0.0, -1e30).astype(jnp.float32) for u in every]

    def total(piece):
        return jnp.broadcast_to(jnp.sum(piece, axis=0, keepdims=True), (half, lanes))

    squares = [jnp.zeros((half, lanes), jnp.float32) for _ in every]
    for group in range(feat // GROUP):
        rows = pl.ds(group * GROUP, GROUP)
        for t in every:
            field = load_attended(t, rows).astype(jnp.float32)
            fields[t, rows, :] = field
            ups[t, rows, :] = load_upstream(t, rows).astype(jnp.float32)
            low, high = field[:half], field[half:]
            squares[t] = squares[t] + (low * low + high * high)
    inverse = [lax.rsqrt(total(squares[t]) * (1.0 / feat) + 1e-06) for t in every]

    raw = {pair: jnp.zeros((half, lanes), jnp.float32) for pair in pairs}
    grad = {pair: jnp.zeros((half, lanes), jnp.float32) for pair in pairs}
    for group in range(feat // half):
        rows = pl.ds(group * half, half)
        gain = load_gain(rows)
        here = [fields[t, rows, :] for t in every]
        above = [ups[t, rows, :] for t in every]
        scaled = [here[t] * inverse[t] for t in every]
        gained = [scaled[t] * gain for t in every]
        for t in every:
            normed[t, rows, :] = scaled[t]
        for t, u in pairs:
            raw[t, u] = raw[t, u] + gained[t] * scaled[u]
            grad[t, u] = grad[t, u] + above[t] * here[u]

    value_part, score_part = {}, {}
    for t in every:
        seen = range(t + 1)
        for u in seen:
            raw[t, u] = total(raw[t, u])
            grad[t, u] = total(grad[t, u]) * valid[t]
        scores = [raw[t, u] * score_scale + bias[u] for u in seen]
        largest = functools.reduce(jnp.maximum, scores)
        raised = [jnp.exp(score - largest) for score in scores]
        over = 1.0 / functools.reduce(jnp.add, raised)
        weights = [piece * over for piece in raised]
        mean_grad = functools.reduce(jnp.add, [weights[u] * grad[t, u] for u in seen])
        for u in seen:
            rounded = weights[u].astype(jnp.bfloat16).astype(jnp.float32)
            value_part[t, u] = (rounded + (1.0 if u == t else 0.0)) * valid[t]
            score_part[t, u] = weights[u] * (grad[t, u] - mean_grad) * score_scale

    both = {(t, u): score_part[t, u] * (2.0 if t == u else 1.0) for t, u in pairs}
    both.update({(u, t): both[t, u] for t, u in pairs})
    raw.update({(u, t): raw[t, u] for t, u in pairs})
    mean_part = [
        functools.reduce(jnp.add, [both[u, v] * raw[u, v] for v in every]) * (1.0 / feat)
        for u in every
    ]

    all_mixed = []
    for group in range(feat // GROUP):
        outs = [[] for _ in every]
        for side in range(2):
            rows = pl.ds(group * GROUP + side * half, half)
            gain = load_gain(rows)
            scaled = [normed[t, rows, :] for t in every]
            above = [ups[t, rows, :] for t in every]
            mixed = jnp.zeros((half, lanes), jnp.float32)
            for u in every:
                crossed = functools.reduce(jnp.add, [both[u, v] * scaled[v] for v in every])
                mixed = mixed + crossed * scaled[u]
                from_norm = inverse[u] * (gain * crossed - scaled[u] * mean_part[u])
                direct = functools.reduce(
                    jnp.add, [value_part[t, u] * above[t] for t in range(u, frames)]
                )
                outs[u].append(direct + from_norm)
            all_mixed.append(mixed)
        for u in every:
            grad_ref[u, pl.ds(group * GROUP, GROUP), :] = jnp.concatenate(
                outs[u], axis=0
            ).astype(jnp.bfloat16)
    return jnp.concatenate(all_mixed, axis=0)


def fetch_kernel(*refs):
    *refs, arrived = refs
    number = len(refs) // 2
    copies = [
        pltpu.make_async_copy(source, target, arrived.at[index])
        for index, (source, target) in enumerate(zip(refs[:number], refs[number:]))
    ]
    for copy in copies:
        copy.start()
    for copy in copies:
        copy.wait()


def fetch(*fields):
    return pl.pallas_call(
        fetch_kernel,
        in_specs=[pl.BlockSpec(memory_space=pltpu.HBM)] * len(fields),
        out_specs=[pl.BlockSpec(memory_space=pltpu.VMEM)] * len(fields),
        out_shape=[jax.ShapeDtypeStruct(field.shape, field.dtype) for field in fields],
        scratch_shapes=[pltpu.SemaphoreType.DMA((len(fields),))],
        compiler_params=params(0),
        cost_estimate=cost(1),
        name="fetch",
    )(*[in_hbm(field) for field in fields])


def temporal_kernel(frames, spaces, length_ref, task_ref, *refs):
    attended_refs, (gain_ref, own_ref, *other_refs), refs = (
        refs[: frames - 1],
        refs[frames - 1 : frames - 1 + 2 * spaces],
        refs[frames - 1 + 2 * spaces :],
    )
    grad_refs, (mixed_ref, attended, grads, wide) = refs[:frames], refs[frames:]
    heads, lanes = own_ref.shape[1], own_ref.shape[3]
    half = frames // 2
    mixed_ref[...] = jnp.full(mixed_ref.shape, task_ref[0].astype(jnp.float32))

    def load_upstream(space, head, t, rows):
        if space == 0:
            return own_ref[t, head, rows, :]
        return other_refs[2 * space - 2 + t // half][t % half, head, rows, :]

    places = [
        pl.ds(pl.multiple_of(partner("space", space) * lanes, lanes), lanes)
        for space in range(spaces)
    ]
    for head in range(heads):
        for space, here in enumerate(places):
            attended[head, space, partner("tm", 0)] = own_ref[frames + space, head]
            for distance, ref in enumerate(attended_refs):
                attended[head, space, partner("tm", distance + 1)] = ref[head, :, here]
        mixed = [
            temporal_part(
                length_ref[0],
                lambda t, rows: attended[head, space, t, rows, :],
                functools.partial(load_upstream, space, head),
                lambda rows: gain_ref[head, rows, :],
                wide.at[head % 2, space, 0],
                wide.at[head % 2, space, 1],
                wide.at[head % 2, space, 2],
                grads.at[head, space],
            )
            for space in range(spaces)
        ]
        summed = functools.reduce(jnp.add, mixed)
        mixed_ref[pl.ds(head, 1), :] = jnp.sum(summed.T, axis=0, keepdims=True) * 0.5
        for distance, ref in enumerate(grad_refs):
            frame = partner("tm", distance)
            for space, here in enumerate(places):
                ref[head, :, here] = grads[head, space, frame]


def temporal(lengths, task_ids, attended, upstream, gain):
    _, heads, feat, lanes = upstream[0].shape
    frames, spaces = len(attended) + 1, (len(upstream) + 1) // 2
    patches = spaces * lanes
    rows = -(-(heads + 1) // 8) * 8
    operands = [*attended, gain, *upstream]
    block = (heads, spaces, frames, feat, lanes)
    results = pl.pallas_call(
        functools.partial(temporal_kernel, frames, spaces),
        in_specs=[pl.BlockSpec(memory_space=pltpu.SMEM)] * 2
        + [pl.BlockSpec(memory_space=pltpu.VMEM)] * len(operands),
        out_specs=[pl.BlockSpec(memory_space=pltpu.VMEM)] * (frames + 1),
        scratch_shapes=[
            pltpu.VMEM(block, jnp.bfloat16),
            pltpu.VMEM(block, jnp.bfloat16),
            pltpu.VMEM((2, spaces, 3, frames, feat, lanes), jnp.float32),
        ],
        out_shape=[jax.ShapeDtypeStruct((heads, feat, patches), jnp.bfloat16)] * frames
        + [jax.ShapeDtypeStruct((rows, feat), jnp.float32)],
        compiler_params=params(patches),
        cost_estimate=cost(4),
        name="temporal",
    )(lengths, task_ids, *operands)
    return list(results[:frames]), results[frames]


def gain_gradients(axis, heads, frames, clips, mixed_refs, gains_ref, grad_ref):
    tasks = gains_ref.shape[1]
    rows = sum(ref.shape[0] for ref in mixed_refs) // (frames * clips)
    each = mixed_refs[0].shape[0] // rows
    task_ids = lax.broadcasted_iota(jnp.int32, (tasks, HEAD_DIM), 0).astype(jnp.float32)
    for distance in range(frames):
        for head in range(heads):
            mixed = jnp.zeros((tasks, HEAD_DIM), jnp.float32)
            for clip in range(clips):
                block = distance * clips + clip
                ref, start = mixed_refs[block // each], block % each * rows
                task = ref[pl.ds(start + heads, 1), :]
                row = ref[pl.ds(start + head, 1), :]
                mixed = mixed + jnp.where(task_ids == task, row, 0.0)
            start = (partner(axis, distance) * heads + head) * HEAD_DIM
            cols = pl.ds(pl.multiple_of(start, HEAD_DIM), HEAD_DIM)
            grad_ref[0, :, cols] = gains_ref[1, :, cols] * mixed
            grad_ref[1, :, cols] = gains_ref[0, :, cols] * mixed


def swap(field, axis, size, distance):
    return lax.ppermute(field, axis, [(i, i ^ distance) for i in range(size)])


def split_by_heads(
    query_heads, key_heads, value_heads, cotangent, task_ids, lengths, gains, clips, frames, spaces
):
    patches, feat = query_heads.shape[2:]
    heads = feat // HEAD_DIM
    own = heads // frames
    width = own * HEAD_DIM
    queries, key_rows, values = (
        field.reshape(patches, feat) for field in (query_heads, key_heads, value_heads)
    )
    frame = lax.axis_index("tm")

    pieces = list(pack(cotangent.reshape(cotangent.shape[2:]), frames, spaces))
    queries, pieces = lax.optimization_barrier((queries, pieces))
    for distance in range(1, frames):
        pieces[distance] = swap(pieces[distance], "tm", frames, distance)
    fields = (queries, key_rows, values)
    weights, attended = forward("tm", *fields, frames)
    for distance in range(1, frames):
        attended[distance] = swap(attended[distance], "tm", frames, distance)
    backwards, _ = lax.optimization_barrier((pieces[::-1], weights))
    upstream = list(turn(backwards[::-1], attended[0]))
    for index in range(1, len(upstream)):
        upstream[index] = swap(upstream[index], "space", spaces, (index + 1) // 2)
    rows = lax.dynamic_index_in_dim(gains, task_ids[0], 1, keepdims=False)
    product = lax.dynamic_slice_in_dim(rows[0] * rows[1], frame * width, width, 0)
    gain = jnp.broadcast_to(
        product.reshape(own, HEAD_DIM, 1), (own, HEAD_DIM, patches // spaces)
    )
    attended[1], gain, upstream[0] = lax.optimization_barrier((attended[1], gain, upstream[0]))
    upstream[0], *kept = fetch(upstream[0], *fields)
    grads, mixed = temporal(lengths, task_ids, attended[1:], upstream, gain)
    for distance in reversed(range(1, frames)):
        grads[distance] = swap(grads[distance], "tm", frames, distance)
    here = grads[0]
    for bit in range(clips.bit_length() - 1):
        other = swap(mixed, "dp", clips, 1 << bit)
        if bit == 0:
            here, other = lax.optimization_barrier((here, other))
        mixed = jnp.concatenate([mixed, other], axis=0)
    results = backward("tm", kept, weights, [here], [0])
    mixed, results = lax.optimization_barrier((mixed, results))
    near, grads[1] = lax.optimization_barrier((mixed, grads[1]))
    mixed = [mixed, swap(near, "tm", frames, 1)] + [
        swap(mixed, "tm", frames, distance) for distance in range(2, frames)
    ]
    last = range(frames - 1, 0, -1)
    if frames > 2:
        results = backward("tm", kept, weights, [grads[1]], [1], results)
        last = range(frames - 1, 1, -1)
    grad_queries, grad_keys, grad_gains = backward(
        "tm",
        kept,
        weights,
        [grads[distance] for distance in last],
        list(last),
        results,
        mixed,
        gains,
        (own, frames, clips),
    )
    return (
        grad_queries.reshape(query_heads.shape),
        grad_keys.reshape(query_heads.shape),
        grad_gains,
    )


def temporal_grads(attended, upstream, gain_query, gain_keys, length):
    highest = lax.Precision.HIGHEST
    frames = attended.shape[0]
    score_scale = attended.shape[-1] ** (-0.5)
    floats = attended.astype(jnp.float32)
    inverse_rms = lax.rsqrt(jnp.mean(floats * floats, axis=-1, keepdims=True) + 1e-06)
    normed = floats * inverse_rms
    t_query = normed * gain_query
    t_keys = normed * gain_keys
    scores = jnp.einsum("txhd,uxhd->xhtu", t_query, t_keys, precision=highest) * score_scale
    frame_ids = jnp.arange(frames, dtype=jnp.int32)
    allowed = (frame_ids[None, :] <= frame_ids[:, None]) & (frame_ids[None, :] < length)
    scores = jnp.where(allowed, scores, -1e30)
    weights = jax.nn.softmax(scores, axis=-1)
    weights_low = lax.optimization_barrier(weights.astype(jnp.bfloat16)).astype(jnp.float32)
    valid_rows = (frame_ids < length).astype(jnp.float32)
    masked = upstream.astype(jnp.float32) * valid_rows[:, None, None, None]
    grad_weights = jnp.einsum("txhd,uxhd->xhtu", masked, floats, precision=highest)
    from_values = jnp.einsum("xhtu,txhd->uxhd", weights_low, masked, precision=highest)
    grad_scores = (
        weights
        * (grad_weights - jnp.sum(grad_weights * weights, axis=-1, keepdims=True))
        * score_scale
    )
    grad_tquery = jnp.einsum("xhtu,uxhd->txhd", grad_scores, t_keys, precision=highest)
    grad_tkeys = jnp.einsum("xhtu,txhd->uxhd", grad_scores, t_query, precision=highest)
    grad_normed = grad_tquery * gain_query + grad_tkeys * gain_keys
    grad_gain_query = jnp.sum(grad_tquery * normed, axis=(0, 1))
    grad_gain_keys = jnp.sum(grad_tkeys * normed, axis=(0, 1))
    from_norm = inverse_rms * (
        grad_normed - normed * jnp.mean(grad_normed * normed, axis=-1, keepdims=True)
    )
    grad_total = (masked + from_values + from_norm).astype(jnp.bfloat16)
    return (grad_total, grad_gain_query, grad_gain_keys)


def split_by_patches(query_heads, key_heads, value_heads, cotangent, task_ids, lengths, gains):
    patches, feat = query_heads.shape[2:]
    heads = feat // HEAD_DIM
    queries, key_rows, values = (
        field.reshape(patches, feat) for field in (query_heads, key_heads, value_heads)
    )
    fields = (queries, key_rows, values)
    weights, attended = forward(None, *fields, 1)
    attended_field = jnp.transpose(attended[0], (2, 0, 1)).reshape(1, 1, patches, feat)
    upstream = lax.all_to_all(
        lax.all_to_all(cotangent, "space", split_axis=3, concat_axis=2, tiled=True),
        "tm",
        split_axis=2,
        concat_axis=1,
        tiled=True,
    )
    frames_attended = lax.all_to_all(attended_field, "tm", split_axis=2, concat_axis=1, tiled=True)
    frames, local_patches = frames_attended.shape[1:3]
    selector = (task_ids[0] == jnp.arange(gains.shape[1], dtype=jnp.int32)).astype(jnp.float32)
    gain_query = jnp.sum(selector[:, None] * gains[0], axis=0).reshape(heads, HEAD_DIM)
    gain_keys = jnp.sum(selector[:, None] * gains[1], axis=0).reshape(heads, HEAD_DIM)
    grad_total, grad_gq, grad_gk = temporal_grads(
        frames_attended.reshape(frames, local_patches, heads, HEAD_DIM),
        upstream.reshape(frames, local_patches, heads, HEAD_DIM),
        gain_query,
        gain_keys,
        lengths[0],
    )
    gain_terms = jnp.stack(
        [
            selector[:, None] * grad_gq.reshape(1, feat),
            selector[:, None] * grad_gk.reshape(1, feat),
        ]
    )
    grad_gains = lax.psum(gain_terms, ("dp", "tm"))
    returned = lax.all_to_all(
        grad_total.reshape(1, frames, local_patches, feat),
        "tm",
        split_axis=1,
        concat_axis=2,
        tiled=True,
    )
    head_grads = jnp.transpose(returned.reshape(patches, heads, HEAD_DIM), (1, 2, 0))
    grad_queries, grad_keys = backward(None, fields, weights, [head_grads], [0])
    return (
        grad_queries.reshape(query_heads.shape),
        grad_keys.reshape(query_heads.shape),
        grad_gains,
    )


def solution(mesh):
    clips, frames, spaces = (mesh.shape[axis] for axis in ("dp", "tm", "space"))

    def local(query_heads, *others):
        heads = query_heads.shape[3] // HEAD_DIM
        powers = all(size & (size - 1) == 0 for size in (clips, frames, spaces))
        if powers and 2 <= frames <= 4 and heads % frames == 0:
            return split_by_heads(query_heads, *others, clips, frames, spaces)
        return split_by_patches(query_heads, *others)

    return jax.shard_map(
        local,
        mesh=mesh,
        in_specs=(
            P("dp", "tm", None, "space"),
            P("dp", "tm", None, "space"),
            P("dp", "tm", None, "space"),
            P("dp", "tm", "space", None),
            P("dp"),
            P("dp"),
            P(None, None, "space"),
        ),
        out_specs=(
            P("dp", "tm", None, "space"),
            P("dp", "tm", None, "space"),
            P(None, None, "space"),
        ),
        check_vma=False,
    )
```

```python
import functools

import jax
import jax.numpy as jnp
from jax import lax
from jax.experimental import pallas as pl
from jax.experimental.pallas import tpu as pltpu
from jax.sharding import PartitionSpec as P

HEAD_DIM = 128
GROUP = 16
MIB = 1024 * 1024


def params(patches):
    return pltpu.CompilerParams(vmem_limit_bytes=(16 if patches <= 512 else 60) * MIB)


def cost(microseconds):
    return pl.CostEstimate(flops=int(microseconds * 1e8), bytes_accessed=0, transcendentals=0)


def in_hbm(field):
    return pltpu.with_memory_space_constraint(field, pltpu.HBM)


def columns_dot(left, right):
    return lax.dot_general(
        left, right, (((1,), (1,)), ((), ())), preferred_element_type=jnp.float32
    )


def dot(left, right):
    return jnp.dot(left, right, preferred_element_type=jnp.float32)


def partner(axis, distance):
    return distance if axis is None else jnp.bitwise_xor(lax.axis_index(axis), distance)


def forward_kernel(axis, query_ref, key_ref, value_ref, weights_ref, *refs):
    (queries, key_rows, values, arrived), attended_refs = refs[-4:], refs[:-4]
    score_scale = HEAD_DIM ** (-0.5)
    groups, _, width = queries.shape
    own = width // HEAD_DIM
    copies = []
    for group in range(groups):
        cols = pl.ds(pl.multiple_of(partner(axis, group) * width, HEAD_DIM), width)
        for field, (source, target) in enumerate(
            ((query_ref, queries), (key_ref, key_rows), (value_ref, values))
        ):
            copy = pltpu.make_async_copy(
                source.at[:, cols], target.at[group], arrived.at[group, field]
            )
            copy.start()
            copies.append(copy)
    for group in range(groups):
        for copy in copies[3 * group : 3 * group + 3]:
            copy.wait()
        for head in range(own):
            cols = pl.ds(head * HEAD_DIM, HEAD_DIM)
            scores = columns_dot(key_rows[group, :, cols], queries[group, :, cols])
            largest = jnp.max(scores, axis=0, keepdims=True)
            raised = jnp.exp((scores - largest) * score_scale)
            weights = raised * (1.0 / jnp.sum(raised, axis=0, keepdims=True))
            weights_ref[group * own + head] = weights
            attended = dot(values[group, :, cols].T, weights.astype(jnp.bfloat16))
            attended_refs[group][head] = attended.astype(jnp.bfloat16)


def forward(axis, queries, key_rows, values, groups):
    patches, feat = queries.shape
    heads = feat // HEAD_DIM
    own = heads // groups
    fields = [in_hbm(field) for field in (queries, key_rows, values)]
    weights, *attended = pl.pallas_call(
        functools.partial(forward_kernel, axis),
        in_specs=[pl.BlockSpec(memory_space=pltpu.HBM)] * 3,
        out_specs=[pl.BlockSpec(memory_space=pltpu.VMEM)] * (1 + groups),
        scratch_shapes=[pltpu.VMEM((groups, patches, feat // groups), jnp.bfloat16)] * 3
        + [pltpu.SemaphoreType.DMA((groups, 3))],
        out_shape=[jax.ShapeDtypeStruct((heads, patches, patches), jnp.float32)]
        + [jax.ShapeDtypeStruct((own, HEAD_DIM, patches), jnp.bfloat16)] * groups,
        compiler_params=params(patches),
        cost_estimate=cost(6),
        name="spatial_forward",
    )(*fields)
    return weights, attended


def backward_kernel(axis, distances, gains_of, *refs):
    (query_ref, key_ref, value_ref), weights_ref, refs = refs[:3], refs[3], refs[4:]
    grad_refs, refs = refs[: len(distances)], refs[len(distances) :]
    *refs, gq, gk, sent = refs
    score_scale = HEAD_DIM ** (-0.5)
    own = grad_refs[0].shape[0]
    copies = []

    def send(source, target, semaphore):
        copy = pltpu.make_async_copy(source, target, semaphore)
        copy.start()
        copies.append(copy)

    if gains_of:
        *mixed_refs, gains_ref, _, _, gq_ref, gk_ref, grad_gains_ref, grad_gains = refs
        gain_gradients(axis, *gains_of, mixed_refs, gains_ref, grad_gains)
        send(grad_gains, grad_gains_ref, sent.at[len(distances), 0])
    else:
        gq_ref, gk_ref = refs[-2:]
    starts = [partner(axis, distance) * (own * HEAD_DIM) for distance in distances]
    heads = [(group, head) for group in range(len(distances)) for head in range(own)]
    columns = [
        pl.ds(pl.multiple_of(starts[group] + head * HEAD_DIM, HEAD_DIM), HEAD_DIM)
        for group, head in heads
    ]
    spatial_grads = [
        dot(value_ref[:, cols], grad_refs[group][head])
        for cols, (group, head) in zip(columns, heads)
    ]
    all_scores = []
    for spatial_grad, (group, head) in zip(spatial_grads, heads):
        weights = weights_ref[distances[group] * own + head]
        row_sum = jnp.sum(spatial_grad * weights, axis=0, keepdims=True)
        scores = weights * (spatial_grad - row_sum) * score_scale
        all_scores.append(scores.astype(jnp.bfloat16))
    there = [pl.ds(pl.multiple_of(start, HEAD_DIM), own * HEAD_DIM) for start in starts]
    for scores, cols, (group, head) in zip(all_scores, columns, heads):
        here = pl.ds(head * HEAD_DIM, HEAD_DIM)
        gk[group, :, here] = dot(scores, query_ref[:, cols]).astype(jnp.bfloat16)
    for group, cols in enumerate(there):
        send(gk.at[group], gk_ref.at[:, cols], sent.at[group, 1])
    for scores, cols, (group, head) in zip(all_scores, columns, heads):
        here = pl.ds(head * HEAD_DIM, HEAD_DIM)
        gq[group, :, here] = dot(key_ref[:, cols].T, scores).astype(jnp.bfloat16).T
    for group, cols in enumerate(there):
        send(gq.at[group], gq_ref.at[:, cols], sent.at[group, 0])
    for copy in copies:
        copy.wait()


def backward(axis, fields, weights, grads, distances, earlier=(), mixed=(), gains=None, gains_of=()):
    patches, feat = fields[0].shape
    own = grads[0].shape[0]
    operands = [*fields, weights, *grads] + ([*mixed, gains] if gains_of else [])
    block = pltpu.VMEM((len(distances), patches, own * HEAD_DIM), jnp.bfloat16)
    out_shape = [jax.ShapeDtypeStruct((patches, feat), jnp.bfloat16)] * 2
    scratch = [block, block, pltpu.SemaphoreType.DMA((len(distances) + 1, 2))]
    if gains_of:
        out_shape.append(jax.ShapeDtypeStruct(gains.shape, jnp.float32))
        scratch.insert(0, pltpu.VMEM(gains.shape, jnp.float32))
    return pl.pallas_call(
        functools.partial(backward_kernel, axis, distances, gains_of),
        in_specs=[pl.BlockSpec(memory_space=pltpu.VMEM)] * len(operands)
        + [pl.BlockSpec(memory_space=pl.ANY)] * len(earlier),
        out_specs=[pl.BlockSpec(memory_space=pl.ANY)] * len(out_shape),
        scratch_shapes=scratch,
        out_shape=out_shape,
        input_output_aliases={len(operands) + index: index for index in range(len(earlier))},
        compiler_params=params(patches),
        cost_estimate=cost(2),
        name="spatial_backward",
    )(*operands, *earlier)


def pack_kernel(field_ref, *refs):
    *packed_refs, rows, arrived = refs
    chunks, size, _ = rows.shape
    spaces, _, width = packed_refs[0].shape
    copies = [
        pltpu.make_async_copy(
            field_ref.at[pl.ds(chunk * size, size), :], rows.at[chunk], arrived.at[chunk]
        )
        for chunk in range(chunks)
    ]
    for copy in copies:
        copy.start()
    for chunk, copy in enumerate(copies):
        copy.wait()
        for distance, packed_ref in enumerate(packed_refs):
            for space in range(spaces):
                start = (space * len(packed_refs) + partner("tm", distance)) * width
                cols = pl.ds(pl.multiple_of(start, HEAD_DIM), width)
                packed_ref[space, pl.ds(chunk * size, size), :] = rows[chunk, :, cols]


def pack(field, frames, spaces):
    patches, feat = field.shape
    chunks = patches // GROUP
    shape = (spaces, patches, feat // (frames * spaces))
    return pl.pallas_call(
        pack_kernel,
        in_specs=[pl.BlockSpec(memory_space=pltpu.HBM)],
        out_specs=[pl.BlockSpec(memory_space=pltpu.VMEM)] * frames,
        out_shape=[jax.ShapeDtypeStruct(shape, field.dtype)] * frames,
        scratch_shapes=[
            pltpu.VMEM((chunks, patches // chunks, feat), field.dtype),
            pltpu.SemaphoreType.DMA((chunks,)),
        ],
        compiler_params=params(patches),
        cost_estimate=cost(1),
        name="pack_cotangent",
    )(in_hbm(field))


def turn_kernel(frames, *refs):
    piece_refs, (plane_ref, own_hbm, *other_refs), (turned, own_ref, sent) = (
        refs[:frames][::-1],
        refs[frames:-3],
        refs[-3:],
    )
    spaces, lanes, _ = piece_refs[0].shape
    for space in range(spaces):
        place = pl.multiple_of(partner("space", space) * lanes, lanes)
        own_ref[frames + space] = plane_ref[:, :, pl.ds(place, lanes)]
    heads = own_ref.shape[1]
    for space in range(spaces):
        target = turned if space else own_ref
        source = partner("space", space)
        for distance, ref in enumerate(piece_refs):
            frame = partner("tm", distance)
            for head in range(heads):
                cols = pl.ds(head * HEAD_DIM, HEAD_DIM)
                target[frame, head] = ref[source, :, cols].T
        if space == 0:
            copy = pltpu.make_async_copy(own_ref, own_hbm, sent)
            copy.start()
        else:
            half = frames // 2
            other_refs[2 * space - 2][...] = turned[:half]
            other_refs[2 * space - 1][...] = turned[half:]
    copy.wait()


def turn(pieces, plane):
    spaces, patches, feat = pieces[0].shape
    frames, heads = len(pieces), feat // HEAD_DIM
    turned = (heads, HEAD_DIM, patches)
    sizes = [frames + spaces] + [frames // 2, frames - frames // 2] * (spaces - 1)
    return pl.pallas_call(
        functools.partial(turn_kernel, frames),
        in_specs=[pl.BlockSpec(memory_space=pltpu.VMEM)] * (frames + 1),
        out_specs=[pl.BlockSpec(memory_space=pltpu.HBM)]
        + [pl.BlockSpec(memory_space=pltpu.VMEM)] * (len(sizes) - 1),
        out_shape=[jax.ShapeDtypeStruct((size,) + turned, pieces[0].dtype) for size in sizes],
        scratch_shapes=[
            pltpu.VMEM((frames,) + turned, pieces[0].dtype),
            pltpu.VMEM((frames + spaces,) + turned, pieces[0].dtype),
            pltpu.SemaphoreType.DMA,
        ],
        compiler_params=params(patches),
        cost_estimate=cost(2),
        name="turn_cotangent",
    )(*reversed(pieces), plane)


def temporal_part(length, load_upstream, load_gain, fields, ups, normed, grad_ref):
    frames, feat, lanes = grad_ref.shape
    half = GROUP // 2
    score_scale = feat ** (-0.5)
    pairs = [(t, u) for t in range(frames) for u in range(t + 1)]
    every = range(frames)
    valid = [jnp.where(t < length, 1.0, 0.0).astype(jnp.float32) for t in every]
    bias = [jnp.where(u < length, 0.0, -1e30).astype(jnp.float32) for u in every]

    def total(piece):
        return jnp.broadcast_to(jnp.sum(piece, axis=0, keepdims=True), (half, lanes))

    squares = [jnp.zeros((half, lanes), jnp.float32) for _ in every]
    for group in range(feat // GROUP):
        rows = pl.ds(group * GROUP, GROUP)
        for t in every:
            field = fields[t, rows, :]
            ups[t, rows, :] = load_upstream(t, rows).astype(jnp.float32)
            low, high = field[:half], field[half:]
            squares[t] = squares[t] + (low * low + high * high)
    inverse = [lax.rsqrt(total(squares[t]) * (1.0 / feat) + 1e-06) for t in every]

    raw = {pair: jnp.zeros((half, lanes), jnp.float32) for pair in pairs}
    grad = {pair: jnp.zeros((half, lanes), jnp.float32) for pair in pairs}
    for group in range(feat // half):
        rows = pl.ds(group * half, half)
        gain = load_gain(rows)
        here = [fields[t, rows, :] for t in every]
        above = [ups[t, rows, :] for t in every]
        scaled = [here[t] * inverse[t] for t in every]
        gained = [scaled[t] * gain for t in every]
        for t in every:
            normed[t, rows, :] = scaled[t]
        for t, u in pairs:
            raw[t, u] = raw[t, u] + gained[t] * scaled[u]
            grad[t, u] = grad[t, u] + above[t] * here[u]

    value_part, score_part = {}, {}
    for t in every:
        seen = range(t + 1)
        for u in seen:
            raw[t, u] = total(raw[t, u])
            grad[t, u] = total(grad[t, u]) * valid[t]
        scores = [raw[t, u] * score_scale + bias[u] for u in seen]
        largest = functools.reduce(jnp.maximum, scores)
        raised = [jnp.exp(score - largest) for score in scores]
        over = 1.0 / functools.reduce(jnp.add, raised)
        weights = [piece * over for piece in raised]
        mean_grad = functools.reduce(jnp.add, [weights[u] * grad[t, u] for u in seen])
        for u in seen:
            rounded = weights[u].astype(jnp.bfloat16).astype(jnp.float32)
            value_part[t, u] = (rounded + (1.0 if u == t else 0.0)) * valid[t]
            score_part[t, u] = weights[u] * (grad[t, u] - mean_grad) * score_scale

    both = {(t, u): score_part[t, u] * (2.0 if t == u else 1.0) for t, u in pairs}
    both.update({(u, t): both[t, u] for t, u in pairs})
    raw.update({(u, t): raw[t, u] for t, u in pairs})
    mean_part = [
        functools.reduce(jnp.add, [both[u, v] * raw[u, v] for v in every])
        * (1.0 / feat)
        * inverse[u]
        for u in every
    ]
    both = {(u, v): both[u, v] * inverse[u] for u in every for v in every}

    all_mixed = []
    for group in range(feat // GROUP):
        outs = [[] for _ in every]
        for side in range(2):
            rows = pl.ds(group * GROUP + side * half, half)
            gain = load_gain(rows)
            here = [fields[t, rows, :] for t in every]
            scaled = [normed[t, rows, :] for t in every]
            above = [ups[t, rows, :] for t in every]
            mixed = jnp.zeros((half, lanes), jnp.float32)
            for u in every:
                crossed = functools.reduce(jnp.add, [both[u, v] * scaled[v] for v in every])
                mixed = mixed + crossed * here[u]
                from_norm = gain * crossed - scaled[u] * mean_part[u]
                direct = functools.reduce(
                    jnp.add, [value_part[t, u] * above[t] for t in range(u, frames)]
                )
                outs[u].append(direct + from_norm)
            all_mixed.append(mixed)
        for u in every:
            grad_ref[u, pl.ds(group * GROUP, GROUP), :] = jnp.concatenate(
                outs[u], axis=0
            ).astype(jnp.bfloat16)
    return jnp.concatenate(all_mixed, axis=0)


def fetch_kernel(*refs):
    *refs, arrived = refs
    number = len(refs) // 2
    copies = [
        pltpu.make_async_copy(source, target, arrived.at[index])
        for index, (source, target) in enumerate(zip(refs[:number], refs[number:]))
    ]
    for copy in copies:
        copy.start()
    for copy in copies:
        copy.wait()


def fetch(*fields):
    return pl.pallas_call(
        fetch_kernel,
        in_specs=[pl.BlockSpec(memory_space=pltpu.HBM)] * len(fields),
        out_specs=[pl.BlockSpec(memory_space=pltpu.VMEM)] * len(fields),
        out_shape=[jax.ShapeDtypeStruct(field.shape, field.dtype) for field in fields],
        scratch_shapes=[pltpu.SemaphoreType.DMA((len(fields),))],
        compiler_params=params(0),
        cost_estimate=cost(1),
        name="fetch",
    )(*[in_hbm(field) for field in fields])


def temporal_kernel(frames, spaces, length_ref, task_ref, *refs):
    attended_refs, (gain_ref, own_ref, *other_refs), refs = (
        refs[: frames - 1],
        refs[frames - 1 : frames - 1 + 2 * spaces],
        refs[frames - 1 + 2 * spaces :],
    )
    grad_refs, (mixed_ref, grads, wide) = refs[:frames], refs[frames:]
    heads, lanes = own_ref.shape[1], own_ref.shape[3]
    half = frames // 2
    mixed_ref[...] = jnp.full(mixed_ref.shape, task_ref[0].astype(jnp.float32))

    def load_upstream(space, head, t, rows):
        if space == 0:
            return own_ref[t, head, rows, :]
        return other_refs[2 * space - 2 + t // half][t % half, head, rows, :]

    places = [
        pl.ds(pl.multiple_of(partner("space", space) * lanes, lanes), lanes)
        for space in range(spaces)
    ]
    for head in range(heads):
        for space, here in enumerate(places):
            fields = wide.at[head, space, 0]
            fields[partner("tm", 0)] = own_ref[frames + space, head].astype(jnp.float32)
            for distance, ref in enumerate(attended_refs):
                plane = ref[head, :, here].astype(jnp.float32)
                fields[partner("tm", distance + 1)] = plane
        mixed = [
            temporal_part(
                length_ref[0],
                functools.partial(load_upstream, space, head),
                lambda rows: gain_ref[head, rows, :],
                wide.at[head, space, 0],
                wide.at[head, space, 1],
                wide.at[head, space, 2],
                grads.at[head, space],
            )
            for space in range(spaces)
        ]
        summed = functools.reduce(jnp.add, mixed)
        mixed_ref[pl.ds(head, 1), :] = jnp.sum(summed.T, axis=0, keepdims=True) * 0.5
        for distance, ref in enumerate(grad_refs):
            frame = partner("tm", distance)
            for space, here in enumerate(places):
                ref[head, :, here] = grads[head, space, frame]


def temporal(lengths, task_ids, attended, upstream, gain):
    _, heads, feat, lanes = upstream[0].shape
    frames, spaces = len(attended) + 1, (len(upstream) + 1) // 2
    patches = spaces * lanes
    rows = -(-(heads + 1) // 8) * 8
    operands = [*attended, gain, *upstream]
    block = (heads, spaces, frames, feat, lanes)
    results = pl.pallas_call(
        functools.partial(temporal_kernel, frames, spaces),
        in_specs=[pl.BlockSpec(memory_space=pltpu.SMEM)] * 2
        + [pl.BlockSpec(memory_space=pltpu.VMEM)] * len(operands),
        out_specs=[pl.BlockSpec(memory_space=pltpu.VMEM)] * (frames + 1),
        scratch_shapes=[
            pltpu.VMEM(block, jnp.bfloat16),
            pltpu.VMEM((heads, spaces, 3, frames, feat, lanes), jnp.float32),
        ],
        out_shape=[jax.ShapeDtypeStruct((heads, feat, patches), jnp.bfloat16)] * frames
        + [jax.ShapeDtypeStruct((rows, feat), jnp.float32)],
        compiler_params=params(patches),
        cost_estimate=cost(4),
        name="temporal",
    )(lengths, task_ids, *operands)
    return list(results[:frames]), results[frames]


def gain_gradients(axis, heads, frames, clips, mixed_refs, gains_ref, grad_ref):
    tasks = gains_ref.shape[1]
    rows = sum(ref.shape[0] for ref in mixed_refs) // (frames * clips)
    each = mixed_refs[0].shape[0] // rows
    task_ids = lax.broadcasted_iota(jnp.int32, (tasks, HEAD_DIM), 0).astype(jnp.float32)
    for distance in range(frames):
        for head in range(heads):
            mixed = jnp.zeros((tasks, HEAD_DIM), jnp.float32)
            for clip in range(clips):
                block = distance * clips + clip
                ref, start = mixed_refs[block // each], block % each * rows
                task = ref[pl.ds(start + heads, 1), :]
                row = ref[pl.ds(start + head, 1), :]
                mixed = mixed + jnp.where(task_ids == task, row, 0.0)
            start = (partner(axis, distance) * heads + head) * HEAD_DIM
            cols = pl.ds(pl.multiple_of(start, HEAD_DIM), HEAD_DIM)
            grad_ref[0, :, cols] = gains_ref[1, :, cols] * mixed
            grad_ref[1, :, cols] = gains_ref[0, :, cols] * mixed


def swap(field, axis, size, distance):
    return lax.ppermute(field, axis, [(i, i ^ distance) for i in range(size)])


def split_by_heads(
    query_heads, key_heads, value_heads, cotangent, task_ids, lengths, gains, clips, frames, spaces
):
    patches, feat = query_heads.shape[2:]
    heads = feat // HEAD_DIM
    own = heads // frames
    width = own * HEAD_DIM
    queries, key_rows, values = (
        field.reshape(patches, feat) for field in (query_heads, key_heads, value_heads)
    )
    frame = lax.axis_index("tm")

    pieces = list(pack(cotangent.reshape(cotangent.shape[2:]), frames, spaces))
    queries, pieces = lax.optimization_barrier((queries, pieces))
    for distance in range(1, frames):
        pieces[distance] = swap(pieces[distance], "tm", frames, distance)
    fields = (queries, key_rows, values)
    weights, attended = forward("tm", *fields, frames)
    for distance in range(1, frames):
        attended[distance] = swap(attended[distance], "tm", frames, distance)
    backwards, _ = lax.optimization_barrier((pieces[::-1], weights))
    upstream = list(turn(backwards[::-1], attended[0]))
    for index in range(1, len(upstream)):
        upstream[index] = swap(upstream[index], "space", spaces, (index + 1) // 2)
    rows = lax.dynamic_index_in_dim(gains, task_ids[0], 1, keepdims=False)
    product = lax.dynamic_slice_in_dim(rows[0] * rows[1], frame * width, width, 0)
    gain = jnp.broadcast_to(
        product.reshape(own, HEAD_DIM, 1), (own, HEAD_DIM, patches // spaces)
    )
    attended[1], gain, upstream[0] = lax.optimization_barrier((attended[1], gain, upstream[0]))
    upstream[0], *kept = fetch(upstream[0], *fields)
    grads, mixed = temporal(lengths, task_ids, attended[1:], upstream, gain)
    for distance in reversed(range(1, frames)):
        grads[distance] = swap(grads[distance], "tm", frames, distance)
    here = grads[0]
    for bit in range(clips.bit_length() - 1):
        other = swap(mixed, "dp", clips, 1 << bit)
        if bit == 0:
            here, other = lax.optimization_barrier((here, other))
        mixed = jnp.concatenate([mixed, other], axis=0)
    results = backward("tm", kept, weights, [here], [0])
    mixed, results = lax.optimization_barrier((mixed, results))
    near, grads[1] = lax.optimization_barrier((mixed, grads[1]))
    mixed = [mixed, swap(near, "tm", frames, 1)] + [
        swap(mixed, "tm", frames, distance) for distance in range(2, frames)
    ]
    last = range(frames - 1, 0, -1)
    if frames > 2:
        results = backward("tm", kept, weights, [grads[1]], [1], results)
        last = range(frames - 1, 1, -1)
    grad_queries, grad_keys, grad_gains = backward(
        "tm",
        kept,
        weights,
        [grads[distance] for distance in last],
        list(last),
        results,
        mixed,
        gains,
        (own, frames, clips),
    )
    return (
        grad_queries.reshape(query_heads.shape),
        grad_keys.reshape(query_heads.shape),
        grad_gains,
    )


def temporal_grads(attended, upstream, gain_query, gain_keys, length):
    highest = lax.Precision.HIGHEST
    frames = attended.shape[0]
    score_scale = attended.shape[-1] ** (-0.5)
    floats = attended.astype(jnp.float32)
    inverse_rms = lax.rsqrt(jnp.mean(floats * floats, axis=-1, keepdims=True) + 1e-06)
    normed = floats * inverse_rms
    t_query = normed * gain_query
    t_keys = normed * gain_keys
    scores = jnp.einsum("txhd,uxhd->xhtu", t_query, t_keys, precision=highest) * score_scale
    frame_ids = jnp.arange(frames, dtype=jnp.int32)
    allowed = (frame_ids[None, :] <= frame_ids[:, None]) & (frame_ids[None, :] < length)
    scores = jnp.where(allowed, scores, -1e30)
    weights = jax.nn.softmax(scores, axis=-1)
    weights_low = lax.optimization_barrier(weights.astype(jnp.bfloat16)).astype(jnp.float32)
    valid_rows = (frame_ids < length).astype(jnp.float32)
    masked = upstream.astype(jnp.float32) * valid_rows[:, None, None, None]
    grad_weights = jnp.einsum("txhd,uxhd->xhtu", masked, floats, precision=highest)
    from_values = jnp.einsum("xhtu,txhd->uxhd", weights_low, masked, precision=highest)
    grad_scores = (
        weights
        * (grad_weights - jnp.sum(grad_weights * weights, axis=-1, keepdims=True))
        * score_scale
    )
    grad_tquery = jnp.einsum("xhtu,uxhd->txhd", grad_scores, t_keys, precision=highest)
    grad_tkeys = jnp.einsum("xhtu,txhd->uxhd", grad_scores, t_query, precision=highest)
    grad_normed = grad_tquery * gain_query + grad_tkeys * gain_keys
    grad_gain_query = jnp.sum(grad_tquery * normed, axis=(0, 1))
    grad_gain_keys = jnp.sum(grad_tkeys * normed, axis=(0, 1))
    from_norm = inverse_rms * (
        grad_normed - normed * jnp.mean(grad_normed * normed, axis=-1, keepdims=True)
    )
    grad_total = (masked + from_values + from_norm).astype(jnp.bfloat16)
    return (grad_total, grad_gain_query, grad_gain_keys)


def split_by_patches(query_heads, key_heads, value_heads, cotangent, task_ids, lengths, gains):
    patches, feat = query_heads.shape[2:]
    heads = feat // HEAD_DIM
    queries, key_rows, values = (
        field.reshape(patches, feat) for field in (query_heads, key_heads, value_heads)
    )
    fields = (queries, key_rows, values)
    weights, attended = forward(None, *fields, 1)
    attended_field = jnp.transpose(attended[0], (2, 0, 1)).reshape(1, 1, patches, feat)
    upstream = lax.all_to_all(
        lax.all_to_all(cotangent, "space", split_axis=3, concat_axis=2, tiled=True),
        "tm",
        split_axis=2,
        concat_axis=1,
        tiled=True,
    )
    frames_attended = lax.all_to_all(attended_field, "tm", split_axis=2, concat_axis=1, tiled=True)
    frames, local_patches = frames_attended.shape[1:3]
    selector = (task_ids[0] == jnp.arange(gains.shape[1], dtype=jnp.int32)).astype(jnp.float32)
    gain_query = jnp.sum(selector[:, None] * gains[0], axis=0).reshape(heads, HEAD_DIM)
    gain_keys = jnp.sum(selector[:, None] * gains[1], axis=0).reshape(heads, HEAD_DIM)
    grad_total, grad_gq, grad_gk = temporal_grads(
        frames_attended.reshape(frames, local_patches, heads, HEAD_DIM),
        upstream.reshape(frames, local_patches, heads, HEAD_DIM),
        gain_query,
        gain_keys,
        lengths[0],
    )
    gain_terms = jnp.stack(
        [
            selector[:, None] * grad_gq.reshape(1, feat),
            selector[:, None] * grad_gk.reshape(1, feat),
        ]
    )
    grad_gains = lax.psum(gain_terms, ("dp", "tm"))
    returned = lax.all_to_all(
        grad_total.reshape(1, frames, local_patches, feat),
        "tm",
        split_axis=1,
        concat_axis=2,
        tiled=True,
    )
    head_grads = jnp.transpose(returned.reshape(patches, heads, HEAD_DIM), (1, 2, 0))
    grad_queries, grad_keys = backward(None, fields, weights, [head_grads], [0])
    return (
        grad_queries.reshape(query_heads.shape),
        grad_keys.reshape(query_heads.shape),
        grad_gains,
    )


def solution(mesh):
    clips, frames, spaces = (mesh.shape[axis] for axis in ("dp", "tm", "space"))

    def local(query_heads, *others):
        heads = query_heads.shape[3] // HEAD_DIM
        powers = all(size & (size - 1) == 0 for size in (clips, frames, spaces))
        if powers and 2 <= frames <= 4 and heads % frames == 0:
            return split_by_heads(query_heads, *others, clips, frames, spaces)
        return split_by_patches(query_heads, *others)

    return jax.shard_map(
        local,
        mesh=mesh,
        in_specs=(
            P("dp", "tm", None, "space"),
            P("dp", "tm", None, "space"),
            P("dp", "tm", None, "space"),
            P("dp", "tm", "space", None),
            P("dp"),
            P("dp"),
            P(None, None, "space"),
        ),
        out_specs=(
            P("dp", "tm", None, "space"),
            P("dp", "tm", None, "space"),
            P(None, None, "space"),
        ),
        check_vma=False,
    )
```
